128 devices in a mesh: seq: 8 (over z, core), shard: 16 (over x, y).
Axes of the slice: x: 4, y: 4, z: 4, core: 2. Of those that a mesh axis runs over, the one named last changes fastest.
Arguments:
- block_input: bfloat16 [16, 1024, 1536], P('shard', 'seq'), may hold values from -6 to 6
- lengths: int32 [16], P('shard'), may hold values from 256 to 1024, as said below
- routes: int32 [16, 1024, 6], P('shard', 'seq'), may hold values from 0 to 31, all different within a row; in each aligned block of 128 rows (0 to 127, 128 to 255, ..., all dimensions but the last counted through in order) at most 32 rows name the same one
- out_cotangent: bfloat16 [16, 1024, 1536], P('shard', 'seq'), may hold values from -6 to 6
- mixer_gain: bfloat16 [1536], P('shard'), may hold values from 0.5 to 1.5
- in_weight: bfloat16 [1536, 6448], P('shard'), may hold values from -0.15625 to 0.15625
- conv_weight: bfloat16 [4, 3328], P(None, 'shard'), may hold values from -3 to 3
- conv_bias: bfloat16 [3328], P('shard'), may hold values from -3 to 3
- step_bias: bfloat16 [48], P('shard'), may hold values from -5 to -1
- decay_log: bfloat16 [48], P('shard'), may hold values from 0 to 2.5
- skip_gain: bfloat16 [48], P('shard'), may hold values from 0.5 to 1.5
- norm_gain: bfloat16 [3072], P('shard'), may hold values from 0.5 to 1.5
- out_weight: bfloat16 [3072, 1536], P('shard'), may hold values from -0.109375 to 0.109375
- moe_gain: bfloat16 [1536], P('shard'), may hold values from 0.5 to 1.5
- router_weight: bfloat16 [1536, 32], P('shard'), may hold values from -0.078125 to 0.078125
- shared_gate: bfloat16 [1536, 1024], P('shard'), may hold values from -0.15625 to 0.15625
- shared_up: bfloat16 [1536, 1024], P('shard'), may hold values from -0.15625 to 0.15625
- shared_down: bfloat16 [1024, 1536], P('shard'), may hold values from -0.375 to 0.375
- expert_gate: bfloat16 [32, 1536, 512], P('shard'), may hold values from -0.15625 to 0.15625
- expert_up: bfloat16 [32, 1536, 512], P('shard'), may hold values from -0.15625 to 0.15625
- expert_down: bfloat16 [32, 512, 1536], P('shard'), may hold values from -1 to 1
Outputs:
- block_output: bfloat16 [16, 1024, 1536], P('shard', 'seq')
- input_grad: float32 [16, 1024, 1536], P('shard', 'seq')
- grad_mixer_gain: float32 [1536], P('shard')
- grad_in_weight: float32 [1536, 6448], P('shard')
- grad_conv_weight: float32 [4, 3328], P(None, 'shard')
- grad_conv_bias: float32 [3328], P('shard')
- grad_step_bias: float32 [48], P('shard')
- grad_decay_log: float32 [48], P('shard')
- grad_skip_gain: float32 [48], P('shard')
- grad_norm_gain: float32 [3072], P('shard')
- grad_out_weight: float32 [3072, 1536], P('shard')
- grad_moe_gain: float32 [1536], P('shard')
- grad_router_weight: float32 [1536, 32], P('shard')
- grad_shared_gate: float32 [1536, 1024], P('shard')
- grad_shared_up: float32 [1536, 1024], P('shard')
- grad_shared_down: float32 [1024, 1536], P('shard')
- grad_expert_gate: float32 [32, 1536, 512], P('shard')
- grad_expert_up: float32 [32, 1536, 512], P('shard')
- grad_expert_down: float32 [32, 512, 1536], P('shard')
The draws below stay inside these ranges and needn't reach their ends.
Inputs may be any that keep to these rules, and one draw needn't show every extreme that they name: lengths[s] counts the live leading positions of sequence s; exactly 8 sequences, drawn from the seed, are full. `routes`: each row names 6 different experts; among the rows of one device no expert is named more than 32 times, and on some device some expert exactly 32 times.
All inputs are finite; a program needn't handle non-finite values.
Results may differ from the reference program's by a relative error of at most 0.035.
Values may be sent and summed in bfloat16 or wider, within the bound.
No kernel may reach another device: no remote copies, remote signals or barrier semaphores. Data moves between devices by JAX's collectives and lax.ppermute only.
A program may use at most 320 MiB of HBM per device.

```python
import math
import jax
import jax.numpy as jnp
import numpy as np
from jax import lax

D = 1536
H = 48
FE = 512
FS = 1024
KC = 4
TOPK = 6
BLOCK = 256
TOK_DEV = 128
EXPERTS = 32
CAP = 32
LENGTH = 1024
SEQS = 16
DI = 3072
CONV = 3328
PROJ = 6448


def draw_lengths(key, part):
    key = jax.random.fold_in(key, 11)
    key_cut, key_order = jax.random.split(key)
    shortening = jax.random.randint(key_cut, (SEQS,), 0, LENGTH - LENGTH // 4 + 1)
    ranking = jax.random.permutation(key_order, SEQS)
    is_full = ranking < (SEQS + 1) // 2
    return jnp.where(is_full, LENGTH, LENGTH - shortening).astype(jnp.int32)


def block_scale(stream_key, dims, cuts, smallest, high):
    loudness, own = 1.0, jax.random.fold_in(stream_key, 6)
    for position, parts in cuts:
        heights = jnp.exp(jax.random.uniform(jax.random.fold_in(own, position), (parts,), jnp.float32, smallest / len(cuts), high / len(cuts)))
        loudness = loudness * jnp.repeat(heights, dims[position] // parts).reshape([-1 if axis == position else 1 for axis in range(len(dims))])
    return loudness


def shared_out(stream_key, own, number, rows, number_of, top, limit, skew):
    sequence = jax.random.permutation(stream_key, number_of)
    crowded, ordinary = load_shares(number_of, rows * top, limit, skew, True), load_shares(number_of, rows * top, limit, skew, False)
    places = jnp.arange(number_of)

    def named(tallies, turn):
        used = int((tallies > 0).sum())
        fixed = max(1, used // 4)
        passed = fixed + (places - fixed + turn * (used - fixed)) % max(1, number_of - fixed)
        return jnp.zeros((number_of,), jnp.int32).at[sequence[jnp.where(places < fixed, places, passed)]].set(jnp.asarray(tallies, jnp.int32))

    tallies = jnp.where(number % 4 == 0, named(crowded, number // 4), named(ordinary, number - number // 4 - 1))
    mixed = jax.random.permutation(jax.random.fold_in(own, 3), number_of)
    giver, receiver = mixed[0:number_of // 2 * 2:2], mixed[1:number_of // 2 * 2:2]
    slack = jnp.minimum(tallies[giver] - 1, limit - tallies[receiver]) // 2
    slack = jnp.where((giver == sequence[0]) | (receiver == sequence[0]) | (tallies[receiver] == 0), 0, jnp.maximum(slack, 0))
    passed = jax.random.randint(jax.random.fold_in(own, 4), (number_of // 2,), 0, 1 << 20) % (slack + 1)
    tallies = tallies.at[giver].add(-passed).at[receiver].add(passed)
    items = jnp.searchsorted(jnp.cumsum(tallies), jnp.arange(rows * top), side="right").astype(jnp.int32)
    grid = items.reshape(top, rows).T
    grid = grid[jax.random.permutation(jax.random.fold_in(own, 1), rows)]
    turn = jax.random.randint(jax.random.fold_in(own, 2), (rows, 1), 0, top)
    return jnp.take_along_axis(grid, (jnp.arange(top)[None, :] + turn) % top, axis=1)


def load_shares(amount, total, reach, skew, full):
    portions = [(1 << 20) // math.isqrt(grade ** skew) + 1 for grade in range(1, amount + 1)]
    largest = reach if full else min(reach, max(-(-total // amount), total * portions[0] // sum(portions)))
    least = 1 if total - largest >= amount - 1 else 0
    given, rest = [largest] + [least] * (amount - 1), total - largest - least * (amount - 1)
    while rest > 0:
        candidates = [i for i in range(1, amount) if given[i] < largest] or [i for i in range(1, amount) if given[i] < reach]
        whole, remaining = sum([portions[i] for i in candidates]), rest
        for i in candidates:
            addition = min(reach - given[i], max(1, remaining * portions[i] // whole), rest)
            given[i] = given[i] + addition
            rest = rest - addition
    return np.array(given)


def bell_draw(stream_key, extent, scale, bound, cuts=(), kind=jnp.bfloat16):
    values = jax.random.normal(stream_key, extent, jnp.float32) * scale
    if len(cuts) > 0:
        values = block_scale(stream_key, extent, cuts, -0.22, 0.18) * values
    return jnp.clip(values, min=-bound, max=bound).astype(kind)


def setup_inputs(seed: int = 0) -> dict:
    splits = jax.random.split(jax.random.key(seed), 22)
    block_input = bell_draw(splits[0], (SEQS, LENGTH, D), 1.0, 6.0, ((0, 16), (1, 8)))
    lengths = draw_lengths(jax.random.fold_in(splits[21], 71), 0)
    routes_keys = jax.random.split(jax.random.fold_in(splits[2], 1), SEQS * LENGTH // TOK_DEV)
    routes_turns = jax.random.permutation(jax.random.fold_in(splits[2], 3), SEQS * LENGTH // TOK_DEV)
    routes = jax.vmap(lambda own, number: shared_out(jax.random.fold_in(splits[2], 2), own, number, TOK_DEV, EXPERTS, TOPK, CAP, 2))(routes_keys, routes_turns).reshape((SEQS, LENGTH, TOPK))
    out_cotangent = bell_draw(splits[3], (SEQS, LENGTH, D), 1.0, 6.0, ((0, 16), (1, 8)))
    mixer_gain = jnp.clip(1.0 + 0.1 * jax.random.normal(splits[4], (D,), jnp.float32), 0.5, 1.5).astype(jnp.bfloat16)
    in_weight = bell_draw(splits[5], (D, PROJ), D ** -0.5, 0.15625, ((0, 16),))
    conv_weight = bell_draw(splits[6], (KC, CONV), KC ** -0.5, 3.0, ((1, 16),))
    conv_bias = bell_draw(splits[7], (CONV,), 0.5, 3.0, ((0, 16),))
    step_bias = jnp.clip(-5.0 + 4.0 * jax.random.uniform(splits[8], (H,), jnp.float32) ** block_scale(splits[8], (H,), ((0, 16),), -0.2, 0.2), -5.0, -1.0).astype(jnp.bfloat16)
    decay_log = jnp.clip(2.5 * jax.random.uniform(splits[9], (H,), jnp.float32) ** block_scale(splits[9], (H,), ((0, 16),), -0.2, 0.2), 0.0, 2.5).astype(jnp.bfloat16)
    skip_gain = jnp.clip(0.5 + 1.0 * jax.random.uniform(splits[10], (H,), jnp.float32) ** block_scale(splits[10], (H,), ((0, 16),), -0.2, 0.2), 0.5, 1.5).astype(jnp.bfloat16)
    norm_gain = jnp.clip(1.0 + 0.1 * jax.random.normal(splits[11], (DI,), jnp.float32), 0.5, 1.5).astype(jnp.bfloat16)
    out_weight = bell_draw(splits[12], (DI, D), DI ** -0.5, 0.109375, ((0, 16),))
    moe_gain = jnp.clip(1.0 + 0.1 * jax.random.normal(splits[13], (D,), jnp.float32), 0.5, 1.5).astype(jnp.bfloat16)
    router_weight = bell_draw(splits[14], (D, EXPERTS), (4 * D) ** -0.5, 0.078125, ((0, 16),))
    shared_gate = bell_draw(splits[15], (D, FS), D ** -0.5, 0.15625, ((0, 16),))
    shared_up = bell_draw(splits[16], (D, FS), D ** -0.5, 0.15625, ((0, 16),))
    shared_down = bell_draw(splits[17], (FS, D), (FS // 4) ** -0.5, 0.375, ((0, 16),))
    expert_gate = bell_draw(splits[18], (EXPERTS, D, FE), D ** -0.5, 0.15625, ((0, 16),))
    expert_up = bell_draw(splits[19], (EXPERTS, D, FE), D ** -0.5, 0.15625, ((0, 16),))
    expert_down = bell_draw(splits[20], (EXPERTS, FE, D), (FE // 16) ** -0.5, 1.0, ((0, 16),))
    return dict(block_input=block_input, lengths=lengths, routes=routes, out_cotangent=out_cotangent, mixer_gain=mixer_gain, in_weight=in_weight, conv_weight=conv_weight, conv_bias=conv_bias, step_bias=step_bias, decay_log=decay_log, skip_gain=skip_gain, norm_gain=norm_gain, out_weight=out_weight, moe_gain=moe_gain, router_weight=router_weight, shared_gate=shared_gate, shared_up=shared_up, shared_down=shared_down, expert_gate=expert_gate, expert_up=expert_up, expert_down=expert_down)


epsilon = 1e-05
highest = lax.Precision.HIGHEST

@jax.custom_vjp
def low(v):
    return lax.optimization_barrier(v.astype(jnp.bfloat16)).astype(jnp.float32)

@jax.custom_vjp
def low_back(v):
    return v

def low_keep(v):
    return (low(v), None)

def low_pass(kept, grad):
    return (grad,)

def back_keep(v):
    return (v, None)

def back_low(kept, grad):
    return (low(grad),)
low.defvjp(low_keep, low_pass)
low_back.defvjp(back_keep, back_low)

def matmul_high(left, right):
    return jnp.dot(left, right, precision=highest, preferred_element_type=jnp.float32)

def rms_scale(values, gain):
    return values * lax.rsqrt(lax.optimization_barrier(jnp.mean(values * values, axis=-1, keepdims=True)) + epsilon) * gain

def block_scan(ssm_state, block_piece, decay_rate):
    in_block, step_block, key_block, query_block = block_piece
    cumulative = jnp.cumsum(step_block * decay_rate[None, :], axis=0)
    positions = jnp.arange(cumulative.shape[0])
    causal = positions[:, None] >= positions[None, :]
    decay_gap = cumulative.T[:, :, None] - cumulative.T[:, None, :]
    decay_table = jnp.where(causal[None], jnp.exp(jnp.where(causal[None], decay_gap, 0.0)), 0.0)
    intersection = jnp.dot(query_block, key_block.T, precision=highest)
    scaled = in_block * step_block[:, :, None]
    within = jnp.einsum('hij,jhp->ihp', decay_table * intersection[None], scaled, precision=highest)
    across = jnp.einsum('in,hpn->ihp', query_block, ssm_state, precision=highest) * jnp.exp(cumulative)[:, :, None]
    to_end = jnp.exp(cumulative[-1][None, :] - cumulative)
    new_state = ssm_state * jnp.exp(cumulative[-1])[:, None, None] + jnp.einsum('jn,jhp->hpn', key_block, scaled * to_end[:, :, None], precision=highest)
    return (new_state, within + across)

def mixer(mixer_raw, step_raw, keys_raw, conv_taps, conv_shift, step_offset, decay_logs, skip_scale):
    seq_length, width = mixer_raw.shape
    head_count = step_raw.shape[1]
    head_size = width // head_count
    state_dim = keys_raw.shape[1] // 2
    kernel = conv_taps.shape[0]
    joined = jnp.concatenate([mixer_raw, keys_raw], axis=1)
    padded = jnp.pad(joined, ((kernel - 1, 0), (0, 0)))
    convolved = conv_shift[None, :]
    for tap_index in range(kernel):
        convolved = convolved + conv_taps[tap_index][None, :] * padded[tap_index:tap_index + seq_length]
    active = jax.nn.silu(convolved)
    mixer_in = active[:, :width]
    step_size = jax.nn.softplus(step_raw + step_offset[None, :])
    decay_rate = -jnp.exp(decay_logs)
    blocks = seq_length // BLOCK
    pieces = (mixer_in.reshape(blocks, BLOCK, head_count, head_size), step_size.reshape(blocks, BLOCK, head_count), active[:, width:width + state_dim].reshape(blocks, BLOCK, state_dim), active[:, width + state_dim:].reshape(blocks, BLOCK, state_dim))

    def one_block(ssm_state, block_piece):
        return block_scan(ssm_state, block_piece, decay_rate)
    initial = jnp.zeros((head_count, head_size, state_dim), jnp.float32)
    final_state, outputs = lax.scan(jax.checkpoint(one_block), initial, pieces)
    result = outputs.reshape(seq_length, head_count, head_size) + skip_scale[None, :, None] * mixer_in.reshape(seq_length, head_count, head_size)
    return result.reshape(seq_length, width)

def expert_mix(moe_in, route_ids, gate_weights, expert_gate, expert_up, expert_down):
    row_count = moe_in.shape[0]
    flat_ids = route_ids.reshape(-1)
    flat_gates = gate_weights.reshape(-1)
    capacity_rows = row_count // TOK_DEV * CAP

    def one_expert(running, expert):
        expert_id, weight_gate, weight_up, weight_down = expert
        matches = flat_ids == expert_id
        picked = jnp.nonzero(matches, size=capacity_rows, fill_value=0)[0].astype(jnp.int32)
        is_valid = (jnp.arange(capacity_rows) < jnp.sum(matches)).astype(jnp.float32)
        owner_row = picked // TOPK
        gathered = low_back(moe_in[owner_row])
        gate_pre = low_back(matmul_high(gathered, weight_gate))
        up_pre = low_back(matmul_high(gathered, weight_up))
        hidden = low(jax.nn.silu(gate_pre) * up_pre)
        result = low_back(low(matmul_high(hidden, weight_down)))
        row_scale = flat_gates[picked] * is_valid
        return (running.at[owner_row].add(result * row_scale[:, None]), None)
    initial = jnp.zeros_like(moe_in)
    combined, unused = lax.scan(jax.checkpoint(one_expert), initial, (jnp.arange(EXPERTS, dtype=jnp.int32), expert_gate, expert_up, expert_down))
    return combined

def forward(params, tokens, route_ids, live_mask):
    mixer_gain, in_weight, conv_weight, conv_bias, step_bias, decay_log, skip_gain, norm_gain, out_weight, moe_gain, router_weight, shared_gate, shared_up, shared_down, expert_gate, expert_up, expert_down = params
    seq_count, seq_length, model_dim = tokens.shape
    rows_flat = tokens.reshape(seq_count * seq_length, model_dim)
    inner_dim = norm_gain.shape[0]
    head_count = step_bias.shape[0]
    state_dim = (conv_weight.shape[1] - inner_dim) // 2
    normed = low(rms_scale(rows_flat, mixer_gain))
    projected = low_back(matmul_high(normed, in_weight))
    gate_input = projected[:, :inner_dim]
    conv_feed = low(projected[:, inner_dim:2 * inner_dim + 2 * state_dim])
    step_raw = low(projected[:, 2 * inner_dim + 2 * state_dim:])
    mixed_out = jax.vmap(mixer, in_axes=(0, 0, 0, None, None, None, None, None))(conv_feed[:, :inner_dim].reshape(seq_count, seq_length, inner_dim), step_raw.reshape(seq_count, seq_length, head_count), conv_feed[:, inner_dim:].reshape(seq_count, seq_length, 2 * state_dim), conv_weight, conv_bias, step_bias, decay_log, skip_gain)
    mixed_out = low_back(low(mixed_out.reshape(seq_count * seq_length, inner_dim)))
    gated_out = low(rms_scale(mixed_out * jax.nn.silu(gate_input), norm_gain))
    residual = rows_flat + low_back(matmul_high(gated_out, out_weight))
    moe_in = low(rms_scale(residual, moe_gain))
    logits = matmul_high(moe_in, router_weight)
    gate_weights = jax.nn.softmax(jnp.take_along_axis(logits, route_ids, axis=1), axis=1)
    gate_pre = low_back(matmul_high(moe_in, shared_gate))
    up_pre = low_back(matmul_high(moe_in, shared_up))
    shared_act = low(jax.nn.silu(gate_pre) * up_pre)
    combined = expert_mix(moe_in, route_ids, gate_weights, expert_gate, expert_up, expert_down)
    block_sum = (residual + matmul_high(shared_act, shared_down) + combined) * live_mask[:, None]
    return block_sum.reshape(seq_count, seq_length, model_dim)

def reference(block_input, lengths, routes, out_cotangent, mixer_gain, in_weight, conv_weight, conv_bias, step_bias, decay_log, skip_gain, norm_gain, out_weight, moe_gain, router_weight, shared_gate, shared_up, shared_down, expert_gate, expert_up, expert_down):
    params = tuple((weight.astype(jnp.float32) for weight in (mixer_gain, in_weight, conv_weight, conv_bias, step_bias, decay_log, skip_gain, norm_gain, out_weight, moe_gain, router_weight, shared_gate, shared_up, shared_down, expert_gate, expert_up, expert_down)))
    seq_count = block_input.shape[0]
    group_size = max((candidate for candidate in range(1, seq_count + 1) if seq_count % candidate == 0 and candidate * LENGTH <= max(4096, LENGTH)))
    group_count = seq_count // group_size
    live_all = (jnp.arange(LENGTH, dtype=jnp.int32)[None, :] < lengths[:, None]).astype(jnp.float32)

    def one_group(running, portion):
        tokens, route_part, live_part, cot_part = portion

        def apply_block(weights, inputs):
            return forward(weights, inputs, route_part.reshape(-1, TOPK), live_part.reshape(-1))
        outputs, pullback = jax.vjp(apply_block, params, tokens)
        weight_grads, input_grads = pullback(cot_part)
        return (jax.tree.map(jnp.add, running, weight_grads), (outputs, input_grads))
    zero_grads = jax.tree.map(jnp.zeros_like, params)
    totals, (outputs, input_grads) = lax.scan(one_group, zero_grads, (block_input.astype(jnp.float32).reshape(group_count, group_size, LENGTH, D), routes.reshape(group_count, group_size, LENGTH, TOPK), live_all.reshape(group_count, group_size, LENGTH), out_cotangent.astype(jnp.float32).reshape(group_count, group_size, LENGTH, D)))
    return (outputs.reshape(seq_count, LENGTH, D).astype(jnp.bfloat16), input_grads.reshape(seq_count, LENGTH, D), totals[0], totals[1], totals[2], totals[3], totals[4], totals[5], totals[6], totals[7], totals[8], totals[9], totals[10], totals[11], totals[12], totals[13], totals[14], totals[15], totals[16])
```

```python
import jax
import jax.numpy as jnp
from jax import lax
from jax.sharding import PartitionSpec as P

BLOCK = 256
CAP = 32


epsilon = 1e-05
highest = lax.Precision.HIGHEST
both_axes = ("seq", "shard")


def times(left, right):
    return jnp.dot(left, right, preferred_element_type=jnp.float32)


def times_transposed(left, right):
    return lax.dot_general(
        left, right, (((1,), (1,)), ((), ())), preferred_element_type=jnp.float32
    )


def transposed_times(left, right):
    return lax.dot_general(
        left, right, (((0,), (0,)), ((), ())), preferred_element_type=jnp.float32
    )


def silu_slope(values):
    sigma = jax.nn.sigmoid(values)
    return sigma * (1.0 + values * (1.0 - sigma))


def row_scale(values):
    return lax.rsqrt(jnp.mean(values * values, axis=-1, keepdims=True) + epsilon)


def block_scan(ssm_state, block_piece, decay_rate):
    in_block, step_block, key_block, query_block = block_piece
    cumulative = jnp.cumsum(step_block * decay_rate[None, :], axis=0)
    positions = jnp.arange(cumulative.shape[0])
    causal = positions[:, None] >= positions[None, :]
    decay_gap = cumulative.T[:, :, None] - cumulative.T[:, None, :]
    decay_table = jnp.where(causal[None], jnp.exp(jnp.where(causal[None], decay_gap, 0.0)), 0.0)
    intersection = jnp.dot(query_block, key_block.T, precision=highest)
    scaled = in_block * step_block[:, :, None]
    within = jnp.einsum("hij,jhp->ihp", decay_table * intersection[None], scaled, precision=highest)
    across = (
        jnp.einsum("in,hpn->ihp", query_block, ssm_state, precision=highest)
        * jnp.exp(cumulative)[:, :, None]
    )
    to_end = jnp.exp(cumulative[-1][None, :] - cumulative)
    new_state = ssm_state * jnp.exp(cumulative[-1])[:, None, None] + jnp.einsum(
        "jn,jhp->hpn", key_block, scaled * to_end[:, :, None], precision=highest
    )
    return (new_state, within + across)


def mixer(
    mixer_raw, step_raw, keys_raw, conv_taps, conv_shift, step_offset, decay_logs, skip_scale
):
    seq_length, width = mixer_raw.shape
    head_count = step_raw.shape[1]
    head_size = width // head_count
    state_dim = keys_raw.shape[1] // 2
    kernel = conv_taps.shape[0]
    joined = jnp.concatenate([mixer_raw, keys_raw], axis=1)
    padded = jnp.pad(joined, ((kernel - 1, 0), (0, 0)))
    convolved = conv_shift[None, :]
    for tap_index in range(kernel):
        convolved = (
            convolved + conv_taps[tap_index][None, :] * padded[tap_index : tap_index + seq_length]
        )
    active = jax.nn.silu(convolved)
    mixer_in = active[:, :width]
    step_size = jax.nn.softplus(step_raw + step_offset[None, :])
    decay_rate = -jnp.exp(decay_logs)
    blocks = seq_length // BLOCK
    pieces = (
        mixer_in.reshape(blocks, BLOCK, head_count, head_size),
        step_size.reshape(blocks, BLOCK, head_count),
        active[:, width : width + state_dim].reshape(blocks, BLOCK, state_dim),
        active[:, width + state_dim :].reshape(blocks, BLOCK, state_dim),
    )

    def one_block(ssm_state, block_piece):
        return block_scan(ssm_state, block_piece, decay_rate)

    initial = jnp.zeros((head_count, head_size, state_dim), jnp.float32)
    final_state, outputs = lax.scan(jax.checkpoint(one_block), initial, pieces)
    result = outputs.reshape(seq_length, head_count, head_size) + skip_scale[
        None, :, None
    ] * mixer_in.reshape(seq_length, head_count, head_size)
    return result.reshape(seq_length, width)


def on_device(
    block_input,
    lengths,
    routes,
    out_cotangent,
    mixer_gain,
    in_weight,
    conv_weight,
    conv_bias,
    step_bias,
    decay_log,
    skip_gain,
    norm_gain,
    out_weight,
    moe_gain,
    router_weight,
    shared_gate,
    shared_up,
    shared_down,
    expert_gate,
    expert_up,
    expert_down,
):
    sq = lax.axis_size("seq")
    sh = lax.axis_size("shard")
    q = lax.axis_index("seq")
    f32 = jnp.float32
    bf = jnp.bfloat16
    x_low = block_input[0]
    toks, dim = x_low.shape
    seq_rows = toks * sq
    heads = step_bias.shape[0] * sh
    inner = norm_gain.shape[0] * sh
    conv_all = conv_bias.shape[0] * sh
    keys_w = conv_all - inner
    gh = heads // sq
    gw = inner // sq
    rows_w = in_weight.shape[0]
    experts = router_weight.shape[1]
    local_e = expert_gate.shape[0]
    fs = shared_gate.shape[1]
    gf = fs // sq
    taps = conv_weight.shape[0]
    conv_own = conv_bias.shape[0]
    head_own = step_bias.shape[0]

    gain_col = mixer_gain.astype(f32)[:, None]

    def cols(start, width):
        return lax.dynamic_slice_in_dim(in_weight, start, width, 1)

    w_cols = jnp.concatenate(
        [
            cols(q * gw, gw),
            cols(inner + q * gw, gw),
            in_weight[:, 2 * inner : 2 * inner + keys_w],
            cols(2 * inner + keys_w + q * gh, gh),
        ],
        axis=1,
    )
    w_cols = (w_cols.astype(f32) * gain_col).astype(bf)
    used = 2 * gw + keys_w + gh
    small = jnp.concatenate(
        [conv_weight.reshape(-1), conv_bias, step_bias, decay_log, skip_gain]
    )
    small_cols = -(-small.shape[0] // rows_w)
    small = jnp.pad(small, (0, small_cols * rows_w - small.shape[0])).reshape(rows_w, small_cols)
    packed = jnp.concatenate(
        [w_cols, small, router_weight, moe_gain[:, None]], axis=1
    )
    at_small = used
    at_router = at_small + small_cols
    at_moe = at_router + experts
    total = -(-(at_moe + 1) // 128) * 128
    packed = jnp.pad(packed, ((0, 0), (0, total - packed.shape[1])))

    w_all = lax.all_gather(packed, "shard", axis=0, tiled=True)
    x_all = lax.all_gather(x_low, "seq", axis=0, tiled=True)

    out_scaled = (norm_gain.astype(f32)[:, None] * out_weight.astype(f32)).astype(bf)
    own_out = out_weight.shape[0] // sq
    own_down = shared_down.shape[0] // sq
    piece = jnp.concatenate(
        [
            lax.dynamic_slice_in_dim(out_scaled, q * own_out, own_out, 0),
            lax.dynamic_slice_in_dim(shared_down, q * own_down, own_down, 0),
        ],
        axis=0,
    )
    ratio = sh // sq
    forward_pairs = []
    for a in range(sh):
        for j in range(sq):
            s_to = sq * (a % ratio) + j
            q_to = a // ratio
            forward_pairs.append((j * sh + a, q_to * sh + s_to))
    backward_pairs = [(b, a) for a, b in forward_pairs]
    piece = lax.ppermute(piece, both_axes, forward_pairs)
    rows_all = lax.all_gather(piece, "shard", axis=0)
    w_out = rows_all[:, :own_out].reshape(gw, dim)
    w_down = rows_all[:, own_out:].reshape(gf, dim)
    shared_cols = jnp.concatenate(
        [
            lax.dynamic_slice_in_dim(shared_gate, q * gf, gf, 1),
            lax.dynamic_slice_in_dim(shared_up, q * gf, gf, 1),
        ],
        axis=1,
    )
    w_shared = lax.all_gather(shared_cols, "shard", axis=0, tiled=True)

    route_ids = routes[0]
    expert_ids = jnp.arange(experts, dtype=jnp.int32)
    named = jnp.any(route_ids[:, :, None] == expert_ids[None, None, :], axis=1).astype(f32)
    earlier = (
        jnp.arange(toks)[:, None] > jnp.arange(toks)[None, :]
    ).astype(f32)
    rank = jnp.dot(earlier, named)
    dispatch = (
        (named.T[:, None, :] > 0.0)
        & (rank.T[:, None, :] == jnp.arange(CAP, dtype=f32)[None, :, None])
    ).astype(bf)
    slots = experts * CAP
    dispatch_flat = dispatch.reshape(slots, toks)
    live = (q * toks + jnp.arange(toks, dtype=jnp.int32) < lengths[0]).astype(f32)
    cot = out_cotangent[0].astype(f32) * live[:, None]
    cot_low = cot.astype(bf)

    def to_experts(rows):
        return lax.all_to_all(
            rows.reshape(experts, CAP, rows.shape[-1]),
            "shard",
            split_axis=0,
            concat_axis=1,
            tiled=True,
        )

    cot_ext = jnp.concatenate(
        [cot_low, named.astype(bf), jnp.zeros((toks, 128 - experts), bf)], axis=1
    )
    cot_rows_ext = to_experts(times(dispatch_flat, cot_ext).astype(bf))
    cot_rows = cot_rows_ext[:, :, :dim]
    row_mask = cot_rows_ext[:, :, dim : dim + experts].astype(f32)
    cot_all = lax.all_gather(cot_low, "seq", axis=0, tiled=True)

    x_wide = x_all.astype(f32)
    x_r = row_scale(x_wide)
    proj = times(x_all, w_all) * x_r
    gate_in = proj[:, :gw]
    feed_low = proj[:, gw : 2 * gw + keys_w].astype(bf)
    step_low = proj[:, 2 * gw + keys_w : used].astype(bf)

    small_all = w_all.reshape(sh, rows_w, total)[:, :, at_small:at_router].reshape(sh, -1)
    at = taps * conv_own
    conv_full = (
        small_all[:, :at].reshape(sh, taps, conv_own).transpose(1, 0, 2).reshape(taps, conv_all)
    )
    offset_full = small_all[:, at : at + conv_own].reshape(conv_all)
    at = at + conv_own
    bias_full = small_all[:, at : at + head_own].reshape(heads)
    decay_full = small_all[:, at + head_own : at + 2 * head_own].reshape(heads)
    skip_full = small_all[:, at + 2 * head_own : at + 3 * head_own].reshape(heads)
    router_full = w_all[:, at_router:at_moe]
    moe_gain_full = w_all[:, at_moe].astype(f32)

    def group(values, width):
        return lax.dynamic_slice_in_dim(values, q * width, width, values.ndim - 1)

    conv_local = jnp.concatenate([group(conv_full, gw), conv_full[:, inner:]], axis=1).astype(f32)
    offset_local = jnp.concatenate([group(offset_full, gw), offset_full[inner:]]).astype(f32)
    bias_local = group(bias_full, gh).astype(f32)
    decay_local = group(decay_full, gh).astype(f32)
    skip_local = group(skip_full, gh).astype(f32)

    mixed_out, mixer_back = jax.vjp(
        mixer,
        feed_low[:, :gw].astype(f32),
        step_low.astype(f32),
        feed_low[:, gw:].astype(f32),
        conv_local,
        offset_local,
        bias_local,
        decay_local,
        skip_local,
    )
    mixed = mixed_out.astype(bf).astype(f32)

    gate_act = jax.nn.silu(gate_in)
    q_val = mixed * gate_act
    square = lax.psum(jnp.sum(q_val * q_val, axis=1).reshape(sq, toks), "seq")
    q_r = lax.rsqrt(square / inner + epsilon).reshape(seq_rows, 1)
    out_part = times(q_val.astype(bf), w_out).astype(bf)
    out_sum = lax.psum_scatter(out_part, "seq", scatter_dimension=0, tiled=True)
    tok_r = lax.dynamic_slice_in_dim(q_r, q * toks, toks, 0)
    x_tok = x_low.astype(f32)
    added = out_sum.astype(f32) * tok_r
    resid = x_tok + added

    resid_r = row_scale(resid)
    resid_n = resid * resid_r
    moe_in = (resid_n * moe_gain_full[None, :]).astype(bf)
    moe_all = lax.all_gather(moe_in, "seq", axis=0, tiled=True)
    logits = times(moe_in, router_full)

    def masked_softmax(values, mask):
        top = jnp.max(jnp.where(mask > 0.0, values, -jnp.inf), axis=-1, keepdims=True)
        top = jnp.where(top > -jnp.inf, top, 0.0)
        powers = jnp.where(mask > 0.0, jnp.exp(jnp.where(mask > 0.0, values - top, 0.0)), 0.0)
        return powers / jnp.maximum(jnp.sum(powers, axis=-1, keepdims=True), 1e-30)

    gates = masked_softmax(logits, named)
    rows = to_experts(times(dispatch_flat, moe_in).astype(bf))
    row_logits = lax.dot_general(
        rows, router_full, (((2,), (0,)), ((), ())), preferred_element_type=f32
    )
    row_gates = masked_softmax(row_logits, row_mask)
    own_ids = lax.axis_index("shard") * local_e + jnp.arange(local_e, dtype=jnp.int32)
    own_pick = (own_ids[:, None] == expert_ids[None, :]).astype(f32)
    row_gate = jnp.sum(row_gates * own_pick[:, None, :], axis=2, keepdims=True)

    d_raw = jnp.einsum("ecd,efd->ecf", cot_rows, expert_down, preferred_element_type=f32)
    e_gate = jnp.einsum("ecd,edf->ecf", rows, expert_gate, preferred_element_type=f32)
    e_up = jnp.einsum("ecd,edf->ecf", rows, expert_up, preferred_element_type=f32)
    e_sig = jax.nn.sigmoid(e_gate)
    e_silu = e_gate * e_sig
    e_act = (e_silu * e_up).astype(bf)
    d_gate_row = jnp.sum(e_act.astype(f32) * d_raw, axis=2, keepdims=True)
    d_act = row_gate * d_raw
    d_g = (d_act * e_up * (e_sig * (1.0 + e_gate * (1.0 - e_sig)))).astype(bf)
    d_v = (d_act * e_silu).astype(bf)
    d_row = jnp.einsum("ecf,edf->ecd", d_g, expert_gate, preferred_element_type=f32) + jnp.einsum(
        "ecf,edf->ecd", d_v, expert_up, preferred_element_type=f32
    )
    hi = d_gate_row.astype(bf)
    lo = (d_gate_row - hi.astype(f32)).astype(bf)
    back_rows = jnp.concatenate(
        [d_row.astype(bf), hi, lo, jnp.zeros(hi.shape[:2] + (126,), bf)], axis=2
    )

    def from_experts(values):
        return lax.all_to_all(values, "shard", split_axis=1, concat_axis=0, tiled=True)

    d_returned = from_experts(back_rows)
    e_out = jnp.einsum("ecf,efd->ecd", e_act, expert_down, preferred_element_type=f32).astype(bf)
    scaled_act = (row_gate * e_act.astype(f32)).astype(bf)
    grad_e_down = jnp.einsum("ecf,ecd->efd", scaled_act, cot_rows, preferred_element_type=f32)
    grad_e_gate = jnp.einsum("ecd,ecf->edf", rows, d_g, preferred_element_type=f32)
    grad_e_up = jnp.einsum("ecd,ecf->edf", rows, d_v, preferred_element_type=f32)
    e_sum = lax.psum(
        (grad_e_gate.astype(bf), grad_e_up.astype(bf), grad_e_down.astype(bf)), "seq"
    )

    s_both = times(moe_all, w_shared)
    s_gate, s_up = s_both[:, :gf], s_both[:, gf:]
    s_sig = jax.nn.sigmoid(s_gate)
    s_silu = s_gate * s_sig
    s_act = (s_silu * s_up).astype(bf)
    d_sh = times_transposed(cot_all, w_down)
    d_both = jnp.concatenate(
        [
            (d_sh * s_up * (s_sig * (1.0 + s_gate * (1.0 - s_sig)))).astype(bf),
            (d_sh * s_silu).astype(bf),
        ],
        axis=1,
    )
    d_moe_part = times_transposed(d_both, w_shared).astype(bf)
    d_moe_shared = lax.psum_scatter(d_moe_part, "seq", scatter_dimension=0, tiled=True)
    shared_part = times(s_act, w_down).astype(bf)
    shared_sum = lax.psum_scatter(shared_part, "seq", scatter_dimension=0, tiled=True)

    d_flat = d_returned.reshape(slots, dim + 128)
    gate_back = jnp.sum(
        d_flat[:, dim : dim + 2].astype(f32), axis=1
    ).reshape(experts, CAP)
    d_gates = jnp.sum(dispatch.astype(f32) * gate_back[:, :, None], axis=1).T
    d_logits = gates * (d_gates - jnp.sum(gates * d_gates, axis=1, keepdims=True))
    d_moe = (
        transposed_times(dispatch_flat, d_flat[:, :dim])
        + d_moe_shared.astype(f32)
        + jnp.dot(d_logits, router_full.astype(f32).T, precision=highest)
    )
    grad_router = jnp.dot(moe_in.astype(f32).T, d_logits, precision=highest)
    grad_moe = jnp.sum(d_moe * resid_n, axis=0)
    d_scaled = d_moe * moe_gain_full[None, :]
    d_resid = (
        cot
        + d_scaled * resid_r
        - resid_n * (resid_r * jnp.mean(d_scaled * resid_n, axis=1, keepdims=True))
    )
    d_o = d_resid.astype(bf)
    kappa = jnp.sum(d_o.astype(f32) * added, axis=1) / inner
    d_o_all = lax.all_gather(d_o, "seq", axis=0, tiled=True)
    kappa_all = lax.all_gather(kappa.reshape(1, toks), "seq", axis=0).reshape(seq_rows, 1)

    returned = from_experts(e_out)
    weighted = (gates.T[:, None, :] * dispatch.astype(f32)).reshape(slots, toks)
    combined = lax.dot_general(
        weighted,
        returned.reshape(slots, dim).astype(f32),
        (((0,), (0,)), ((), ())),
        preferred_element_type=f32,
    )
    block_output = ((resid + shared_sum.astype(f32) + combined) * live[:, None]).astype(bf)[None]

    d_gated = times_transposed(d_o_all, w_out)
    d_q = q_r * d_gated - q_val * (q_r * q_r * kappa_all)
    d_mixed = (d_q * gate_act).astype(bf)
    d_gate_in = d_q * mixed * silu_slope(gate_in)
    gated_low = (q_val * q_r).astype(bf)
    grad_out_part = transposed_times(gated_low, d_o_all)
    grad_down_part = transposed_times(s_act, cot_all)
    grad_shared_part = transposed_times(moe_all, d_both)

    def sum_over_shard(values):
        moved = lax.all_to_all(values.astype(bf), "shard", split_axis=0, concat_axis=0, tiled=True)
        return jnp.sum(moved.astype(f32), axis=0)

    rows_part = jnp.concatenate(
        [grad_out_part.reshape(sh, own_out, dim), grad_down_part.reshape(sh, own_down, dim)],
        axis=1,
    )
    rows_sum = sum_over_shard(rows_part)
    rows_sum = lax.ppermute(rows_sum.astype(bf), both_axes, backward_pairs)
    rows_grad = lax.all_gather(rows_sum, "seq", axis=0)
    grad_out_raw = rows_grad[:, :own_out].reshape(sq * own_out, dim).astype(f32)
    grad_down = rows_grad[:, own_out:].reshape(sq * own_down, dim).astype(f32)
    grad_out = norm_gain.astype(f32)[:, None] * grad_out_raw
    grad_norm = jnp.sum(out_weight.astype(f32) * grad_out_raw, axis=1)

    mid_part = jnp.concatenate(
        [
            grad_shared_part,
            grad_router,
            grad_moe[:, None],
            jnp.zeros((dim, 128 - experts - 1), f32),
        ],
        axis=1,
    )
    mid_sum = sum_over_shard(mid_part.reshape(sh, rows_w, 2 * gf + 128))
    mid_all = lax.all_gather(mid_sum.astype(bf), "seq", axis=0).astype(f32)
    grad_shared_gate = mid_all[:, :, :gf].transpose(1, 0, 2).reshape(rows_w, fs)
    grad_shared_up = mid_all[:, :, gf : 2 * gf].transpose(1, 0, 2).reshape(rows_w, fs)
    mid_rest = jnp.sum(mid_all[:, :, 2 * gf :], axis=0)
    grad_router_weight = mid_rest[:, :experts]
    grad_moe_gain = mid_rest[:, experts]

    (
        d_mixer_raw,
        d_step_raw,
        d_keys_raw,
        grad_conv_local,
        grad_offset_local,
        grad_bias_local,
        grad_decay_local,
        grad_skip_local,
    ) = mixer_back(d_mixed.astype(f32))
    d_proj = jnp.concatenate([d_gate_in, d_mixer_raw, d_keys_raw, d_step_raw], axis=1)
    d_proj = (d_proj * x_r).astype(bf)
    d_proj = jnp.pad(d_proj, ((0, 0), (0, total - used)))
    back_part = times_transposed(d_proj, w_all).astype(bf)
    back_sum = lax.psum_scatter(back_part, "seq", scatter_dimension=0, tiled=True).astype(f32)
    tok_x_r = row_scale(x_tok)
    x_n = x_tok * tok_x_r
    input_grad = (
        d_resid + back_sum - x_n * (tok_x_r * jnp.mean(back_sum * x_tok, axis=1, keepdims=True))
    )[None]

    grad_in_part = transposed_times(x_all, d_proj)[:, :used]

    def spread(local, count):
        wide = jnp.zeros(local.shape[:-1] + (count,), f32)
        return lax.dynamic_update_slice_in_dim(wide, local, q * local.shape[-1], local.ndim - 1)

    conv_rows = jnp.concatenate([grad_conv_local, grad_offset_local[None]], axis=0)
    conv_wide = jnp.concatenate([spread(conv_rows[:, :gw], inner), conv_rows[:, gw:]], axis=1)
    head_wide = spread(jnp.stack([grad_bias_local, grad_decay_local, grad_skip_local]), heads)
    small_part = jnp.concatenate(
        [
            conv_wide.reshape(taps + 1, sh, conv_own).transpose(1, 0, 2).reshape(sh, -1),
            head_wide.reshape(3, sh, head_own).transpose(1, 0, 2).reshape(sh, -1),
        ],
        axis=1,
    )
    small_count = small_part.shape[1]
    small_part = jnp.pad(
        small_part, ((0, 0), (0, rows_w * small_cols - small_count))
    ).reshape(sh, rows_w, small_cols)
    last_part = jnp.concatenate(
        [
            grad_in_part.reshape(sh, rows_w, used),
            small_part,
            jnp.zeros((sh, rows_w, total - used - small_cols), f32),
        ],
        axis=2,
    )
    last_sum = sum_over_shard(last_part)
    last_all = lax.all_gather(last_sum.astype(bf), "seq", axis=0).astype(f32)

    def side_by_side(start, width):
        return last_all[:, :, start : start + width].transpose(1, 0, 2).reshape(rows_w, sq * width)

    grad_in_raw = jnp.concatenate(
        [
            side_by_side(0, gw),
            side_by_side(gw, gw),
            jnp.sum(last_all[:, :, 2 * gw : 2 * gw + keys_w], axis=0),
            side_by_side(2 * gw + keys_w, gh),
        ],
        axis=1,
    )
    grad_in = gain_col * grad_in_raw
    grad_mixer_gain = jnp.sum(in_weight.astype(f32) * grad_in_raw, axis=1)
    small_sum = jnp.sum(last_all[:, :, used : used + small_cols], axis=0).reshape(-1)
    at = taps * conv_own
    grad_conv = small_sum[:at].reshape(taps, conv_own)
    grad_offset = small_sum[at : at + conv_own]
    at = at + conv_own
    grad_bias = small_sum[at : at + head_own]
    grad_decay = small_sum[at + head_own : at + 2 * head_own]
    grad_skip = small_sum[at + 2 * head_own : at + 3 * head_own]
    return (
        block_output,
        input_grad,
        grad_mixer_gain,
        grad_in,
        grad_conv,
        grad_offset,
        grad_bias,
        grad_decay,
        grad_skip,
        grad_norm,
        grad_out,
        grad_moe_gain,
        grad_router_weight,
        grad_shared_gate,
        grad_shared_up,
        grad_down,
        e_sum[0].astype(f32),
        e_sum[1].astype(f32),
        e_sum[2].astype(f32),
    )


def solution(mesh):
    placed = (
        P("shard", "seq", None),
        P("shard"),
        P("shard", "seq", None),
        P("shard", "seq", None),
        P("shard"),
        P("shard", None),
        P(None, "shard"),
        P("shard"),
        P("shard"),
        P("shard"),
        P("shard"),
        P("shard"),
        P("shard", None),
        P("shard"),
        P("shard", None),
        P("shard", None),
        P("shard", None),
        P("shard", None),
        P("shard", None, None),
        P("shard", None, None),
        P("shard", None, None),
    )
    return jax.shard_map(
        on_device,
        mesh=mesh,
        in_specs=placed,
        out_specs=(
            P("shard", "seq", None),
            P("shard", "seq", None),
            P("shard"),
            P("shard", None),
            P(None, "shard"),
            P("shard"),
            P("shard"),
            P("shard"),
            P("shard"),
            P("shard"),
            P("shard", None),
            P("shard"),
            P("shard", None),
            P("shard", None),
            P("shard", None),
            P("shard", None),
            P("shard", None, None),
            P("shard", None, None),
            P("shard", None, None),
        ),
        check_vma=False,
    )
```

```python
import jax
import jax.numpy as jnp
from jax import lax
from jax.experimental import pallas as pl
from jax.experimental.pallas import tpu as pltpu
from jax.sharding import PartitionSpec as P

CAP = 32


epsilon = 1e-05
highest = lax.Precision.HIGHEST
both_axes = ("seq", "shard")


def times(left, right):
    return jnp.dot(left, right, preferred_element_type=jnp.float32)


def times_transposed(left, right):
    return lax.dot_general(
        left, right, (((1,), (1,)), ((), ())), preferred_element_type=jnp.float32
    )


def transposed_times(left, right):
    return lax.dot_general(
        left, right, (((0,), (0,)), ((), ())), preferred_element_type=jnp.float32
    )


def silu_slope(values):
    sigma = jax.nn.sigmoid(values)
    return sigma * (1.0 + values * (1.0 - sigma))


def row_scale(values):
    return lax.rsqrt(jnp.mean(values * values, axis=-1, keepdims=True) + epsilon)


CHUNK = 128
WIDE = 384
CONVW = 640
PAIRS = 3
HEADS_HERE = 6


def split_two(values):
    high = values.astype(jnp.bfloat16)
    return high, (values - high.astype(jnp.float32)).astype(jnp.bfloat16)


def ones_times(ones, values):
    high, low = split_two(values)
    return times(ones, high) + times(ones, low)


def times_ones(values, ones):
    high, low = split_two(values)
    return times(high, ones) + times(low, ones)


def transposed_times_ones(values, ones):
    high, low = split_two(values)
    return transposed_times(high, ones) + transposed_times(low, ones)


def grid_of(shape):
    rows = lax.broadcasted_iota(jnp.int32, shape, 0)
    columns = lax.broadcasted_iota(jnp.int32, shape, 1)
    return rows, columns


def mark(condition):
    return jnp.where(condition, 1.0, 0.0).astype(jnp.bfloat16)


def chunk_parts(proj, prev, has_prev, taps_ref, head_ref, pad_ref):
    f32, bf = jnp.float32, jnp.bfloat16
    feed = proj[:, WIDE : WIDE + CONVW].astype(bf).astype(f32)
    before = prev[:, WIDE : WIDE + CONVW].astype(bf).astype(f32)
    pad_ref[0:8, :] = jnp.where(has_prev, before, 0.0)
    pad_ref[8 : 8 + CHUNK, :] = feed
    conv = taps_ref[4:5, :]
    for tap in range(4):
        conv = conv + taps_ref[tap : tap + 1, :] * pad_ref[5 + tap : 5 + tap + CHUNK, :]
    sig = jax.nn.sigmoid(conv)
    act = conv * sig
    u = act[:, :WIDE]
    key = act[:, WIDE : WIDE + 128].astype(bf)
    query = act[:, WIDE + 128 :].astype(bf)
    step_low = proj[:, WIDE + CONVW :].astype(bf).astype(f32)
    pre = step_low + head_ref[0:1, :]
    rows, columns = grid_of((CHUNK, 128))
    here = columns < HEADS_HERE
    dt = jnp.where(here, jnp.maximum(pre, 0.0) + jnp.log1p(jnp.exp(-jnp.abs(pre))), 0.0)
    la = dt * head_ref[1:2, :]
    lower = mark(rows >= columns)
    cum = ones_times(lower, la)
    end = cum[CHUNK - 1 : CHUNK, :]
    wide_rows, wide_columns = grid_of((128, WIDE))
    widen = mark(wide_columns // 64 == wide_rows)
    dt_w = times_ones(dt, widen)
    e_w = times_ones(jnp.exp(cum), widen)
    w_w = times_ones(jnp.exp(end - cum), widen)
    full_rows, full_columns = grid_of((128, 2 * PAIRS * 128))
    la_full = times_ones(la, mark(full_columns // 128 == full_rows))
    scores = times_transposed(query, key)
    return dict(
        conv=conv, sig=sig, u=u, key=key, query=query, pre=pre, here=here, dt=dt, lower=lower,
        dt_w=dt_w, e_w=e_w, w_w=w_w, la_full=la_full, scores=scores, xs=u * dt_w,
    )


def pair_table(parts, pair):
    rows, columns = grid_of((CHUNK, 256))
    local = columns % 128
    steps = jnp.where(rows > local, parts["la_full"][:, 256 * pair : 256 * pair + 256], 0.0)
    gap = ones_times(parts["lower"], steps)
    causal = rows >= local
    decay = jnp.where(causal, jnp.exp(jnp.where(causal, gap, 0.0)), 0.0)
    scores = parts["scores"]
    return decay, decay * jnp.concatenate([scores, scores], axis=1)


def stack_heads(values, pair):
    both = values[:, 128 * pair : 128 * pair + 128]
    first = lax.broadcasted_iota(jnp.int32, both.shape, 1) < 64
    return jnp.concatenate(
        [jnp.where(first, both, 0.0), jnp.where(first, 0.0, both)], axis=0
    ).astype(jnp.bfloat16)


def scan_forward_kernel(
    proj_ref, prev_ref, taps_ref, head_ref, skip_ref,
    mixed_ref, q_ref, square_ref, start_ref, state_ref, pad_ref,
):
    f32, bf = jnp.float32, jnp.bfloat16
    chunk = pl.program_id(0)

    @pl.when(chunk == 0)
    def _():
        state_ref[...] = jnp.zeros(state_ref.shape, f32)

    parts = chunk_parts(
        proj_ref[...], prev_ref[...], chunk > 0, taps_ref, head_ref, pad_ref
    )
    state = state_ref[...]
    start_ref[0] = state
    xs = parts["xs"]
    inside = []
    for pair in range(PAIRS):
        _, table = pair_table(parts, pair)
        inside.append(times(table.astype(bf), stack_heads(xs, pair)))
    across = times(parts["query"], state.astype(bf))
    y = (
        jnp.concatenate(inside, axis=1)
        + parts["e_w"] * across
        + skip_ref[0:1, :] * parts["u"]
    )
    mixed = y.astype(bf)
    mixed_ref[...] = mixed
    gate = proj_ref[:, :WIDE]
    q_val = mixed.astype(f32) * (gate * jax.nn.sigmoid(gate))
    q_ref[...] = q_val.astype(bf)
    square_ref[...] = jnp.sum(q_val * q_val, axis=1, keepdims=True)
    state_ref[...] = state * parts["e_w"][CHUNK - 1 : CHUNK, :] + transposed_times(
        parts["key"], (xs * parts["w_w"]).astype(bf)
    )


def scan_backward_kernel(
    proj_ref, prev_ref, mixed_ref, d_gated_ref, rows_ref, start_ref, taps_ref, head_ref, skip_ref,
    d_proj_ref, d_taps_ref, d_head_ref, d_skip_ref,
    state_ref, pad_ref, late_ref,
):
    f32, bf = jnp.float32, jnp.bfloat16
    step = pl.program_id(0)
    last = pl.num_programs(0) - 1

    @pl.when(step == 0)
    def _():
        state_ref[...] = jnp.zeros(state_ref.shape, f32)
        late_ref[CHUNK : CHUNK + 8, :] = jnp.zeros((8, CONVW), f32)
        d_taps_ref[...] = jnp.zeros(d_taps_ref.shape, f32)
        d_head_ref[...] = jnp.zeros(d_head_ref.shape, f32)
        d_skip_ref[...] = jnp.zeros(d_skip_ref.shape, f32)

    parts = chunk_parts(
        proj_ref[...], prev_ref[...], step < last, taps_ref, head_ref, pad_ref
    )
    u, key, query, xs = parts["u"], parts["key"], parts["query"], parts["xs"]
    e_w, w_w, dt_w = parts["e_w"], parts["w_w"], parts["dt_w"]

    gate = proj_ref[:, :WIDE]
    gate_sig = jax.nn.sigmoid(gate)
    gate_act = gate * gate_sig
    mixed = mixed_ref[...].astype(f32)
    q_val = mixed * gate_act
    q_r = rows_ref[:, 0:1]
    d_q = q_r * d_gated_ref[...] - q_val * (q_r * q_r * rows_ref[:, 1:2])
    d_gate = d_q * mixed * (gate_sig * (1.0 + gate * (1.0 - gate_sig)))
    d_y = (d_q * gate_act).astype(bf).astype(f32)

    start = start_ref[0]
    start_low = start.astype(bf)
    d_end = state_ref[...]
    d_end_low = d_end.astype(bf)
    xw = xs * w_w
    ye = d_y * e_w
    ye_low = ye.astype(bf)
    across = times(query, start_low)
    pulled = times(key, d_end_low)
    d_query = times_transposed(ye_low, start_low)
    d_key = times_transposed(xw.astype(bf), d_end_low)
    state_ref[...] = d_end * e_w[CHUNK - 1 : CHUNK, :] + transposed_times(query, ye_low)
    d_scores = jnp.zeros((CHUNK, 128), f32)
    turns = jnp.zeros((CHUNK, 128), f32)
    d_xs = []
    for pair in range(PAIRS):
        decay, table = pair_table(parts, pair)
        xs_two = stack_heads(xs, pair)
        dy_two = stack_heads(d_y, pair)
        d_table = times_transposed(d_y[:, 128 * pair : 128 * pair + 128].astype(bf), xs_two)
        d_decay = d_table * decay
        d_scores = d_scores + d_decay[:, :128] + d_decay[:, 128:]
        d_gap = d_table * table
        table_low = table.astype(bf)
        d_xs.append(
            transposed_times(
                jnp.concatenate([table_low[:, :128], table_low[:, 128:]], axis=0), dy_two
            )
        )
        two_rows, two_columns = grid_of((256, 128))
        own = mark(two_columns == 2 * pair + two_rows // 128)
        turns = turns + times_ones(d_gap, own)
        turns = turns - transposed_times_ones(
            jnp.concatenate([d_gap[:, :128], d_gap[:, 128:]], axis=0), own
        )
    d_xs = jnp.concatenate(d_xs, axis=1) + w_w * pulled
    d_scores_low = d_scores.astype(bf)
    d_query = d_query + times(d_scores_low, key)
    d_key = d_key + transposed_times(d_scores_low, query)

    rows, columns = grid_of((CHUNK, 128))
    upper = mark(columns >= rows)
    strict = mark(columns < rows)
    sum_rows, sum_columns = grid_of((WIDE, 128))
    per_head = mark(sum_rows // 64 == sum_columns)
    end_row = jnp.sum(d_end * start, axis=0, keepdims=True) * e_w[CHUNK - 1 : CHUNK, :]
    wide = ones_times(upper, ye * across) + ones_times(strict, xw * pulled) + end_row
    d_la = ones_times(upper, turns) + times_ones(wide, per_head)
    d_dt = times_ones(d_xs * u, per_head) + d_la * head_ref[1:2, :]
    d_pre = jnp.where(parts["here"], d_dt * jax.nn.sigmoid(parts["pre"]), 0.0)
    d_head_ref[0:1, :] += jnp.sum(d_pre, axis=0, keepdims=True)
    d_head_ref[1:2, :] += jnp.sum(d_la * parts["dt"], axis=0, keepdims=True)
    d_skip_ref[0:1, :] += jnp.sum(d_y * u, axis=0, keepdims=True)

    d_u = d_xs * dt_w + skip_ref[0:1, :] * d_y
    conv, sig = parts["conv"], parts["sig"]
    d_conv = jnp.concatenate([d_u, d_key, d_query], axis=1) * (sig * (1.0 + conv * (1.0 - sig)))
    late_ref[0:CHUNK, :] = d_conv
    d_feed = jnp.zeros((CHUNK, CONVW), f32)
    for tap in range(4):
        d_feed = d_feed + taps_ref[tap : tap + 1, :] * late_ref[3 - tap : 3 - tap + CHUNK, :]
        d_taps_ref[tap : tap + 1, :] += jnp.sum(
            d_conv * pad_ref[5 + tap : 5 + tap + CHUNK, :], axis=0, keepdims=True
        )
    d_taps_ref[4:5, :] += jnp.sum(d_conv, axis=0, keepdims=True)
    late_ref[CHUNK : CHUNK + 8, :] = d_conv[0:8, :]
    scale = rows_ref[:, 2:3]
    d_proj_ref[:, :WIDE] = (d_gate * scale).astype(bf)
    d_proj_ref[:, WIDE : WIDE + CONVW] = (d_feed * scale).astype(bf)
    d_proj_ref[:, WIDE + CONVW :] = (d_pre * scale).astype(bf)


def whole(shape):
    return pl.BlockSpec(shape, lambda step: (0,) * len(shape))


def scan_forward(proj, taps, head, skip):
    rows, width = proj.shape
    chunks = rows // CHUNK
    by_chunk = lambda step: (step, 0)
    return pl.pallas_call(
        scan_forward_kernel,
        grid=(chunks,),
        in_specs=[
            pl.BlockSpec((CHUNK, width), by_chunk),
            pl.BlockSpec((8, width), lambda step: (jnp.maximum(step * (CHUNK // 8) - 1, 0), 0)),
            whole(taps.shape),
            whole(head.shape),
            whole(skip.shape),
        ],
        out_specs=[
            pl.BlockSpec((CHUNK, WIDE), by_chunk),
            pl.BlockSpec((CHUNK, WIDE), by_chunk),
            pl.BlockSpec((CHUNK, 1), by_chunk),
            pl.BlockSpec((1, 128, WIDE), lambda step: (step, 0, 0)),
        ],
        out_shape=[
            jax.ShapeDtypeStruct((rows, WIDE), jnp.bfloat16),
            jax.ShapeDtypeStruct((rows, WIDE), jnp.bfloat16),
            jax.ShapeDtypeStruct((rows, 1), jnp.float32),
            jax.ShapeDtypeStruct((chunks, 128, WIDE), jnp.float32),
        ],
        scratch_shapes=[
            pltpu.VMEM((128, WIDE), jnp.float32),
            pltpu.VMEM((CHUNK + 8, CONVW), jnp.float32),
        ],
        compiler_params=pltpu.CompilerParams(vmem_limit_bytes=32 << 20),
        cost_estimate=pl.CostEstimate(
            flops=3 << 30, bytes_accessed=12 << 20, transcendentals=4 << 20
        ),
        name="scan_forward",
    )(proj, proj, taps, head, skip)


def scan_backward(proj, mixed, d_gated, row_values, starts, taps, head, skip):
    rows, width = proj.shape
    chunks = rows // CHUNK
    by_chunk = lambda step: (chunks - 1 - step, 0)
    return pl.pallas_call(
        scan_backward_kernel,
        grid=(chunks,),
        in_specs=[
            pl.BlockSpec((CHUNK, width), by_chunk),
            pl.BlockSpec(
                (8, width),
                lambda step: (jnp.maximum((chunks - 1 - step) * (CHUNK // 8) - 1, 0), 0),
            ),
            pl.BlockSpec((CHUNK, WIDE), by_chunk),
            pl.BlockSpec((CHUNK, WIDE), by_chunk),
            pl.BlockSpec((CHUNK, row_values.shape[1]), by_chunk),
            pl.BlockSpec((1, 128, WIDE), lambda step: (chunks - 1 - step, 0, 0)),
            whole(taps.shape),
            whole(head.shape),
            whole(skip.shape),
        ],
        out_specs=[
            pl.BlockSpec((CHUNK, width), by_chunk),
            whole((8, CONVW)),
            whole((8, 128)),
            whole((8, WIDE)),
        ],
        out_shape=[
            jax.ShapeDtypeStruct((rows, width), jnp.bfloat16),
            jax.ShapeDtypeStruct((8, CONVW), jnp.float32),
            jax.ShapeDtypeStruct((8, 128), jnp.float32),
            jax.ShapeDtypeStruct((8, WIDE), jnp.float32),
        ],
        scratch_shapes=[
            pltpu.VMEM((128, WIDE), jnp.float32),
            pltpu.VMEM((CHUNK + 8, CONVW), jnp.float32),
            pltpu.VMEM((CHUNK + 8, CONVW), jnp.float32),
        ],
        compiler_params=pltpu.CompilerParams(vmem_limit_bytes=48 << 20),
        cost_estimate=pl.CostEstimate(
            flops=10 << 30, bytes_accessed=20 << 20, transcendentals=8 << 20
        ),
        name="scan_backward",
    )(proj, proj, mixed, d_gated, row_values, starts, taps, head, skip)


def on_device(
    block_input,
    lengths,
    routes,
    out_cotangent,
    mixer_gain,
    in_weight,
    conv_weight,
    conv_bias,
    step_bias,
    decay_log,
    skip_gain,
    norm_gain,
    out_weight,
    moe_gain,
    router_weight,
    shared_gate,
    shared_up,
    shared_down,
    expert_gate,
    expert_up,
    expert_down,
):
    sq = lax.axis_size("seq")
    sh = lax.axis_size("shard")
    q = lax.axis_index("seq")
    f32 = jnp.float32
    bf = jnp.bfloat16
    x_low = block_input[0]
    toks, dim = x_low.shape
    seq_rows = toks * sq
    heads = step_bias.shape[0] * sh
    inner = norm_gain.shape[0] * sh
    conv_all = conv_bias.shape[0] * sh
    keys_w = conv_all - inner
    gh = heads // sq
    gw = inner // sq
    rows_w = in_weight.shape[0]
    experts = router_weight.shape[1]
    local_e = expert_gate.shape[0]
    fs = shared_gate.shape[1]
    gf = fs // sq
    taps = conv_weight.shape[0]
    conv_own = conv_bias.shape[0]
    head_own = step_bias.shape[0]

    gain_col = mixer_gain.astype(f32)[:, None]

    def cols(start, width):
        return lax.dynamic_slice_in_dim(in_weight, start, width, 1)

    w_cols = jnp.concatenate(
        [
            cols(q * gw, gw),
            cols(inner + q * gw, gw),
            in_weight[:, 2 * inner : 2 * inner + keys_w],
            cols(2 * inner + keys_w + q * gh, gh),
        ],
        axis=1,
    )
    w_cols = (w_cols.astype(f32) * gain_col).astype(bf)
    used = 2 * gw + keys_w + gh
    small = jnp.concatenate(
        [conv_weight.reshape(-1), conv_bias, step_bias, decay_log, skip_gain]
    )
    small_cols = -(-small.shape[0] // rows_w)
    small = jnp.pad(small, (0, small_cols * rows_w - small.shape[0])).reshape(rows_w, small_cols)
    packed = jnp.concatenate(
        [w_cols, small, router_weight, moe_gain[:, None]], axis=1
    )
    at_small = used
    at_router = at_small + small_cols
    at_moe = at_router + experts
    total = -(-(at_moe + 1) // 128) * 128
    packed = jnp.pad(packed, ((0, 0), (0, total - packed.shape[1])))

    w_all = lax.all_gather(packed, "shard", axis=0, tiled=True)
    x_all = lax.all_to_all(
        jnp.broadcast_to(x_low[None], (sq, toks, dim)), "seq", split_axis=0, concat_axis=0, tiled=True
    ).reshape(seq_rows, dim)

    out_scaled = (norm_gain.astype(f32)[:, None] * out_weight.astype(f32)).astype(bf)
    own_out = out_weight.shape[0] // sq
    own_down = shared_down.shape[0] // sq
    piece = jnp.concatenate(
        [
            lax.dynamic_slice_in_dim(out_scaled, q * own_out, own_out, 0),
            lax.dynamic_slice_in_dim(shared_down, q * own_down, own_down, 0),
        ],
        axis=0,
    )
    ratio = sh // sq
    forward_pairs = []
    for a in range(sh):
        for j in range(sq):
            s_to = sq * (a % ratio) + j
            q_to = a // ratio
            forward_pairs.append((j * sh + a, q_to * sh + s_to))
    backward_pairs = [(b, a) for a, b in forward_pairs]
    piece = lax.ppermute(piece, both_axes, forward_pairs)
    shared_cols = jnp.concatenate(
        [
            lax.dynamic_slice_in_dim(shared_gate, q * gf, gf, 1),
            lax.dynamic_slice_in_dim(shared_up, q * gf, gf, 1),
        ],
        axis=1,
    )
    fold = rows_w * 2 * gf // dim
    bands = dim // (2 * gf)
    shared_rows = jnp.concatenate(
        [shared_cols[fold * band : fold * band + fold] for band in range(bands)], axis=1
    )
    piece = jnp.concatenate([piece, shared_rows], axis=0)
    piece, w_all = lax.optimization_barrier((piece, w_all))
    rows_all = lax.all_gather(piece, "shard", axis=0)
    own_rows = own_out + own_down
    w_out = rows_all[:, :own_out].reshape(gw, dim)
    w_down = rows_all[:, own_out:own_rows].reshape(gf, dim)
    w_shared = (
        rows_all[:, own_rows:]
        .reshape(sh, fold, bands, 2 * gf)
        .transpose(0, 2, 1, 3)
        .reshape(dim, 2 * gf)
    )

    route_ids = routes[0]
    expert_ids = jnp.arange(experts, dtype=jnp.int32)
    named = jnp.any(route_ids[:, :, None] == expert_ids[None, None, :], axis=1).astype(f32)
    earlier = (
        jnp.arange(toks)[:, None] > jnp.arange(toks)[None, :]
    ).astype(f32)
    rank = jnp.dot(earlier, named)
    dispatch = (
        (named.T[:, None, :] > 0.0)
        & (rank.T[:, None, :] == jnp.arange(CAP, dtype=f32)[None, :, None])
    ).astype(bf)
    slots = experts * CAP
    dispatch_flat = dispatch.reshape(slots, toks)
    live = (q * toks + jnp.arange(toks, dtype=jnp.int32) < lengths[0]).astype(f32)
    cot = out_cotangent[0].astype(f32) * live[:, None]
    cot_low = cot.astype(bf)

    def to_experts(rows):
        return lax.all_to_all(
            rows.reshape(experts, CAP, rows.shape[-1]),
            "shard",
            split_axis=0,
            concat_axis=1,
            tiled=True,
        )

    cot_ext = jnp.concatenate(
        [cot_low, named.astype(bf), jnp.zeros((toks, 128 - experts), bf)], axis=1
    )
    cot_rows_ext = to_experts(times(dispatch_flat, cot_ext).astype(bf))

    x_wide = x_all.astype(f32)
    x_r = row_scale(x_wide)
    proj = times(x_all, w_all) * x_r

    small_all = w_all.reshape(sh, rows_w, total)[:, :, at_small:at_router].reshape(sh, -1)
    at = taps * conv_own
    conv_full = (
        small_all[:, :at].reshape(sh, taps, conv_own).transpose(1, 0, 2).reshape(taps, conv_all)
    )
    offset_full = small_all[:, at : at + conv_own].reshape(conv_all)
    at = at + conv_own
    bias_full = small_all[:, at : at + head_own].reshape(heads)
    decay_full = small_all[:, at + head_own : at + 2 * head_own].reshape(heads)
    skip_full = small_all[:, at + 2 * head_own : at + 3 * head_own].reshape(heads)
    router_full = w_all[:, at_router:at_moe]
    moe_gain_full = w_all[:, at_moe].astype(f32)

    def group(values, width):
        return lax.dynamic_slice_in_dim(values, q * width, width, values.ndim - 1)

    conv_local = jnp.concatenate([group(conv_full, gw), conv_full[:, inner:]], axis=1).astype(f32)
    offset_local = jnp.concatenate([group(offset_full, gw), offset_full[inner:]]).astype(f32)
    bias_local = group(bias_full, gh).astype(f32)
    decay_local = group(decay_full, gh).astype(f32)
    skip_local = group(skip_full, gh).astype(f32)

    per_head = gw // gh
    taps_in = jnp.concatenate(
        [conv_local, offset_local[None], jnp.zeros((8 - taps - 1, gw + keys_w), f32)], axis=0
    )
    decay_rate = -jnp.exp(decay_local)
    head_in = jnp.pad(jnp.stack([bias_local, decay_rate]), ((0, 6), (0, 128 - gh)))
    skip_in = jnp.broadcast_to(jnp.repeat(skip_local, per_head)[None], (8, gw))
    mixed, q_low, square_part, starts = scan_forward(proj, taps_in, head_in, skip_in)

    out_part = times(q_low, w_out).astype(bf)
    out_sum = lax.psum_scatter(out_part, "seq", scatter_dimension=0, tiled=True)
    square = lax.psum(square_part.reshape(sq, toks), "seq")
    q_r = lax.rsqrt(square / inner + epsilon).reshape(seq_rows, 1)
    out_sum, cot_rows_ext = lax.optimization_barrier((out_sum, cot_rows_ext))
    cot_rows = cot_rows_ext[:, :, :dim]
    row_mask = cot_rows_ext[:, :, dim : dim + experts].astype(f32)
    tok_r = lax.dynamic_slice_in_dim(q_r, q * toks, toks, 0)
    x_tok = x_low.astype(f32)
    added = out_sum.astype(f32) * tok_r
    resid = x_tok + added

    resid_r = row_scale(resid)
    resid_n = resid * resid_r
    moe_in = (resid_n * moe_gain_full[None, :]).astype(bf)
    moe_all = lax.all_gather(moe_in, "seq", axis=0, tiled=True)
    cot_late, moe_all = lax.optimization_barrier((cot_low, moe_all))
    cot_all = lax.all_gather(cot_late, "seq", axis=0, tiled=True)
    logits = times(moe_in, router_full)

    def masked_softmax(values, mask):
        top = jnp.max(jnp.where(mask > 0.0, values, -jnp.inf), axis=-1, keepdims=True)
        top = jnp.where(top > -jnp.inf, top, 0.0)
        powers = jnp.where(mask > 0.0, jnp.exp(jnp.where(mask > 0.0, values - top, 0.0)), 0.0)
        return powers / jnp.maximum(jnp.sum(powers, axis=-1, keepdims=True), 1e-30)

    gates = masked_softmax(logits, named)
    rows = to_experts(times(dispatch_flat, moe_in).astype(bf))
    row_logits = lax.dot_general(
        rows, router_full, (((2,), (0,)), ((), ())), preferred_element_type=f32
    )
    row_gates = masked_softmax(row_logits, row_mask)
    own_ids = lax.axis_index("shard") * local_e + jnp.arange(local_e, dtype=jnp.int32)
    own_pick = (own_ids[:, None] == expert_ids[None, :]).astype(f32)
    row_gate = jnp.sum(row_gates * own_pick[:, None, :], axis=2, keepdims=True)

    d_raw = jnp.einsum("ecd,efd->ecf", cot_rows, expert_down, preferred_element_type=f32)
    e_gate = jnp.einsum("ecd,edf->ecf", rows, expert_gate, preferred_element_type=f32)
    e_up = jnp.einsum("ecd,edf->ecf", rows, expert_up, preferred_element_type=f32)
    e_sig = jax.nn.sigmoid(e_gate)
    e_silu = e_gate * e_sig
    e_act = (e_silu * e_up).astype(bf)
    d_gate_row = jnp.sum(e_act.astype(f32) * d_raw, axis=2, keepdims=True)
    d_act = row_gate * d_raw
    d_g = (d_act * e_up * (e_sig * (1.0 + e_gate * (1.0 - e_sig)))).astype(bf)
    d_v = (d_act * e_silu).astype(bf)
    d_row = jnp.einsum("ecf,edf->ecd", d_g, expert_gate, preferred_element_type=f32) + jnp.einsum(
        "ecf,edf->ecd", d_v, expert_up, preferred_element_type=f32
    )
    hi = d_gate_row.astype(bf)
    lo = (d_gate_row - hi.astype(f32)).astype(bf)
    back_rows = jnp.concatenate(
        [d_row.astype(bf), hi, lo, jnp.zeros(hi.shape[:2] + (126,), bf)], axis=2
    )

    def from_experts(values):
        return lax.all_to_all(values, "shard", split_axis=1, concat_axis=0, tiled=True)

    d_returned = from_experts(back_rows)
    e_out = jnp.einsum("ecf,efd->ecd", e_act, expert_down, preferred_element_type=f32).astype(bf)
    scaled_act = (row_gate * e_act.astype(f32)).astype(bf)
    grad_e_down = jnp.einsum("ecf,ecd->efd", scaled_act, cot_rows, preferred_element_type=f32)
    grad_e_gate = jnp.einsum("ecd,ecf->edf", rows, d_g, preferred_element_type=f32)
    grad_e_up = jnp.einsum("ecd,ecf->edf", rows, d_v, preferred_element_type=f32)
    e_sum = lax.psum(
        (grad_e_gate.astype(bf), grad_e_up.astype(bf), grad_e_down.astype(bf)), "seq"
    )

    s_both = times(moe_all, w_shared)
    s_gate, s_up = s_both[:, :gf], s_both[:, gf:]
    s_sig = jax.nn.sigmoid(s_gate)
    s_silu = s_gate * s_sig
    s_act = (s_silu * s_up).astype(bf)
    d_sh = times_transposed(cot_all, w_down)
    d_both = jnp.concatenate(
        [
            (d_sh * s_up * (s_sig * (1.0 + s_gate * (1.0 - s_sig)))).astype(bf),
            (d_sh * s_silu).astype(bf),
        ],
        axis=1,
    )
    d_moe_part = times_transposed(d_both, w_shared).astype(bf)
    d_moe_shared = lax.psum_scatter(d_moe_part, "seq", scatter_dimension=0, tiled=True)
    shared_part = times(s_act, w_down).astype(bf)
    shared_sum = lax.psum_scatter(shared_part, "seq", scatter_dimension=0, tiled=True)

    d_flat = d_returned.reshape(slots, dim + 128)
    gate_back = jnp.sum(
        d_flat[:, dim : dim + 2].astype(f32), axis=1
    ).reshape(experts, CAP)
    d_gates = jnp.sum(dispatch.astype(f32) * gate_back[:, :, None], axis=1).T
    d_logits = gates * (d_gates - jnp.sum(gates * d_gates, axis=1, keepdims=True))
    d_moe = (
        transposed_times(dispatch_flat, d_flat[:, :dim])
        + d_moe_shared.astype(f32)
        + jnp.dot(d_logits, router_full.astype(f32).T, precision=highest)
    )
    grad_router = jnp.dot(moe_in.astype(f32).T, d_logits, precision=highest)
    grad_moe = jnp.sum(d_moe * resid_n, axis=0)
    d_scaled = d_moe * moe_gain_full[None, :]
    d_resid = (
        cot
        + d_scaled * resid_r
        - resid_n * (resid_r * jnp.mean(d_scaled * resid_n, axis=1, keepdims=True))
    )
    d_o = d_resid.astype(bf)
    kappa = jnp.sum(d_o.astype(f32) * added, axis=1) / inner
    d_o_all = lax.all_gather(d_o, "seq", axis=0, tiled=True)
    kappa_all = lax.all_gather(kappa.reshape(1, toks), "seq", axis=0).reshape(seq_rows, 1)

    returned = from_experts(e_out)
    weighted = (gates.T[:, None, :] * dispatch.astype(f32)).reshape(slots, toks)
    combined = lax.dot_general(
        weighted,
        returned.reshape(slots, dim).astype(f32),
        (((0,), (0,)), ((), ())),
        preferred_element_type=f32,
    )
    block_output = ((resid + shared_sum.astype(f32) + combined) * live[:, None]).astype(bf)[None]

    d_gated = times_transposed(d_o_all, w_out)
    grad_out_part = transposed_times(q_low, (q_r * d_o_all.astype(f32)).astype(bf))
    grad_down_part = transposed_times(s_act, cot_all)
    grad_shared_part = transposed_times(moe_all, d_both)

    def to_shards(values):
        return lax.all_to_all(values.astype(bf), "shard", split_axis=0, concat_axis=0, tiled=True)

    rows_part = jnp.concatenate(
        [grad_out_part.reshape(sh, own_out, dim), grad_down_part.reshape(sh, own_down, dim)],
        axis=1,
    )
    mid_part = jnp.concatenate(
        [
            grad_shared_part,
            grad_router,
            grad_moe[:, None],
            jnp.zeros((dim, 128 - experts - 1), f32),
        ],
        axis=1,
    )
    moved_rows = to_shards(rows_part)
    moved_mid = to_shards(mid_part.reshape(sh, rows_w, 2 * gf + 128))

    row_values = jnp.concatenate(
        [q_r, kappa_all, x_r, jnp.zeros((seq_rows, 5), f32)], axis=1
    )
    d_proj, d_taps, d_head, d_skip = scan_backward(
        proj, mixed, d_gated, row_values, starts, taps_in, head_in, skip_in
    )
    grad_conv_local = d_taps[:taps]
    grad_offset_local = d_taps[taps]
    grad_bias_local = d_head[0, :gh]
    grad_decay_local = d_head[1, :gh] * decay_rate
    grad_skip_local = jnp.sum(d_skip[0].reshape(gh, per_head), axis=1)
    d_proj, moved_rows, moved_mid = lax.optimization_barrier((d_proj, moved_rows, moved_mid))
    rows_sum = jnp.sum(moved_rows.astype(f32), axis=0)
    rows_sum = lax.ppermute(rows_sum.astype(bf), both_axes, backward_pairs)
    rows_grad = lax.all_gather(rows_sum, "seq", axis=0)
    grad_out_raw = rows_grad[:, :own_out].reshape(sq * own_out, dim).astype(f32)
    grad_down = rows_grad[:, own_out:].reshape(sq * own_down, dim).astype(f32)
    grad_out = norm_gain.astype(f32)[:, None] * grad_out_raw
    grad_norm = jnp.sum(out_weight.astype(f32) * grad_out_raw, axis=1)

    mid_sum = jnp.sum(moved_mid.astype(f32), axis=0)
    mid_all = lax.all_gather(mid_sum.astype(bf), "seq", axis=0).astype(f32)
    grad_shared_gate = mid_all[:, :, :gf].transpose(1, 0, 2).reshape(rows_w, fs)
    grad_shared_up = mid_all[:, :, gf : 2 * gf].transpose(1, 0, 2).reshape(rows_w, fs)
    mid_rest = jnp.sum(mid_all[:, :, 2 * gf :], axis=0)
    grad_router_weight = mid_rest[:, :experts]
    grad_moe_gain = mid_rest[:, experts]

    back_part = times_transposed(d_proj, w_all).astype(bf)
    back_sum = lax.psum_scatter(back_part, "seq", scatter_dimension=0, tiled=True).astype(f32)
    tok_x_r = row_scale(x_tok)
    x_n = x_tok * tok_x_r
    input_grad = (
        d_resid + back_sum - x_n * (tok_x_r * jnp.mean(back_sum * x_tok, axis=1, keepdims=True))
    )[None]

    grad_in_part = transposed_times(x_all, d_proj)[:, :used]

    def spread(local, count):
        wide = jnp.zeros(local.shape[:-1] + (count,), f32)
        return lax.dynamic_update_slice_in_dim(wide, local, q * local.shape[-1], local.ndim - 1)

    conv_rows = jnp.concatenate([grad_conv_local, grad_offset_local[None]], axis=0)
    conv_wide = jnp.concatenate([spread(conv_rows[:, :gw], inner), conv_rows[:, gw:]], axis=1)
    head_wide = spread(jnp.stack([grad_bias_local, grad_decay_local, grad_skip_local]), heads)
    small_part = jnp.concatenate(
        [
            conv_wide.reshape(taps + 1, sh, conv_own).transpose(1, 0, 2).reshape(sh, -1),
            head_wide.reshape(3, sh, head_own).transpose(1, 0, 2).reshape(sh, -1),
        ],
        axis=1,
    )
    small_count = small_part.shape[1]
    small_part = jnp.pad(
        small_part, ((0, 0), (0, rows_w * small_cols - small_count))
    ).reshape(sh, rows_w, small_cols)
    last_part = jnp.concatenate(
        [
            grad_in_part.reshape(sh, rows_w, used),
            small_part,
            jnp.zeros((sh, rows_w, total - used - small_cols), f32),
        ],
        axis=2,
    )
    last_sum = jnp.sum(to_shards(last_part).astype(f32), axis=0)
    last_all = lax.all_gather(last_sum.astype(bf), "seq", axis=0).astype(f32)

    def side_by_side(start, width):
        return last_all[:, :, start : start + width].transpose(1, 0, 2).reshape(rows_w, sq * width)

    grad_in_raw = jnp.concatenate(
        [
            side_by_side(0, gw),
            side_by_side(gw, gw),
            jnp.sum(last_all[:, :, 2 * gw : 2 * gw + keys_w], axis=0),
            side_by_side(2 * gw + keys_w, gh),
        ],
        axis=1,
    )
    grad_in = gain_col * grad_in_raw
    grad_mixer_gain = jnp.sum(in_weight.astype(f32) * grad_in_raw, axis=1)
    small_sum = jnp.sum(last_all[:, :, used : used + small_cols], axis=0).reshape(-1)
    at = taps * conv_own
    grad_conv = small_sum[:at].reshape(taps, conv_own)
    grad_offset = small_sum[at : at + conv_own]
    at = at + conv_own
    grad_bias = small_sum[at : at + head_own]
    grad_decay = small_sum[at + head_own : at + 2 * head_own]
    grad_skip = small_sum[at + 2 * head_own : at + 3 * head_own]
    return (
        block_output,
        input_grad,
        grad_mixer_gain,
        grad_in,
        grad_conv,
        grad_offset,
        grad_bias,
        grad_decay,
        grad_skip,
        grad_norm,
        grad_out,
        grad_moe_gain,
        grad_router_weight,
        grad_shared_gate,
        grad_shared_up,
        grad_down,
        e_sum[0].astype(f32),
        e_sum[1].astype(f32),
        e_sum[2].astype(f32),
    )


def solution(mesh):
    placed = (
        P("shard", "seq", None),
        P("shard"),
        P("shard", "seq", None),
        P("shard", "seq", None),
        P("shard"),
        P("shard", None),
        P(None, "shard"),
        P("shard"),
        P("shard"),
        P("shard"),
        P("shard"),
        P("shard"),
        P("shard", None),
        P("shard"),
        P("shard", None),
        P("shard", None),
        P("shard", None),
        P("shard", None),
        P("shard", None, None),
        P("shard", None, None),
        P("shard", None, None),
    )
    return jax.shard_map(
        on_device,
        mesh=mesh,
        in_specs=placed,
        out_specs=(
            P("shard", "seq", None),
            P("shard", "seq", None),
            P("shard"),
            P("shard", None),
            P(None, "shard"),
            P("shard"),
            P("shard"),
            P("shard"),
            P("shard"),
            P("shard"),
            P("shard", None),
            P("shard"),
            P("shard", None),
            P("shard", None),
            P("shard", None),
            P("shard", None),
            P("shard", None, None),
            P("shard", None, None),
            P("shard", None, None),
        ),
        check_vma=False,
    )
```

```python
import jax
import jax.numpy as jnp
from jax import lax
from jax.experimental import pallas as pl
from jax.experimental.pallas import tpu as pltpu
from jax.sharding import PartitionSpec as P

CAP = 32


epsilon = 1e-05
highest = lax.Precision.HIGHEST
both_axes = ("seq", "shard")


def times(left, right):
    return jnp.dot(left, right, preferred_element_type=jnp.float32)


def times_transposed(left, right):
    return lax.dot_general(
        left, right, (((1,), (1,)), ((), ())), preferred_element_type=jnp.float32
    )


def transposed_times(left, right):
    return lax.dot_general(
        left, right, (((0,), (0,)), ((), ())), preferred_element_type=jnp.float32
    )


def silu_slope(values):
    sigma = jax.nn.sigmoid(values)
    return sigma * (1.0 + values * (1.0 - sigma))


def row_scale(values):
    return lax.rsqrt(jnp.mean(values * values, axis=-1, keepdims=True) + epsilon)


CHUNK = 128
WIDE = 384
CONVW = 640
PAIRS = 3
HEADS_HERE = 6


def split_two(values):
    high = values.astype(jnp.bfloat16)
    return high, (values - high.astype(jnp.float32)).astype(jnp.bfloat16)


def ones_times(ones, values):
    high, low = split_two(values)
    return times(ones, high) + times(ones, low)


def times_ones(values, ones):
    high, low = split_two(values)
    return times(high, ones) + times(low, ones)


def transposed_times_ones(values, ones):
    high, low = split_two(values)
    return transposed_times(high, ones) + transposed_times(low, ones)


def grid_of(shape):
    rows = lax.broadcasted_iota(jnp.int32, shape, 0)
    columns = lax.broadcasted_iota(jnp.int32, shape, 1)
    return rows, columns


def mark(condition):
    return jnp.where(condition, 1.0, 0.0).astype(jnp.bfloat16)


def chunk_parts(proj, prev, has_prev, taps_ref, head_ref, pad_ref):
    f32, bf = jnp.float32, jnp.bfloat16
    feed = proj[:, WIDE : WIDE + CONVW].astype(bf).astype(f32)
    before = prev[:, WIDE : WIDE + CONVW].astype(bf).astype(f32)
    pad_ref[0:8, :] = jnp.where(has_prev, before, 0.0)
    pad_ref[8 : 8 + CHUNK, :] = feed
    conv = taps_ref[4:5, :]
    for tap in range(4):
        conv = conv + taps_ref[tap : tap + 1, :] * pad_ref[5 + tap : 5 + tap + CHUNK, :]
    sig = jax.nn.sigmoid(conv)
    act = conv * sig
    u = act[:, :WIDE]
    key = act[:, WIDE : WIDE + 128].astype(bf)
    query = act[:, WIDE + 128 :].astype(bf)
    step_low = proj[:, WIDE + CONVW :].astype(bf).astype(f32)
    pre = step_low + head_ref[0:1, :]
    rows, columns = grid_of((CHUNK, 128))
    here = columns < HEADS_HERE
    dt = jnp.where(here, jnp.maximum(pre, 0.0) + jnp.log1p(jnp.exp(-jnp.abs(pre))), 0.0)
    la = dt * head_ref[1:2, :]
    lower = mark(rows >= columns)
    cum = ones_times(lower, la)
    end = cum[CHUNK - 1 : CHUNK, :]
    wide_rows, wide_columns = grid_of((128, WIDE))
    widen = mark(wide_columns // 64 == wide_rows)
    dt_w = times_ones(dt, widen)
    e_w = times_ones(jnp.exp(cum), widen)
    w_w = times_ones(jnp.exp(end - cum), widen)
    full_rows, full_columns = grid_of((128, 2 * PAIRS * 128))
    la_full = times_ones(la, mark(full_columns // 128 == full_rows))
    scores = times_transposed(query, key)
    return dict(
        conv=conv, sig=sig, u=u, key=key, query=query, pre=pre, here=here, dt=dt, lower=lower,
        dt_w=dt_w, e_w=e_w, w_w=w_w, la_full=la_full, scores=scores, xs=u * dt_w,
    )


def pair_table(parts, pair):
    rows, columns = grid_of((CHUNK, 256))
    local = columns % 128
    steps = jnp.where(rows > local, parts["la_full"][:, 256 * pair : 256 * pair + 256], 0.0)
    gap = ones_times(parts["lower"], steps)
    causal = rows >= local
    decay = jnp.where(causal, jnp.exp(jnp.where(causal, gap, 0.0)), 0.0)
    scores = parts["scores"]
    return decay, decay * jnp.concatenate([scores, scores], axis=1)


def stack_heads(values, pair):
    both = values[:, 128 * pair : 128 * pair + 128]
    first = lax.broadcasted_iota(jnp.int32, both.shape, 1) < 64
    return jnp.concatenate(
        [jnp.where(first, both, 0.0), jnp.where(first, 0.0, both)], axis=0
    ).astype(jnp.bfloat16)


def scan_forward_kernel(
    proj_ref, prev_ref, taps_ref, head_ref, skip_ref,
    mixed_ref, q_ref, square_ref, start_ref, state_ref, pad_ref,
):
    f32, bf = jnp.float32, jnp.bfloat16
    chunk = pl.program_id(0)

    @pl.when(chunk == 0)
    def _():
        state_ref[...] = jnp.zeros(state_ref.shape, f32)

    parts = chunk_parts(
        proj_ref[...], prev_ref[...], chunk > 0, taps_ref, head_ref, pad_ref
    )
    state = state_ref[...]
    start_ref[0] = state
    xs = parts["xs"]
    inside = []
    for pair in range(PAIRS):
        _, table = pair_table(parts, pair)
        inside.append(times(table.astype(bf), stack_heads(xs, pair)))
    across = times(parts["query"], state.astype(bf))
    y = (
        jnp.concatenate(inside, axis=1)
        + parts["e_w"] * across
        + skip_ref[0:1, :] * parts["u"]
    )
    mixed = y.astype(bf)
    mixed_ref[...] = mixed
    gate = proj_ref[:, :WIDE]
    q_val = mixed.astype(f32) * (gate * jax.nn.sigmoid(gate))
    q_ref[...] = q_val.astype(bf)
    square_ref[...] = jnp.sum(q_val * q_val, axis=1, keepdims=True)
    state_ref[...] = state * parts["e_w"][CHUNK - 1 : CHUNK, :] + transposed_times(
        parts["key"], (xs * parts["w_w"]).astype(bf)
    )


def scan_backward_kernel(
    proj_ref, prev_ref, mixed_ref, d_gated_ref, rows_ref, start_ref, taps_ref, head_ref, skip_ref,
    d_proj_ref, d_taps_ref, d_head_ref, d_skip_ref,
    state_ref, pad_ref, late_ref,
):
    f32, bf = jnp.float32, jnp.bfloat16
    step = pl.program_id(0)
    last = pl.num_programs(0) - 1

    @pl.when(step == 0)
    def _():
        state_ref[...] = jnp.zeros(state_ref.shape, f32)
        late_ref[CHUNK : CHUNK + 8, :] = jnp.zeros((8, CONVW), f32)
        d_taps_ref[...] = jnp.zeros(d_taps_ref.shape, f32)
        d_head_ref[...] = jnp.zeros(d_head_ref.shape, f32)
        d_skip_ref[...] = jnp.zeros(d_skip_ref.shape, f32)

    parts = chunk_parts(
        proj_ref[...], prev_ref[...], step < last, taps_ref, head_ref, pad_ref
    )
    u, key, query, xs = parts["u"], parts["key"], parts["query"], parts["xs"]
    e_w, w_w, dt_w = parts["e_w"], parts["w_w"], parts["dt_w"]

    gate = proj_ref[:, :WIDE]
    gate_sig = jax.nn.sigmoid(gate)
    gate_act = gate * gate_sig
    mixed = mixed_ref[...].astype(f32)
    q_val = mixed * gate_act
    q_r = rows_ref[:, 0:1]
    d_q = q_r * d_gated_ref[...] - q_val * (q_r * q_r * rows_ref[:, 1:2])
    d_gate = d_q * mixed * (gate_sig * (1.0 + gate * (1.0 - gate_sig)))
    d_y = (d_q * gate_act).astype(bf).astype(f32)

    start = start_ref[0]
    start_low = start.astype(bf)
    d_end = state_ref[...]
    d_end_low = d_end.astype(bf)
    xw = xs * w_w
    ye = d_y * e_w
    ye_low = ye.astype(bf)
    across = times(query, start_low)
    pulled = times(key, d_end_low)
    d_query = times_transposed(ye_low, start_low)
    d_key = times_transposed(xw.astype(bf), d_end_low)
    state_ref[...] = d_end * e_w[CHUNK - 1 : CHUNK, :] + transposed_times(query, ye_low)
    d_scores = jnp.zeros((CHUNK, 128), f32)
    turns = jnp.zeros((CHUNK, 128), f32)
    d_xs = []
    for pair in range(PAIRS):
        decay, table = pair_table(parts, pair)
        xs_two = stack_heads(xs, pair)
        dy_two = stack_heads(d_y, pair)
        d_table = times_transposed(d_y[:, 128 * pair : 128 * pair + 128].astype(bf), xs_two)
        d_decay = d_table * decay
        d_scores = d_scores + d_decay[:, :128] + d_decay[:, 128:]
        d_gap = d_table * table
        table_low = table.astype(bf)
        d_xs.append(
            transposed_times(
                jnp.concatenate([table_low[:, :128], table_low[:, 128:]], axis=0), dy_two
            )
        )
        two_rows, two_columns = grid_of((256, 128))
        own = mark(two_columns == 2 * pair + two_rows // 128)
        turns = turns + times_ones(d_gap, own)
        turns = turns - transposed_times_ones(
            jnp.concatenate([d_gap[:, :128], d_gap[:, 128:]], axis=0), own
        )
    d_xs = jnp.concatenate(d_xs, axis=1) + w_w * pulled
    d_scores_low = d_scores.astype(bf)
    d_query = d_query + times(d_scores_low, key)
    d_key = d_key + transposed_times(d_scores_low, query)

    rows, columns = grid_of((CHUNK, 128))
    upper = mark(columns >= rows)
    strict = mark(columns < rows)
    sum_rows, sum_columns = grid_of((WIDE, 128))
    per_head = mark(sum_rows // 64 == sum_columns)
    end_row = jnp.sum(d_end * start, axis=0, keepdims=True) * e_w[CHUNK - 1 : CHUNK, :]
    wide = ones_times(upper, ye * across) + ones_times(strict, xw * pulled) + end_row
    d_la = ones_times(upper, turns) + times_ones(wide, per_head)
    d_dt = times_ones(d_xs * u, per_head) + d_la * head_ref[1:2, :]
    d_pre = jnp.where(parts["here"], d_dt * jax.nn.sigmoid(parts["pre"]), 0.0)
    d_head_ref[0:1, :] += jnp.sum(d_pre, axis=0, keepdims=True)
    d_head_ref[1:2, :] += jnp.sum(d_la * parts["dt"], axis=0, keepdims=True)
    d_skip_ref[0:1, :] += jnp.sum(d_y * u, axis=0, keepdims=True)

    d_u = d_xs * dt_w + skip_ref[0:1, :] * d_y
    conv, sig = parts["conv"], parts["sig"]
    d_conv = jnp.concatenate([d_u, d_key, d_query], axis=1) * (sig * (1.0 + conv * (1.0 - sig)))
    late_ref[0:CHUNK, :] = d_conv
    d_feed = jnp.zeros((CHUNK, CONVW), f32)
    for tap in range(4):
        d_feed = d_feed + taps_ref[tap : tap + 1, :] * late_ref[3 - tap : 3 - tap + CHUNK, :]
        d_taps_ref[tap : tap + 1, :] += jnp.sum(
            d_conv * pad_ref[5 + tap : 5 + tap + CHUNK, :], axis=0, keepdims=True
        )
    d_taps_ref[4:5, :] += jnp.sum(d_conv, axis=0, keepdims=True)
    late_ref[CHUNK : CHUNK + 8, :] = d_conv[0:8, :]
    scale = rows_ref[:, 2:3]
    d_proj_ref[:, :WIDE] = (d_gate * scale).astype(bf)
    d_proj_ref[:, WIDE : WIDE + CONVW] = (d_feed * scale).astype(bf)
    d_proj_ref[:, WIDE + CONVW :] = (d_pre * scale).astype(bf)


def whole(shape):
    return pl.BlockSpec(shape, lambda step: (0,) * len(shape))


def scan_forward(proj, taps, head, skip):
    rows, width = proj.shape
    chunks = rows // CHUNK
    by_chunk = lambda step: (step, 0)
    return pl.pallas_call(
        scan_forward_kernel,
        grid=(chunks,),
        in_specs=[
            pl.BlockSpec((CHUNK, width), by_chunk),
            pl.BlockSpec((8, width), lambda step: (jnp.maximum(step * (CHUNK // 8) - 1, 0), 0)),
            whole(taps.shape),
            whole(head.shape),
            whole(skip.shape),
        ],
        out_specs=[
            pl.BlockSpec((CHUNK, WIDE), by_chunk),
            pl.BlockSpec((CHUNK, WIDE), by_chunk),
            pl.BlockSpec((CHUNK, 1), by_chunk),
            pl.BlockSpec((1, 128, WIDE), lambda step: (step, 0, 0)),
        ],
        out_shape=[
            jax.ShapeDtypeStruct((rows, WIDE), jnp.bfloat16),
            jax.ShapeDtypeStruct((rows, WIDE), jnp.bfloat16),
            jax.ShapeDtypeStruct((rows, 1), jnp.float32),
            jax.ShapeDtypeStruct((chunks, 128, WIDE), jnp.float32),
        ],
        scratch_shapes=[
            pltpu.VMEM((128, WIDE), jnp.float32),
            pltpu.VMEM((CHUNK + 8, CONVW), jnp.float32),
        ],
        compiler_params=pltpu.CompilerParams(vmem_limit_bytes=32 << 20),
        cost_estimate=pl.CostEstimate(
            flops=3 << 30, bytes_accessed=12 << 20, transcendentals=4 << 20
        ),
        name="scan_forward",
    )(proj, proj, taps, head, skip)


def scan_backward(proj, mixed, d_gated, row_values, starts, taps, head, skip):
    rows, width = proj.shape
    chunks = rows // CHUNK
    by_chunk = lambda step: (chunks - 1 - step, 0)
    return pl.pallas_call(
        scan_backward_kernel,
        grid=(chunks,),
        in_specs=[
            pl.BlockSpec((CHUNK, width), by_chunk),
            pl.BlockSpec(
                (8, width),
                lambda step: (jnp.maximum((chunks - 1 - step) * (CHUNK // 8) - 1, 0), 0),
            ),
            pl.BlockSpec((CHUNK, WIDE), by_chunk),
            pl.BlockSpec((CHUNK, WIDE), by_chunk),
            pl.BlockSpec((CHUNK, row_values.shape[1]), by_chunk),
            pl.BlockSpec((1, 128, WIDE), lambda step: (chunks - 1 - step, 0, 0)),
            whole(taps.shape),
            whole(head.shape),
            whole(skip.shape),
        ],
        out_specs=[
            pl.BlockSpec((CHUNK, width), by_chunk),
            whole((8, CONVW)),
            whole((8, 128)),
            whole((8, WIDE)),
        ],
        out_shape=[
            jax.ShapeDtypeStruct((rows, width), jnp.bfloat16),
            jax.ShapeDtypeStruct((8, CONVW), jnp.float32),
            jax.ShapeDtypeStruct((8, 128), jnp.float32),
            jax.ShapeDtypeStruct((8, WIDE), jnp.float32),
        ],
        scratch_shapes=[
            pltpu.VMEM((128, WIDE), jnp.float32),
            pltpu.VMEM((CHUNK + 8, CONVW), jnp.float32),
            pltpu.VMEM((CHUNK + 8, CONVW), jnp.float32),
        ],
        compiler_params=pltpu.CompilerParams(vmem_limit_bytes=48 << 20),
        cost_estimate=pl.CostEstimate(
            flops=10 << 30, bytes_accessed=20 << 20, transcendentals=8 << 20
        ),
        name="scan_backward",
    )(proj, proj, mixed, d_gated, row_values, starts, taps, head, skip)


def expert_early_kernel(cot_ref, down_ref, raw_ref):
    cot = cot_ref[...].reshape(-1, cot_ref.shape[-1])
    raw_ref[0] = times_transposed(cot, down_ref[0])


def expert_main_kernel(
    rows_ref, routed_ref, raw_ref, gate_ref, up_ref, router_ref, marks_ref,
    back_ref, act_ref, scaled_ref, d_g_ref, d_v_ref,
):
    f32, bf = jnp.float32, jnp.bfloat16
    dim = rows_ref.shape[-1]
    rows = rows_ref[...].reshape(-1, dim)
    routed = routed_ref[...].reshape(-1, 128).astype(f32) > 0.0
    logits = times(rows, router_ref[...])
    top = jnp.max(jnp.where(routed, logits, -1e30), axis=1, keepdims=True)
    powers = jnp.where(routed, jnp.exp(jnp.where(routed, logits - top, 0.0)), 0.0)
    own = jnp.sum(powers * marks_ref[0, 0:1, :], axis=1, keepdims=True)
    gate = own / jnp.maximum(jnp.sum(powers, axis=1, keepdims=True), 1e-30)
    g = times(rows, gate_ref[0])
    v = times(rows, up_ref[0])
    sig = jax.nn.sigmoid(g)
    silu = g * sig
    act = (silu * v).astype(bf)
    act_wide = act.astype(f32)
    raw = raw_ref[0]
    d_gate = jnp.sum(act_wide * raw, axis=1, keepdims=True)
    d_act = gate * raw
    d_g = (d_act * v * (sig * (1.0 + g * (1.0 - sig)))).astype(bf)
    d_v = (d_act * silu).astype(bf)
    d_row = times_transposed(d_g, gate_ref[0]) + times_transposed(d_v, up_ref[0])
    high = d_gate.astype(bf).astype(f32)
    scalars = high * marks_ref[0, 1:2, :] + (d_gate - high) * marks_ref[0, 2:3, :]
    lead = back_ref.shape[:-1]
    back_ref[:, :, :, :dim] = d_row.astype(bf).reshape(*lead, dim)
    back_ref[:, :, :, dim:] = scalars.astype(bf).reshape(*lead, 128)
    act_ref[0] = act
    scaled_ref[0] = (gate * act_wide).astype(bf)
    d_g_ref[0] = d_g
    d_v_ref[0] = d_v


def expert_late_kernel(
    rows_ref, cot_ref, act_ref, scaled_ref, d_g_ref, d_v_ref, down_ref,
    out_ref, grads_ref,
):
    bf = jnp.bfloat16
    dim = rows_ref.shape[-1]
    rows = rows_ref[...].reshape(-1, dim)
    cot = cot_ref[...].reshape(-1, dim)
    out_ref[...] = times(act_ref[0], down_ref[0]).astype(bf).reshape(out_ref.shape)
    units = act_ref.shape[-1]
    grads_ref[0, :dim] = transposed_times(rows, d_g_ref[0]).astype(bf)
    grads_ref[0, dim : 2 * dim] = transposed_times(rows, d_v_ref[0]).astype(bf)
    for block in range(dim // units):
        at = 2 * dim + block * units
        grads_ref[0, at : at + units] = transposed_times(
            scaled_ref[0], cot[:, block * units : block * units + units]
        ).astype(bf)


def expert_slots(shape, start=0):
    return pl.BlockSpec(
        (shape[0], 1) + tuple(shape[2:]), lambda e: (0, e) + (0,) * (len(shape) - 3) + (start,)
    )


def per_expert(shape):
    return pl.BlockSpec((1,) + tuple(shape[1:]), lambda e: (e,) + (0,) * (len(shape) - 1))


def expert_params(flops, moved):
    return dict(
        compiler_params=pltpu.CompilerParams(vmem_limit_bytes=56 << 20),
        cost_estimate=pl.CostEstimate(flops=flops, bytes_accessed=moved, transcendentals=1 << 19),
    )


def expert_early(cot_rows, down):
    sources, local, cap, _ = cot_rows.shape
    units, dim = down.shape[1:]
    return pl.pallas_call(
        expert_early_kernel,
        grid=(local,),
        in_specs=[expert_slots((sources, local, cap, dim)), per_expert(down.shape)],
        out_specs=per_expert((local, sources * cap, units)),
        out_shape=jax.ShapeDtypeStruct((local, sources * cap, units), jnp.float32),
        name="expert_early",
        **expert_params(2 << 30, 8 << 20),
    )(cot_rows, down)


def expert_main(rows, cot_rows, raw, gate, up, w_all, marks):
    sources, local, cap, dim = rows.shape
    units = gate.shape[2]
    count = sources * cap
    hidden = jax.ShapeDtypeStruct((local, count, units), jnp.bfloat16)
    back = (sources, local, cap, dim + 128)
    return pl.pallas_call(
        expert_main_kernel,
        grid=(local,),
        in_specs=[
            expert_slots(rows.shape),
            expert_slots((sources, local, cap, 128), dim // 128),
            per_expert(raw.shape),
            per_expert(gate.shape),
            per_expert(up.shape),
            pl.BlockSpec((dim, 128), lambda e: (0, w_all.shape[1] // 128 - 1)),
            per_expert(marks.shape),
        ],
        out_specs=[expert_slots(back)] + [per_expert(hidden.shape)] * 4,
        out_shape=[jax.ShapeDtypeStruct(back, jnp.bfloat16)] + [hidden] * 4,
        name="expert_main",
        **expert_params(8 << 30, 20 << 20),
    )(rows, cot_rows, raw, gate, up, w_all, marks)


def expert_late(rows, cot_rows, act, scaled, d_g, d_v, down):
    sources, local, cap, dim = rows.shape
    units = down.shape[1]
    grads = (local, 3 * dim, units)
    return pl.pallas_call(
        expert_late_kernel,
        grid=(local,),
        in_specs=[expert_slots(rows.shape), expert_slots(rows.shape)]
        + [per_expert(act.shape)] * 4
        + [per_expert(down.shape)],
        out_specs=[
            expert_slots(rows.shape),
            per_expert(grads),
        ],
        out_shape=[
            jax.ShapeDtypeStruct(rows.shape, jnp.bfloat16),
            jax.ShapeDtypeStruct(grads, jnp.bfloat16),
        ],
        name="expert_late",
        **expert_params(7 << 30, 24 << 20),
    )(rows, cot_rows, act, scaled, d_g, d_v, down)


def assemble_kernel(gate_ref, rest_ref, weight_ref, gain_ref, grad_ref, small_ref):
    f32, bf = jnp.float32, jnp.bfloat16
    groups = gate_ref.shape[0]
    inner = groups * WIDE
    gain = gain_ref[...]
    grad_gain = jnp.zeros(gain.shape, f32)
    keys = jnp.zeros((gain.shape[0], 256), f32)
    tail = jnp.zeros((gain.shape[0], 128), f32)
    steps = jnp.zeros((gain.shape[0], 128), f32)
    rows, columns = grid_of((128, 128))

    def put(start, values):
        nonlocal grad_gain
        stop = start + values.shape[1]
        weight = weight_ref[:, start:stop].astype(f32)
        grad_gain = grad_gain + jnp.sum(weight * values, axis=1, keepdims=True)
        grad_ref[:, start:stop] = values * gain

    for group in range(groups):
        put(group * WIDE, gate_ref[group, :, :WIDE].astype(f32))
        put(inner + group * WIDE, rest_ref[group, :, :WIDE].astype(f32))
        keys = keys + rest_ref[group, :, WIDE:CONVW].astype(f32)
        last = rest_ref[group, :, CONVW:]
        tail = tail + last.astype(f32)
        moved = mark((rows < HEADS_HERE) & (columns == rows + HEADS_HERE * group))
        steps = steps + times(last, moved)
    put(2 * inner, keys)
    put(2 * inner + 256, steps[:, : groups * HEADS_HERE])
    lane = lax.broadcasted_iota(jnp.int32, tail.shape, 1)
    small_ref[...] = jnp.where(lane == 0, grad_gain, tail)


def assemble(gate_sums, rest_sums, in_weight, gain):
    rows, width = in_weight.shape
    return pl.pallas_call(
        assemble_kernel,
        in_specs=[pl.BlockSpec(memory_space=pltpu.VMEM)] * 4,
        out_specs=[pl.BlockSpec(memory_space=pltpu.VMEM)] * 2,
        out_shape=[
            jax.ShapeDtypeStruct((rows, width), jnp.float32),
            jax.ShapeDtypeStruct((rows, 128), jnp.float32),
        ],
        compiler_params=pltpu.CompilerParams(vmem_limit_bytes=32 << 20),
        cost_estimate=pl.CostEstimate(flops=4 << 20, bytes_accessed=8 << 20, transcendentals=0),
        name="assemble",
    )(gate_sums, rest_sums, in_weight, gain)


def sum_expert_grads(grads, q):
    f32, bf = jnp.float32, jnp.bfloat16
    size = lax.axis_size("seq")
    core, z = q % 2, q // 2
    mates = [(i, i ^ 1) for i in range(size)]
    near = [(i, 2 * ((i // 2) ^ 1) + i % 2) for i in range(size)]
    far = [(i, 2 * (size // 2 - 1 - i // 2) + i % 2) for i in range(size)]
    inner = ((z == 1) | (z == 2)).astype(jnp.int32)
    high = (z >= 2).astype(jnp.int32)

    def add(left, right):
        return (left.astype(f32) + right.astype(f32)).astype(bf)

    def halve(values, bit, pairs):
        parts = values.reshape(2, values.shape[0] // 2, values.shape[1])
        sent = lax.dynamic_index_in_dim(parts, 1 - bit, 0, keepdims=False)
        kept = lax.dynamic_index_in_dim(parts, bit, 0, keepdims=False)
        return add(kept, lax.ppermute(sent, "seq", pairs))

    def double(values, bit, pairs):
        other = lax.ppermute(values, "seq", pairs)
        both = jnp.stack([values, other])
        return jnp.where(bit == 0, both, both[::-1]).reshape(-1, values.shape[-1])

    flat = grads.reshape(2 * grads.shape[1], grads.shape[2])
    mine = halve(flat, core, mates)
    cutoff = mine.shape[0] // 2
    first, second = mine[:cutoff], mine[cutoff:]
    first, second = halve(first, inner, near), halve(second, high, far)
    first, second = halve(first, high, far), halve(second, inner, near)
    first, second = double(first, high, far), double(second, inner, near)
    first, second = double(first, inner, near), double(second, high, far)
    return double(jnp.concatenate([first, second], axis=0), core, mates).reshape(grads.shape)


def on_device(
    block_input,
    lengths,
    routes,
    out_cotangent,
    mixer_gain,
    in_weight,
    conv_weight,
    conv_bias,
    step_bias,
    decay_log,
    skip_gain,
    norm_gain,
    out_weight,
    moe_gain,
    router_weight,
    shared_gate,
    shared_up,
    shared_down,
    expert_gate,
    expert_up,
    expert_down,
):
    sq = lax.axis_size("seq")
    sh = lax.axis_size("shard")
    q = lax.axis_index("seq")
    f32 = jnp.float32
    bf = jnp.bfloat16
    x_low = block_input[0]
    toks, dim = x_low.shape
    seq_rows = toks * sq
    heads = step_bias.shape[0] * sh
    inner = norm_gain.shape[0] * sh
    conv_all = conv_bias.shape[0] * sh
    keys_w = conv_all - inner
    gh = heads // sq
    gw = inner // sq
    rows_w = in_weight.shape[0]
    experts = router_weight.shape[1]
    local_e = expert_gate.shape[0]
    fs = shared_gate.shape[1]
    gf = fs // sq
    taps = conv_weight.shape[0]
    conv_own = conv_bias.shape[0]
    head_own = step_bias.shape[0]

    gain_col = mixer_gain.astype(f32)[:, None]

    def cols(start, width):
        return lax.dynamic_slice_in_dim(in_weight, start, width, 1)

    w_cols = jnp.concatenate(
        [
            cols(q * gw, gw),
            cols(inner + q * gw, gw),
            in_weight[:, 2 * inner : 2 * inner + keys_w],
            cols(2 * inner + keys_w + q * gh, gh),
        ],
        axis=1,
    )
    w_cols = (w_cols.astype(f32) * gain_col).astype(bf)
    used = 2 * gw + keys_w + gh
    small = jnp.concatenate(
        [conv_weight.reshape(-1), conv_bias, step_bias, decay_log, skip_gain]
    )
    small_cols = -(-small.shape[0] // rows_w)
    small = jnp.pad(small, (0, small_cols * rows_w - small.shape[0])).reshape(rows_w, small_cols)
    packed = jnp.concatenate(
        [w_cols, small, router_weight, moe_gain[:, None]], axis=1
    )
    at_small = used
    at_router = at_small + small_cols
    at_moe = at_router + experts
    total = -(-(at_moe + 1) // 128) * 128
    packed = jnp.pad(packed, ((0, 0), (0, total - packed.shape[1])))

    def to_shards(values):
        return lax.all_to_all(values, "shard", split_axis=0, concat_axis=0, tiled=True)

    x_all = lax.all_gather(x_low, "seq", axis=0, tiled=True)
    w_all = to_shards(jnp.broadcast_to(packed[None], (sh, rows_w, total))).reshape(dim, total)

    out_scaled = (norm_gain.astype(f32)[:, None] * out_weight.astype(f32)).astype(bf)
    own_out = out_weight.shape[0] // sq
    own_down = shared_down.shape[0] // sq
    piece = jnp.concatenate(
        [
            lax.dynamic_slice_in_dim(out_scaled, q * own_out, own_out, 0),
            lax.dynamic_slice_in_dim(shared_down, q * own_down, own_down, 0),
        ],
        axis=0,
    )
    ratio = sh // sq
    forward_pairs = []
    for a in range(sh):
        for j in range(sq):
            s_to = sq * (a % ratio) + j
            q_to = a // ratio
            forward_pairs.append((j * sh + a, q_to * sh + s_to))
    backward_pairs = [(b, a) for a, b in forward_pairs]
    piece = lax.ppermute(piece, both_axes, forward_pairs)
    shared_cols = jnp.concatenate(
        [
            lax.dynamic_slice_in_dim(shared_gate, q * gf, gf, 1),
            lax.dynamic_slice_in_dim(shared_up, q * gf, gf, 1),
        ],
        axis=1,
    )
    fold = rows_w * 2 * gf // dim
    bands = dim // (2 * gf)
    shared_rows = jnp.concatenate(
        [shared_cols[fold * band : fold * band + fold] for band in range(bands)], axis=1
    )
    piece = jnp.concatenate([piece, shared_rows], axis=0)
    rows_all = lax.all_gather(piece, "shard", axis=0)
    own_rows = own_out + own_down
    w_out = rows_all[:, :own_out].reshape(gw, dim)
    w_down = rows_all[:, own_out:own_rows].reshape(gf, dim)
    w_shared = (
        rows_all[:, own_rows:]
        .reshape(sh, fold, bands, 2 * gf)
        .transpose(0, 2, 1, 3)
        .reshape(dim, 2 * gf)
    )

    route_ids = routes[0]
    expert_ids = jnp.arange(experts, dtype=jnp.int32)
    named = jnp.any(route_ids[:, :, None] == expert_ids[None, None, :], axis=1).astype(f32)
    earlier = (
        jnp.arange(toks)[:, None] > jnp.arange(toks)[None, :]
    ).astype(f32)
    rank = jnp.dot(earlier, named)
    dispatch = (
        (named.T[:, None, :] > 0.0)
        & (rank.T[:, None, :] == jnp.arange(CAP, dtype=f32)[None, :, None])
    ).astype(bf)
    slots = experts * CAP
    dispatch_flat = dispatch.reshape(slots, toks)
    live = (q * toks + jnp.arange(toks, dtype=jnp.int32) < lengths[0]).astype(f32)
    cot = out_cotangent[0].astype(f32) * live[:, None]
    cot_low = cot.astype(bf)

    local_slots = (sh, local_e, CAP)

    def dispatched(values):
        sent = times(dispatch_flat, values).astype(bf)
        return to_shards(sent.reshape(sh, local_e * CAP, -1)).reshape(*local_slots, -1)

    router_lane = at_router - (total - 128)
    lanes = jnp.arange(128, dtype=jnp.int32)
    named_lanes = jnp.pad(named, ((0, 0), (router_lane, 128 - router_lane - experts)))
    cot_rows = dispatched(jnp.concatenate([cot_low, named_lanes.astype(bf)], axis=1))

    x_wide = x_all.astype(f32)
    x_r = row_scale(x_wide)
    proj = times(x_all, w_all) * x_r

    small_all = w_all[:, at_small:at_router].reshape(sh, -1)
    at = taps * conv_own
    conv_full = (
        small_all[:, :at].reshape(sh, taps, conv_own).transpose(1, 0, 2).reshape(taps, conv_all)
    )
    offset_full = small_all[:, at : at + conv_own].reshape(conv_all)
    at = at + conv_own
    bias_full = small_all[:, at : at + head_own].reshape(heads)
    decay_full = small_all[:, at + head_own : at + 2 * head_own].reshape(heads)
    skip_full = small_all[:, at + 2 * head_own : at + 3 * head_own].reshape(heads)
    router_full = w_all[:, at_router:at_moe]
    moe_gain_full = w_all[:, at_moe].astype(f32)

    def group(values, width):
        return lax.dynamic_slice_in_dim(values, q * width, width, values.ndim - 1)

    conv_local = jnp.concatenate([group(conv_full, gw), conv_full[:, inner:]], axis=1).astype(f32)
    offset_local = jnp.concatenate([group(offset_full, gw), offset_full[inner:]]).astype(f32)
    bias_local = group(bias_full, gh).astype(f32)
    decay_local = group(decay_full, gh).astype(f32)
    skip_local = group(skip_full, gh).astype(f32)

    per_head = gw // gh
    taps_in = jnp.concatenate(
        [conv_local, offset_local[None], jnp.zeros((8 - taps - 1, gw + keys_w), f32)], axis=0
    )
    decay_rate = -jnp.exp(decay_local)
    head_in = jnp.pad(jnp.stack([bias_local, decay_rate]), ((0, 6), (0, 128 - gh)))
    skip_in = jnp.broadcast_to(jnp.repeat(skip_local, per_head)[None], (8, gw))
    mixed, q_low, square_part, starts = scan_forward(proj, taps_in, head_in, skip_in)

    w_out, cot_rows = lax.optimization_barrier((w_out, cot_rows))
    out_part = times(q_low, w_out).astype(bf)
    out_sum = lax.psum_scatter(out_part, "seq", scatter_dimension=0, tiled=True)
    square = lax.psum(square_part.reshape(sq, toks), "seq")
    q_r = lax.rsqrt(square / inner + epsilon).reshape(seq_rows, 1)
    d_raw = expert_early(cot_rows, expert_down)
    cot_late, _ = lax.optimization_barrier((cot_low, out_sum[:16, :128]))
    cot_all = lax.all_gather(cot_late, "seq", axis=0, tiled=True)
    tok_r = lax.dynamic_slice_in_dim(q_r, q * toks, toks, 0)
    x_tok = x_low.astype(f32)
    added = out_sum.astype(f32) * tok_r
    resid = x_tok + added

    resid_r = row_scale(resid)
    resid_n = resid * resid_r
    moe_in = (resid_n * moe_gain_full[None, :]).astype(bf)
    moe_all = lax.all_gather(moe_in, "seq", axis=0, tiled=True)

    logits = times(moe_in, w_all[:, total - 128 :])
    top = jnp.max(jnp.where(named_lanes > 0.0, logits, -1e30), axis=1, keepdims=True)
    powers = jnp.where(
        named_lanes > 0.0, jnp.exp(jnp.where(named_lanes > 0.0, logits - top, 0.0)), 0.0
    )
    gates = (powers / jnp.sum(powers, axis=1, keepdims=True))[
        :, router_lane : router_lane + experts
    ]
    rows = dispatched(moe_in)
    own_ids = lax.axis_index("shard") * local_e + jnp.arange(local_e, dtype=jnp.int32)
    marks = jnp.stack(
        [own_ids + router_lane, own_ids, own_ids + 64] + [jnp.full_like(own_ids, -1)] * 5, axis=1
    )
    marks = (marks[:, :, None] == lanes[None, None, :]).astype(f32)
    back_rows, e_act, e_scaled, d_g, d_v = expert_main(
        rows, cot_rows, d_raw, expert_gate, expert_up, w_all, marks
    )
    d_returned = to_shards(back_rows.reshape(sh, local_e * CAP, dim + 128))
    e_out, e_grads = expert_late(rows, cot_rows, e_act, e_scaled, d_g, d_v, expert_down)
    returned = to_shards(e_out.reshape(sh, local_e * CAP, dim))

    s_both = times(moe_all, w_shared)
    s_gate, s_up = s_both[:, :gf], s_both[:, gf:]
    s_sig = jax.nn.sigmoid(s_gate)
    s_silu = s_gate * s_sig
    s_act = (s_silu * s_up).astype(bf)
    d_sh = times_transposed(cot_all, w_down)
    d_both = jnp.concatenate(
        [
            (d_sh * s_up * (s_sig * (1.0 + s_gate * (1.0 - s_sig)))).astype(bf),
            (d_sh * s_silu).astype(bf),
        ],
        axis=1,
    )
    d_moe_part = times_transposed(d_both, w_shared).astype(bf)
    d_moe_shared = lax.psum_scatter(d_moe_part, "seq", scatter_dimension=0, tiled=True)

    d_flat = transposed_times(dispatch_flat, d_returned.reshape(slots, dim + 128))
    d_gates = d_flat[:, dim : dim + experts] + d_flat[:, dim + 64 : dim + 64 + experts]
    d_logits = gates * (d_gates - jnp.sum(gates * d_gates, axis=1, keepdims=True))
    d_moe = (
        d_flat[:, :dim]
        + d_moe_shared.astype(f32)
        + jnp.dot(d_logits, router_full.astype(f32).T, precision=highest)
    )
    grad_router = jnp.dot(moe_in.astype(f32).T, d_logits, precision=highest)
    grad_moe = jnp.sum(d_moe * resid_n, axis=0)
    d_scaled = d_moe * moe_gain_full[None, :]
    d_resid = (
        cot
        + d_scaled * resid_r
        - resid_n * (resid_r * jnp.mean(d_scaled * resid_n, axis=1, keepdims=True))
    )
    d_o = d_resid.astype(bf)
    kappa = jnp.sum(d_o.astype(f32) * added, axis=1) / inner
    d_o_all = lax.all_gather(d_o, "seq", axis=0, tiled=True)
    kappa_all = lax.all_gather(kappa.reshape(1, toks), "seq", axis=0).reshape(seq_rows, 1)

    s_late, _ = lax.optimization_barrier((s_act, d_o_all[:16, :128]))
    shared_part = times(s_late, w_down).astype(bf)
    shared_sum = lax.psum_scatter(shared_part, "seq", scatter_dimension=0, tiled=True)
    weighted = (gates.T[:, None, :] * dispatch.astype(f32)).reshape(slots, toks)
    combined = transposed_times(weighted.astype(bf), returned.reshape(slots, dim))
    block_output = ((resid + shared_sum.astype(f32) + combined) * live[:, None]).astype(bf)[None]

    d_gated = times_transposed(d_o_all, w_out)
    grad_out_part = transposed_times(q_low, (q_r * d_o_all.astype(f32)).astype(bf))
    grad_down_part = transposed_times(s_act, cot_all)
    grad_shared_part = transposed_times(moe_all, d_both)

    rows_part = jnp.concatenate(
        [grad_out_part.reshape(sh, own_out, dim), grad_down_part.reshape(sh, own_down, dim)],
        axis=1,
    )
    moved_rows = to_shards(rows_part.astype(bf))

    row_values = jnp.concatenate(
        [q_r, kappa_all, x_r, jnp.zeros((seq_rows, 5), f32)], axis=1
    )
    d_proj, d_taps, d_head, d_skip = scan_backward(
        proj, mixed, d_gated, row_values, starts, taps_in, head_in, skip_in
    )
    grad_conv_local = d_taps[:taps]
    grad_offset_local = d_taps[taps]
    grad_bias_local = d_head[0, :gh]
    grad_decay_local = d_head[1, :gh] * decay_rate
    grad_skip_local = jnp.sum(d_skip[0].reshape(gh, per_head), axis=1)
    d_proj, moved_rows = lax.optimization_barrier((d_proj, moved_rows))
    d_gate_low = d_proj[:, :gw]
    mid_part = jnp.concatenate(
        [
            transposed_times(x_all, d_gate_low),
            grad_shared_part,
            grad_router,
            grad_moe[:, None],
            jnp.zeros((dim, 128 - experts - 1), f32),
        ],
        axis=1,
    )
    mid_width = mid_part.shape[1]
    moved_mid = to_shards(mid_part.astype(bf).reshape(sh, rows_w, mid_width))
    rows_sum = jnp.sum(moved_rows.astype(f32), axis=0).astype(bf)
    rows_sum = lax.ppermute(rows_sum, both_axes, backward_pairs)

    e_all = sum_expert_grads(e_grads, q)
    grad_e_gate = e_all[:, :dim].astype(f32)
    grad_e_up = e_all[:, dim : 2 * dim].astype(f32)
    units = expert_gate.shape[2]
    grad_e_down = (
        e_all[:, 2 * dim :]
        .reshape(local_e, dim // units, units, units)
        .transpose(0, 2, 1, 3)
        .reshape(local_e, units, dim)
        .astype(f32)
    )
    back_part = times_transposed(d_proj, w_all).astype(bf)
    back_sum = lax.psum_scatter(back_part, "seq", scatter_dimension=0, tiled=True).astype(f32)
    tok_x_r = row_scale(x_tok)
    x_n = x_tok * tok_x_r
    input_grad = (
        d_resid + back_sum - x_n * (tok_x_r * jnp.mean(back_sum * x_tok, axis=1, keepdims=True))
    )[None]

    rest = total - gw
    grad_in_part = transposed_times(x_all, d_proj[:, gw:])

    def spread(local, count):
        wide = jnp.zeros(local.shape[:-1] + (count,), f32)
        return lax.dynamic_update_slice_in_dim(wide, local, q * local.shape[-1], local.ndim - 1)

    conv_rows = jnp.concatenate([grad_conv_local, grad_offset_local[None]], axis=0)
    conv_wide = jnp.concatenate([spread(conv_rows[:, :gw], inner), conv_rows[:, gw:]], axis=1)
    head_wide = spread(jnp.stack([grad_bias_local, grad_decay_local, grad_skip_local]), heads)
    small_part = jnp.concatenate(
        [
            conv_wide.reshape(taps + 1, sh, conv_own).transpose(1, 0, 2).reshape(sh, -1),
            head_wide.reshape(3, sh, head_own).transpose(1, 0, 2).reshape(sh, -1),
        ],
        axis=1,
    )
    small_count = small_part.shape[1]
    small_part = jnp.pad(
        small_part, ((0, 0), (0, rows_w * small_cols - small_count))
    ).reshape(sh, rows_w, small_cols)
    small_at = used - gw
    last_part = grad_in_part + jnp.pad(
        small_part.reshape(dim, small_cols), ((0, 0), (small_at, rest - small_at - small_cols))
    )
    last_part, moved_mid = lax.optimization_barrier((last_part.astype(bf), moved_mid))
    moved_last = to_shards(last_part.reshape(sh, rows_w, rest))
    mid_sum = jnp.sum(moved_mid.astype(f32), axis=0).astype(bf)
    side = lax.all_gather(
        jnp.concatenate([rows_sum, mid_sum.reshape(rows_w * mid_width // dim, dim)], axis=0),
        "seq",
        axis=0,
    )
    rows_grad = side[:, :own_rows]
    mid_all = side[:, own_rows:].reshape(sq, rows_w, mid_width)
    last_sum = jnp.sum(moved_last.astype(f32), axis=0).astype(bf)
    last_all = lax.all_gather(last_sum, "seq", axis=0)

    grad_out_raw = rows_grad[:, :own_out].reshape(sq * own_out, dim).astype(f32)
    grad_down = rows_grad[:, own_out:].reshape(sq * own_down, dim).astype(f32)
    grad_out = norm_gain.astype(f32)[:, None] * grad_out_raw
    grad_norm = jnp.sum(out_weight.astype(f32) * grad_out_raw, axis=1)
    mid_all_f = mid_all[:, :, gw:].astype(f32)
    grad_shared_gate = mid_all_f[:, :, :gf].transpose(1, 0, 2).reshape(rows_w, fs)
    grad_shared_up = mid_all_f[:, :, gf : 2 * gf].transpose(1, 0, 2).reshape(rows_w, fs)
    mid_rest = jnp.sum(mid_all_f[:, :, 2 * gf :], axis=0)
    grad_router_weight = mid_rest[:, :experts]
    grad_moe_gain = mid_rest[:, experts]
    grad_in, tail_sums = assemble(mid_all, last_all, in_weight, gain_col)
    grad_mixer_gain = tail_sums[:, 0]
    lane_at = used - (total - 128)
    small_sum = tail_sums[:, lane_at : lane_at + small_cols].reshape(-1)
    at = taps * conv_own
    grad_conv = small_sum[:at].reshape(taps, conv_own)
    grad_offset = small_sum[at : at + conv_own]
    at = at + conv_own
    grad_bias = small_sum[at : at + head_own]
    grad_decay = small_sum[at + head_own : at + 2 * head_own]
    grad_skip = small_sum[at + 2 * head_own : at + 3 * head_own]
    return (
        block_output,
        input_grad,
        grad_mixer_gain,
        grad_in,
        grad_conv,
        grad_offset,
        grad_bias,
        grad_decay,
        grad_skip,
        grad_norm,
        grad_out,
        grad_moe_gain,
        grad_router_weight,
        grad_shared_gate,
        grad_shared_up,
        grad_down,
        grad_e_gate,
        grad_e_up,
        grad_e_down,
    )


def solution(mesh):
    placed = (
        P("shard", "seq", None),
        P("shard"),
        P("shard", "seq", None),
        P("shard", "seq", None),
        P("shard"),
        P("shard", None),
        P(None, "shard"),
        P("shard"),
        P("shard"),
        P("shard"),
        P("shard"),
        P("shard"),
        P("shard", None),
        P("shard"),
        P("shard", None),
        P("shard", None),
        P("shard", None),
        P("shard", None),
        P("shard", None, None),
        P("shard", None, None),
        P("shard", None, None),
    )
    return jax.shard_map(
        on_device,
        mesh=mesh,
        in_specs=placed,
        out_specs=(
            P("shard", "seq", None),
            P("shard", "seq", None),
            P("shard"),
            P("shard", None),
            P(None, "shard"),
            P("shard"),
            P("shard"),
            P("shard"),
            P("shard"),
            P("shard"),
            P("shard", None),
            P("shard"),
            P("shard", None),
            P("shard", None),
            P("shard", None),
            P("shard", None),
            P("shard", None, None),
            P("shard", None, None),
            P("shard", None, None),
        ),
        check_vma=False,
    )
```

```python
import functools

import jax
import jax.numpy as jnp
from jax import lax
from jax.experimental import pallas as pl
from jax.experimental.pallas import tpu as pltpu
from jax.sharding import PartitionSpec as P

CAP = 32


epsilon = 1e-05
highest = lax.Precision.HIGHEST
both_axes = ("seq", "shard")


def times(left, right):
    return jnp.dot(left, right, preferred_element_type=jnp.float32)


def times_transposed(left, right):
    return lax.dot_general(
        left, right, (((1,), (1,)), ((), ())), preferred_element_type=jnp.float32
    )


def transposed_times(left, right):
    return lax.dot_general(
        left, right, (((0,), (0,)), ((), ())), preferred_element_type=jnp.float32
    )


def after(value, other):
    corner = other[(0,) * (other.ndim - 1)][:1].astype(jnp.float32)
    return (value.astype(jnp.float32) + 0.0 * corner).astype(value.dtype)


def silu_slope(values):
    sigma = jax.nn.sigmoid(values)
    return sigma * (1.0 + values * (1.0 - sigma))


def row_scale(values):
    return lax.rsqrt(jnp.mean(values * values, axis=-1, keepdims=True) + epsilon)


CHUNK = 128
WIDE = 384
CONVW = 640
PAIRS = 3
HEADS_HERE = 6


def split_two(values):
    high = values.astype(jnp.bfloat16)
    return high, (values - high.astype(jnp.float32)).astype(jnp.bfloat16)


def ones_times(ones, values):
    high, low = split_two(values)
    return times(ones, high) + times(ones, low)


def times_ones(values, ones):
    high, low = split_two(values)
    return times(high, ones) + times(low, ones)


def transposed_times_ones(values, ones):
    high, low = split_two(values)
    return transposed_times(high, ones) + transposed_times(low, ones)


def grid_of(shape):
    rows = lax.broadcasted_iota(jnp.int32, shape, 0)
    columns = lax.broadcasted_iota(jnp.int32, shape, 1)
    return rows, columns


def mark(condition):
    return jnp.where(condition, 1.0, 0.0).astype(jnp.bfloat16)


def chunk_parts(proj, prev, has_prev, taps_ref, head_ref, pad_ref):
    f32, bf = jnp.float32, jnp.bfloat16
    feed = proj[:, WIDE : WIDE + CONVW].astype(bf).astype(f32)
    before = prev[:, WIDE : WIDE + CONVW].astype(bf).astype(f32)
    pad_ref[0:8, :] = jnp.where(has_prev, before, 0.0)
    pad_ref[8 : 8 + CHUNK, :] = feed
    conv = taps_ref[4:5, :]
    for tap in range(4):
        conv = conv + taps_ref[tap : tap + 1, :] * pad_ref[5 + tap : 5 + tap + CHUNK, :]
    sig = jax.nn.sigmoid(conv)
    act = conv * sig
    u = act[:, :WIDE]
    key = act[:, WIDE : WIDE + 128].astype(bf)
    query = act[:, WIDE + 128 :].astype(bf)
    step_low = proj[:, WIDE + CONVW :].astype(bf).astype(f32)
    pre = step_low + head_ref[0:1, :]
    rows, columns = grid_of((CHUNK, 128))
    here = columns < HEADS_HERE
    dt = jnp.where(here, jnp.maximum(pre, 0.0) + jnp.log1p(jnp.exp(-jnp.abs(pre))), 0.0)
    la = dt * head_ref[1:2, :]
    lower = mark(rows >= columns)
    cum = ones_times(lower, la)
    end = cum[CHUNK - 1 : CHUNK, :]
    wide_rows, wide_columns = grid_of((128, WIDE))
    widen = mark(wide_columns // 64 == wide_rows)
    dt_w = times_ones(dt, widen)
    e_w = times_ones(jnp.exp(cum), widen)
    w_w = times_ones(jnp.exp(end - cum), widen)
    full_rows, full_columns = grid_of((128, 2 * PAIRS * 128))
    la_full = times_ones(la, mark(full_columns // 128 == full_rows))
    scores = times_transposed(query, key)
    return dict(
        conv=conv, sig=sig, u=u, key=key, query=query, pre=pre, here=here, dt=dt, lower=lower,
        dt_w=dt_w, e_w=e_w, w_w=w_w, la_full=la_full, scores=scores, xs=u * dt_w,
    )


def pair_table(parts, pair):
    rows, columns = grid_of((CHUNK, 256))
    local = columns % 128
    steps = jnp.where(rows > local, parts["la_full"][:, 256 * pair : 256 * pair + 256], 0.0)
    gap = ones_times(parts["lower"], steps)
    causal = rows >= local
    decay = jnp.where(causal, jnp.exp(jnp.where(causal, gap, 0.0)), 0.0)
    scores = parts["scores"]
    return decay, decay * jnp.concatenate([scores, scores], axis=1)


def stack_heads(values, pair):
    both = values[:, 128 * pair : 128 * pair + 128]
    first = lax.broadcasted_iota(jnp.int32, both.shape, 1) < 64
    return jnp.concatenate(
        [jnp.where(first, both, 0.0), jnp.where(first, 0.0, both)], axis=0
    ).astype(jnp.bfloat16)


def scan_forward_kernel(
    proj_ref, prev_ref, taps_ref, head_ref, skip_ref,
    mixed_ref, q_ref, square_ref, start_ref, state_ref, pad_ref,
):
    f32, bf = jnp.float32, jnp.bfloat16
    chunk = pl.program_id(0)

    @pl.when(chunk == 0)
    def _():
        state_ref[...] = jnp.zeros(state_ref.shape, f32)

    parts = chunk_parts(
        proj_ref[...], prev_ref[...], chunk > 0, taps_ref, head_ref, pad_ref
    )
    state = state_ref[...]
    start_ref[0] = state
    xs = parts["xs"]
    inside = []
    for pair in range(PAIRS):
        _, table = pair_table(parts, pair)
        inside.append(times(table.astype(bf), stack_heads(xs, pair)))
    across = times(parts["query"], state.astype(bf))
    y = (
        jnp.concatenate(inside, axis=1)
        + parts["e_w"] * across
        + skip_ref[0:1, :] * parts["u"]
    )
    mixed = y.astype(bf)
    mixed_ref[...] = mixed
    gate = proj_ref[:, :WIDE]
    q_val = mixed.astype(f32) * (gate * jax.nn.sigmoid(gate))
    q_ref[...] = q_val.astype(bf)
    square_ref[...] = jnp.sum(q_val * q_val, axis=1, keepdims=True)
    state_ref[...] = state * parts["e_w"][CHUNK - 1 : CHUNK, :] + transposed_times(
        parts["key"], (xs * parts["w_w"]).astype(bf)
    )


def scan_backward_kernel(
    proj_ref, prev_ref, mixed_ref, d_gated_ref, rows_ref, start_ref, taps_ref, head_ref, skip_ref,
    earlier_0, earlier_1, earlier_2, d_proj_ref, d_taps_ref, d_head_ref, d_skip_ref,
    state_ref, pad_ref, late_ref,
):
    f32, bf = jnp.float32, jnp.bfloat16
    step = pl.program_id(0)
    last = pl.num_programs(0) - 1

    @pl.when(step == 0)
    def _():
        state_ref[...] = jnp.zeros(state_ref.shape, f32)
        late_ref[CHUNK : CHUNK + 8, :] = jnp.zeros((8, CONVW), f32)
        d_taps_ref[...] = jnp.zeros(d_taps_ref.shape, f32)
        d_head_ref[...] = jnp.zeros(d_head_ref.shape, f32)
        d_skip_ref[...] = jnp.zeros(d_skip_ref.shape, f32)

    parts = chunk_parts(
        proj_ref[...], prev_ref[...], step < last, taps_ref, head_ref, pad_ref
    )
    u, key, query, xs = parts["u"], parts["key"], parts["query"], parts["xs"]
    e_w, w_w, dt_w = parts["e_w"], parts["w_w"], parts["dt_w"]

    gate = proj_ref[:, :WIDE]
    gate_sig = jax.nn.sigmoid(gate)
    gate_act = gate * gate_sig
    mixed = mixed_ref[...].astype(f32)
    q_val = mixed * gate_act
    q_r = rows_ref[:, 0:1]
    d_q = q_r * d_gated_ref[...] - q_val * (q_r * q_r * rows_ref[:, 1:2])
    d_gate = d_q * mixed * (gate_sig * (1.0 + gate * (1.0 - gate_sig)))
    d_y = (d_q * gate_act).astype(bf).astype(f32)

    start = start_ref[0]
    start_low = start.astype(bf)
    d_end = state_ref[...]
    d_end_low = d_end.astype(bf)
    xw = xs * w_w
    ye = d_y * e_w
    ye_low = ye.astype(bf)
    across = times(query, start_low)
    pulled = times(key, d_end_low)
    d_query = times_transposed(ye_low, start_low)
    d_key = times_transposed(xw.astype(bf), d_end_low)
    state_ref[...] = d_end * e_w[CHUNK - 1 : CHUNK, :] + transposed_times(query, ye_low)
    d_scores = jnp.zeros((CHUNK, 128), f32)
    turns = jnp.zeros((CHUNK, 128), f32)
    d_xs = []
    for pair in range(PAIRS):
        decay, table = pair_table(parts, pair)
        xs_two = stack_heads(xs, pair)
        dy_two = stack_heads(d_y, pair)
        d_table = times_transposed(d_y[:, 128 * pair : 128 * pair + 128].astype(bf), xs_two)
        d_decay = d_table * decay
        d_scores = d_scores + d_decay[:, :128] + d_decay[:, 128:]
        d_gap = d_table * table
        table_low = table.astype(bf)
        d_xs.append(
            transposed_times(
                jnp.concatenate([table_low[:, :128], table_low[:, 128:]], axis=0), dy_two
            )
        )
        two_rows, two_columns = grid_of((256, 128))
        own = mark(two_columns == 2 * pair + two_rows // 128)
        turns = turns + times_ones(d_gap, own)
        turns = turns - transposed_times_ones(
            jnp.concatenate([d_gap[:, :128], d_gap[:, 128:]], axis=0), own
        )
    d_xs = jnp.concatenate(d_xs, axis=1) + w_w * pulled
    d_scores_low = d_scores.astype(bf)
    d_query = d_query + times(d_scores_low, key)
    d_key = d_key + transposed_times(d_scores_low, query)

    rows, columns = grid_of((CHUNK, 128))
    upper = mark(columns >= rows)
    strict = mark(columns < rows)
    sum_rows, sum_columns = grid_of((WIDE, 128))
    per_head = mark(sum_rows // 64 == sum_columns)
    end_row = jnp.sum(d_end * start, axis=0, keepdims=True) * e_w[CHUNK - 1 : CHUNK, :]
    wide = ones_times(upper, ye * across) + ones_times(strict, xw * pulled) + end_row
    d_la = ones_times(upper, turns) + times_ones(wide, per_head)
    d_dt = times_ones(d_xs * u, per_head) + d_la * head_ref[1:2, :]
    d_pre = jnp.where(parts["here"], d_dt * jax.nn.sigmoid(parts["pre"]), 0.0)
    d_head_ref[0:1, :] += jnp.sum(d_pre, axis=0, keepdims=True)
    d_head_ref[1:2, :] += jnp.sum(d_la * parts["dt"], axis=0, keepdims=True)
    d_skip_ref[0:1, :] += jnp.sum(d_y * u, axis=0, keepdims=True)

    d_u = d_xs * dt_w + skip_ref[0:1, :] * d_y
    conv, sig = parts["conv"], parts["sig"]
    d_conv = jnp.concatenate([d_u, d_key, d_query], axis=1) * (sig * (1.0 + conv * (1.0 - sig)))
    late_ref[0:CHUNK, :] = d_conv
    d_feed = jnp.zeros((CHUNK, CONVW), f32)
    for tap in range(4):
        d_feed = d_feed + taps_ref[tap : tap + 1, :] * late_ref[3 - tap : 3 - tap + CHUNK, :]
        d_taps_ref[tap : tap + 1, :] += jnp.sum(
            d_conv * pad_ref[5 + tap : 5 + tap + CHUNK, :], axis=0, keepdims=True
        )
    d_taps_ref[4:5, :] += jnp.sum(d_conv, axis=0, keepdims=True)
    late_ref[CHUNK : CHUNK + 8, :] = d_conv[0:8, :]
    scale = rows_ref[:, 2:3]
    d_proj_ref[:, :WIDE] = (d_gate * scale).astype(bf)
    d_proj_ref[:, WIDE : WIDE + CONVW] = (d_feed * scale).astype(bf)
    d_proj_ref[:, WIDE + CONVW :] = (d_pre * scale).astype(bf)


def corner_of(array):
    return pl.BlockSpec(
        (1,) * (array.ndim - 2) + (16, 128), lambda *step: (0,) * array.ndim
    )


def whole(shape):
    return pl.BlockSpec(shape, lambda step: (0,) * len(shape))


def scan_forward(proj, taps, head, skip):
    rows, width = proj.shape
    chunks = rows // CHUNK
    by_chunk = lambda step: (step, 0)
    return pl.pallas_call(
        scan_forward_kernel,
        grid=(chunks,),
        in_specs=[
            pl.BlockSpec((CHUNK, width), by_chunk),
            pl.BlockSpec((8, width), lambda step: (jnp.maximum(step * (CHUNK // 8) - 1, 0), 0)),
            whole(taps.shape),
            whole(head.shape),
            whole(skip.shape),
        ],
        out_specs=[
            pl.BlockSpec((CHUNK, WIDE), by_chunk),
            pl.BlockSpec((CHUNK, WIDE), by_chunk),
            pl.BlockSpec((CHUNK, 1), by_chunk),
            pl.BlockSpec((1, 128, WIDE), lambda step: (step, 0, 0)),
        ],
        out_shape=[
            jax.ShapeDtypeStruct((rows, WIDE), jnp.bfloat16),
            jax.ShapeDtypeStruct((rows, WIDE), jnp.bfloat16),
            jax.ShapeDtypeStruct((rows, 1), jnp.float32),
            jax.ShapeDtypeStruct((chunks, 128, WIDE), jnp.float32),
        ],
        scratch_shapes=[
            pltpu.VMEM((128, WIDE), jnp.float32),
            pltpu.VMEM((CHUNK + 8, CONVW), jnp.float32),
        ],
        compiler_params=pltpu.CompilerParams(vmem_limit_bytes=32 << 20),
        cost_estimate=pl.CostEstimate(
            flops=3 << 30, bytes_accessed=12 << 20, transcendentals=4 << 20
        ),
        name="scan_forward",
    )(proj, proj, taps, head, skip)


def scan_backward(proj, mixed, d_gated, row_values, starts, taps, head, skip, earlier):
    rows, width = proj.shape
    chunks = rows // CHUNK
    by_chunk = lambda step: (chunks - 1 - step, 0)
    return pl.pallas_call(
        scan_backward_kernel,
        grid=(chunks,),
        in_specs=[
            pl.BlockSpec((CHUNK, width), by_chunk),
            pl.BlockSpec(
                (8, width),
                lambda step: (jnp.maximum((chunks - 1 - step) * (CHUNK // 8) - 1, 0), 0),
            ),
            pl.BlockSpec((CHUNK, WIDE), by_chunk),
            pl.BlockSpec((CHUNK, WIDE), by_chunk),
            pl.BlockSpec((CHUNK, row_values.shape[1]), by_chunk),
            pl.BlockSpec((1, 128, WIDE), lambda step: (chunks - 1 - step, 0, 0)),
            whole(taps.shape),
            whole(head.shape),
            whole(skip.shape),
            *map(corner_of, earlier),
        ],
        out_specs=[
            pl.BlockSpec((CHUNK, width), by_chunk),
            whole((8, CONVW)),
            whole((8, 128)),
            whole((8, WIDE)),
        ],
        out_shape=[
            jax.ShapeDtypeStruct((rows, width), jnp.bfloat16),
            jax.ShapeDtypeStruct((8, CONVW), jnp.float32),
            jax.ShapeDtypeStruct((8, 128), jnp.float32),
            jax.ShapeDtypeStruct((8, WIDE), jnp.float32),
        ],
        scratch_shapes=[
            pltpu.VMEM((128, WIDE), jnp.float32),
            pltpu.VMEM((CHUNK + 8, CONVW), jnp.float32),
            pltpu.VMEM((CHUNK + 8, CONVW), jnp.float32),
        ],
        compiler_params=pltpu.CompilerParams(vmem_limit_bytes=48 << 20),
        cost_estimate=pl.CostEstimate(
            flops=10 << 30, bytes_accessed=20 << 20, transcendentals=8 << 20
        ),
        name="scan_backward",
    )(proj, proj, mixed, d_gated, row_values, starts, taps, head, skip, *earlier)


def expert_early_kernel(cot_ref, down_ref, raw_ref):
    cot = cot_ref[...].reshape(-1, cot_ref.shape[-1])
    raw_ref[0] = times_transposed(cot, down_ref[0])


def expert_main_kernel(
    rows_ref, routed_ref, raw_ref, gate_ref, up_ref, router_ref, marks_ref, earlier_ref,
    back_ref, act_ref, scaled_ref, d_g_ref, d_v_ref,
):
    f32, bf = jnp.float32, jnp.bfloat16
    dim = rows_ref.shape[-1]
    rows = rows_ref[...].reshape(-1, dim)
    routed = routed_ref[...].reshape(-1, 128).astype(f32) > 0.0
    logits = times(rows, router_ref[...])
    top = jnp.max(jnp.where(routed, logits, -1e30), axis=1, keepdims=True)
    powers = jnp.where(routed, jnp.exp(jnp.where(routed, logits - top, 0.0)), 0.0)
    own = jnp.sum(powers * marks_ref[0, 0:1, :], axis=1, keepdims=True)
    gate = own / jnp.maximum(jnp.sum(powers, axis=1, keepdims=True), 1e-30)
    g = times(rows, gate_ref[0])
    v = times(rows, up_ref[0])
    sig = jax.nn.sigmoid(g)
    silu = g * sig
    act = (silu * v).astype(bf)
    act_wide = act.astype(f32)
    raw = raw_ref[0]
    d_gate = jnp.sum(act_wide * raw, axis=1, keepdims=True)
    d_act = gate * raw
    d_g = (d_act * v * (sig * (1.0 + g * (1.0 - sig)))).astype(bf)
    d_v = (d_act * silu).astype(bf)
    d_row = times_transposed(d_g, gate_ref[0]) + times_transposed(d_v, up_ref[0])
    high = d_gate.astype(bf).astype(f32)
    scalars = high * marks_ref[0, 1:2, :] + (d_gate - high) * marks_ref[0, 2:3, :]
    lead = back_ref.shape[:-1]
    back_ref[:, :, :, :dim] = d_row.astype(bf).reshape(*lead, dim)
    back_ref[:, :, :, dim:] = scalars.astype(bf).reshape(*lead, 128)
    act_ref[0] = act
    scaled_ref[0] = (gate * act_wide).astype(bf)
    d_g_ref[0] = d_g
    d_v_ref[0] = d_v


def expert_late_kernel(
    rows_ref, cot_ref, act_ref, scaled_ref, d_g_ref, d_v_ref, down_ref,
    out_ref, grads_ref,
):
    bf = jnp.bfloat16
    dim = rows_ref.shape[-1]
    rows = rows_ref[...].reshape(-1, dim)
    cot = cot_ref[...].reshape(-1, dim)
    out_ref[...] = times(act_ref[0], down_ref[0]).astype(bf).reshape(out_ref.shape)
    units = act_ref.shape[-1]
    grads_ref[0, :dim] = transposed_times(rows, d_g_ref[0]).astype(bf)
    grads_ref[0, dim : 2 * dim] = transposed_times(rows, d_v_ref[0]).astype(bf)
    for block in range(dim // units):
        at = 2 * dim + block * units
        grads_ref[0, at : at + units] = transposed_times(
            scaled_ref[0], cot[:, block * units : block * units + units]
        ).astype(bf)


def expert_slots(shape, start=0):
    return pl.BlockSpec(
        (shape[0], 1) + tuple(shape[2:]), lambda e: (0, e) + (0,) * (len(shape) - 3) + (start,)
    )


def per_expert(shape):
    return pl.BlockSpec((1,) + tuple(shape[1:]), lambda e: (e,) + (0,) * (len(shape) - 1))


def expert_params(flops, moved):
    return dict(
        compiler_params=pltpu.CompilerParams(vmem_limit_bytes=56 << 20),
        cost_estimate=pl.CostEstimate(flops=flops, bytes_accessed=moved, transcendentals=1 << 19),
    )


def expert_early(cot_rows, down):
    sources, local, cap, _ = cot_rows.shape
    units, dim = down.shape[1:]
    return pl.pallas_call(
        expert_early_kernel,
        grid=(local,),
        in_specs=[expert_slots((sources, local, cap, dim)), per_expert(down.shape)],
        out_specs=per_expert((local, sources * cap, units)),
        out_shape=jax.ShapeDtypeStruct((local, sources * cap, units), jnp.float32),
        name="expert_early",
        **expert_params(2 << 30, 8 << 20),
    )(cot_rows, down)


def expert_main(rows, cot_rows, raw, gate, up, w_all, marks, earlier):
    sources, local, cap, dim = rows.shape
    units = gate.shape[2]
    count = sources * cap
    hidden = jax.ShapeDtypeStruct((local, count, units), jnp.bfloat16)
    back = (sources, local, cap, dim + 128)
    return pl.pallas_call(
        expert_main_kernel,
        grid=(local,),
        in_specs=[
            expert_slots(rows.shape),
            expert_slots((sources, local, cap, 128), dim // 128),
            per_expert(raw.shape),
            per_expert(gate.shape),
            per_expert(up.shape),
            pl.BlockSpec((dim, 128), lambda e: (0, w_all.shape[1] // 128 - 1)),
            per_expert(marks.shape),
            corner_of(earlier),
        ],
        out_specs=[expert_slots(back)] + [per_expert(hidden.shape)] * 4,
        out_shape=[jax.ShapeDtypeStruct(back, jnp.bfloat16)] + [hidden] * 4,
        name="expert_main",
        **expert_params(8 << 30, 20 << 20),
    )(rows, cot_rows, raw, gate, up, w_all, marks, earlier)


def expert_late(rows, cot_rows, act, scaled, d_g, d_v, down):
    sources, local, cap, dim = rows.shape
    units = down.shape[1]
    grads = (local, 3 * dim, units)
    return pl.pallas_call(
        expert_late_kernel,
        grid=(local,),
        in_specs=[expert_slots(rows.shape), expert_slots(rows.shape)]
        + [per_expert(act.shape)] * 4
        + [per_expert(down.shape)],
        out_specs=[
            expert_slots(rows.shape),
            per_expert(grads),
        ],
        out_shape=[
            jax.ShapeDtypeStruct(rows.shape, jnp.bfloat16),
            jax.ShapeDtypeStruct(grads, jnp.bfloat16),
        ],
        name="expert_late",
        **expert_params(7 << 30, 24 << 20),
    )(rows, cot_rows, act, scaled, d_g, d_v, down)


def assemble_kernel(
    own_out, own_down, side_ref, in_ref, in_gain_ref, out_ref, out_gain_ref,
    grad_in_ref, tail_ref, grad_out_ref, norm_ref, grad_down_ref, gate_ref, up_ref, mid_ref,
):
    f32 = jnp.float32
    groups = side_ref.shape[0]
    inner = groups * WIDE
    bands = out_ref.shape[1] // WIDE
    rows_w = in_ref.shape[0]
    gain = in_gain_ref[...]
    at_down = bands * own_out
    at_mid = at_down + bands * own_down
    at_in = at_mid + rows_w
    units = gate_ref.shape[1] // groups

    def block(group, start, rows):
        return side_ref[group, start : start + rows, :].astype(f32)

    grad_gain = jnp.zeros((rows_w, 1), f32)
    keys = jnp.zeros((rows_w, 256), f32)
    tail = jnp.zeros((rows_w, 128), f32)
    steps = jnp.zeros((rows_w, 128), f32)
    mid = jnp.zeros((rows_w, 128), f32)
    rows, columns = grid_of((128, 128))

    def put(start, values):
        stop = start + values.shape[1]
        grad_in_ref[:, start:stop] = values * gain
        weight = in_ref[:, start:stop].astype(f32)
        return jnp.sum(weight * values, axis=1, keepdims=True)

    for group in range(groups):
        grad_gain += put(group * WIDE, block(group, at_in, rows_w))
        grad_gain += put(inner + group * WIDE, block(group, at_in + rows_w, rows_w))
        last = block(group, at_in + 2 * rows_w, rows_w)
        keys = keys + last[:, :256]
        tail = tail + last[:, 256:]
        moved = mark((rows < HEADS_HERE) & (columns == rows + HEADS_HERE * group))
        steps = steps + times(last[:, 256:].astype(jnp.bfloat16), moved)
        shared = block(group, at_mid, rows_w)
        gate_ref[:, units * group : units * group + units] = shared[:, :units]
        up_ref[:, units * group : units * group + units] = shared[:, units : 2 * units]
        mid = mid + shared[:, 2 * units :]
    grad_gain += put(2 * inner, keys)
    grad_gain += put(2 * inner + 256, steps[:, : groups * HEADS_HERE])
    lane = lax.broadcasted_iota(jnp.int32, tail.shape, 1)
    tail_ref[...] = jnp.where(lane == 0, grad_gain, tail)
    mid_ref[...] = mid

    for group in range(groups):
        sums = jnp.zeros((own_out, 1), f32)
        mine = slice(own_out * group, own_out * group + own_out)
        for band in range(bands):
            wide = slice(WIDE * band, WIDE * band + WIDE)
            values = block(group, own_out * band, own_out)
            grad_out_ref[mine, wide] = values * out_gain_ref[mine, :]
            sums += jnp.sum(out_ref[mine, wide].astype(f32) * values, axis=1, keepdims=True)
            grad_down_ref[own_down * group : own_down * group + own_down, wide] = block(
                group, at_down + own_down * band, own_down
            )
        norm_ref[mine, :] = sums


def assemble(side, in_weight, in_gain, out_weight, out_gain, own_out, own_down):
    groups = side.shape[0]
    rows, width = in_weight.shape
    out_rows, dim = out_weight.shape
    shapes = [
        (rows, width),
        (rows, 128),
        (out_rows, dim),
        (out_rows, 1),
        (groups * own_down, dim),
        (rows, groups * 128),
        (rows, groups * 128),
        (rows, 128),
    ]
    return pl.pallas_call(
        functools.partial(assemble_kernel, own_out, own_down),
        in_specs=[pl.BlockSpec(memory_space=pltpu.VMEM)] * 5,
        out_specs=[pl.BlockSpec(memory_space=pltpu.VMEM)] * len(shapes),
        out_shape=[jax.ShapeDtypeStruct(shape, jnp.float32) for shape in shapes],
        compiler_params=pltpu.CompilerParams(vmem_limit_bytes=40 << 20),
        cost_estimate=pl.CostEstimate(flops=8 << 20, bytes_accessed=12 << 20, transcendentals=0),
        name="assemble",
    )(side, in_weight, in_gain, out_weight, out_gain)


def halve(values, bit, pairs):
    f32 = jnp.float32
    parts = values.reshape(2, values.shape[0] // 2, values.shape[1])
    sent = lax.dynamic_index_in_dim(parts, 1 - bit, 0, keepdims=False)
    kept = lax.dynamic_index_in_dim(parts, bit, 0, keepdims=False)
    other = lax.ppermute(sent, "seq", pairs)
    return (kept.astype(f32) + other.astype(f32)).astype(jnp.bfloat16)


def double(values, bit, pairs):
    other = lax.ppermute(values, "seq", pairs)
    first = jnp.where(bit == 0, values, other)
    second = jnp.where(bit == 0, other, values)
    return jnp.concatenate([first, second], axis=0)


def unpack_kernel(core_ref, own_ref, other_ref, gate_ref, up_ref, down_ref):
    part = pl.program_id(1)
    block = jnp.where(pl.program_id(0) == 0, own_ref[...], other_ref[...]).astype(jnp.float32)
    units = block.shape[1]

    @pl.when(part == 0)
    def _():
        gate_ref[0] = block

    @pl.when(part == 1)
    def _():
        up_ref[0] = block

    @pl.when(part == 2)
    def _():
        for at in range(0, block.shape[0], units):
            down_ref[0, :, at : at + units] = block[at : at + units]


def unpack_expert_grads(own, other, core):
    rows, units = own.shape
    dim = rows // 3
    to_expert = lambda who, part, core: (jnp.where(who == 0, core[0], 1 - core[0]), 0, 0)
    return pl.pallas_call(
        unpack_kernel,
        grid_spec=pltpu.PrefetchScalarGridSpec(
            num_scalar_prefetch=1,
            grid=(2, 3),
            in_specs=[
                pl.BlockSpec((dim, units), lambda who, part, core: (jnp.where(who == 0, part, 2), 0)),
                pl.BlockSpec((dim, units), lambda who, part, core: (jnp.where(who == 0, 0, part), 0)),
            ],
            out_specs=[
                pl.BlockSpec((1, dim, units), to_expert),
                pl.BlockSpec((1, dim, units), to_expert),
                pl.BlockSpec((1, units, dim), to_expert),
            ],
        ),
        out_shape=[
            jax.ShapeDtypeStruct((2, dim, units), jnp.float32),
            jax.ShapeDtypeStruct((2, dim, units), jnp.float32),
            jax.ShapeDtypeStruct((2, units, dim), jnp.float32),
        ],
        compiler_params=pltpu.CompilerParams(vmem_limit_bytes=40 << 20),
        cost_estimate=pl.CostEstimate(flops=1 << 20, bytes_accessed=28 << 20, transcendentals=0),
        name="unpack_expert_grads",
    )(core.reshape(1), own, other)


def on_device(
    block_input,
    lengths,
    routes,
    out_cotangent,
    mixer_gain,
    in_weight,
    conv_weight,
    conv_bias,
    step_bias,
    decay_log,
    skip_gain,
    norm_gain,
    out_weight,
    moe_gain,
    router_weight,
    shared_gate,
    shared_up,
    shared_down,
    expert_gate,
    expert_up,
    expert_down,
):
    sq = lax.axis_size("seq")
    sh = lax.axis_size("shard")
    q = lax.axis_index("seq")
    f32 = jnp.float32
    bf = jnp.bfloat16
    x_low = block_input[0]
    toks, dim = x_low.shape
    seq_rows = toks * sq
    heads = step_bias.shape[0] * sh
    inner = norm_gain.shape[0] * sh
    conv_all = conv_bias.shape[0] * sh
    keys_w = conv_all - inner
    gh = heads // sq
    gw = inner // sq
    rows_w = in_weight.shape[0]
    experts = router_weight.shape[1]
    local_e = expert_gate.shape[0]
    fs = shared_gate.shape[1]
    gf = fs // sq
    taps = conv_weight.shape[0]
    conv_own = conv_bias.shape[0]
    head_own = step_bias.shape[0]

    gain_col = mixer_gain.astype(f32)[:, None]

    def cols(start, width):
        return lax.dynamic_slice_in_dim(in_weight, start, width, 1)

    w_cols = jnp.concatenate(
        [
            cols(q * gw, gw),
            cols(inner + q * gw, gw),
            in_weight[:, 2 * inner : 2 * inner + keys_w],
            cols(2 * inner + keys_w + q * gh, gh),
        ],
        axis=1,
    )
    w_cols = (w_cols.astype(f32) * gain_col).astype(bf)
    used = 2 * gw + keys_w + gh
    small = jnp.concatenate(
        [conv_weight.reshape(-1), conv_bias, step_bias, decay_log, skip_gain]
    )
    small_cols = -(-small.shape[0] // rows_w)
    small = jnp.pad(small, (0, small_cols * rows_w - small.shape[0])).reshape(rows_w, small_cols)
    packed = jnp.concatenate(
        [w_cols, small, router_weight, moe_gain[:, None]], axis=1
    )
    at_small = used
    at_router = at_small + small_cols
    at_moe = at_router + experts
    total = -(-(at_moe + 1) // 128) * 128
    packed = jnp.pad(packed, ((0, 0), (0, total - packed.shape[1])))

    def to_shards(values):
        return lax.all_to_all(values, "shard", split_axis=0, concat_axis=0, tiled=True)

    x_all = lax.all_gather(x_low, "seq", axis=0, tiled=True)
    w_all = to_shards(jnp.broadcast_to(packed[None], (sh, rows_w, total))).reshape(dim, total)

    out_scaled = (norm_gain.astype(f32)[:, None] * out_weight.astype(f32)).astype(bf)
    own_out = out_weight.shape[0] // sq
    own_down = shared_down.shape[0] // sq
    piece = jnp.concatenate(
        [
            lax.dynamic_slice_in_dim(out_scaled, q * own_out, own_out, 0),
            lax.dynamic_slice_in_dim(shared_down, q * own_down, own_down, 0),
        ],
        axis=0,
    )
    ratio = sh // sq
    forward_pairs = []
    for a in range(sh):
        for j in range(sq):
            s_to = sq * (a % ratio) + j
            q_to = a // ratio
            forward_pairs.append((j * sh + a, q_to * sh + s_to))
    backward_pairs = [(b, a) for a, b in forward_pairs]
    piece = lax.ppermute(piece, both_axes, forward_pairs)
    shared_cols = jnp.concatenate(
        [
            lax.dynamic_slice_in_dim(shared_gate, q * gf, gf, 1),
            lax.dynamic_slice_in_dim(shared_up, q * gf, gf, 1),
        ],
        axis=1,
    )
    fold = rows_w * 2 * gf // dim
    bands = dim // (2 * gf)
    shared_rows = jnp.concatenate(
        [shared_cols[fold * band : fold * band + fold] for band in range(bands)], axis=1
    )
    piece = jnp.concatenate([piece, shared_rows], axis=0)
    rows_all = to_shards(jnp.broadcast_to(piece[None], (sh,) + piece.shape))
    own_rows = own_out + own_down
    w_out = rows_all[:, :own_out].reshape(gw, dim)
    w_down = rows_all[:, own_out:own_rows].reshape(gf, dim)
    w_shared = (
        rows_all[:, own_rows:]
        .reshape(sh, fold, bands, 2 * gf)
        .transpose(0, 2, 1, 3)
        .reshape(dim, 2 * gf)
    )

    route_ids = routes[0]
    expert_ids = jnp.arange(experts, dtype=jnp.int32)
    named = jnp.any(route_ids[:, :, None] == expert_ids[None, None, :], axis=1).astype(f32)
    earlier = (
        jnp.arange(toks)[:, None] > jnp.arange(toks)[None, :]
    ).astype(f32)
    rank = jnp.dot(earlier, named)
    dispatch = (
        (named.T[:, None, :] > 0.0)
        & (rank.T[:, None, :] == jnp.arange(CAP, dtype=f32)[None, :, None])
    ).astype(bf)
    slots = experts * CAP
    dispatch_flat = dispatch.reshape(slots, toks)
    live = (q * toks + jnp.arange(toks, dtype=jnp.int32) < lengths[0]).astype(f32)
    cot = out_cotangent[0].astype(f32) * live[:, None]
    cot_low = cot.astype(bf)

    local_slots = (sh, local_e, CAP)

    def dispatched(values):
        sent = times(dispatch_flat, values).astype(bf)
        return to_shards(sent.reshape(sh, local_e * CAP, -1)).reshape(*local_slots, -1)

    router_lane = at_router - (total - 128)
    lanes = jnp.arange(128, dtype=jnp.int32)
    named_lanes = jnp.pad(named, ((0, 0), (router_lane, 128 - router_lane - experts)))
    cot_rows = dispatched(jnp.concatenate([cot_low, named_lanes.astype(bf)], axis=1))

    x_wide = x_all.astype(f32)
    x_r = row_scale(x_wide)
    proj = times(x_all, w_all) * x_r

    small_all = w_all[:, at_small:at_router].reshape(sh, -1)
    at = taps * conv_own
    conv_full = (
        small_all[:, :at].reshape(sh, taps, conv_own).transpose(1, 0, 2).reshape(taps, conv_all)
    )
    offset_full = small_all[:, at : at + conv_own].reshape(conv_all)
    at = at + conv_own
    bias_full = small_all[:, at : at + head_own].reshape(heads)
    decay_full = small_all[:, at + head_own : at + 2 * head_own].reshape(heads)
    skip_full = small_all[:, at + 2 * head_own : at + 3 * head_own].reshape(heads)
    router_full = w_all[:, at_router:at_moe]
    moe_gain_full = w_all[:, at_moe].astype(f32)

    def group(values, width):
        return lax.dynamic_slice_in_dim(values, q * width, width, values.ndim - 1)

    conv_local = jnp.concatenate([group(conv_full, gw), conv_full[:, inner:]], axis=1).astype(f32)
    offset_local = jnp.concatenate([group(offset_full, gw), offset_full[inner:]]).astype(f32)
    bias_local = group(bias_full, gh).astype(f32)
    decay_local = group(decay_full, gh).astype(f32)
    skip_local = group(skip_full, gh).astype(f32)

    per_head = gw // gh
    taps_in = jnp.concatenate(
        [conv_local, offset_local[None], jnp.zeros((8 - taps - 1, gw + keys_w), f32)], axis=0
    )
    decay_rate = -jnp.exp(decay_local)
    head_in = jnp.pad(jnp.stack([bias_local, decay_rate]), ((0, 6), (0, 128 - gh)))
    skip_in = jnp.broadcast_to(jnp.repeat(skip_local, per_head)[None], (8, gw))
    mixed, q_low, square_part, starts = scan_forward(proj, taps_in, head_in, skip_in)

    cot_all = lax.all_gather(after(cot_low, w_all), "seq", axis=0, tiled=True)
    w_out, cot_rows, cot_all = lax.optimization_barrier((w_out, cot_rows, cot_all))
    out_part = times(q_low, w_out).astype(bf)
    out_sum = lax.psum_scatter(out_part, "seq", scatter_dimension=0, tiled=True)
    square = lax.psum(square_part.reshape(sq, toks), "seq")
    q_r = lax.rsqrt(square / inner + epsilon).reshape(seq_rows, 1)
    d_raw = expert_early(cot_rows, expert_down)
    tok_r = after(lax.dynamic_slice_in_dim(q_r, q * toks, toks, 0), d_raw)
    x_tok = x_low.astype(f32)
    added = out_sum.astype(f32) * tok_r
    resid = x_tok + added

    resid_r = row_scale(resid)
    resid_n = resid * resid_r
    moe_in = (resid_n * moe_gain_full[None, :]).astype(bf)
    moe_all = lax.all_gather(moe_in, "seq", axis=0, tiled=True)

    logits = times(moe_in, w_all[:, total - 128 :])
    top = jnp.max(jnp.where(named_lanes > 0.0, logits, -1e30), axis=1, keepdims=True)
    powers = jnp.where(
        named_lanes > 0.0, jnp.exp(jnp.where(named_lanes > 0.0, logits - top, 0.0)), 0.0
    )
    gates = (powers / jnp.sum(powers, axis=1, keepdims=True))[
        :, router_lane : router_lane + experts
    ]
    rows = dispatched(moe_in)
    own_ids = lax.axis_index("shard") * local_e + jnp.arange(local_e, dtype=jnp.int32)
    marks = jnp.stack(
        [own_ids + router_lane, own_ids, own_ids + 64] + [jnp.full_like(own_ids, -1)] * 5, axis=1
    )
    marks = (marks[:, :, None] == lanes[None, None, :]).astype(f32)

    s_both = times(moe_all, w_shared)
    s_gate, s_up = s_both[:, :gf], s_both[:, gf:]
    s_sig = jax.nn.sigmoid(s_gate)
    s_silu = s_gate * s_sig
    s_act = (s_silu * s_up).astype(bf)
    d_sh = times_transposed(cot_all, w_down)
    d_both = jnp.concatenate(
        [
            (d_sh * s_up * (s_sig * (1.0 + s_gate * (1.0 - s_sig)))).astype(bf),
            (d_sh * s_silu).astype(bf),
        ],
        axis=1,
    )
    d_moe_part = times_transposed(d_both, w_shared).astype(bf)
    d_moe_shared = lax.psum_scatter(d_moe_part, "seq", scatter_dimension=0, tiled=True)

    back_rows, e_act, e_scaled, d_g, d_v = expert_main(
        rows, cot_rows, d_raw, expert_gate, expert_up, w_all, marks, d_moe_part
    )
    d_returned = to_shards(back_rows.reshape(sh, local_e * CAP, dim + 128))
    e_out, e_grads = expert_late(rows, cot_rows, e_act, e_scaled, d_g, d_v, expert_down)
    d_returned, e_out = lax.optimization_barrier((d_returned, e_out))
    returned = to_shards(e_out.reshape(sh, local_e * CAP, dim))

    core, z_at = q % 2, q // 2
    mates = [(i, i ^ 1) for i in range(sq)]
    near = [(i, 2 * ((i // 2) ^ 1) + i % 2) for i in range(sq)]
    far = [(i, 2 * (sq // 2 - 1 - i // 2) + i % 2) for i in range(sq)]
    is_inner = ((z_at == 1) | (z_at == 2)).astype(jnp.int32)
    is_high = (z_at >= 2).astype(jnp.int32)
    e_mine = halve(e_grads.reshape(-1, e_grads.shape[2]), core, mates)
    cutoff = e_mine.shape[0] // 2
    e_one = halve(e_mine[:cutoff], is_inner, near)
    e_two = halve(e_mine[cutoff:], is_high, far)
    e_one, e_two = halve(e_one, is_high, far), halve(e_two, is_inner, near)

    d_flat = transposed_times(dispatch_flat, d_returned.reshape(slots, dim + 128))
    d_gates = d_flat[:, dim : dim + experts] + d_flat[:, dim + 64 : dim + 64 + experts]
    d_logits = gates * (d_gates - jnp.sum(gates * d_gates, axis=1, keepdims=True))
    d_moe = (
        d_flat[:, :dim]
        + d_moe_shared.astype(f32)
        + jnp.dot(d_logits, router_full.astype(f32).T, precision=highest)
    )
    grad_router = jnp.dot(moe_in.astype(f32).T, d_logits, precision=highest)
    grad_moe = jnp.sum(d_moe * resid_n, axis=0)
    d_scaled = d_moe * moe_gain_full[None, :]
    d_resid = (
        cot
        + d_scaled * resid_r
        - resid_n * (resid_r * jnp.mean(d_scaled * resid_n, axis=1, keepdims=True))
    )
    d_o = d_resid.astype(bf)
    kappa = jnp.sum(d_o.astype(f32) * added, axis=1) / inner
    d_o_all = lax.all_gather(d_o, "seq", axis=0, tiled=True)
    kappa_all = lax.all_gather(after(kappa, e_mine).reshape(1, toks), "seq", axis=0)
    kappa_all = kappa_all.reshape(seq_rows, 1)


    d_gated = times_transposed(d_o_all, w_out)
    grad_out_part = transposed_times(
        q_low, (after(q_r, kappa_all) * d_o_all.astype(f32)).astype(bf)
    )
    grad_down_part = transposed_times(s_act, cot_all)
    grad_shared_part = transposed_times(moe_all, d_both)

    mid_part = jnp.concatenate(
        [
            grad_shared_part,
            grad_router,
            grad_moe[:, None],
            jnp.zeros((dim, 128 - experts - 1), f32),
        ],
        axis=1,
    )
    lane_w = mid_part.shape[1]
    bands = dim // lane_w

    def to_bands(values):
        return jnp.concatenate(
            [values[:, :, band * lane_w : band * lane_w + lane_w] for band in range(bands)], axis=1
        )

    early_part = jnp.concatenate(
        [
            to_bands(grad_out_part.astype(bf).reshape(sh, own_out, dim)),
            to_bands(grad_down_part.astype(bf).reshape(sh, own_down, dim)),
            mid_part.astype(bf).reshape(sh, rows_w, lane_w),
        ],
        axis=1,
    )
    moved_early = to_shards(early_part)

    row_values = jnp.concatenate(
        [q_r, kappa_all, x_r, jnp.zeros((seq_rows, 5), f32)], axis=1
    )
    d_proj, d_taps, d_head, d_skip = scan_backward(
        proj, mixed, d_gated, row_values, starts, taps_in, head_in, skip_in, (returned, e_one, e_two)
    )
    grad_conv_local = d_taps[:taps]
    grad_offset_local = d_taps[taps]
    grad_bias_local = d_head[0, :gh]
    grad_decay_local = d_head[1, :gh] * decay_rate
    grad_skip_local = jnp.sum(d_skip[0].reshape(gh, per_head), axis=1)
    back_part = times_transposed(d_proj, w_all).astype(bf)
    shared_part = times(s_act, w_down).astype(bf)
    both_sum = lax.psum_scatter(
        jnp.concatenate([back_part, shared_part], axis=1), "seq", scatter_dimension=0, tiled=True
    ).astype(f32)
    back_sum, shared_sum = both_sum[:, :dim], both_sum[:, dim:]
    weighted = (gates.T[:, None, :] * dispatch.astype(f32)).reshape(slots, toks)
    combined = transposed_times(weighted.astype(bf), returned.reshape(slots, dim))
    block_output = ((resid + shared_sum + combined) * live[:, None]).astype(bf)[None]
    tok_x_r = row_scale(x_tok)
    x_n = x_tok * tok_x_r
    input_grad = (
        d_resid + back_sum - x_n * (tok_x_r * jnp.mean(back_sum * x_tok, axis=1, keepdims=True))
    )[None]

    grad_in_part = transposed_times(x_all, d_proj)

    def spread(local, count):
        wide = jnp.zeros(local.shape[:-1] + (count,), f32)
        return lax.dynamic_update_slice_in_dim(wide, local, q * local.shape[-1], local.ndim - 1)

    conv_rows = jnp.concatenate([grad_conv_local, grad_offset_local[None]], axis=0)
    conv_wide = jnp.concatenate([spread(conv_rows[:, :gw], inner), conv_rows[:, gw:]], axis=1)
    head_wide = spread(jnp.stack([grad_bias_local, grad_decay_local, grad_skip_local]), heads)
    small_part = jnp.concatenate(
        [
            conv_wide.reshape(taps + 1, sh, conv_own).transpose(1, 0, 2).reshape(sh, -1),
            head_wide.reshape(3, sh, head_own).transpose(1, 0, 2).reshape(sh, -1),
        ],
        axis=1,
    )
    small_count = small_part.shape[1]
    small_part = jnp.pad(
        small_part, ((0, 0), (0, rows_w * small_cols - small_count))
    ).reshape(sh, rows_w, small_cols)
    last_part = grad_in_part + jnp.pad(
        small_part.reshape(dim, small_cols), ((0, 0), (used, total - used - small_cols))
    )
    last_part, moved_early = lax.optimization_barrier((last_part.astype(bf), moved_early))
    early_sum = jnp.sum(moved_early.astype(f32), axis=0).astype(bf)
    rows_sum = lax.ppermute(early_sum[: bands * own_rows], both_axes, backward_pairs)
    e_one, e_two = after(e_one, last_part), after(e_two, last_part)
    e_one, e_two = double(e_one, is_high, far), double(e_two, is_inner, near)
    e_one, e_two = double(e_one, is_inner, near), double(e_two, is_high, far)
    moved_last = to_shards(last_part.reshape(sh, rows_w, total))
    last_sum = jnp.sum(moved_last.astype(f32), axis=0)
    last_sum = after(after(after(last_sum, e_one), e_two), both_sum).astype(bf)
    e_mine = jnp.concatenate([e_one, e_two], axis=0)
    e_other = lax.ppermute(e_mine, "seq", mates)
    grad_e_gate, grad_e_up, grad_e_down = unpack_expert_grads(e_mine, e_other, core)
    side = lax.all_gather(
        jnp.concatenate(
            [rows_sum, early_sum[bands * own_rows :]]
            + [last_sum[:, lane_w * i : lane_w * i + lane_w] for i in range(total // lane_w)],
            axis=0,
        ),
        "seq",
        axis=0,
    )
    gain_out = norm_gain.astype(f32)[:, None]
    (
        grad_in,
        tail_sums,
        grad_out,
        norm_sums,
        grad_down,
        grad_shared_gate,
        grad_shared_up,
        mid_sums,
    ) = assemble(side, in_weight, gain_col, out_weight, gain_out, own_out, own_down)
    grad_norm = norm_sums[:, 0]
    grad_router_weight = mid_sums[:, :experts]
    grad_moe_gain = mid_sums[:, experts]
    grad_mixer_gain = tail_sums[:, 0]
    lane_at = used - (total - 128)
    small_sum = tail_sums[:, lane_at : lane_at + small_cols].reshape(-1)
    at = taps * conv_own
    grad_conv = small_sum[:at].reshape(taps, conv_own)
    grad_offset = small_sum[at : at + conv_own]
    at = at + conv_own
    grad_bias = small_sum[at : at + head_own]
    grad_decay = small_sum[at + head_own : at + 2 * head_own]
    grad_skip = small_sum[at + 2 * head_own : at + 3 * head_own]
    return (
        block_output,
        input_grad,
        grad_mixer_gain,
        grad_in,
        grad_conv,
        grad_offset,
        grad_bias,
        grad_decay,
        grad_skip,
        grad_norm,
        grad_out,
        grad_moe_gain,
        grad_router_weight,
        grad_shared_gate,
        grad_shared_up,
        grad_down,
        grad_e_gate,
        grad_e_up,
        grad_e_down,
    )


def solution(mesh):
    placed = (
        P("shard", "seq", None),
        P("shard"),
        P("shard", "seq", None),
        P("shard", "seq", None),
        P("shard"),
        P("shard", None),
        P(None, "shard"),
        P("shard"),
        P("shard"),
        P("shard"),
        P("shard"),
        P("shard"),
        P("shard", None),
        P("shard"),
        P("shard", None),
        P("shard", None),
        P("shard", None),
        P("shard", None),
        P("shard", None, None),
        P("shard", None, None),
        P("shard", None, None),
    )
    return jax.shard_map(
        on_device,
        mesh=mesh,
        in_specs=placed,
        out_specs=(
            P("shard", "seq", None),
            P("shard", "seq", None),
            P("shard"),
            P("shard", None),
            P(None, "shard"),
            P("shard"),
            P("shard"),
            P("shard"),
            P("shard"),
            P("shard"),
            P("shard", None),
            P("shard"),
            P("shard", None),
            P("shard", None),
            P("shard", None),
            P("shard", None),
            P("shard", None, None),
            P("shard", None, None),
            P("shard", None, None),
        ),
        check_vma=False,
    )
```

```python
import functools

import jax
import jax.numpy as jnp
from jax import lax
from jax.experimental import pallas as pl
from jax.experimental.pallas import tpu as pltpu
from jax.sharding import PartitionSpec as P

CAP = 32


epsilon = 1e-05
highest = lax.Precision.HIGHEST
both_axes = ("seq", "shard")


def times(left, right):
    return jnp.dot(left, right, preferred_element_type=jnp.float32)


def times_transposed(left, right):
    return lax.dot_general(
        left, right, (((1,), (1,)), ((), ())), preferred_element_type=jnp.float32
    )


def transposed_times(left, right):
    return lax.dot_general(
        left, right, (((0,), (0,)), ((), ())), preferred_element_type=jnp.float32
    )


def after(value, other):
    corner = other[(0,) * (other.ndim - 1)][:1].astype(jnp.float32)
    return (value.astype(jnp.float32) + 0.0 * corner).astype(value.dtype)


def silu_slope(values):
    sigma = jax.nn.sigmoid(values)
    return sigma * (1.0 + values * (1.0 - sigma))


def row_scale(values):
    return lax.rsqrt(jnp.mean(values * values, axis=-1, keepdims=True) + epsilon)


CHUNK = 128
WIDE = 384
CONVW = 640
PAIRS = 3
HEADS_HERE = 6


def split_two(values):
    high = values.astype(jnp.bfloat16)
    return high, (values - high.astype(jnp.float32)).astype(jnp.bfloat16)


def ones_times(ones, values):
    high, low = split_two(values)
    return times(ones, high) + times(ones, low)


def times_ones(values, ones):
    high, low = split_two(values)
    return times(high, ones) + times(low, ones)


def transposed_times_ones(values, ones):
    high, low = split_two(values)
    return transposed_times(high, ones) + transposed_times(low, ones)


def grid_of(shape):
    rows = lax.broadcasted_iota(jnp.int32, shape, 0)
    columns = lax.broadcasted_iota(jnp.int32, shape, 1)
    return rows, columns


def mark(condition):
    return jnp.where(condition, 1.0, 0.0).astype(jnp.bfloat16)


def chunk_parts(proj, prev, has_prev, taps_ref, head_ref, pad_ref):
    f32, bf = jnp.float32, jnp.bfloat16
    feed = proj[:, WIDE : WIDE + CONVW].astype(bf).astype(f32)
    before = prev[:, WIDE : WIDE + CONVW].astype(bf).astype(f32)
    pad_ref[0:8, :] = jnp.where(has_prev, before, 0.0)
    pad_ref[8 : 8 + CHUNK, :] = feed
    conv = taps_ref[4:5, :]
    for tap in range(4):
        conv = conv + taps_ref[tap : tap + 1, :] * pad_ref[5 + tap : 5 + tap + CHUNK, :]
    sig = jax.nn.sigmoid(conv)
    act = conv * sig
    u = act[:, :WIDE]
    key = act[:, WIDE : WIDE + 128].astype(bf)
    query = act[:, WIDE + 128 :].astype(bf)
    step_low = proj[:, WIDE + CONVW :].astype(bf).astype(f32)
    pre = step_low + head_ref[0:1, :]
    rows, columns = grid_of((CHUNK, 128))
    here = columns < HEADS_HERE
    dt = jnp.where(here, jnp.maximum(pre, 0.0) + jnp.log1p(jnp.exp(-jnp.abs(pre))), 0.0)
    la = dt * head_ref[1:2, :]
    lower = mark(rows >= columns)
    cum = ones_times(lower, la)
    end = cum[CHUNK - 1 : CHUNK, :]
    wide_rows, wide_columns = grid_of((128, WIDE))
    widen = mark(wide_columns // 64 == wide_rows)
    dt_w = times_ones(dt, widen)
    e_w = times_ones(jnp.exp(cum), widen)
    w_w = times_ones(jnp.exp(end - cum), widen)
    full_rows, full_columns = grid_of((128, 2 * PAIRS * 128))
    la_full = times_ones(la, mark(full_columns // 128 == full_rows))
    scores = times_transposed(query, key)
    return dict(
        conv=conv, sig=sig, u=u, key=key, query=query, pre=pre, here=here, dt=dt, lower=lower,
        dt_w=dt_w, e_w=e_w, w_w=w_w, la_full=la_full, scores=scores, xs=u * dt_w,
    )


def pair_table(parts, pair):
    rows, columns = grid_of((CHUNK, 256))
    local = columns % 128
    steps = jnp.where(rows > local, parts["la_full"][:, 256 * pair : 256 * pair + 256], 0.0)
    gap = ones_times(parts["lower"], steps)
    causal = rows >= local
    decay = jnp.where(causal, jnp.exp(jnp.where(causal, gap, 0.0)), 0.0)
    scores = parts["scores"]
    return decay, decay * jnp.concatenate([scores, scores], axis=1)


def stack_heads(values, pair):
    both = values[:, 128 * pair : 128 * pair + 128]
    first = lax.broadcasted_iota(jnp.int32, both.shape, 1) < 64
    return jnp.concatenate(
        [jnp.where(first, both, 0.0), jnp.where(first, 0.0, both)], axis=0
    ).astype(jnp.bfloat16)


def scan_forward_kernel(
    proj_ref, prev_ref, taps_ref, head_ref, skip_ref,
    mixed_ref, q_ref, square_ref, start_ref, state_ref, pad_ref,
):
    f32, bf = jnp.float32, jnp.bfloat16
    chunk = pl.program_id(0)

    @pl.when(chunk == 0)
    def _():
        state_ref[...] = jnp.zeros(state_ref.shape, f32)

    parts = chunk_parts(
        proj_ref[...], prev_ref[...], chunk > 0, taps_ref, head_ref, pad_ref
    )
    state = state_ref[...]
    start_ref[0] = state
    xs = parts["xs"]
    inside = []
    for pair in range(PAIRS):
        _, table = pair_table(parts, pair)
        inside.append(times(table.astype(bf), stack_heads(xs, pair)))
    across = times(parts["query"], state.astype(bf))
    y = (
        jnp.concatenate(inside, axis=1)
        + parts["e_w"] * across
        + skip_ref[0:1, :] * parts["u"]
    )
    mixed = y.astype(bf)
    mixed_ref[...] = mixed
    gate = proj_ref[:, :WIDE]
    q_val = mixed.astype(f32) * (gate * jax.nn.sigmoid(gate))
    q_ref[...] = q_val.astype(bf)
    square_ref[...] = jnp.sum(q_val * q_val, axis=1, keepdims=True)
    state_ref[...] = state * parts["e_w"][CHUNK - 1 : CHUNK, :] + transposed_times(
        parts["key"], (xs * parts["w_w"]).astype(bf)
    )


def scan_backward_kernel(
    proj_ref, prev_ref, mixed_ref, d_gated_ref, rows_ref, start_ref, taps_ref, head_ref, skip_ref,
    earlier_0, earlier_1, earlier_2, d_proj_ref, d_taps_ref, d_head_ref, d_skip_ref,
    state_ref, pad_ref, late_ref,
):
    f32, bf = jnp.float32, jnp.bfloat16
    step = pl.program_id(0)
    last = pl.num_programs(0) - 1

    @pl.when(step == 0)
    def _():
        state_ref[...] = jnp.zeros(state_ref.shape, f32)
        late_ref[CHUNK : CHUNK + 8, :] = jnp.zeros((8, CONVW), f32)
        d_taps_ref[...] = jnp.zeros(d_taps_ref.shape, f32)
        d_head_ref[...] = jnp.zeros(d_head_ref.shape, f32)
        d_skip_ref[...] = jnp.zeros(d_skip_ref.shape, f32)

    parts = chunk_parts(
        proj_ref[...], prev_ref[...], step < last, taps_ref, head_ref, pad_ref
    )
    u, key, query, xs = parts["u"], parts["key"], parts["query"], parts["xs"]
    e_w, w_w, dt_w = parts["e_w"], parts["w_w"], parts["dt_w"]

    gate = proj_ref[:, :WIDE]
    gate_sig = jax.nn.sigmoid(gate)
    gate_act = gate * gate_sig
    mixed = mixed_ref[...].astype(f32)
    q_val = mixed * gate_act
    q_r = rows_ref[:, 0:1]
    d_q = q_r * d_gated_ref[...] - q_val * (q_r * q_r * rows_ref[:, 1:2])
    d_gate = d_q * mixed * (gate_sig * (1.0 + gate * (1.0 - gate_sig)))
    d_y = (d_q * gate_act).astype(bf).astype(f32)

    start = start_ref[0]
    start_low = start.astype(bf)
    d_end = state_ref[...]
    d_end_low = d_end.astype(bf)
    xw = xs * w_w
    ye = d_y * e_w
    ye_low = ye.astype(bf)
    across = times(query, start_low)
    pulled = times(key, d_end_low)
    d_query = times_transposed(ye_low, start_low)
    d_key = times_transposed(xw.astype(bf), d_end_low)
    state_ref[...] = d_end * e_w[CHUNK - 1 : CHUNK, :] + transposed_times(query, ye_low)
    d_scores = jnp.zeros((CHUNK, 128), f32)
    turns = jnp.zeros((CHUNK, 128), f32)
    d_xs = []
    for pair in range(PAIRS):
        decay, table = pair_table(parts, pair)
        xs_two = stack_heads(xs, pair)
        dy_two = stack_heads(d_y, pair)
        d_table = times_transposed(d_y[:, 128 * pair : 128 * pair + 128].astype(bf), xs_two)
        d_decay = d_table * decay
        d_scores = d_scores + d_decay[:, :128] + d_decay[:, 128:]
        d_gap = d_table * table
        table_low = table.astype(bf)
        d_xs.append(
            transposed_times(
                jnp.concatenate([table_low[:, :128], table_low[:, 128:]], axis=0), dy_two
            )
        )
        two_rows, two_columns = grid_of((256, 128))
        own = mark(two_columns == 2 * pair + two_rows // 128)
        turns = turns + times_ones(d_gap, own)
        turns = turns - transposed_times_ones(
            jnp.concatenate([d_gap[:, :128], d_gap[:, 128:]], axis=0), own
        )
    d_xs = jnp.concatenate(d_xs, axis=1) + w_w * pulled
    d_scores_low = d_scores.astype(bf)
    d_query = d_query + times(d_scores_low, key)
    d_key = d_key + transposed_times(d_scores_low, query)

    rows, columns = grid_of((CHUNK, 128))
    upper = mark(columns >= rows)
    strict = mark(columns < rows)
    sum_rows, sum_columns = grid_of((WIDE, 128))
    per_head = mark(sum_rows // 64 == sum_columns)
    end_row = jnp.sum(d_end * start, axis=0, keepdims=True) * e_w[CHUNK - 1 : CHUNK, :]
    wide = ones_times(upper, ye * across) + ones_times(strict, xw * pulled) + end_row
    d_la = ones_times(upper, turns) + times_ones(wide, per_head)
    d_dt = times_ones(d_xs * u, per_head) + d_la * head_ref[1:2, :]
    d_pre = jnp.where(parts["here"], d_dt * jax.nn.sigmoid(parts["pre"]), 0.0)
    d_head_ref[0:1, :] += jnp.sum(d_pre, axis=0, keepdims=True)
    d_head_ref[1:2, :] += jnp.sum(d_la * parts["dt"], axis=0, keepdims=True)
    d_skip_ref[0:1, :] += jnp.sum(d_y * u, axis=0, keepdims=True)

    d_u = d_xs * dt_w + skip_ref[0:1, :] * d_y
    conv, sig = parts["conv"], parts["sig"]
    d_conv = jnp.concatenate([d_u, d_key, d_query], axis=1) * (sig * (1.0 + conv * (1.0 - sig)))
    late_ref[0:CHUNK, :] = d_conv
    d_feed = jnp.zeros((CHUNK, CONVW), f32)
    for tap in range(4):
        d_feed = d_feed + taps_ref[tap : tap + 1, :] * late_ref[3 - tap : 3 - tap + CHUNK, :]
        d_taps_ref[tap : tap + 1, :] += jnp.sum(
            d_conv * pad_ref[5 + tap : 5 + tap + CHUNK, :], axis=0, keepdims=True
        )
    d_taps_ref[4:5, :] += jnp.sum(d_conv, axis=0, keepdims=True)
    late_ref[CHUNK : CHUNK + 8, :] = d_conv[0:8, :]
    scale = rows_ref[:, 2:3]
    d_proj_ref[:, :WIDE] = (d_gate * scale).astype(bf)
    d_proj_ref[:, WIDE : WIDE + CONVW] = (d_feed * scale).astype(bf)
    d_proj_ref[:, WIDE + CONVW :] = (d_pre * scale).astype(bf)


def corner_of(array):
    return pl.BlockSpec(
        (1,) * (array.ndim - 2) + (16, 128), lambda *step: (0,) * array.ndim
    )


def whole(shape):
    return pl.BlockSpec(shape, lambda step: (0,) * len(shape))


def scan_forward(proj, taps, head, skip):
    rows, width = proj.shape
    chunks = rows // CHUNK
    by_chunk = lambda step: (step, 0)
    return pl.pallas_call(
        scan_forward_kernel,
        grid=(chunks,),
        in_specs=[
            pl.BlockSpec((CHUNK, width), by_chunk),
            pl.BlockSpec((8, width), lambda step: (jnp.maximum(step * (CHUNK // 8) - 1, 0), 0)),
            whole(taps.shape),
            whole(head.shape),
            whole(skip.shape),
        ],
        out_specs=[
            pl.BlockSpec((CHUNK, WIDE), by_chunk),
            pl.BlockSpec((CHUNK, WIDE), by_chunk),
            pl.BlockSpec((CHUNK, 1), by_chunk),
            pl.BlockSpec((1, 128, WIDE), lambda step: (step, 0, 0)),
        ],
        out_shape=[
            jax.ShapeDtypeStruct((rows, WIDE), jnp.bfloat16),
            jax.ShapeDtypeStruct((rows, WIDE), jnp.bfloat16),
            jax.ShapeDtypeStruct((rows, 1), jnp.float32),
            jax.ShapeDtypeStruct((chunks, 128, WIDE), jnp.float32),
        ],
        scratch_shapes=[
            pltpu.VMEM((128, WIDE), jnp.float32),
            pltpu.VMEM((CHUNK + 8, CONVW), jnp.float32),
        ],
        compiler_params=pltpu.CompilerParams(vmem_limit_bytes=32 << 20),
        cost_estimate=pl.CostEstimate(
            flops=3 << 30, bytes_accessed=12 << 20, transcendentals=4 << 20
        ),
        name="scan_forward",
    )(proj, proj, taps, head, skip)


def scan_backward(proj, mixed, d_gated, row_values, starts, taps, head, skip, earlier):
    rows, width = proj.shape
    chunks = rows // CHUNK
    by_chunk = lambda step: (chunks - 1 - step, 0)
    return pl.pallas_call(
        scan_backward_kernel,
        grid=(chunks,),
        in_specs=[
            pl.BlockSpec((CHUNK, width), by_chunk),
            pl.BlockSpec(
                (8, width),
                lambda step: (jnp.maximum((chunks - 1 - step) * (CHUNK // 8) - 1, 0), 0),
            ),
            pl.BlockSpec((CHUNK, WIDE), by_chunk),
            pl.BlockSpec((CHUNK, WIDE), by_chunk),
            pl.BlockSpec((CHUNK, row_values.shape[1]), by_chunk),
            pl.BlockSpec((1, 128, WIDE), lambda step: (chunks - 1 - step, 0, 0)),
            whole(taps.shape),
            whole(head.shape),
            whole(skip.shape),
            *map(corner_of, earlier),
        ],
        out_specs=[
            pl.BlockSpec((CHUNK, width), by_chunk),
            whole((8, CONVW)),
            whole((8, 128)),
            whole((8, WIDE)),
        ],
        out_shape=[
            jax.ShapeDtypeStruct((rows, width), jnp.bfloat16),
            jax.ShapeDtypeStruct((8, CONVW), jnp.float32),
            jax.ShapeDtypeStruct((8, 128), jnp.float32),
            jax.ShapeDtypeStruct((8, WIDE), jnp.float32),
        ],
        scratch_shapes=[
            pltpu.VMEM((128, WIDE), jnp.float32),
            pltpu.VMEM((CHUNK + 8, CONVW), jnp.float32),
            pltpu.VMEM((CHUNK + 8, CONVW), jnp.float32),
        ],
        compiler_params=pltpu.CompilerParams(vmem_limit_bytes=48 << 20),
        cost_estimate=pl.CostEstimate(
            flops=10 << 30, bytes_accessed=20 << 20, transcendentals=8 << 20
        ),
        name="scan_backward",
    )(proj, proj, mixed, d_gated, row_values, starts, taps, head, skip, *earlier)


def expert_early_kernel(cot_ref, down_ref, raw_ref):
    cot = cot_ref[...].reshape(-1, cot_ref.shape[-1])
    raw_ref[0] = times_transposed(cot, down_ref[0])


def expert_main_kernel(
    rows_ref, routed_ref, raw_ref, gate_ref, up_ref, router_ref, marks_ref,
    moe_ref, cot_ref, shared_ref, down_ref,
    back_ref, act_ref, scaled_ref, d_g_ref, d_v_ref, both_ref, s_act_ref, d_both_ref,
):
    f32, bf = jnp.float32, jnp.bfloat16
    dim = rows_ref.shape[-1]
    rows = rows_ref[...].reshape(-1, dim)
    routed = routed_ref[...].reshape(-1, 128).astype(f32) > 0.0
    logits = times(rows, router_ref[...])
    top = jnp.max(jnp.where(routed, logits, -1e30), axis=1, keepdims=True)
    powers = jnp.where(routed, jnp.exp(jnp.where(routed, logits - top, 0.0)), 0.0)
    own = jnp.sum(powers * marks_ref[0, 0:1, :], axis=1, keepdims=True)
    gate = own / jnp.maximum(jnp.sum(powers, axis=1, keepdims=True), 1e-30)
    g = times(rows, gate_ref[0])
    v = times(rows, up_ref[0])
    sig = jax.nn.sigmoid(g)
    silu = g * sig
    act = (silu * v).astype(bf)
    act_wide = act.astype(f32)
    raw = raw_ref[0]
    d_gate = jnp.sum(act_wide * raw, axis=1, keepdims=True)
    d_act = gate * raw
    d_g = (d_act * v * (sig * (1.0 + g * (1.0 - sig)))).astype(bf)
    d_v = (d_act * silu).astype(bf)
    d_row = times_transposed(d_g, gate_ref[0]) + times_transposed(d_v, up_ref[0])
    high = d_gate.astype(bf).astype(f32)
    scalars = high * marks_ref[0, 1:2, :] + (d_gate - high) * marks_ref[0, 2:3, :]
    lead = back_ref.shape[:-1]
    back_ref[:, :, :, :dim] = d_row.astype(bf).reshape(*lead, dim)
    back_ref[:, :, :, dim:] = scalars.astype(bf).reshape(*lead, 128)
    act_ref[0] = act
    scaled_ref[0] = (gate * act_wide).astype(bf)
    d_g_ref[0] = d_g
    d_v_ref[0] = d_v

    units = down_ref.shape[0]
    s_both = times(moe_ref[...], shared_ref[...])
    s_gate, s_up = s_both[:, :units], s_both[:, units:]
    s_sig = jax.nn.sigmoid(s_gate)
    s_silu = s_gate * s_sig
    s_act = (s_silu * s_up).astype(bf)
    d_sh = times_transposed(cot_ref[...], down_ref[...])
    d_gs = (d_sh * s_up * (s_sig * (1.0 + s_gate * (1.0 - s_sig)))).astype(bf)
    d_both = jnp.concatenate([d_gs, (d_sh * s_silu).astype(bf)], axis=1)
    both_ref[:, :dim] = times_transposed(d_both, shared_ref[...]).astype(bf)
    both_ref[:, dim:] = times(s_act, down_ref[...]).astype(bf)
    s_act_ref[...] = s_act
    d_both_ref[...] = d_both


def expert_late_kernel(
    rows_ref, cot_ref, act_ref, scaled_ref, d_g_ref, d_v_ref, down_ref,
    out_ref, grads_ref,
):
    bf = jnp.bfloat16
    dim = rows_ref.shape[-1]
    rows = rows_ref[...].reshape(-1, dim)
    cot = cot_ref[...].reshape(-1, dim)
    out_ref[...] = times(act_ref[0], down_ref[0]).astype(bf).reshape(out_ref.shape)
    units = act_ref.shape[-1]
    grads_ref[0, :dim] = transposed_times(rows, d_g_ref[0]).astype(bf)
    grads_ref[0, dim : 2 * dim] = transposed_times(rows, d_v_ref[0]).astype(bf)
    for block in range(dim // units):
        at = 2 * dim + block * units
        grads_ref[0, at : at + units] = transposed_times(
            scaled_ref[0], cot[:, block * units : block * units + units]
        ).astype(bf)


def expert_slots(shape, start=0):
    return pl.BlockSpec(
        (shape[0], 1) + tuple(shape[2:]), lambda e: (0, e) + (0,) * (len(shape) - 3) + (start,)
    )


def per_expert(shape):
    return pl.BlockSpec((1,) + tuple(shape[1:]), lambda e: (e,) + (0,) * (len(shape) - 1))


def expert_params(flops, moved):
    return dict(
        compiler_params=pltpu.CompilerParams(vmem_limit_bytes=56 << 20),
        cost_estimate=pl.CostEstimate(flops=flops, bytes_accessed=moved, transcendentals=1 << 19),
    )


def expert_early(cot_rows, down):
    sources, local, cap, _ = cot_rows.shape
    units, dim = down.shape[1:]
    return pl.pallas_call(
        expert_early_kernel,
        grid=(local,),
        in_specs=[expert_slots((sources, local, cap, dim)), per_expert(down.shape)],
        out_specs=per_expert((local, sources * cap, units)),
        out_shape=jax.ShapeDtypeStruct((local, sources * cap, units), jnp.float32),
        name="expert_early",
        **expert_params(2 << 30, 8 << 20),
    )(cot_rows, down)


def expert_main(rows, cot_rows, raw, gate, up, w_all, marks, moe_all, cot_all, w_shared, w_down):
    sources, local, cap, dim = rows.shape
    units = gate.shape[2]
    count = sources * cap
    hidden = jax.ShapeDtypeStruct((local, count, units), jnp.bfloat16)
    back = (sources, local, cap, dim + 128)
    seq_rows = moe_all.shape[0]
    shared_units = w_down.shape[0]
    share = lambda width: pl.BlockSpec((seq_rows // local, width), lambda e: (e, 0))
    return pl.pallas_call(
        expert_main_kernel,
        grid=(local,),
        in_specs=[
            expert_slots(rows.shape),
            expert_slots((sources, local, cap, 128), dim // 128),
            per_expert(raw.shape),
            per_expert(gate.shape),
            per_expert(up.shape),
            pl.BlockSpec((dim, 128), lambda e: (0, w_all.shape[1] // 128 - 1)),
            per_expert(marks.shape),
            share(dim),
            share(dim),
            whole(w_shared.shape),
            whole(w_down.shape),
        ],
        out_specs=[expert_slots(back)]
        + [per_expert(hidden.shape)] * 4
        + [share(2 * dim), share(shared_units), share(2 * shared_units)],
        out_shape=[jax.ShapeDtypeStruct(back, jnp.bfloat16)]
        + [hidden] * 4
        + [
            jax.ShapeDtypeStruct((seq_rows, width), jnp.bfloat16)
            for width in (2 * dim, shared_units, 2 * shared_units)
        ],
        name="expert_main",
        **expert_params(8 << 30, 20 << 20),
    )(rows, cot_rows, raw, gate, up, w_all, marks, moe_all, cot_all, w_shared, w_down)


def expert_late(rows, cot_rows, act, scaled, d_g, d_v, down):
    sources, local, cap, dim = rows.shape
    units = down.shape[1]
    grads = (local, 3 * dim, units)
    return pl.pallas_call(
        expert_late_kernel,
        grid=(local,),
        in_specs=[expert_slots(rows.shape), expert_slots(rows.shape)]
        + [per_expert(act.shape)] * 4
        + [per_expert(down.shape)],
        out_specs=[
            expert_slots(rows.shape),
            per_expert(grads),
        ],
        out_shape=[
            jax.ShapeDtypeStruct(rows.shape, jnp.bfloat16),
            jax.ShapeDtypeStruct(grads, jnp.bfloat16),
        ],
        name="expert_late",
        **expert_params(7 << 30, 24 << 20),
    )(rows, cot_rows, act, scaled, d_g, d_v, down)


def assemble_kernel(
    own_out, own_down, side_ref, in_ref, in_gain_ref, out_ref, out_gain_ref,
    grad_in_ref, tail_ref, grad_out_ref, norm_ref, grad_down_ref, gate_ref, up_ref, mid_ref,
):
    f32 = jnp.float32
    groups = side_ref.shape[0]
    inner = groups * WIDE
    bands = out_ref.shape[1] // WIDE
    rows_w = in_ref.shape[0]
    gain = in_gain_ref[...]
    at_down = bands * own_out
    at_mid = at_down + bands * own_down
    at_in = at_mid + rows_w
    units = gate_ref.shape[1] // groups

    def block(group, start, rows):
        return side_ref[group, start : start + rows, :].astype(f32)

    grad_gain = jnp.zeros((rows_w, 1), f32)
    keys = jnp.zeros((rows_w, 256), f32)
    tail = jnp.zeros((rows_w, 128), f32)
    steps = jnp.zeros((rows_w, 128), f32)
    mid = jnp.zeros((rows_w, 128), f32)
    rows, columns = grid_of((128, 128))

    def put(start, values):
        stop = start + values.shape[1]
        grad_in_ref[:, start:stop] = values * gain
        weight = in_ref[:, start:stop].astype(f32)
        return jnp.sum(weight * values, axis=1, keepdims=True)

    for group in range(groups):
        grad_gain += put(group * WIDE, block(group, at_in, rows_w))
        grad_gain += put(inner + group * WIDE, block(group, at_in + rows_w, rows_w))
        last = block(group, at_in + 2 * rows_w, rows_w)
        keys = keys + last[:, :256]
        tail = tail + last[:, 256:]
        moved = mark((rows < HEADS_HERE) & (columns == rows + HEADS_HERE * group))
        steps = steps + times(last[:, 256:].astype(jnp.bfloat16), moved)
        shared = block(group, at_mid, rows_w)
        gate_ref[:, units * group : units * group + units] = shared[:, :units]
        up_ref[:, units * group : units * group + units] = shared[:, units : 2 * units]
        mid = mid + shared[:, 2 * units :]
    grad_gain += put(2 * inner, keys)
    grad_gain += put(2 * inner + 256, steps[:, : groups * HEADS_HERE])
    lane = lax.broadcasted_iota(jnp.int32, tail.shape, 1)
    tail_ref[...] = jnp.where(lane == 0, grad_gain, tail)
    mid_ref[...] = mid

    for group in range(groups):
        sums = jnp.zeros((own_out, 1), f32)
        mine = slice(own_out * group, own_out * group + own_out)
        for band in range(bands):
            wide = slice(WIDE * band, WIDE * band + WIDE)
            values = block(group, own_out * band, own_out)
            grad_out_ref[mine, wide] = values * out_gain_ref[mine, :]
            sums += jnp.sum(out_ref[mine, wide].astype(f32) * values, axis=1, keepdims=True)
            grad_down_ref[own_down * group : own_down * group + own_down, wide] = block(
                group, at_down + own_down * band, own_down
            )
        norm_ref[mine, :] = sums


def assemble(side, in_weight, in_gain, out_weight, out_gain, own_out, own_down):
    groups = side.shape[0]
    rows, width = in_weight.shape
    out_rows, dim = out_weight.shape
    shapes = [
        (rows, width),
        (rows, 128),
        (out_rows, dim),
        (out_rows, 1),
        (groups * own_down, dim),
        (rows, groups * 128),
        (rows, groups * 128),
        (rows, 128),
    ]
    return pl.pallas_call(
        functools.partial(assemble_kernel, own_out, own_down),
        in_specs=[pl.BlockSpec(memory_space=pltpu.VMEM)] * 5,
        out_specs=[pl.BlockSpec(memory_space=pltpu.VMEM)] * len(shapes),
        out_shape=[jax.ShapeDtypeStruct(shape, jnp.float32) for shape in shapes],
        compiler_params=pltpu.CompilerParams(vmem_limit_bytes=40 << 20),
        cost_estimate=pl.CostEstimate(flops=8 << 20, bytes_accessed=12 << 20, transcendentals=0),
        name="assemble",
    )(side, in_weight, in_gain, out_weight, out_gain)


def gather_rows(values, core, z_at, mates):
    cores = 2
    chips = len(mates) // cores
    column = [values]
    for hop in range(1, chips):
        pairs = [
            (i, (i // cores + hop) % chips * cores + i % cores) for i in range(len(mates))
        ]
        column.append(lax.ppermute(values, "seq", pairs))
    column = jnp.stack(column)
    both = jnp.stack([column, lax.ppermute(column, "seq", mates)], axis=1)
    both = both.reshape((len(mates),) + values.shape)
    ordered = [
        lax.dynamic_index_in_dim(both, (z_at - z) % chips * cores + (c ^ core), 0, keepdims=False)
        for z in range(chips)
        for c in range(cores)
    ]
    return jnp.concatenate(ordered, axis=0)


def halve(values, bit, pairs):
    f32 = jnp.float32
    parts = values.reshape(2, values.shape[0] // 2, values.shape[1])
    sent = lax.dynamic_index_in_dim(parts, 1 - bit, 0, keepdims=False)
    kept = lax.dynamic_index_in_dim(parts, bit, 0, keepdims=False)
    other = lax.ppermute(sent, "seq", pairs)
    return (kept.astype(f32) + other.astype(f32)).astype(jnp.bfloat16)


def double(values, bit, pairs):
    other = lax.ppermute(values, "seq", pairs)
    first = jnp.where(bit == 0, values, other)
    second = jnp.where(bit == 0, other, values)
    return jnp.concatenate([first, second], axis=0)


def unpack_kernel(core_ref, own_ref, other_ref, gate_ref, up_ref, down_ref):
    part = pl.program_id(1)
    block = jnp.where(pl.program_id(0) == 0, own_ref[...], other_ref[...]).astype(jnp.float32)
    units = block.shape[1]

    @pl.when(part == 0)
    def _():
        gate_ref[0] = block

    @pl.when(part == 1)
    def _():
        up_ref[0] = block

    @pl.when(part == 2)
    def _():
        for at in range(0, block.shape[0], units):
            down_ref[0, :, at : at + units] = block[at : at + units]


def unpack_expert_grads(own, other, core):
    rows, units = own.shape
    dim = rows // 3
    to_expert = lambda who, part, core: (jnp.where(who == 0, core[0], 1 - core[0]), 0, 0)
    return pl.pallas_call(
        unpack_kernel,
        grid_spec=pltpu.PrefetchScalarGridSpec(
            num_scalar_prefetch=1,
            grid=(2, 3),
            in_specs=[
                pl.BlockSpec((dim, units), lambda who, part, core: (jnp.where(who == 0, part, 2), 0)),
                pl.BlockSpec((dim, units), lambda who, part, core: (jnp.where(who == 0, 0, part), 0)),
            ],
            out_specs=[
                pl.BlockSpec((1, dim, units), to_expert),
                pl.BlockSpec((1, dim, units), to_expert),
                pl.BlockSpec((1, units, dim), to_expert),
            ],
        ),
        out_shape=[
            jax.ShapeDtypeStruct((2, dim, units), jnp.float32),
            jax.ShapeDtypeStruct((2, dim, units), jnp.float32),
            jax.ShapeDtypeStruct((2, units, dim), jnp.float32),
        ],
        compiler_params=pltpu.CompilerParams(vmem_limit_bytes=40 << 20),
        cost_estimate=pl.CostEstimate(flops=1 << 20, bytes_accessed=28 << 20, transcendentals=0),
        name="unpack_expert_grads",
    )(core.reshape(1), own, other)


def on_device(
    block_input,
    lengths,
    routes,
    out_cotangent,
    mixer_gain,
    in_weight,
    conv_weight,
    conv_bias,
    step_bias,
    decay_log,
    skip_gain,
    norm_gain,
    out_weight,
    moe_gain,
    router_weight,
    shared_gate,
    shared_up,
    shared_down,
    expert_gate,
    expert_up,
    expert_down,
):
    sq = lax.axis_size("seq")
    sh = lax.axis_size("shard")
    q = lax.axis_index("seq")
    f32 = jnp.float32
    bf = jnp.bfloat16
    x_low = block_input[0]
    toks, dim = x_low.shape
    seq_rows = toks * sq
    heads = step_bias.shape[0] * sh
    inner = norm_gain.shape[0] * sh
    conv_all = conv_bias.shape[0] * sh
    keys_w = conv_all - inner
    gh = heads // sq
    gw = inner // sq
    rows_w = in_weight.shape[0]
    experts = router_weight.shape[1]
    local_e = expert_gate.shape[0]
    fs = shared_gate.shape[1]
    gf = fs // sq
    taps = conv_weight.shape[0]
    conv_own = conv_bias.shape[0]
    head_own = step_bias.shape[0]

    gain_col = mixer_gain.astype(f32)[:, None]

    def cols(start, width):
        return lax.dynamic_slice_in_dim(in_weight, start, width, 1)

    w_cols = jnp.concatenate(
        [
            cols(q * gw, gw),
            cols(inner + q * gw, gw),
            in_weight[:, 2 * inner : 2 * inner + keys_w],
            cols(2 * inner + keys_w + q * gh, gh),
        ],
        axis=1,
    )
    w_cols = (w_cols.astype(f32) * gain_col).astype(bf)
    used = 2 * gw + keys_w + gh
    small = jnp.concatenate(
        [conv_weight.reshape(-1), conv_bias, step_bias, decay_log, skip_gain]
    )
    small_cols = -(-small.shape[0] // rows_w)
    small = jnp.pad(small, (0, small_cols * rows_w - small.shape[0])).reshape(rows_w, small_cols)
    packed = jnp.concatenate(
        [w_cols, small, router_weight, moe_gain[:, None]], axis=1
    )
    at_small = used
    at_router = at_small + small_cols
    at_moe = at_router + experts
    total = -(-(at_moe + 1) // 128) * 128
    packed = jnp.pad(packed, ((0, 0), (0, total - packed.shape[1])))

    def to_shards(values):
        return lax.all_to_all(values, "shard", split_axis=0, concat_axis=0, tiled=True)

    w_all = lax.all_gather(packed, "shard", axis=0, tiled=True)
    core, z_at = q % 2, q // 2
    mates = [(i, i ^ 1) for i in range(sq)]
    x_all = gather_rows(x_low, core, z_at, mates)

    out_scaled = (norm_gain.astype(f32)[:, None] * out_weight.astype(f32)).astype(bf)
    own_out = out_weight.shape[0] // sq
    own_down = shared_down.shape[0] // sq
    piece = jnp.concatenate(
        [
            lax.dynamic_slice_in_dim(out_scaled, q * own_out, own_out, 0),
            lax.dynamic_slice_in_dim(shared_down, q * own_down, own_down, 0),
        ],
        axis=0,
    )
    ratio = sh // sq
    forward_pairs = []
    for a in range(sh):
        for j in range(sq):
            s_to = sq * (a % ratio) + j
            q_to = a // ratio
            forward_pairs.append((j * sh + a, q_to * sh + s_to))
    backward_pairs = [(b, a) for a, b in forward_pairs]
    piece = lax.ppermute(piece, both_axes, forward_pairs)
    shared_cols = jnp.concatenate(
        [
            lax.dynamic_slice_in_dim(shared_gate, q * gf, gf, 1),
            lax.dynamic_slice_in_dim(shared_up, q * gf, gf, 1),
        ],
        axis=1,
    )
    fold = rows_w * 2 * gf // dim
    bands = dim // (2 * gf)
    shared_rows = jnp.concatenate(
        [shared_cols[fold * band : fold * band + fold] for band in range(bands)], axis=1
    )
    piece = jnp.concatenate([piece, shared_rows], axis=0)
    route_ids = routes[0]
    expert_ids = jnp.arange(experts, dtype=jnp.int32)
    named = jnp.any(route_ids[:, :, None] == expert_ids[None, None, :], axis=1).astype(f32)
    earlier = (
        jnp.arange(toks)[:, None] > jnp.arange(toks)[None, :]
    ).astype(f32)
    rank = jnp.dot(earlier, named)
    dispatch = (
        (named.T[:, None, :] > 0.0)
        & (rank.T[:, None, :] == jnp.arange(CAP, dtype=f32)[None, :, None])
    ).astype(bf)
    slots = experts * CAP
    dispatch_flat = dispatch.reshape(slots, toks)
    live = (q * toks + jnp.arange(toks, dtype=jnp.int32) < lengths[0]).astype(f32)
    cot = out_cotangent[0].astype(f32) * live[:, None]
    cot_low = cot.astype(bf)

    local_slots = (sh, local_e, CAP)

    def dispatched(values):
        sent = times(dispatch_flat, values).astype(bf)
        return to_shards(sent.reshape(sh, local_e * CAP, -1)).reshape(*local_slots, -1)

    router_lane = at_router - (total - 128)
    lanes = jnp.arange(128, dtype=jnp.int32)
    named_lanes = jnp.pad(named, ((0, 0), (router_lane, 128 - router_lane - experts)))
    cot_rows = dispatched(jnp.concatenate([cot_low, named_lanes.astype(bf)], axis=1))

    w_all, cot_rows = lax.optimization_barrier((w_all, cot_rows))
    piece = after(piece, cot_rows)
    rows_all = to_shards(jnp.broadcast_to(piece[None], (sh,) + piece.shape))
    own_rows = own_out + own_down
    w_out = rows_all[:, :own_out].reshape(gw, dim)
    w_down = rows_all[:, own_out:own_rows].reshape(gf, dim)
    w_shared = (
        rows_all[:, own_rows:]
        .reshape(sh, fold, bands, 2 * gf)
        .transpose(0, 2, 1, 3)
        .reshape(dim, 2 * gf)
    )

    x_wide = x_all.astype(f32)
    x_r = row_scale(x_wide)
    proj = times(x_all, w_all) * x_r

    small_all = w_all[:, at_small:at_router].reshape(sh, -1)
    at = taps * conv_own
    conv_full = (
        small_all[:, :at].reshape(sh, taps, conv_own).transpose(1, 0, 2).reshape(taps, conv_all)
    )
    offset_full = small_all[:, at : at + conv_own].reshape(conv_all)
    at = at + conv_own
    bias_full = small_all[:, at : at + head_own].reshape(heads)
    decay_full = small_all[:, at + head_own : at + 2 * head_own].reshape(heads)
    skip_full = small_all[:, at + 2 * head_own : at + 3 * head_own].reshape(heads)
    router_full = w_all[:, at_router:at_moe]
    moe_gain_full = w_all[:, at_moe].astype(f32)

    def group(values, width):
        return lax.dynamic_slice_in_dim(values, q * width, width, values.ndim - 1)

    conv_local = jnp.concatenate([group(conv_full, gw), conv_full[:, inner:]], axis=1).astype(f32)
    offset_local = jnp.concatenate([group(offset_full, gw), offset_full[inner:]]).astype(f32)
    bias_local = group(bias_full, gh).astype(f32)
    decay_local = group(decay_full, gh).astype(f32)
    skip_local = group(skip_full, gh).astype(f32)

    per_head = gw // gh
    taps_in = jnp.concatenate(
        [conv_local, offset_local[None], jnp.zeros((8 - taps - 1, gw + keys_w), f32)], axis=0
    )
    decay_rate = -jnp.exp(decay_local)
    head_in = jnp.pad(jnp.stack([bias_local, decay_rate]), ((0, 6), (0, 128 - gh)))
    skip_in = jnp.broadcast_to(jnp.repeat(skip_local, per_head)[None], (8, gw))
    mixed, q_low, square_part, starts = scan_forward(proj, taps_in, head_in, skip_in)

    cot_all = lax.all_gather(after(cot_low, w_all), "seq", axis=0, tiled=True)
    w_out, cot_all = lax.optimization_barrier((w_out, cot_all))
    out_part = times(q_low, w_out).astype(bf)
    out_sum = lax.psum_scatter(out_part, "seq", scatter_dimension=0, tiled=True)
    square = lax.psum(square_part.reshape(sq, toks), "seq")
    q_r = lax.rsqrt(square / inner + epsilon).reshape(seq_rows, 1)
    d_raw = expert_early(cot_rows, expert_down)
    tok_r = after(lax.dynamic_slice_in_dim(q_r, q * toks, toks, 0), d_raw)
    x_tok = x_low.astype(f32)
    added = out_sum.astype(f32) * tok_r
    resid = x_tok + added

    resid_r = row_scale(resid)
    resid_n = resid * resid_r
    moe_in = (resid_n * moe_gain_full[None, :]).astype(bf)
    moe_all = lax.all_gather(moe_in, "seq", axis=0, tiled=True)

    logits = times(moe_in, w_all[:, total - 128 :])
    top = jnp.max(jnp.where(named_lanes > 0.0, logits, -1e30), axis=1, keepdims=True)
    powers = jnp.where(
        named_lanes > 0.0, jnp.exp(jnp.where(named_lanes > 0.0, logits - top, 0.0)), 0.0
    )
    gates = (powers / jnp.sum(powers, axis=1, keepdims=True))[
        :, router_lane : router_lane + experts
    ]
    rows = dispatched(moe_in)
    own_ids = lax.axis_index("shard") * local_e + jnp.arange(local_e, dtype=jnp.int32)
    marks = jnp.stack(
        [own_ids + router_lane, own_ids, own_ids + 64] + [jnp.full_like(own_ids, -1)] * 5, axis=1
    )
    marks = (marks[:, :, None] == lanes[None, None, :]).astype(f32)

    back_rows, e_act, e_scaled, d_g, d_v, both_part, s_act, d_both = expert_main(
        rows,
        cot_rows,
        d_raw,
        expert_gate,
        expert_up,
        w_all,
        marks,
        moe_all,
        cot_all,
        w_shared,
        w_down,
    )
    shared_both = lax.psum_scatter(both_part, "seq", scatter_dimension=0, tiled=True)
    d_moe_shared = shared_both[:, :dim]
    shared_sum = shared_both[:, dim:]
    d_returned = to_shards(back_rows.reshape(sh, local_e * CAP, dim + 128))
    e_out, e_grads = expert_late(rows, cot_rows, e_act, e_scaled, d_g, d_v, expert_down)
    d_returned, e_out = lax.optimization_barrier((d_returned, e_out))
    returned = to_shards(e_out.reshape(sh, local_e * CAP, dim))

    near = [(i, 2 * ((i // 2) ^ 1) + i % 2) for i in range(sq)]
    far = [(i, 2 * (sq // 2 - 1 - i // 2) + i % 2) for i in range(sq)]
    is_inner = ((z_at == 1) | (z_at == 2)).astype(jnp.int32)
    is_high = (z_at >= 2).astype(jnp.int32)
    e_mine = halve(e_grads.reshape(-1, e_grads.shape[2]), core, mates)
    cutoff = e_mine.shape[0] // 2

    d_flat = transposed_times(dispatch_flat, d_returned.reshape(slots, dim + 128))
    d_gates = d_flat[:, dim : dim + experts] + d_flat[:, dim + 64 : dim + 64 + experts]
    d_logits = gates * (d_gates - jnp.sum(gates * d_gates, axis=1, keepdims=True))
    d_moe = (
        d_flat[:, :dim]
        + d_moe_shared.astype(f32)
        + jnp.dot(d_logits, router_full.astype(f32).T, precision=highest)
    )
    grad_router = jnp.dot(moe_in.astype(f32).T, d_logits, precision=highest)
    grad_moe = jnp.sum(d_moe * resid_n, axis=0)
    d_scaled = d_moe * moe_gain_full[None, :]
    d_resid = (
        cot
        + d_scaled * resid_r
        - resid_n * (resid_r * jnp.mean(d_scaled * resid_n, axis=1, keepdims=True))
    )
    d_o = d_resid.astype(bf)
    kappa = jnp.sum(d_o.astype(f32) * added, axis=1) / inner
    kappa_high = kappa.astype(bf)
    kappa_low = (kappa - kappa_high.astype(f32)).astype(bf)
    d_o_ext = jnp.concatenate(
        [d_o, kappa_high[:, None], kappa_low[:, None], jnp.zeros((toks, 126), bf)], axis=1
    )
    d_o_all = lax.all_gather(d_o_ext, "seq", axis=0, tiled=True)
    kappa_all = jnp.sum(d_o_all[:, dim : dim + 2].astype(f32), axis=1, keepdims=True)

    d_gated = times_transposed(d_o_all, jnp.pad(w_out, ((0, 0), (0, 128))))
    grad_out_part = transposed_times(q_low, (q_r * d_o_all[:, :dim].astype(f32)).astype(bf))
    grad_down_part = transposed_times(s_act, cot_all)
    grad_shared_part = transposed_times(moe_all, d_both)

    mid_part = jnp.concatenate(
        [
            grad_shared_part,
            grad_router,
            grad_moe[:, None],
            jnp.zeros((dim, 128 - experts - 1), f32),
        ],
        axis=1,
    )
    lane_w = mid_part.shape[1]
    bands = dim // lane_w

    def to_bands(values):
        return jnp.concatenate(
            [values[:, :, band * lane_w : band * lane_w + lane_w] for band in range(bands)], axis=1
        )

    early_part = jnp.concatenate(
        [
            to_bands(grad_out_part.astype(bf).reshape(sh, own_out, dim)),
            to_bands(grad_down_part.astype(bf).reshape(sh, own_down, dim)),
            mid_part.astype(bf).reshape(sh, rows_w, lane_w),
        ],
        axis=1,
    )
    moved_early = to_shards(early_part)

    e_late = after(e_mine, d_o_all)
    e_one = halve(e_late[:cutoff], is_inner, near)
    e_two = halve(e_late[cutoff:], is_high, far)
    row_values = jnp.concatenate(
        [q_r, kappa_all, x_r, jnp.zeros((seq_rows, 5), f32)], axis=1
    )
    d_proj, d_taps, d_head, d_skip = scan_backward(
        proj, mixed, d_gated, row_values, starts, taps_in, head_in, skip_in, (returned, e_one, e_two)
    )
    grad_conv_local = d_taps[:taps]
    grad_offset_local = d_taps[taps]
    grad_bias_local = d_head[0, :gh]
    grad_decay_local = d_head[1, :gh] * decay_rate
    grad_skip_local = jnp.sum(d_skip[0].reshape(gh, per_head), axis=1)
    d_proj, moved_early = lax.optimization_barrier((d_proj, moved_early))
    back_part = times_transposed(d_proj, w_all).astype(bf)
    back_sum = lax.psum_scatter(back_part, "seq", scatter_dimension=0, tiled=True).astype(f32)
    weighted = (gates.T[:, None, :] * dispatch.astype(f32)).reshape(slots, toks)
    combined = transposed_times(weighted.astype(bf), returned.reshape(slots, dim))
    block_output = ((resid + shared_sum.astype(f32) + combined) * live[:, None]).astype(bf)[None]
    tok_x_r = row_scale(x_tok)
    x_n = x_tok * tok_x_r
    input_grad = (
        d_resid + back_sum - x_n * (tok_x_r * jnp.mean(back_sum * x_tok, axis=1, keepdims=True))
    )[None]

    grad_in_part = transposed_times(x_all, d_proj)

    def spread(local, count):
        wide = jnp.zeros(local.shape[:-1] + (count,), f32)
        return lax.dynamic_update_slice_in_dim(wide, local, q * local.shape[-1], local.ndim - 1)

    conv_rows = jnp.concatenate([grad_conv_local, grad_offset_local[None]], axis=0)
    conv_wide = jnp.concatenate([spread(conv_rows[:, :gw], inner), conv_rows[:, gw:]], axis=1)
    head_wide = spread(jnp.stack([grad_bias_local, grad_decay_local, grad_skip_local]), heads)
    small_part = jnp.concatenate(
        [
            conv_wide.reshape(taps + 1, sh, conv_own).transpose(1, 0, 2).reshape(sh, -1),
            head_wide.reshape(3, sh, head_own).transpose(1, 0, 2).reshape(sh, -1),
        ],
        axis=1,
    )
    small_count = small_part.shape[1]
    small_part = jnp.pad(
        small_part, ((0, 0), (0, rows_w * small_cols - small_count))
    ).reshape(sh, rows_w, small_cols)
    last_part = grad_in_part + jnp.pad(
        small_part.reshape(dim, small_cols), ((0, 0), (used, total - used - small_cols))
    )
    last_part = last_part.astype(bf)
    early_sum = jnp.sum(moved_early.astype(f32), axis=0).astype(bf)
    rows_sum = lax.ppermute(early_sum[: bands * own_rows], both_axes, backward_pairs)
    e_one, e_two = halve(e_one, is_high, far), halve(e_two, is_inner, near)
    e_one, e_two = after(e_one, last_part), after(e_two, last_part)
    e_one, e_two = double(e_one, is_high, far), double(e_two, is_inner, near)
    e_one, e_two = double(e_one, is_inner, near), double(e_two, is_high, far)
    moved_last = to_shards(last_part.reshape(sh, rows_w, total))
    last_sum = jnp.sum(moved_last.astype(f32), axis=0)
    last_sum = after(after(after(last_sum, e_one), e_two), back_sum).astype(bf)
    e_mine = jnp.concatenate([e_one, e_two], axis=0)
    e_other = lax.ppermute(e_mine, "seq", mates)
    grad_e_gate, grad_e_up, grad_e_down = unpack_expert_grads(e_mine, e_other, core)
    side = lax.all_gather(
        jnp.concatenate(
            [rows_sum, early_sum[bands * own_rows :]]
            + [last_sum[:, lane_w * i : lane_w * i + lane_w] for i in range(total // lane_w)],
            axis=0,
        ),
        "seq",
        axis=0,
    )
    gain_out = norm_gain.astype(f32)[:, None]
    (
        grad_in,
        tail_sums,
        grad_out,
        norm_sums,
        grad_down,
        grad_shared_gate,
        grad_shared_up,
        mid_sums,
    ) = assemble(side, in_weight, gain_col, out_weight, gain_out, own_out, own_down)
    grad_norm = norm_sums[:, 0]
    grad_router_weight = mid_sums[:, :experts]
    grad_moe_gain = mid_sums[:, experts]
    grad_mixer_gain = tail_sums[:, 0]
    lane_at = used - (total - 128)
    small_sum = tail_sums[:, lane_at : lane_at + small_cols].reshape(-1)
    at = taps * conv_own
    grad_conv = small_sum[:at].reshape(taps, conv_own)
    grad_offset = small_sum[at : at + conv_own]
    at = at + conv_own
    grad_bias = small_sum[at : at + head_own]
    grad_decay = small_sum[at + head_own : at + 2 * head_own]
    grad_skip = small_sum[at + 2 * head_own : at + 3 * head_own]
    return (
        block_output,
        input_grad,
        grad_mixer_gain,
        grad_in,
        grad_conv,
        grad_offset,
        grad_bias,
        grad_decay,
        grad_skip,
        grad_norm,
        grad_out,
        grad_moe_gain,
        grad_router_weight,
        grad_shared_gate,
        grad_shared_up,
        grad_down,
        grad_e_gate,
        grad_e_up,
        grad_e_down,
    )


def solution(mesh):
    placed = (
        P("shard", "seq", None),
        P("shard"),
        P("shard", "seq", None),
        P("shard", "seq", None),
        P("shard"),
        P("shard", None),
        P(None, "shard"),
        P("shard"),
        P("shard"),
        P("shard"),
        P("shard"),
        P("shard"),
        P("shard", None),
        P("shard"),
        P("shard", None),
        P("shard", None),
        P("shard", None),
        P("shard", None),
        P("shard", None, None),
        P("shard", None, None),
        P("shard", None, None),
    )
    return jax.shard_map(
        on_device,
        mesh=mesh,
        in_specs=placed,
        out_specs=(
            P("shard", "seq", None),
            P("shard", "seq", None),
            P("shard"),
            P("shard", None),
            P(None, "shard"),
            P("shard"),
            P("shard"),
            P("shard"),
            P("shard"),
            P("shard"),
            P("shard", None),
            P("shard"),
            P("shard", None),
            P("shard", None),
            P("shard", None),
            P("shard", None),
            P("shard", None, None),
            P("shard", None, None),
            P("shard", None, None),
        ),
        check_vma=False,
    )
```

```python
import functools

import jax
import jax.numpy as jnp
from jax import lax
from jax.experimental import pallas as pl
from jax.experimental.pallas import tpu as pltpu
from jax.sharding import PartitionSpec as P

CAP = 32


epsilon = 1e-05
highest = lax.Precision.HIGHEST
both_axes = ("seq", "shard")


def times(left, right):
    return jnp.dot(left, right, preferred_element_type=jnp.float32)


def times_transposed(left, right):
    return lax.dot_general(
        left, right, (((1,), (1,)), ((), ())), preferred_element_type=jnp.float32
    )


def transposed_times(left, right):
    return lax.dot_general(
        left, right, (((0,), (0,)), ((), ())), preferred_element_type=jnp.float32
    )


def after(value, other):
    corner = other[(0,) * (other.ndim - 1)][:1].astype(jnp.float32)
    return (value.astype(jnp.float32) + 0.0 * corner).astype(value.dtype)


def silu_slope(values):
    sigma = jax.nn.sigmoid(values)
    return sigma * (1.0 + values * (1.0 - sigma))


def row_scale(values):
    return lax.rsqrt(jnp.mean(values * values, axis=-1, keepdims=True) + epsilon)


CHUNK = 128
WIDE = 384
CONVW = 640
PAIRS = 3
HEADS_HERE = 6


def split_two(values):
    high = values.astype(jnp.bfloat16)
    return high, (values - high.astype(jnp.float32)).astype(jnp.bfloat16)


def ones_times(ones, values):
    high, low = split_two(values)
    return times(ones, high) + times(ones, low)


def times_ones(values, ones):
    high, low = split_two(values)
    return times(high, ones) + times(low, ones)


def transposed_times_ones(values, ones):
    high, low = split_two(values)
    return transposed_times(high, ones) + transposed_times(low, ones)


def grid_of(shape):
    rows = lax.broadcasted_iota(jnp.int32, shape, 0)
    columns = lax.broadcasted_iota(jnp.int32, shape, 1)
    return rows, columns


def mark(condition):
    return jnp.where(condition, 1.0, 0.0).astype(jnp.bfloat16)


def chunk_parts(proj, prev, has_prev, taps_ref, head_ref, pad_ref):
    f32, bf = jnp.float32, jnp.bfloat16
    feed = proj[:, WIDE : WIDE + CONVW].astype(bf).astype(f32)
    before = prev[:, WIDE : WIDE + CONVW].astype(bf).astype(f32)
    pad_ref[0:8, :] = jnp.where(has_prev, before, 0.0)
    pad_ref[8 : 8 + CHUNK, :] = feed
    conv = taps_ref[4:5, :]
    for tap in range(4):
        conv = conv + taps_ref[tap : tap + 1, :] * pad_ref[5 + tap : 5 + tap + CHUNK, :]
    sig = jax.nn.sigmoid(conv)
    act = conv * sig
    u = act[:, :WIDE]
    key = act[:, WIDE : WIDE + 128].astype(bf)
    query = act[:, WIDE + 128 :].astype(bf)
    step_low = proj[:, WIDE + CONVW :].astype(bf).astype(f32)
    pre = step_low + head_ref[0:1, :]
    rows, columns = grid_of((CHUNK, 128))
    here = columns < HEADS_HERE
    dt = jnp.where(here, jnp.maximum(pre, 0.0) + jnp.log1p(jnp.exp(-jnp.abs(pre))), 0.0)
    la = dt * head_ref[1:2, :]
    lower = mark(rows >= columns)
    cum = ones_times(lower, la)
    end = cum[CHUNK - 1 : CHUNK, :]
    wide_rows, wide_columns = grid_of((128, WIDE))
    widen = mark(wide_columns // 64 == wide_rows)
    dt_w = times_ones(dt, widen)
    e_w = times_ones(jnp.exp(cum), widen)
    w_w = times_ones(jnp.exp(end - cum), widen)
    full_rows, full_columns = grid_of((128, 2 * PAIRS * 128))
    la_full = times_ones(la, mark(full_columns // 128 == full_rows))
    scores = times_transposed(query, key)
    return dict(
        conv=conv, sig=sig, u=u, key=key, query=query, pre=pre, here=here, dt=dt, lower=lower,
        dt_w=dt_w, e_w=e_w, w_w=w_w, la_full=la_full, scores=scores, xs=u * dt_w,
    )


def pair_table(parts, pair):
    rows, columns = grid_of((CHUNK, 256))
    local = columns % 128
    steps = jnp.where(rows > local, parts["la_full"][:, 256 * pair : 256 * pair + 256], 0.0)
    gap = ones_times(parts["lower"], steps)
    causal = rows >= local
    decay = jnp.where(causal, jnp.exp(jnp.where(causal, gap, 0.0)), 0.0)
    scores = parts["scores"]
    return decay, decay * jnp.concatenate([scores, scores], axis=1)


def stack_heads(values, pair):
    both = values[:, 128 * pair : 128 * pair + 128]
    first = lax.broadcasted_iota(jnp.int32, both.shape, 1) < 64
    return jnp.concatenate(
        [jnp.where(first, both, 0.0), jnp.where(first, 0.0, both)], axis=0
    ).astype(jnp.bfloat16)


def scan_forward_kernel(
    proj_ref, prev_ref, taps_ref, head_ref, skip_ref, earlier_ref,
    mixed_ref, q_ref, square_ref, start_ref, state_ref, pad_ref,
):
    f32, bf = jnp.float32, jnp.bfloat16
    chunk = pl.program_id(0)

    @pl.when(chunk == 0)
    def _():
        state_ref[...] = jnp.zeros(state_ref.shape, f32)

    parts = chunk_parts(
        proj_ref[...], prev_ref[...], chunk > 0, taps_ref, head_ref, pad_ref
    )
    state = state_ref[...]
    start_ref[0] = state
    xs = parts["xs"]
    inside = []
    for pair in range(PAIRS):
        _, table = pair_table(parts, pair)
        inside.append(times(table.astype(bf), stack_heads(xs, pair)))
    across = times(parts["query"], state.astype(bf))
    y = (
        jnp.concatenate(inside, axis=1)
        + parts["e_w"] * across
        + skip_ref[0:1, :] * parts["u"]
    )
    mixed = y.astype(bf)
    mixed_ref[...] = mixed
    gate = proj_ref[:, :WIDE]
    q_val = mixed.astype(f32) * (gate * jax.nn.sigmoid(gate))
    q_ref[...] = q_val.astype(bf)
    square_ref[...] = jnp.sum(q_val * q_val, axis=1, keepdims=True)
    state_ref[...] = state * parts["e_w"][CHUNK - 1 : CHUNK, :] + transposed_times(
        parts["key"], (xs * parts["w_w"]).astype(bf)
    )


def scan_backward_kernel(
    chunks, proj_ref, prev_ref, mixed_ref, d_gated_ref, rows_ref, start_ref, taps_ref, head_ref,
    skip_ref, held_ref, carry_in_ref, sums_in_ref, earlier_0, earlier_1,
    d_proj_ref, carry_ref, sums_ref,
    state_ref, pad_ref, late_ref,
):
    f32, bf = jnp.float32, jnp.bfloat16
    step = pl.program_id(0)
    chunk = chunks[1] - 1 - step
    d_taps_ref = sums_ref.at[0:8, :]
    d_head_ref = sums_ref.at[8:16, 0:128]
    d_skip_ref = sums_ref.at[16:24, 0:WIDE]

    @pl.when(step == 0)
    def _():
        state_ref[...] = carry_in_ref[0:128, 0:WIDE]
        late_ref[CHUNK : CHUNK + 8, :] = carry_in_ref[128:136, :]
        sums_ref[...] = sums_in_ref[...]

    parts = chunk_parts(
        proj_ref[...], prev_ref[...], chunk > 0, taps_ref, head_ref, pad_ref
    )
    u, key, query, xs = parts["u"], parts["key"], parts["query"], parts["xs"]
    e_w, w_w, dt_w = parts["e_w"], parts["w_w"], parts["dt_w"]

    gate = proj_ref[:, :WIDE]
    gate_sig = jax.nn.sigmoid(gate)
    gate_act = gate * gate_sig
    mixed = mixed_ref[...].astype(f32)
    q_val = mixed * gate_act
    q_r = rows_ref[:, 0:1]
    d_q = q_r * d_gated_ref[...] - q_val * (q_r * q_r * rows_ref[:, 1:2])
    d_gate = d_q * mixed * (gate_sig * (1.0 + gate * (1.0 - gate_sig)))
    d_y = (d_q * gate_act).astype(bf).astype(f32)

    start = start_ref[0]
    start_low = start.astype(bf)
    d_end = state_ref[...]
    d_end_low = d_end.astype(bf)
    xw = xs * w_w
    ye = d_y * e_w
    ye_low = ye.astype(bf)
    across = times(query, start_low)
    pulled = times(key, d_end_low)
    d_query = times_transposed(ye_low, start_low)
    d_key = times_transposed(xw.astype(bf), d_end_low)
    state_ref[...] = d_end * e_w[CHUNK - 1 : CHUNK, :] + transposed_times(query, ye_low)
    d_scores = jnp.zeros((CHUNK, 128), f32)
    turns = jnp.zeros((CHUNK, 128), f32)
    d_xs = []
    for pair in range(PAIRS):
        decay, table = pair_table(parts, pair)
        xs_two = stack_heads(xs, pair)
        dy_two = stack_heads(d_y, pair)
        d_table = times_transposed(d_y[:, 128 * pair : 128 * pair + 128].astype(bf), xs_two)
        d_decay = d_table * decay
        d_scores = d_scores + d_decay[:, :128] + d_decay[:, 128:]
        d_gap = d_table * table
        table_low = table.astype(bf)
        d_xs.append(
            transposed_times(
                jnp.concatenate([table_low[:, :128], table_low[:, 128:]], axis=0), dy_two
            )
        )
        two_rows, two_columns = grid_of((256, 128))
        own = mark(two_columns == 2 * pair + two_rows // 128)
        turns = turns + times_ones(d_gap, own)
        turns = turns - transposed_times_ones(
            jnp.concatenate([d_gap[:, :128], d_gap[:, 128:]], axis=0), own
        )
    d_xs = jnp.concatenate(d_xs, axis=1) + w_w * pulled
    d_scores_low = d_scores.astype(bf)
    d_query = d_query + times(d_scores_low, key)
    d_key = d_key + transposed_times(d_scores_low, query)

    rows, columns = grid_of((CHUNK, 128))
    upper = mark(columns >= rows)
    strict = mark(columns < rows)
    sum_rows, sum_columns = grid_of((WIDE, 128))
    per_head = mark(sum_rows // 64 == sum_columns)
    end_row = jnp.sum(d_end * start, axis=0, keepdims=True) * e_w[CHUNK - 1 : CHUNK, :]
    wide = ones_times(upper, ye * across) + ones_times(strict, xw * pulled) + end_row
    d_la = ones_times(upper, turns) + times_ones(wide, per_head)
    d_dt = times_ones(d_xs * u, per_head) + d_la * head_ref[1:2, :]
    d_pre = jnp.where(parts["here"], d_dt * jax.nn.sigmoid(parts["pre"]), 0.0)
    d_head_ref[0:1, :] += jnp.sum(d_pre, axis=0, keepdims=True)
    d_head_ref[1:2, :] += jnp.sum(d_la * parts["dt"], axis=0, keepdims=True)
    d_skip_ref[0:1, :] += jnp.sum(d_y * u, axis=0, keepdims=True)

    d_u = d_xs * dt_w + skip_ref[0:1, :] * d_y
    conv, sig = parts["conv"], parts["sig"]
    d_conv = jnp.concatenate([d_u, d_key, d_query], axis=1) * (sig * (1.0 + conv * (1.0 - sig)))
    late_ref[0:CHUNK, :] = d_conv
    d_feed = jnp.zeros((CHUNK, CONVW), f32)
    for tap in range(4):
        d_feed = d_feed + taps_ref[tap : tap + 1, :] * late_ref[3 - tap : 3 - tap + CHUNK, :]
        d_taps_ref[tap : tap + 1, :] += jnp.sum(
            d_conv * pad_ref[5 + tap : 5 + tap + CHUNK, :], axis=0, keepdims=True
        )
    d_taps_ref[4:5, :] += jnp.sum(d_conv, axis=0, keepdims=True)
    late_ref[CHUNK : CHUNK + 8, :] = d_conv[0:8, :]
    carry_ref[0:128, 0:WIDE] = state_ref[...]
    carry_ref[128:136, :] = d_conv[0:8, :]
    scale = rows_ref[:, 2:3]
    d_proj_ref[:, :WIDE] = (d_gate * scale).astype(bf)
    d_proj_ref[:, WIDE : WIDE + CONVW] = (d_feed * scale).astype(bf)
    d_proj_ref[:, WIDE + CONVW :] = (d_pre * scale).astype(bf)


def corner_of(array):
    return pl.BlockSpec(
        (1,) * (array.ndim - 2) + (16, 128), lambda *step: (0,) * array.ndim
    )


def whole(shape):
    return pl.BlockSpec(shape, lambda step: (0,) * len(shape))


def scan_forward(proj, taps, head, skip, earlier):
    rows, width = proj.shape
    chunks = rows // CHUNK
    by_chunk = lambda step: (step, 0)
    return pl.pallas_call(
        scan_forward_kernel,
        grid=(chunks,),
        in_specs=[
            pl.BlockSpec((CHUNK, width), by_chunk),
            pl.BlockSpec((8, width), lambda step: (jnp.maximum(step * (CHUNK // 8) - 1, 0), 0)),
            whole(taps.shape),
            whole(head.shape),
            whole(skip.shape),
            corner_of(earlier),
        ],
        out_specs=[
            pl.BlockSpec((CHUNK, WIDE), by_chunk),
            pl.BlockSpec((CHUNK, WIDE), by_chunk),
            pl.BlockSpec((CHUNK, 1), by_chunk),
            pl.BlockSpec((1, 128, WIDE), lambda step: (step, 0, 0)),
        ],
        out_shape=[
            jax.ShapeDtypeStruct((rows, WIDE), jnp.bfloat16),
            jax.ShapeDtypeStruct((rows, WIDE), jnp.bfloat16),
            jax.ShapeDtypeStruct((rows, 1), jnp.float32),
            jax.ShapeDtypeStruct((chunks, 128, WIDE), jnp.float32),
        ],
        scratch_shapes=[
            pltpu.VMEM((128, WIDE), jnp.float32),
            pltpu.VMEM((CHUNK + 8, CONVW), jnp.float32),
        ],
        compiler_params=pltpu.CompilerParams(vmem_limit_bytes=32 << 20),
        cost_estimate=pl.CostEstimate(
            flops=3 << 30, bytes_accessed=12 << 20, transcendentals=4 << 20
        ),
        name="scan_forward",
    )(proj, proj, taps, head, skip, earlier)


def scan_backward(chunks, inputs, held, carry, sums, earlier):
    proj, mixed, d_gated, row_values, starts, taps, head, skip = inputs
    width = proj.shape[1]
    at = lambda step: chunks[1] - 1 - step
    by_chunk = lambda step: (at(step), 0)
    return pl.pallas_call(
        functools.partial(scan_backward_kernel, chunks),
        grid=(chunks[1] - chunks[0],),
        in_specs=[
            pl.BlockSpec((CHUNK, width), by_chunk),
            pl.BlockSpec(
                (8, width), lambda step: (jnp.maximum(at(step) * (CHUNK // 8) - 1, 0), 0)
            ),
            pl.BlockSpec((CHUNK, WIDE), by_chunk),
            pl.BlockSpec((CHUNK, WIDE), by_chunk),
            pl.BlockSpec((CHUNK, row_values.shape[1]), by_chunk),
            pl.BlockSpec((1, 128, WIDE), lambda step: (at(step), 0, 0)),
            whole(taps.shape),
            whole(head.shape),
            whole(skip.shape),
            pl.BlockSpec(memory_space=pl.ANY),
            whole(carry.shape),
            whole(sums.shape),
            *map(corner_of, earlier),
        ],
        out_specs=[
            pl.BlockSpec((CHUNK, width), by_chunk),
            whole(carry.shape),
            whole(sums.shape),
        ],
        out_shape=[
            jax.ShapeDtypeStruct(held.shape, held.dtype),
            jax.ShapeDtypeStruct(carry.shape, jnp.float32),
            jax.ShapeDtypeStruct(sums.shape, jnp.float32),
        ],
        scratch_shapes=[
            pltpu.VMEM((128, WIDE), jnp.float32),
            pltpu.VMEM((CHUNK + 8, CONVW), jnp.float32),
            pltpu.VMEM((CHUNK + 8, CONVW), jnp.float32),
        ],
        input_output_aliases={9: 0},
        compiler_params=pltpu.CompilerParams(vmem_limit_bytes=48 << 20),
        cost_estimate=pl.CostEstimate(
            flops=10 << 30, bytes_accessed=20 << 20, transcendentals=8 << 20
        ),
        name="scan_backward",
    )(proj, proj, mixed, d_gated, row_values, starts, taps, head, skip, held, carry, sums, *earlier)


def expert_early_kernel(cot_ref, down_ref, raw_ref):
    cot = cot_ref[...].reshape(-1, cot_ref.shape[-1])
    raw_ref[0] = times_transposed(cot, down_ref[0])


def expert_main_kernel(
    rows_ref, routed_ref, raw_ref, gate_ref, up_ref, router_ref, marks_ref,
    moe_ref, cot_ref, shared_ref, down_ref,
    back_ref, act_ref, scaled_ref, d_g_ref, d_v_ref, both_ref, s_act_ref, d_both_ref,
):
    f32, bf = jnp.float32, jnp.bfloat16
    dim = rows_ref.shape[-1]
    rows = rows_ref[...].reshape(-1, dim)
    routed = routed_ref[...].reshape(-1, 128).astype(f32) > 0.0
    logits = times(rows, router_ref[...])
    top = jnp.max(jnp.where(routed, logits, -1e30), axis=1, keepdims=True)
    powers = jnp.where(routed, jnp.exp(jnp.where(routed, logits - top, 0.0)), 0.0)
    own = jnp.sum(powers * marks_ref[0, 0:1, :], axis=1, keepdims=True)
    gate = own / jnp.maximum(jnp.sum(powers, axis=1, keepdims=True), 1e-30)
    g = times(rows, gate_ref[0])
    v = times(rows, up_ref[0])
    sig = jax.nn.sigmoid(g)
    silu = g * sig
    act = (silu * v).astype(bf)
    act_wide = act.astype(f32)
    raw = raw_ref[0]
    d_gate = jnp.sum(act_wide * raw, axis=1, keepdims=True)
    d_act = gate * raw
    d_g = (d_act * v * (sig * (1.0 + g * (1.0 - sig)))).astype(bf)
    d_v = (d_act * silu).astype(bf)
    d_row = times_transposed(d_g, gate_ref[0]) + times_transposed(d_v, up_ref[0])
    high = d_gate.astype(bf).astype(f32)
    scalars = high * marks_ref[0, 1:2, :] + (d_gate - high) * marks_ref[0, 2:3, :]
    lead = back_ref.shape[:-1]
    back_ref[:, :, :, :dim] = d_row.astype(bf).reshape(*lead, dim)
    back_ref[:, :, :, dim:] = scalars.astype(bf).reshape(*lead, 128)
    act_ref[0] = act
    scaled_ref[0] = (gate * act_wide).astype(bf)
    d_g_ref[0] = d_g
    d_v_ref[0] = d_v

    units = down_ref.shape[0]
    s_both = times(moe_ref[...], shared_ref[...])
    s_gate, s_up = s_both[:, :units], s_both[:, units:]
    s_sig = jax.nn.sigmoid(s_gate)
    s_silu = s_gate * s_sig
    s_act = (s_silu * s_up).astype(bf)
    d_sh = times_transposed(cot_ref[...], down_ref[...])
    d_gs = (d_sh * s_up * (s_sig * (1.0 + s_gate * (1.0 - s_sig)))).astype(bf)
    d_both = jnp.concatenate([d_gs, (d_sh * s_silu).astype(bf)], axis=1)
    both_ref[:, :dim] = times_transposed(d_both, shared_ref[...]).astype(bf)
    both_ref[:, dim:] = times(s_act, down_ref[...]).astype(bf)
    s_act_ref[...] = s_act
    d_both_ref[...] = d_both


def expert_late_kernel(
    rows_ref, cot_ref, act_ref, scaled_ref, d_g_ref, d_v_ref, down_ref,
    out_ref, grads_ref,
):
    bf = jnp.bfloat16
    dim = rows_ref.shape[-1]
    rows = rows_ref[...].reshape(-1, dim)
    cot = cot_ref[...].reshape(-1, dim)
    out_ref[...] = times(act_ref[0], down_ref[0]).astype(bf).reshape(out_ref.shape)
    units = act_ref.shape[-1]
    grads_ref[0, :dim] = transposed_times(rows, d_g_ref[0]).astype(bf)
    grads_ref[0, dim : 2 * dim] = transposed_times(rows, d_v_ref[0]).astype(bf)
    for block in range(dim // units):
        at = 2 * dim + block * units
        grads_ref[0, at : at + units] = transposed_times(
            scaled_ref[0], cot[:, block * units : block * units + units]
        ).astype(bf)


def expert_slots(shape, start=0):
    return pl.BlockSpec(
        (shape[0], 1) + tuple(shape[2:]), lambda e: (0, e) + (0,) * (len(shape) - 3) + (start,)
    )


def per_expert(shape):
    return pl.BlockSpec((1,) + tuple(shape[1:]), lambda e: (e,) + (0,) * (len(shape) - 1))


def expert_params(flops, moved):
    return dict(
        compiler_params=pltpu.CompilerParams(vmem_limit_bytes=56 << 20),
        cost_estimate=pl.CostEstimate(flops=flops, bytes_accessed=moved, transcendentals=1 << 19),
    )


def expert_early(cot_rows, down):
    sources, local, cap, _ = cot_rows.shape
    units, dim = down.shape[1:]
    return pl.pallas_call(
        expert_early_kernel,
        grid=(local,),
        in_specs=[expert_slots((sources, local, cap, dim)), per_expert(down.shape)],
        out_specs=per_expert((local, sources * cap, units)),
        out_shape=jax.ShapeDtypeStruct((local, sources * cap, units), jnp.float32),
        name="expert_early",
        **expert_params(2 << 30, 8 << 20),
    )(cot_rows, down)


def expert_main(rows, cot_rows, raw, gate, up, w_all, marks, moe_all, cot_all, w_shared, w_down):
    sources, local, cap, dim = rows.shape
    units = gate.shape[2]
    count = sources * cap
    hidden = jax.ShapeDtypeStruct((local, count, units), jnp.bfloat16)
    back = (sources, local, cap, dim + 128)
    seq_rows = moe_all.shape[0]
    shared_units = w_down.shape[0]
    share = lambda width: pl.BlockSpec((seq_rows // local, width), lambda e: (e, 0))
    return pl.pallas_call(
        expert_main_kernel,
        grid=(local,),
        in_specs=[
            expert_slots(rows.shape),
            expert_slots((sources, local, cap, 128), dim // 128),
            per_expert(raw.shape),
            per_expert(gate.shape),
            per_expert(up.shape),
            pl.BlockSpec((dim, 128), lambda e: (0, w_all.shape[1] // 128 - 1)),
            per_expert(marks.shape),
            share(dim),
            share(dim),
            whole(w_shared.shape),
            whole(w_down.shape),
        ],
        out_specs=[expert_slots(back)]
        + [per_expert(hidden.shape)] * 4
        + [share(2 * dim), share(shared_units), share(2 * shared_units)],
        out_shape=[jax.ShapeDtypeStruct(back, jnp.bfloat16)]
        + [hidden] * 4
        + [
            jax.ShapeDtypeStruct((seq_rows, width), jnp.bfloat16)
            for width in (2 * dim, shared_units, 2 * shared_units)
        ],
        name="expert_main",
        **expert_params(8 << 30, 20 << 20),
    )(rows, cot_rows, raw, gate, up, w_all, marks, moe_all, cot_all, w_shared, w_down)


def expert_late(rows, cot_rows, act, scaled, d_g, d_v, down):
    sources, local, cap, dim = rows.shape
    units = down.shape[1]
    grads = (local, 3 * dim, units)
    return pl.pallas_call(
        expert_late_kernel,
        grid=(local,),
        in_specs=[expert_slots(rows.shape), expert_slots(rows.shape)]
        + [per_expert(act.shape)] * 4
        + [per_expert(down.shape)],
        out_specs=[
            expert_slots(rows.shape),
            per_expert(grads),
        ],
        out_shape=[
            jax.ShapeDtypeStruct(rows.shape, jnp.bfloat16),
            jax.ShapeDtypeStruct(grads, jnp.bfloat16),
        ],
        name="expert_late",
        **expert_params(7 << 30, 24 << 20),
    )(rows, cot_rows, act, scaled, d_g, d_v, down)


def assemble_kernel(
    own_out, own_down, side_ref, in_ref, in_gain_ref, out_ref, out_gain_ref,
    grad_in_ref, tail_ref, grad_out_ref, norm_ref, grad_down_ref, gate_ref, up_ref, mid_ref,
):
    f32 = jnp.float32
    groups = side_ref.shape[0]
    inner = groups * WIDE
    bands = out_ref.shape[1] // WIDE
    rows_w = in_ref.shape[0]
    gain = in_gain_ref[...]
    at_down = bands * own_out
    at_mid = at_down + bands * own_down
    at_in = at_mid + rows_w
    units = gate_ref.shape[1] // groups

    def block(group, start, rows):
        return side_ref[group, start : start + rows, :].astype(f32)

    grad_gain = jnp.zeros((rows_w, 1), f32)
    keys = jnp.zeros((rows_w, 256), f32)
    tail = jnp.zeros((rows_w, 128), f32)
    steps = jnp.zeros((rows_w, 128), f32)
    mid = jnp.zeros((rows_w, 128), f32)
    rows, columns = grid_of((128, 128))

    def put(start, values):
        stop = start + values.shape[1]
        grad_in_ref[:, start:stop] = values * gain
        weight = in_ref[:, start:stop].astype(f32)
        return jnp.sum(weight * values, axis=1, keepdims=True)

    for group in range(groups):
        grad_gain += put(group * WIDE, block(group, at_in, rows_w))
        grad_gain += put(inner + group * WIDE, block(group, at_in + rows_w, rows_w))
        last = block(group, at_in + 2 * rows_w, rows_w)
        keys = keys + last[:, :256]
        tail = tail + last[:, 256:]
        moved = mark((rows < HEADS_HERE) & (columns == rows + HEADS_HERE * group))
        steps = steps + times(last[:, 256:].astype(jnp.bfloat16), moved)
        shared = block(group, at_mid, rows_w)
        gate_ref[:, units * group : units * group + units] = shared[:, :units]
        up_ref[:, units * group : units * group + units] = shared[:, units : 2 * units]
        mid = mid + shared[:, 2 * units :]
    grad_gain += put(2 * inner, keys)
    grad_gain += put(2 * inner + 256, steps[:, : groups * HEADS_HERE])
    lane = lax.broadcasted_iota(jnp.int32, tail.shape, 1)
    tail_ref[...] = jnp.where(lane == 0, grad_gain, tail)
    mid_ref[...] = mid

    for group in range(groups):
        sums = jnp.zeros((own_out, 1), f32)
        mine = slice(own_out * group, own_out * group + own_out)
        for band in range(bands):
            wide = slice(WIDE * band, WIDE * band + WIDE)
            values = block(group, own_out * band, own_out)
            grad_out_ref[mine, wide] = values * out_gain_ref[mine, :]
            sums += jnp.sum(out_ref[mine, wide].astype(f32) * values, axis=1, keepdims=True)
            grad_down_ref[own_down * group : own_down * group + own_down, wide] = block(
                group, at_down + own_down * band, own_down
            )
        norm_ref[mine, :] = sums


def assemble(side, in_weight, in_gain, out_weight, out_gain, own_out, own_down):
    groups = side.shape[0]
    rows, width = in_weight.shape
    out_rows, dim = out_weight.shape
    shapes = [
        (rows, width),
        (rows, 128),
        (out_rows, dim),
        (out_rows, 1),
        (groups * own_down, dim),
        (rows, groups * 128),
        (rows, groups * 128),
        (rows, 128),
    ]
    return pl.pallas_call(
        functools.partial(assemble_kernel, own_out, own_down),
        in_specs=[pl.BlockSpec(memory_space=pltpu.VMEM)] * 5,
        out_specs=[pl.BlockSpec(memory_space=pltpu.VMEM)] * len(shapes),
        out_shape=[jax.ShapeDtypeStruct(shape, jnp.float32) for shape in shapes],
        compiler_params=pltpu.CompilerParams(vmem_limit_bytes=40 << 20),
        cost_estimate=pl.CostEstimate(flops=8 << 20, bytes_accessed=12 << 20, transcendentals=0),
        name="assemble",
    )(side, in_weight, in_gain, out_weight, out_gain)


def gather_rows(values, core, z_at, mates):
    cores = 2
    chips = len(mates) // cores
    column = [values]
    for hop in range(1, chips):
        pairs = [
            (i, (i // cores + hop) % chips * cores + i % cores) for i in range(len(mates))
        ]
        column.append(lax.ppermute(values, "seq", pairs))
    column = jnp.stack(column)
    both = jnp.stack([column, lax.ppermute(column, "seq", mates)], axis=1)
    both = both.reshape((len(mates),) + values.shape)
    ordered = [
        lax.dynamic_index_in_dim(both, (z_at - z) % chips * cores + (c ^ core), 0, keepdims=False)
        for z in range(chips)
        for c in range(cores)
    ]
    return jnp.concatenate(ordered, axis=0)


def halve(values, bit, pairs):
    f32 = jnp.float32
    parts = values.reshape(2, values.shape[0] // 2, values.shape[1])
    sent = lax.dynamic_index_in_dim(parts, 1 - bit, 0, keepdims=False)
    kept = lax.dynamic_index_in_dim(parts, bit, 0, keepdims=False)
    other = lax.ppermute(sent, "seq", pairs)
    return (kept.astype(f32) + other.astype(f32)).astype(jnp.bfloat16)


def double(values, bit, pairs):
    other = lax.ppermute(values, "seq", pairs)
    first = jnp.where(bit == 0, values, other)
    second = jnp.where(bit == 0, other, values)
    return jnp.concatenate([first, second], axis=0)


def unpack_kernel(core_ref, own_ref, other_ref, gate_ref, up_ref, down_ref):
    part = pl.program_id(1)
    block = jnp.where(pl.program_id(0) == 0, own_ref[...], other_ref[...]).astype(jnp.float32)
    units = block.shape[1]

    @pl.when(part == 0)
    def _():
        gate_ref[0] = block

    @pl.when(part == 1)
    def _():
        up_ref[0] = block

    @pl.when(part == 2)
    def _():
        for at in range(0, block.shape[0], units):
            down_ref[0, :, at : at + units] = block[at : at + units]


def unpack_expert_grads(own, other, core):
    rows, units = own.shape
    dim = rows // 3
    to_expert = lambda who, part, core: (jnp.where(who == 0, core[0], 1 - core[0]), 0, 0)
    return pl.pallas_call(
        unpack_kernel,
        grid_spec=pltpu.PrefetchScalarGridSpec(
            num_scalar_prefetch=1,
            grid=(2, 3),
            in_specs=[
                pl.BlockSpec((dim, units), lambda who, part, core: (jnp.where(who == 0, part, 2), 0)),
                pl.BlockSpec((dim, units), lambda who, part, core: (jnp.where(who == 0, 0, part), 0)),
            ],
            out_specs=[
                pl.BlockSpec((1, dim, units), to_expert),
                pl.BlockSpec((1, dim, units), to_expert),
                pl.BlockSpec((1, units, dim), to_expert),
            ],
        ),
        out_shape=[
            jax.ShapeDtypeStruct((2, dim, units), jnp.float32),
            jax.ShapeDtypeStruct((2, dim, units), jnp.float32),
            jax.ShapeDtypeStruct((2, units, dim), jnp.float32),
        ],
        compiler_params=pltpu.CompilerParams(vmem_limit_bytes=40 << 20),
        cost_estimate=pl.CostEstimate(flops=1 << 20, bytes_accessed=28 << 20, transcendentals=0),
        name="unpack_expert_grads",
    )(core.reshape(1), own, other)


def on_device(
    block_input,
    lengths,
    routes,
    out_cotangent,
    mixer_gain,
    in_weight,
    conv_weight,
    conv_bias,
    step_bias,
    decay_log,
    skip_gain,
    norm_gain,
    out_weight,
    moe_gain,
    router_weight,
    shared_gate,
    shared_up,
    shared_down,
    expert_gate,
    expert_up,
    expert_down,
):
    sq = lax.axis_size("seq")
    sh = lax.axis_size("shard")
    q = lax.axis_index("seq")
    f32 = jnp.float32
    bf = jnp.bfloat16
    x_low = block_input[0]
    toks, dim = x_low.shape
    seq_rows = toks * sq
    heads = step_bias.shape[0] * sh
    inner = norm_gain.shape[0] * sh
    conv_all = conv_bias.shape[0] * sh
    keys_w = conv_all - inner
    gh = heads // sq
    gw = inner // sq
    rows_w = in_weight.shape[0]
    experts = router_weight.shape[1]
    local_e = expert_gate.shape[0]
    fs = shared_gate.shape[1]
    gf = fs // sq
    taps = conv_weight.shape[0]
    conv_own = conv_bias.shape[0]
    head_own = step_bias.shape[0]

    gain_col = mixer_gain.astype(f32)[:, None]

    def cols(start, width):
        return lax.dynamic_slice_in_dim(in_weight, start, width, 1)

    w_cols = jnp.concatenate(
        [
            cols(q * gw, gw),
            cols(inner + q * gw, gw),
            in_weight[:, 2 * inner : 2 * inner + keys_w],
            cols(2 * inner + keys_w + q * gh, gh),
        ],
        axis=1,
    )
    w_cols = (w_cols.astype(f32) * gain_col).astype(bf)
    used = 2 * gw + keys_w + gh
    small = jnp.concatenate(
        [conv_weight.reshape(-1), conv_bias, step_bias, decay_log, skip_gain]
    )
    small_cols = -(-small.shape[0] // rows_w)
    small = jnp.pad(small, (0, small_cols * rows_w - small.shape[0])).reshape(rows_w, small_cols)
    packed = jnp.concatenate(
        [w_cols, small, router_weight, moe_gain[:, None]], axis=1
    )
    at_small = used
    at_router = at_small + small_cols
    at_moe = at_router + experts
    total = -(-(at_moe + 1) // 128) * 128
    packed = jnp.pad(packed, ((0, 0), (0, total - packed.shape[1])))

    def to_shards(values):
        return lax.all_to_all(values, "shard", split_axis=0, concat_axis=0, tiled=True)

    w_all = lax.all_gather(packed, "shard", axis=0, tiled=True)
    core, z_at = q % 2, q // 2
    mates = [(i, i ^ 1) for i in range(sq)]
    x_all = gather_rows(x_low, core, z_at, mates)

    out_scaled = (norm_gain.astype(f32)[:, None] * out_weight.astype(f32)).astype(bf)
    own_out = out_weight.shape[0] // sq
    own_down = shared_down.shape[0] // sq
    piece = jnp.concatenate(
        [
            lax.dynamic_slice_in_dim(out_scaled, q * own_out, own_out, 0),
            lax.dynamic_slice_in_dim(shared_down, q * own_down, own_down, 0),
        ],
        axis=0,
    )
    ratio = sh // sq
    forward_pairs = []
    for a in range(sh):
        for j in range(sq):
            s_to = sq * (a % ratio) + j
            q_to = a // ratio
            forward_pairs.append((j * sh + a, q_to * sh + s_to))
    backward_pairs = [(b, a) for a, b in forward_pairs]
    piece = lax.ppermute(piece, both_axes, forward_pairs)
    shared_cols = jnp.concatenate(
        [
            lax.dynamic_slice_in_dim(shared_gate, q * gf, gf, 1),
            lax.dynamic_slice_in_dim(shared_up, q * gf, gf, 1),
        ],
        axis=1,
    )
    fold = rows_w * 2 * gf // dim
    bands = dim // (2 * gf)
    shared_rows = jnp.concatenate(
        [shared_cols[fold * band : fold * band + fold] for band in range(bands)], axis=1
    )
    piece = jnp.concatenate([piece, shared_rows], axis=0)
    piece = after(piece, w_all)
    rows_all = to_shards(jnp.broadcast_to(piece[None], (sh,) + piece.shape))
    own_rows = own_out + own_down
    w_out = rows_all[:, :own_out].reshape(gw, dim)
    w_down = rows_all[:, own_out:own_rows].reshape(gf, dim)
    w_shared = (
        rows_all[:, own_rows:]
        .reshape(sh, fold, bands, 2 * gf)
        .transpose(0, 2, 1, 3)
        .reshape(dim, 2 * gf)
    )

    route_ids = routes[0]
    expert_ids = jnp.arange(experts, dtype=jnp.int32)
    named = jnp.any(route_ids[:, :, None] == expert_ids[None, None, :], axis=1).astype(f32)
    earlier = (
        jnp.arange(toks)[:, None] > jnp.arange(toks)[None, :]
    ).astype(f32)
    rank = jnp.dot(earlier, named)
    dispatch = (
        (named.T[:, None, :] > 0.0)
        & (rank.T[:, None, :] == jnp.arange(CAP, dtype=f32)[None, :, None])
    ).astype(bf)
    slots = experts * CAP
    dispatch_flat = dispatch.reshape(slots, toks)
    live = (q * toks + jnp.arange(toks, dtype=jnp.int32) < lengths[0]).astype(f32)
    cot = out_cotangent[0].astype(f32) * live[:, None]
    cot_low = cot.astype(bf)

    local_slots = (sh, local_e, CAP)

    def in_slots(values):
        return times(dispatch_flat, values).astype(bf).reshape(sh, local_e * CAP, -1)

    def dispatched(sent):
        return to_shards(sent).reshape(*local_slots, -1)

    router_lane = at_router - (total - 128)
    lanes = jnp.arange(128, dtype=jnp.int32)
    named_lanes = jnp.pad(named, ((0, 0), (router_lane, 128 - router_lane - experts)))
    cot_sent = in_slots(jnp.concatenate([cot_low, named_lanes.astype(bf)], axis=1))
    cot_rows = dispatched(cot_sent)

    x_wide = x_all.astype(f32)
    x_r = row_scale(x_wide)
    proj = times(x_all, w_all) * x_r

    small_all = w_all[:, at_small:at_router].reshape(sh, -1)
    at = taps * conv_own
    conv_full = (
        small_all[:, :at].reshape(sh, taps, conv_own).transpose(1, 0, 2).reshape(taps, conv_all)
    )
    offset_full = small_all[:, at : at + conv_own].reshape(conv_all)
    at = at + conv_own
    bias_full = small_all[:, at : at + head_own].reshape(heads)
    decay_full = small_all[:, at + head_own : at + 2 * head_own].reshape(heads)
    skip_full = small_all[:, at + 2 * head_own : at + 3 * head_own].reshape(heads)
    router_full = w_all[:, at_router:at_moe]
    moe_gain_full = w_all[:, at_moe].astype(f32)

    def group(values, width):
        return lax.dynamic_slice_in_dim(values, q * width, width, values.ndim - 1)

    conv_local = jnp.concatenate([group(conv_full, gw), conv_full[:, inner:]], axis=1).astype(f32)
    offset_local = jnp.concatenate([group(offset_full, gw), offset_full[inner:]]).astype(f32)
    bias_local = group(bias_full, gh).astype(f32)
    decay_local = group(decay_full, gh).astype(f32)
    skip_local = group(skip_full, gh).astype(f32)

    per_head = gw // gh
    taps_in = jnp.concatenate(
        [conv_local, offset_local[None], jnp.zeros((8 - taps - 1, gw + keys_w), f32)], axis=0
    )
    decay_rate = -jnp.exp(decay_local)
    head_in = jnp.pad(jnp.stack([bias_local, decay_rate]), ((0, 6), (0, 128 - gh)))
    skip_in = jnp.broadcast_to(jnp.repeat(skip_local, per_head)[None], (8, gw))
    mixed, q_low, square_part, starts = scan_forward(
        proj, taps_in, head_in, skip_in, cot_sent
    )

    cot_all = lax.all_gather(after(cot_low, w_all), "seq", axis=0, tiled=True)
    w_out, cot_all = lax.optimization_barrier((w_out, cot_all))
    out_part = times(q_low, w_out).astype(bf)
    out_sum = lax.psum_scatter(out_part, "seq", scatter_dimension=0, tiled=True)
    square = lax.psum(square_part.reshape(sq, toks), "seq")
    q_r = lax.rsqrt(square / inner + epsilon).reshape(seq_rows, 1)
    d_raw = expert_early(cot_rows, expert_down)
    tok_r = after(lax.dynamic_slice_in_dim(q_r, q * toks, toks, 0), cot_rows)
    x_tok = x_low.astype(f32)
    added = out_sum.astype(f32) * tok_r
    resid = x_tok + added

    resid_r = row_scale(resid)
    resid_n = resid * resid_r
    moe_in = (resid_n * moe_gain_full[None, :]).astype(bf)
    moe_all = lax.all_gather(moe_in, "seq", axis=0, tiled=True)

    logits = times(moe_in, w_all[:, total - 128 :])
    top = jnp.max(jnp.where(named_lanes > 0.0, logits, -1e30), axis=1, keepdims=True)
    powers = jnp.where(
        named_lanes > 0.0, jnp.exp(jnp.where(named_lanes > 0.0, logits - top, 0.0)), 0.0
    )
    gates = (powers / jnp.sum(powers, axis=1, keepdims=True))[
        :, router_lane : router_lane + experts
    ]
    rows = dispatched(in_slots(moe_in))
    own_ids = lax.axis_index("shard") * local_e + jnp.arange(local_e, dtype=jnp.int32)
    marks = jnp.stack(
        [own_ids + router_lane, own_ids, own_ids + 64] + [jnp.full_like(own_ids, -1)] * 5, axis=1
    )
    marks = (marks[:, :, None] == lanes[None, None, :]).astype(f32)

    back_rows, e_act, e_scaled, d_g, d_v, both_part, s_act, d_both = expert_main(
        rows,
        cot_rows,
        d_raw,
        expert_gate,
        expert_up,
        w_all,
        marks,
        moe_all,
        cot_all,
        w_shared,
        w_down,
    )
    shared_both = lax.psum_scatter(both_part, "seq", scatter_dimension=0, tiled=True)
    d_moe_shared = shared_both[:, :dim]
    shared_sum = shared_both[:, dim:]
    d_returned = to_shards(back_rows.reshape(sh, local_e * CAP, dim + 128))
    e_out, e_grads = expert_late(rows, cot_rows, e_act, e_scaled, d_g, d_v, expert_down)
    d_returned, e_out = lax.optimization_barrier((d_returned, e_out))
    returned = to_shards(e_out.reshape(sh, local_e * CAP, dim))

    near = [(i, 2 * ((i // 2) ^ 1) + i % 2) for i in range(sq)]
    far = [(i, 2 * (sq // 2 - 1 - i // 2) + i % 2) for i in range(sq)]
    is_inner = ((z_at == 1) | (z_at == 2)).astype(jnp.int32)
    is_high = (z_at >= 2).astype(jnp.int32)
    e_mine = jnp.concatenate(
        [
            halve(e_grads[:, dim * part : dim * part + dim].reshape(local_e * dim, -1), core, mates)
            for part in range(3)
        ],
        axis=0,
    )
    cutoff = e_mine.shape[0] // 2

    grad_down_part = transposed_times(s_act, cot_all).astype(bf)
    grad_shared_part = transposed_times(moe_all, d_both).astype(bf)
    gates = after(after(gates, grad_down_part), grad_shared_part)
    d_flat = transposed_times(dispatch_flat, d_returned.reshape(slots, dim + 128))
    d_gates = d_flat[:, dim : dim + experts] + d_flat[:, dim + 64 : dim + 64 + experts]
    d_logits = gates * (d_gates - jnp.sum(gates * d_gates, axis=1, keepdims=True))
    d_moe = (
        d_flat[:, :dim]
        + d_moe_shared.astype(f32)
        + jnp.dot(d_logits, router_full.astype(f32).T, precision=highest)
    )
    grad_router = jnp.dot(moe_in.astype(f32).T, d_logits, precision=highest)
    grad_moe = jnp.sum(d_moe * resid_n, axis=0)
    d_scaled = d_moe * moe_gain_full[None, :]
    d_resid = (
        cot
        + d_scaled * resid_r
        - resid_n * (resid_r * jnp.mean(d_scaled * resid_n, axis=1, keepdims=True))
    )
    d_o = d_resid.astype(bf)
    kappa = jnp.sum(d_o.astype(f32) * added, axis=1) / inner
    for start in range(0, e_mine.shape[0], dim):
        kappa = after(kappa, e_mine[start:])
    kappa_high = kappa.astype(bf)
    kappa_low = (kappa - kappa_high.astype(f32)).astype(bf)
    d_o_ext = jnp.concatenate(
        [d_o, kappa_high[:, None], kappa_low[:, None], jnp.zeros((toks, 126), bf)], axis=1
    )
    d_o_all = lax.all_gather(d_o_ext, "seq", axis=0, tiled=True)
    kappa_all = jnp.sum(d_o_all[:, dim : dim + 2].astype(f32), axis=1, keepdims=True)

    d_gated = times_transposed(d_o_all, jnp.pad(w_out, ((0, 0), (0, 128))))
    grad_out_part = transposed_times(q_low, (q_r * d_o_all[:, :dim].astype(f32)).astype(bf))

    mid_part = jnp.concatenate(
        [
            grad_shared_part,
            grad_router.astype(bf),
            grad_moe[:, None].astype(bf),
            jnp.zeros((dim, 128 - experts - 1), bf),
        ],
        axis=1,
    )
    lane_w = mid_part.shape[1]
    bands = dim // lane_w

    def to_bands(values):
        return jnp.concatenate(
            [values[:, :, band * lane_w : band * lane_w + lane_w] for band in range(bands)], axis=1
        )

    early_part = jnp.concatenate(
        [
            to_bands(grad_out_part.astype(bf).reshape(sh, own_out, dim)),
            to_bands(grad_down_part.reshape(sh, own_down, dim)),
            mid_part.reshape(sh, rows_w, lane_w),
        ],
        axis=1,
    )
    moved_early = to_shards(early_part)

    e_late = after(e_mine, d_o_all)
    e_one = halve(e_late[:cutoff], is_inner, near)
    e_two = halve(e_late[cutoff:], is_high, far)
    row_values = jnp.concatenate(
        [q_r, kappa_all, x_r, jnp.zeros((seq_rows, 5), f32)], axis=1
    )
    scan_inputs = (proj, mixed, d_gated, row_values, starts, taps_in, head_in, skip_in)
    chunks = seq_rows // CHUNK
    middle = chunks // 2
    d_proj, carry, sums = scan_backward(
        (middle, chunks),
        scan_inputs,
        jnp.zeros((seq_rows, total), bf),
        jnp.zeros((136, gw + keys_w), f32),
        jnp.zeros((24, gw + keys_w), f32),
        (returned, early_part),
    )
    d_proj, carry, sums = scan_backward(
        (0, middle), scan_inputs, d_proj, carry, sums, (e_one, e_two)
    )
    d_taps, d_head, d_skip = sums[0:8], sums[8:16, :128], sums[16:24, :gw]
    grad_conv_local = d_taps[:taps]
    grad_offset_local = d_taps[taps]
    grad_bias_local = d_head[0, :gh]
    grad_decay_local = d_head[1, :gh] * decay_rate
    grad_skip_local = jnp.sum(d_skip[0].reshape(gh, per_head), axis=1)
    e_one, e_two = halve(e_one, is_high, far), halve(e_two, is_inner, near)
    d_proj, moved_early = lax.optimization_barrier((d_proj, moved_early))
    back_part = times_transposed(d_proj, w_all).astype(bf)
    back_sum = lax.psum_scatter(back_part, "seq", scatter_dimension=0, tiled=True).astype(f32)
    weighted = (gates.T[:, None, :] * dispatch.astype(f32)).reshape(slots, toks)
    combined = transposed_times(weighted.astype(bf), returned.reshape(slots, dim))
    block_output = ((resid + shared_sum.astype(f32) + combined) * live[:, None]).astype(bf)[None]
    tok_x_r = row_scale(x_tok)
    x_n = x_tok * tok_x_r
    input_grad = (
        d_resid + back_sum - x_n * (tok_x_r * jnp.mean(back_sum * x_tok, axis=1, keepdims=True))
    )[None]

    grad_in_part = transposed_times(x_all, d_proj)

    def spread(local, count):
        wide = jnp.zeros(local.shape[:-1] + (count,), f32)
        return lax.dynamic_update_slice_in_dim(wide, local, q * local.shape[-1], local.ndim - 1)

    conv_rows = jnp.concatenate([grad_conv_local, grad_offset_local[None]], axis=0)
    conv_wide = jnp.concatenate([spread(conv_rows[:, :gw], inner), conv_rows[:, gw:]], axis=1)
    head_wide = spread(jnp.stack([grad_bias_local, grad_decay_local, grad_skip_local]), heads)
    small_part = jnp.concatenate(
        [
            conv_wide.reshape(taps + 1, sh, conv_own).transpose(1, 0, 2).reshape(sh, -1),
            head_wide.reshape(3, sh, head_own).transpose(1, 0, 2).reshape(sh, -1),
        ],
        axis=1,
    )
    small_count = small_part.shape[1]
    small_part = jnp.pad(
        small_part, ((0, 0), (0, rows_w * small_cols - small_count))
    ).reshape(sh, rows_w, small_cols)
    last_part = grad_in_part + jnp.pad(
        small_part.reshape(dim, small_cols), ((0, 0), (used, total - used - small_cols))
    )
    last_part = last_part.astype(bf)
    early_sum = jnp.sum(moved_early.astype(f32), axis=0).astype(bf)
    rows_sum = lax.ppermute(early_sum[: bands * own_rows], both_axes, backward_pairs)
    e_one, e_two = after(e_one, last_part), after(e_two, last_part)
    e_one, e_two = double(e_one, is_high, far), double(e_two, is_inner, near)
    e_one, e_two = double(e_one, is_inner, near), double(e_two, is_high, far)
    moved_last = to_shards(last_part.reshape(sh, rows_w, total))
    last_sum = jnp.sum(moved_last.astype(f32), axis=0)
    last_sum = after(after(after(last_sum, e_one), e_two), back_sum).astype(bf)
    e_mine = jnp.concatenate([e_one, e_two], axis=0)
    e_other = lax.ppermute(e_mine, "seq", mates)
    grad_e_gate, grad_e_up, grad_e_down = unpack_expert_grads(e_mine, e_other, core)
    side = lax.all_gather(
        jnp.concatenate(
            [rows_sum, early_sum[bands * own_rows :]]
            + [last_sum[:, lane_w * i : lane_w * i + lane_w] for i in range(total // lane_w)],
            axis=0,
        ),
        "seq",
        axis=0,
    )
    gain_out = norm_gain.astype(f32)[:, None]
    (
        grad_in,
        tail_sums,
        grad_out,
        norm_sums,
        grad_down,
        grad_shared_gate,
        grad_shared_up,
        mid_sums,
    ) = assemble(side, in_weight, gain_col, out_weight, gain_out, own_out, own_down)
    grad_norm = norm_sums[:, 0]
    grad_router_weight = mid_sums[:, :experts]
    grad_moe_gain = mid_sums[:, experts]
    grad_mixer_gain = tail_sums[:, 0]
    lane_at = used - (total - 128)
    small_sum = tail_sums[:, lane_at : lane_at + small_cols].reshape(-1)
    at = taps * conv_own
    grad_conv = small_sum[:at].reshape(taps, conv_own)
    grad_offset = small_sum[at : at + conv_own]
    at = at + conv_own
    grad_bias = small_sum[at : at + head_own]
    grad_decay = small_sum[at + head_own : at + 2 * head_own]
    grad_skip = small_sum[at + 2 * head_own : at + 3 * head_own]
    return (
        block_output,
        input_grad,
        grad_mixer_gain,
        grad_in,
        grad_conv,
        grad_offset,
        grad_bias,
        grad_decay,
        grad_skip,
        grad_norm,
        grad_out,
        grad_moe_gain,
        grad_router_weight,
        grad_shared_gate,
        grad_shared_up,
        grad_down,
        grad_e_gate,
        grad_e_up,
        grad_e_down,
    )


def solution(mesh):
    placed = (
        P("shard", "seq", None),
        P("shard"),
        P("shard", "seq", None),
        P("shard", "seq", None),
        P("shard"),
        P("shard", None),
        P(None, "shard"),
        P("shard"),
        P("shard"),
        P("shard"),
        P("shard"),
        P("shard"),
        P("shard", None),
        P("shard"),
        P("shard", None),
        P("shard", None),
        P("shard", None),
        P("shard", None),
        P("shard", None, None),
        P("shard", None, None),
        P("shard", None, None),
    )
    return jax.shard_map(
        on_device,
        mesh=mesh,
        in_specs=placed,
        out_specs=(
            P("shard", "seq", None),
            P("shard", "seq", None),
            P("shard"),
            P("shard", None),
            P(None, "shard"),
            P("shard"),
            P("shard"),
            P("shard"),
            P("shard"),
            P("shard"),
            P("shard", None),
            P("shard"),
            P("shard", None),
            P("shard", None),
            P("shard", None),
            P("shard", None),
            P("shard", None, None),
            P("shard", None, None),
            P("shard", None, None),
        ),
        check_vma=False,
    )
```

```python
import functools

import jax
import jax.numpy as jnp
from jax import lax
from jax.experimental import pallas as pl
from jax.experimental.pallas import tpu as pltpu
from jax.sharding import PartitionSpec as P

CAP = 32


epsilon = 1e-05
highest = lax.Precision.HIGHEST
both_axes = ("seq", "shard")


def times(left, right):
    return jnp.dot(left, right, preferred_element_type=jnp.float32)


def times_transposed(left, right):
    return lax.dot_general(
        left, right, (((1,), (1,)), ((), ())), preferred_element_type=jnp.float32
    )


def transposed_times(left, right):
    return lax.dot_general(
        left, right, (((0,), (0,)), ((), ())), preferred_element_type=jnp.float32
    )


def after(value, other):
    corner = other[(0,) * (other.ndim - 1)][:1].astype(jnp.float32)
    return (value.astype(jnp.float32) + 0.0 * corner).astype(value.dtype)


def silu_slope(values):
    sigma = jax.nn.sigmoid(values)
    return sigma * (1.0 + values * (1.0 - sigma))


def row_scale(values):
    return lax.rsqrt(jnp.mean(values * values, axis=-1, keepdims=True) + epsilon)


CHUNK = 128
WIDE = 384
CONVW = 640
PAIRS = 3
HEADS_HERE = 6


def split_two(values):
    high = values.astype(jnp.bfloat16)
    return high, (values - high.astype(jnp.float32)).astype(jnp.bfloat16)


def ones_times(ones, values):
    high, low = split_two(values)
    return times(ones, high) + times(ones, low)


def times_ones(values, ones):
    high, low = split_two(values)
    return times(high, ones) + times(low, ones)


def transposed_times_ones(values, ones):
    high, low = split_two(values)
    return transposed_times(high, ones) + transposed_times(low, ones)


def grid_of(shape):
    rows = lax.broadcasted_iota(jnp.int32, shape, 0)
    columns = lax.broadcasted_iota(jnp.int32, shape, 1)
    return rows, columns


def mark(condition):
    return jnp.where(condition, 1.0, 0.0).astype(jnp.bfloat16)


def chunk_parts(proj, prev, has_prev, taps_ref, head_ref, pad_ref):
    f32, bf = jnp.float32, jnp.bfloat16
    feed = proj[:, WIDE : WIDE + CONVW].astype(bf).astype(f32)
    before = prev[:, WIDE : WIDE + CONVW].astype(bf).astype(f32)
    pad_ref[0:8, :] = jnp.where(has_prev, before, 0.0)
    pad_ref[8 : 8 + CHUNK, :] = feed
    conv = taps_ref[4:5, :]
    for tap in range(4):
        conv = conv + taps_ref[tap : tap + 1, :] * pad_ref[5 + tap : 5 + tap + CHUNK, :]
    sig = jax.nn.sigmoid(conv)
    act = conv * sig
    u = act[:, :WIDE]
    key = act[:, WIDE : WIDE + 128].astype(bf)
    query = act[:, WIDE + 128 :].astype(bf)
    step_low = proj[:, WIDE + CONVW :].astype(bf).astype(f32)
    pre = step_low + head_ref[0:1, :]
    rows, columns = grid_of((CHUNK, 128))
    here = columns < HEADS_HERE
    dt = jnp.where(here, jnp.maximum(pre, 0.0) + jnp.log1p(jnp.exp(-jnp.abs(pre))), 0.0)
    la = dt * head_ref[1:2, :]
    lower = mark(rows >= columns)
    cum = ones_times(lower, la)
    end = cum[CHUNK - 1 : CHUNK, :]
    wide_rows, wide_columns = grid_of((128, WIDE))
    widen = mark(wide_columns // 64 == wide_rows)
    dt_w = times_ones(dt, widen)
    e_w = times_ones(jnp.exp(cum), widen)
    w_w = times_ones(jnp.exp(end - cum), widen)
    full_rows, full_columns = grid_of((128, 2 * PAIRS * 128))
    la_full = times_ones(la, mark(full_columns // 128 == full_rows))
    scores = times_transposed(query, key)
    return dict(
        conv=conv, sig=sig, u=u, key=key, query=query, pre=pre, here=here, dt=dt, lower=lower,
        dt_w=dt_w, e_w=e_w, w_w=w_w, la_full=la_full, scores=scores, xs=u * dt_w,
    )


def pair_table(parts, pair):
    rows, columns = grid_of((CHUNK, 256))
    local = columns % 128
    steps = jnp.where(rows > local, parts["la_full"][:, 256 * pair : 256 * pair + 256], 0.0)
    gap = ones_times(parts["lower"], steps)
    causal = rows >= local
    decay = jnp.where(causal, jnp.exp(jnp.where(causal, gap, 0.0)), 0.0)
    scores = parts["scores"]
    return decay, decay * jnp.concatenate([scores, scores], axis=1)


def stack_heads(values, pair):
    both = values[:, 128 * pair : 128 * pair + 128]
    first = lax.broadcasted_iota(jnp.int32, both.shape, 1) < 64
    return jnp.concatenate(
        [jnp.where(first, both, 0.0), jnp.where(first, 0.0, both)], axis=0
    ).astype(jnp.bfloat16)


def scan_forward_kernel(
    proj_ref, prev_ref, taps_ref, head_ref, skip_ref,
    mixed_ref, q_ref, square_ref, start_ref, state_ref, pad_ref,
):
    f32, bf = jnp.float32, jnp.bfloat16
    chunk = pl.program_id(0)

    @pl.when(chunk == 0)
    def _():
        state_ref[...] = jnp.zeros(state_ref.shape, f32)

    parts = chunk_parts(
        proj_ref[...], prev_ref[...], chunk > 0, taps_ref, head_ref, pad_ref
    )
    state = state_ref[...]
    start_ref[0] = state
    xs = parts["xs"]
    inside = []
    for pair in range(PAIRS):
        _, table = pair_table(parts, pair)
        inside.append(times(table.astype(bf), stack_heads(xs, pair)))
    across = times(parts["query"], state.astype(bf))
    y = (
        jnp.concatenate(inside, axis=1)
        + parts["e_w"] * across
        + skip_ref[0:1, :] * parts["u"]
    )
    mixed = y.astype(bf)
    mixed_ref[...] = mixed
    gate = proj_ref[:, :WIDE]
    q_val = mixed.astype(f32) * (gate * jax.nn.sigmoid(gate))
    q_ref[...] = q_val.astype(bf)
    square_ref[...] = jnp.sum(q_val * q_val, axis=1, keepdims=True)
    state_ref[...] = state * parts["e_w"][CHUNK - 1 : CHUNK, :] + transposed_times(
        parts["key"], (xs * parts["w_w"]).astype(bf)
    )


def scan_backward_kernel(
    chunks, held_count, proj_ref, prev_ref, mixed_ref, d_gated_ref, rows_ref, start_ref, taps_ref,
    head_ref, skip_ref, w_ref, carry_in_ref, sums_in_ref, *refs,
):
    f32, bf = jnp.float32, jnp.bfloat16
    d_proj_ref, back_ref, carry_ref, sums_ref, state_ref, pad_ref, late_ref = refs[held_count:]
    step = pl.program_id(0)
    chunk = chunks[1] - 1 - step
    d_taps_ref = sums_ref.at[0:8, :]
    d_head_ref = sums_ref.at[8:16, 0:128]
    d_skip_ref = sums_ref.at[16:24, 0:WIDE]

    @pl.when(step == 0)
    def _():
        state_ref[...] = carry_in_ref[0:128, 0:WIDE]
        late_ref[CHUNK : CHUNK + 8, :] = carry_in_ref[128:136, :]
        sums_ref[...] = sums_in_ref[...]

    parts = chunk_parts(
        proj_ref[...], prev_ref[...], chunk > 0, taps_ref, head_ref, pad_ref
    )
    u, key, query, xs = parts["u"], parts["key"], parts["query"], parts["xs"]
    e_w, w_w, dt_w = parts["e_w"], parts["w_w"], parts["dt_w"]

    gate = proj_ref[:, :WIDE]
    gate_sig = jax.nn.sigmoid(gate)
    gate_act = gate * gate_sig
    mixed = mixed_ref[...].astype(f32)
    q_val = mixed * gate_act
    q_r = rows_ref[:, 0:1]
    d_q = q_r * d_gated_ref[...] - q_val * (q_r * q_r * rows_ref[:, 1:2])
    d_gate = d_q * mixed * (gate_sig * (1.0 + gate * (1.0 - gate_sig)))
    d_y = (d_q * gate_act).astype(bf).astype(f32)

    start = start_ref[0]
    start_low = start.astype(bf)
    d_end = state_ref[...]
    d_end_low = d_end.astype(bf)
    xw = xs * w_w
    ye = d_y * e_w
    ye_low = ye.astype(bf)
    across = times(query, start_low)
    pulled = times(key, d_end_low)
    d_query = times_transposed(ye_low, start_low)
    d_key = times_transposed(xw.astype(bf), d_end_low)
    state_ref[...] = d_end * e_w[CHUNK - 1 : CHUNK, :] + transposed_times(query, ye_low)
    d_scores = jnp.zeros((CHUNK, 128), f32)
    turns = jnp.zeros((CHUNK, 128), f32)
    d_xs = []
    for pair in range(PAIRS):
        decay, table = pair_table(parts, pair)
        xs_two = stack_heads(xs, pair)
        dy_two = stack_heads(d_y, pair)
        d_table = times_transposed(d_y[:, 128 * pair : 128 * pair + 128].astype(bf), xs_two)
        d_decay = d_table * decay
        d_scores = d_scores + d_decay[:, :128] + d_decay[:, 128:]
        d_gap = d_table * table
        table_low = table.astype(bf)
        d_xs.append(
            transposed_times(
                jnp.concatenate([table_low[:, :128], table_low[:, 128:]], axis=0), dy_two
            )
        )
        two_rows, two_columns = grid_of((256, 128))
        own = mark(two_columns == 2 * pair + two_rows // 128)
        turns = turns + times_ones(d_gap, own)
        turns = turns - transposed_times_ones(
            jnp.concatenate([d_gap[:, :128], d_gap[:, 128:]], axis=0), own
        )
    d_xs = jnp.concatenate(d_xs, axis=1) + w_w * pulled
    d_scores_low = d_scores.astype(bf)
    d_query = d_query + times(d_scores_low, key)
    d_key = d_key + transposed_times(d_scores_low, query)

    rows, columns = grid_of((CHUNK, 128))
    upper = mark(columns >= rows)
    strict = mark(columns < rows)
    sum_rows, sum_columns = grid_of((WIDE, 128))
    per_head = mark(sum_rows // 64 == sum_columns)
    end_row = jnp.sum(d_end * start, axis=0, keepdims=True) * e_w[CHUNK - 1 : CHUNK, :]
    wide = ones_times(upper, ye * across) + ones_times(strict, xw * pulled) + end_row
    d_la = ones_times(upper, turns) + times_ones(wide, per_head)
    d_dt = times_ones(d_xs * u, per_head) + d_la * head_ref[1:2, :]
    d_pre = jnp.where(parts["here"], d_dt * jax.nn.sigmoid(parts["pre"]), 0.0)
    d_head_ref[0:1, :] += jnp.sum(d_pre, axis=0, keepdims=True)
    d_head_ref[1:2, :] += jnp.sum(d_la * parts["dt"], axis=0, keepdims=True)
    d_skip_ref[0:1, :] += jnp.sum(d_y * u, axis=0, keepdims=True)

    d_u = d_xs * dt_w + skip_ref[0:1, :] * d_y
    conv, sig = parts["conv"], parts["sig"]
    d_conv = jnp.concatenate([d_u, d_key, d_query], axis=1) * (sig * (1.0 + conv * (1.0 - sig)))
    late_ref[0:CHUNK, :] = d_conv
    d_feed = jnp.zeros((CHUNK, CONVW), f32)
    for tap in range(4):
        d_feed = d_feed + taps_ref[tap : tap + 1, :] * late_ref[3 - tap : 3 - tap + CHUNK, :]
        d_taps_ref[tap : tap + 1, :] += jnp.sum(
            d_conv * pad_ref[5 + tap : 5 + tap + CHUNK, :], axis=0, keepdims=True
        )
    d_taps_ref[4:5, :] += jnp.sum(d_conv, axis=0, keepdims=True)
    late_ref[CHUNK : CHUNK + 8, :] = d_conv[0:8, :]
    carry_ref[0:128, 0:WIDE] = state_ref[...]
    carry_ref[128:136, :] = d_conv[0:8, :]
    scale = rows_ref[:, 2:3]
    d_proj = jnp.concatenate([d_gate, d_feed, d_pre], axis=1) * scale
    d_proj = d_proj.astype(bf)
    d_proj_ref[...] = d_proj
    back_ref[...] = times_transposed(d_proj, w_ref[...]).astype(bf)


def corner_of(array):
    return pl.BlockSpec(
        (1,) * (array.ndim - 2) + (min(16, array.shape[-2]), 128),
        lambda *step: (0,) * array.ndim,
    )


def whole(shape):
    return pl.BlockSpec(shape, lambda step: (0,) * len(shape))


def project_kernel(x_ref, weights_ref, earlier_ref, proj_ref, scale_ref, w_ref):
    width = weights_ref.shape[2]

    @pl.when(pl.program_id(0) == 0)
    def _():
        w_ref[...] = weights_ref[...].reshape(-1, width)

    x = x_ref[...]
    wide = x.astype(jnp.float32)
    scale = row_scale(wide)
    proj_ref[...] = times(x, w_ref[...]) * scale
    scale_ref[...] = scale


def project(x_all, weights, rows_w, earlier):
    rows, dim = x_all.shape
    sources, _, width = weights.shape
    tile = rows // 4
    return pl.pallas_call(
        project_kernel,
        grid=(4,),
        in_specs=[
            pl.BlockSpec((tile, dim), lambda step: (step, 0)),
            pl.BlockSpec((sources, rows_w, width), lambda step: (0, 0, 0)),
            corner_of(earlier),
        ],
        out_specs=[
            pl.BlockSpec((tile, width), lambda step: (step, 0)),
            pl.BlockSpec((tile, 1), lambda step: (step, 0)),
            pl.BlockSpec((dim, width), lambda step: (0, 0)),
        ],
        out_shape=[
            jax.ShapeDtypeStruct((rows, width), jnp.float32),
            jax.ShapeDtypeStruct((rows, 1), jnp.float32),
            jax.ShapeDtypeStruct((dim, width), jnp.bfloat16),
        ],
        compiler_params=pltpu.CompilerParams(vmem_limit_bytes=40 << 20),
        cost_estimate=pl.CostEstimate(
            flops=2 * rows * dim * width, bytes_accessed=16 << 20, transcendentals=0
        ),
        name="project",
    )(x_all, weights, earlier)


def scan_forward(proj, taps, head, skip):
    rows, width = proj.shape
    chunks = rows // CHUNK
    by_chunk = lambda step: (step, 0)
    return pl.pallas_call(
        scan_forward_kernel,
        grid=(chunks,),
        in_specs=[
            pl.BlockSpec((CHUNK, width), by_chunk),
            pl.BlockSpec((8, width), lambda step: (jnp.maximum(step * (CHUNK // 8) - 1, 0), 0)),
            whole(taps.shape),
            whole(head.shape),
            whole(skip.shape),
        ],
        out_specs=[
            pl.BlockSpec((CHUNK, WIDE), by_chunk),
            pl.BlockSpec((CHUNK, WIDE), by_chunk),
            pl.BlockSpec((CHUNK, 1), by_chunk),
            pl.BlockSpec((1, 128, WIDE), lambda step: (step, 0, 0)),
        ],
        out_shape=[
            jax.ShapeDtypeStruct((rows, WIDE), jnp.bfloat16),
            jax.ShapeDtypeStruct((rows, WIDE), jnp.bfloat16),
            jax.ShapeDtypeStruct((rows, 1), jnp.float32),
            jax.ShapeDtypeStruct((chunks, 128, WIDE), jnp.float32),
        ],
        scratch_shapes=[
            pltpu.VMEM((128, WIDE), jnp.float32),
            pltpu.VMEM((CHUNK + 8, CONVW), jnp.float32),
        ],
        compiler_params=pltpu.CompilerParams(vmem_limit_bytes=32 << 20),
        cost_estimate=pl.CostEstimate(
            flops=3 << 30, bytes_accessed=12 << 20, transcendentals=4 << 20
        ),
        name="scan_forward",
    )(proj, proj, taps, head, skip)


def scan_backward(chunks, inputs, held, carry, sums, earlier):
    proj, mixed, d_gated, row_values, starts, taps, head, skip, w_all = inputs
    rows, width = proj.shape
    dim = w_all.shape[0]
    at = lambda step: chunks[1] - 1 - step
    by_chunk = lambda step: (at(step), 0)
    given = (proj, proj, mixed, d_gated, row_values, starts, taps, head, skip, w_all, carry, sums)
    return pl.pallas_call(
        functools.partial(scan_backward_kernel, chunks, len(held) + len(earlier)),
        grid=(chunks[1] - chunks[0],),
        in_specs=[
            pl.BlockSpec((CHUNK, width), by_chunk),
            pl.BlockSpec(
                (8, width), lambda step: (jnp.maximum(at(step) * (CHUNK // 8) - 1, 0), 0)
            ),
            pl.BlockSpec((CHUNK, WIDE), by_chunk),
            pl.BlockSpec((CHUNK, WIDE), by_chunk),
            pl.BlockSpec((CHUNK, row_values.shape[1]), by_chunk),
            pl.BlockSpec((1, 128, WIDE), lambda step: (at(step), 0, 0)),
            whole(taps.shape),
            whole(head.shape),
            whole(skip.shape),
            whole(w_all.shape),
            whole(carry.shape),
            whole(sums.shape),
            *[pl.BlockSpec(memory_space=pl.ANY) for _ in held],
            *map(corner_of, earlier),
        ],
        out_specs=[
            pl.BlockSpec((CHUNK, width), by_chunk),
            pl.BlockSpec((CHUNK, dim), by_chunk),
            whole(carry.shape),
            whole(sums.shape),
        ],
        out_shape=[
            jax.ShapeDtypeStruct((rows, width), jnp.bfloat16),
            jax.ShapeDtypeStruct((rows, dim), jnp.bfloat16),
            jax.ShapeDtypeStruct(carry.shape, jnp.float32),
            jax.ShapeDtypeStruct(sums.shape, jnp.float32),
        ],
        scratch_shapes=[
            pltpu.VMEM((128, WIDE), jnp.float32),
            pltpu.VMEM((CHUNK + 8, CONVW), jnp.float32),
            pltpu.VMEM((CHUNK + 8, CONVW), jnp.float32),
        ],
        input_output_aliases={len(given) + i: i for i in range(len(held))},
        compiler_params=pltpu.CompilerParams(vmem_limit_bytes=48 << 20),
        cost_estimate=pl.CostEstimate(
            flops=10 << 30, bytes_accessed=20 << 20, transcendentals=8 << 20
        ),
        name="scan_backward",
    )(*given, *held, *earlier)


def expert_early_kernel(cot_ref, down_ref, earlier_ref, raw_ref):
    cot = cot_ref[...].reshape(-1, cot_ref.shape[-1])
    raw_ref[0] = times_transposed(cot, down_ref[0])


def expert_main_kernel(
    rows_ref, routed_ref, raw_ref, gate_ref, up_ref, router_ref, marks_ref,
    moe_ref, cot_ref, shared_ref, down_ref,
    back_ref, act_ref, scaled_ref, d_g_ref, d_v_ref, both_ref, s_act_ref, d_both_ref,
):
    f32, bf = jnp.float32, jnp.bfloat16
    dim = rows_ref.shape[-1]
    rows = rows_ref[...].reshape(-1, dim)
    routed = routed_ref[...].reshape(-1, 128).astype(f32) > 0.0
    logits = times(rows, router_ref[...])
    top = jnp.max(jnp.where(routed, logits, -1e30), axis=1, keepdims=True)
    powers = jnp.where(routed, jnp.exp(jnp.where(routed, logits - top, 0.0)), 0.0)
    own = jnp.sum(powers * marks_ref[0, 0:1, :], axis=1, keepdims=True)
    gate = own / jnp.maximum(jnp.sum(powers, axis=1, keepdims=True), 1e-30)
    g = times(rows, gate_ref[0])
    v = times(rows, up_ref[0])
    sig = jax.nn.sigmoid(g)
    silu = g * sig
    act = (silu * v).astype(bf)
    act_wide = act.astype(f32)
    raw = raw_ref[0]
    d_gate = jnp.sum(act_wide * raw, axis=1, keepdims=True)
    d_act = gate * raw
    d_g = (d_act * v * (sig * (1.0 + g * (1.0 - sig)))).astype(bf)
    d_v = (d_act * silu).astype(bf)
    d_row = times_transposed(d_g, gate_ref[0]) + times_transposed(d_v, up_ref[0])
    high = d_gate.astype(bf).astype(f32)
    scalars = high * marks_ref[0, 1:2, :] + (d_gate - high) * marks_ref[0, 2:3, :]
    lead = back_ref.shape[:-1]
    back_ref[:, :, :, :dim] = d_row.astype(bf).reshape(*lead, dim)
    back_ref[:, :, :, dim:] = scalars.astype(bf).reshape(*lead, 128)
    act_ref[0] = act
    scaled_ref[0] = (gate * act_wide).astype(bf)
    d_g_ref[0] = d_g
    d_v_ref[0] = d_v

    units = down_ref.shape[0]
    s_both = times(moe_ref[...], shared_ref[...])
    s_gate, s_up = s_both[:, :units], s_both[:, units:]
    s_sig = jax.nn.sigmoid(s_gate)
    s_silu = s_gate * s_sig
    s_act = (s_silu * s_up).astype(bf)
    d_sh = times_transposed(cot_ref[...], down_ref[...])
    d_gs = (d_sh * s_up * (s_sig * (1.0 + s_gate * (1.0 - s_sig)))).astype(bf)
    d_both = jnp.concatenate([d_gs, (d_sh * s_silu).astype(bf)], axis=1)
    both_ref[:, :dim] = times_transposed(d_both, shared_ref[...]).astype(bf)
    both_ref[:, dim:] = times(s_act, down_ref[...]).astype(bf)
    s_act_ref[...] = s_act
    d_both_ref[...] = d_both


def expert_late_kernel(
    rows_ref, cot_ref, act_ref, scaled_ref, d_g_ref, d_v_ref, down_ref,
    out_ref, grads_ref,
):
    bf = jnp.bfloat16
    dim = rows_ref.shape[-1]
    rows = rows_ref[...].reshape(-1, dim)
    cot = cot_ref[...].reshape(-1, dim)
    out_ref[...] = times(act_ref[0], down_ref[0]).astype(bf).reshape(out_ref.shape)
    units = act_ref.shape[-1]
    grads_ref[0, :dim] = transposed_times(rows, d_g_ref[0]).astype(bf)
    grads_ref[0, dim : 2 * dim] = transposed_times(rows, d_v_ref[0]).astype(bf)
    for block in range(dim // units):
        at = 2 * dim + block * units
        grads_ref[0, at : at + units] = transposed_times(
            scaled_ref[0], cot[:, block * units : block * units + units]
        ).astype(bf)


def expert_slots(shape, start=0):
    return pl.BlockSpec(
        (shape[0], 1) + tuple(shape[2:]), lambda e: (0, e) + (0,) * (len(shape) - 3) + (start,)
    )


def per_expert(shape):
    return pl.BlockSpec((1,) + tuple(shape[1:]), lambda e: (e,) + (0,) * (len(shape) - 1))


def expert_params(flops, moved):
    return dict(
        compiler_params=pltpu.CompilerParams(vmem_limit_bytes=56 << 20),
        cost_estimate=pl.CostEstimate(flops=flops, bytes_accessed=moved, transcendentals=1 << 19),
    )


def expert_early(cot_rows, down, earlier):
    sources, local, cap, _ = cot_rows.shape
    units, dim = down.shape[1:]
    return pl.pallas_call(
        expert_early_kernel,
        grid=(local,),
        in_specs=[
            expert_slots((sources, local, cap, dim)),
            per_expert(down.shape),
            corner_of(earlier),
        ],
        out_specs=per_expert((local, sources * cap, units)),
        out_shape=jax.ShapeDtypeStruct((local, sources * cap, units), jnp.float32),
        name="expert_early",
        **expert_params(64 << 30, 256 << 20),
    )(cot_rows, down, earlier)


def expert_main(rows, cot_rows, raw, gate, up, w_all, marks, moe_all, cot_all, w_shared, w_down):
    sources, local, cap, dim = rows.shape
    units = gate.shape[2]
    count = sources * cap
    hidden = jax.ShapeDtypeStruct((local, count, units), jnp.bfloat16)
    back = (sources, local, cap, dim + 128)
    seq_rows = moe_all.shape[0]
    shared_units = w_down.shape[0]
    share = lambda width: pl.BlockSpec((seq_rows // local, width), lambda e: (e, 0))
    return pl.pallas_call(
        expert_main_kernel,
        grid=(local,),
        in_specs=[
            expert_slots(rows.shape),
            expert_slots((sources, local, cap, 128), dim // 128),
            per_expert(raw.shape),
            per_expert(gate.shape),
            per_expert(up.shape),
            pl.BlockSpec((dim, 128), lambda e: (0, w_all.shape[1] // 128 - 1)),
            per_expert(marks.shape),
            share(dim),
            share(dim),
            whole(w_shared.shape),
            whole(w_down.shape),
        ],
        out_specs=[expert_slots(back)]
        + [per_expert(hidden.shape)] * 4
        + [share(2 * dim), share(shared_units), share(2 * shared_units)],
        out_shape=[jax.ShapeDtypeStruct(back, jnp.bfloat16)]
        + [hidden] * 4
        + [
            jax.ShapeDtypeStruct((seq_rows, width), jnp.bfloat16)
            for width in (2 * dim, shared_units, 2 * shared_units)
        ],
        name="expert_main",
        **expert_params(8 << 30, 20 << 20),
    )(rows, cot_rows, raw, gate, up, w_all, marks, moe_all, cot_all, w_shared, w_down)


def expert_late(rows, cot_rows, act, scaled, d_g, d_v, down):
    sources, local, cap, dim = rows.shape
    units = down.shape[1]
    grads = (local, 3 * dim, units)
    return pl.pallas_call(
        expert_late_kernel,
        grid=(local,),
        in_specs=[expert_slots(rows.shape), expert_slots(rows.shape)]
        + [per_expert(act.shape)] * 4
        + [per_expert(down.shape)],
        out_specs=[
            expert_slots(rows.shape),
            per_expert(grads),
        ],
        out_shape=[
            jax.ShapeDtypeStruct(rows.shape, jnp.bfloat16),
            jax.ShapeDtypeStruct(grads, jnp.bfloat16),
        ],
        name="expert_late",
        **expert_params(7 << 30, 24 << 20),
    )(rows, cot_rows, act, scaled, d_g, d_v, down)


def assemble_kernel(
    own_out, own_down, side_ref, in_ref, in_gain_ref, out_ref, out_gain_ref,
    grad_in_ref, tail_ref, grad_out_ref, norm_ref, grad_down_ref, gate_ref, up_ref, mid_ref,
):
    f32 = jnp.float32
    groups = side_ref.shape[0]
    inner = groups * WIDE
    bands = out_ref.shape[1] // WIDE
    rows_w = in_ref.shape[0]
    gain = in_gain_ref[...]
    at_down = bands * own_out
    at_mid = at_down + bands * own_down
    at_in = at_mid + rows_w
    units = gate_ref.shape[1] // groups

    def block(group, start, rows):
        return side_ref[group, start : start + rows, :].astype(f32)

    grad_gain = jnp.zeros((rows_w, 1), f32)
    keys = jnp.zeros((rows_w, 256), f32)
    tail = jnp.zeros((rows_w, 128), f32)
    steps = jnp.zeros((rows_w, 128), f32)
    mid = jnp.zeros((rows_w, 128), f32)
    rows, columns = grid_of((128, 128))

    def put(start, values):
        stop = start + values.shape[1]
        grad_in_ref[:, start:stop] = values * gain
        weight = in_ref[:, start:stop].astype(f32)
        return jnp.sum(weight * values, axis=1, keepdims=True)

    for group in range(groups):
        grad_gain += put(group * WIDE, block(group, at_in, rows_w))
        grad_gain += put(inner + group * WIDE, block(group, at_in + rows_w, rows_w))
        last = block(group, at_in + 2 * rows_w, rows_w)
        keys = keys + last[:, :256]
        tail = tail + last[:, 256:]
        moved = mark((rows < HEADS_HERE) & (columns == rows + HEADS_HERE * group))
        steps = steps + times(last[:, 256:].astype(jnp.bfloat16), moved)
        shared = block(group, at_mid, rows_w)
        gate_ref[:, units * group : units * group + units] = shared[:, :units]
        up_ref[:, units * group : units * group + units] = shared[:, units : 2 * units]
        mid = mid + shared[:, 2 * units :]
    grad_gain += put(2 * inner, keys)
    grad_gain += put(2 * inner + 256, steps[:, : groups * HEADS_HERE])
    lane = lax.broadcasted_iota(jnp.int32, tail.shape, 1)
    tail_ref[...] = jnp.where(lane == 0, grad_gain, tail)
    mid_ref[...] = mid

    for group in range(groups):
        sums = jnp.zeros((own_out, 1), f32)
        mine = slice(own_out * group, own_out * group + own_out)
        for band in range(bands):
            wide = slice(WIDE * band, WIDE * band + WIDE)
            values = block(group, own_out * band, own_out)
            grad_out_ref[mine, wide] = values * out_gain_ref[mine, :]
            sums += jnp.sum(out_ref[mine, wide].astype(f32) * values, axis=1, keepdims=True)
            grad_down_ref[own_down * group : own_down * group + own_down, wide] = block(
                group, at_down + own_down * band, own_down
            )
        norm_ref[mine, :] = sums


def assemble(side, in_weight, in_gain, out_weight, out_gain, own_out, own_down):
    groups = side.shape[0]
    rows, width = in_weight.shape
    out_rows, dim = out_weight.shape
    shapes = [
        (rows, width),
        (rows, 128),
        (out_rows, dim),
        (out_rows, 1),
        (groups * own_down, dim),
        (rows, groups * 128),
        (rows, groups * 128),
        (rows, 128),
    ]
    return pl.pallas_call(
        functools.partial(assemble_kernel, own_out, own_down),
        in_specs=[pl.BlockSpec(memory_space=pltpu.VMEM)] * 5,
        out_specs=[pl.BlockSpec(memory_space=pltpu.VMEM)] * len(shapes),
        out_shape=[jax.ShapeDtypeStruct(shape, jnp.float32) for shape in shapes],
        compiler_params=pltpu.CompilerParams(vmem_limit_bytes=40 << 20),
        cost_estimate=pl.CostEstimate(flops=8 << 20, bytes_accessed=12 << 20, transcendentals=0),
        name="assemble",
    )(side, in_weight, in_gain, out_weight, out_gain)


def fold_rows(values, width):
    rest = values[:, width:]
    count = rest.shape[1] * values.shape[0] // width
    parts = [rest[at : at + count] for at in range(0, values.shape[0], count)]
    return jnp.concatenate([values[:, :width], jnp.concatenate(parts, axis=1)], axis=0)


def unfold_rows(values, dim):
    sources, rows, width = values.shape
    count = rows * width // dim
    rest = dim - width
    parts = [values[:, count:, at : at + rest] for at in range(0, width, rest)]
    return jnp.concatenate([values[:, :count], jnp.concatenate(parts, axis=1)], axis=2)


def gather_rows(values, core, z_at, mates):
    cores = 2
    chips = len(mates) // cores
    column = [values]
    for hop in range(1, chips):
        pairs = [
            (i, (i // cores + hop) % chips * cores + i % cores) for i in range(len(mates))
        ]
        column.append(lax.ppermute(values, "seq", pairs))
    column = jnp.stack(column)
    both = jnp.stack([column, lax.ppermute(column, "seq", mates)], axis=1)
    both = both.reshape((len(mates),) + values.shape)
    ordered = [
        lax.dynamic_index_in_dim(both, (z_at - z) % chips * cores + (c ^ core), 0, keepdims=False)
        for z in range(chips)
        for c in range(cores)
    ]
    return jnp.concatenate(ordered, axis=0)


def halve(values, bit, pairs, start=None):
    f32 = jnp.float32
    parts = values.reshape(2, values.shape[0] // 2, values.shape[1])
    sent = lax.dynamic_index_in_dim(parts, 1 - bit, 0, keepdims=False)
    kept = lax.dynamic_index_in_dim(parts, bit, 0, keepdims=False)
    if start is not None:
        sent = after(sent, start)
    other = lax.ppermute(sent, "seq", pairs)
    return (kept.astype(f32) + other.astype(f32)).astype(jnp.bfloat16)


def double(values, bit, pairs):
    other = lax.ppermute(values, "seq", pairs)
    first = jnp.where(bit == 0, values, other)
    second = jnp.where(bit == 0, other, values)
    return jnp.concatenate([first, second], axis=0)


def unpack_kernel(core_ref, own_ref, other_ref, gate_ref, up_ref, down_ref):
    part = pl.program_id(1)
    block = jnp.where(pl.program_id(0) == 0, own_ref[...], other_ref[...]).astype(jnp.float32)
    units = block.shape[1]

    @pl.when(part == 0)
    def _():
        gate_ref[0] = block

    @pl.when(part == 1)
    def _():
        up_ref[0] = block

    @pl.when(part == 2)
    def _():
        for at in range(0, block.shape[0], units):
            down_ref[0, :, at : at + units] = block[at : at + units]


def unpack_expert_grads(own, other, core):
    rows, units = own.shape
    dim = rows // 3
    to_expert = lambda who, part, core: (jnp.where(who == 0, core[0], 1 - core[0]), 0, 0)
    return pl.pallas_call(
        unpack_kernel,
        grid_spec=pltpu.PrefetchScalarGridSpec(
            num_scalar_prefetch=1,
            grid=(2, 3),
            in_specs=[
                pl.BlockSpec((dim, units), lambda who, part, core: (jnp.where(who == 0, part, 2), 0)),
                pl.BlockSpec((dim, units), lambda who, part, core: (jnp.where(who == 0, 0, part), 0)),
            ],
            out_specs=[
                pl.BlockSpec((1, dim, units), to_expert),
                pl.BlockSpec((1, dim, units), to_expert),
                pl.BlockSpec((1, units, dim), to_expert),
            ],
        ),
        out_shape=[
            jax.ShapeDtypeStruct((2, dim, units), jnp.float32),
            jax.ShapeDtypeStruct((2, dim, units), jnp.float32),
            jax.ShapeDtypeStruct((2, units, dim), jnp.float32),
        ],
        compiler_params=pltpu.CompilerParams(vmem_limit_bytes=40 << 20),
        cost_estimate=pl.CostEstimate(flops=1 << 20, bytes_accessed=28 << 20, transcendentals=0),
        name="unpack_expert_grads",
    )(core.reshape(1), own, other)


def on_device(
    block_input,
    lengths,
    routes,
    out_cotangent,
    mixer_gain,
    in_weight,
    conv_weight,
    conv_bias,
    step_bias,
    decay_log,
    skip_gain,
    norm_gain,
    out_weight,
    moe_gain,
    router_weight,
    shared_gate,
    shared_up,
    shared_down,
    expert_gate,
    expert_up,
    expert_down,
):
    sq = lax.axis_size("seq")
    sh = lax.axis_size("shard")
    q = lax.axis_index("seq")
    f32 = jnp.float32
    bf = jnp.bfloat16
    x_low = block_input[0]
    toks, dim = x_low.shape
    seq_rows = toks * sq
    heads = step_bias.shape[0] * sh
    inner = norm_gain.shape[0] * sh
    conv_all = conv_bias.shape[0] * sh
    keys_w = conv_all - inner
    gh = heads // sq
    gw = inner // sq
    rows_w = in_weight.shape[0]
    experts = router_weight.shape[1]
    local_e = expert_gate.shape[0]
    fs = shared_gate.shape[1]
    gf = fs // sq
    taps = conv_weight.shape[0]
    conv_own = conv_bias.shape[0]
    head_own = step_bias.shape[0]

    gain_col = mixer_gain.astype(f32)[:, None]

    def cols(start, width):
        return lax.dynamic_slice_in_dim(in_weight, start, width, 1)

    w_cols = jnp.concatenate(
        [
            cols(q * gw, gw),
            cols(inner + q * gw, gw),
            in_weight[:, 2 * inner : 2 * inner + keys_w],
            cols(2 * inner + keys_w + q * gh, gh),
        ],
        axis=1,
    )
    w_cols = (w_cols.astype(f32) * gain_col).astype(bf)
    used = 2 * gw + keys_w + gh
    small = jnp.concatenate(
        [conv_weight.reshape(-1), conv_bias, step_bias, decay_log, skip_gain]
    )
    small_cols = -(-small.shape[0] // rows_w)
    small = jnp.pad(small, (0, small_cols * rows_w - small.shape[0])).reshape(rows_w, small_cols)
    packed = jnp.concatenate(
        [w_cols, small, router_weight, moe_gain[:, None]], axis=1
    )
    at_small = used
    at_router = at_small + small_cols
    at_moe = at_router + experts
    total = -(-(at_moe + 1) // 128) * 128
    packed = jnp.pad(packed, ((0, 0), (0, total - packed.shape[1])))

    def to_shards(values):
        return lax.all_to_all(values, "shard", split_axis=0, concat_axis=0, tiled=True)

    core, z_at = q % 2, q // 2
    mates = [(i, i ^ 1) for i in range(sq)]
    x_all = gather_rows(x_low, core, z_at, mates)

    out_scaled = (norm_gain.astype(f32)[:, None] * out_weight.astype(f32)).astype(bf)
    own_out = out_weight.shape[0] // sq
    own_down = shared_down.shape[0] // sq
    piece = jnp.concatenate(
        [
            lax.dynamic_slice_in_dim(out_scaled, q * own_out, own_out, 0),
            lax.dynamic_slice_in_dim(shared_down, q * own_down, own_down, 0),
        ],
        axis=0,
    )
    ratio = sh // sq
    forward_pairs = []
    for a in range(sh):
        for j in range(sq):
            s_to = sq * (a % ratio) + j
            q_to = a // ratio
            forward_pairs.append((j * sh + a, q_to * sh + s_to))
    backward_pairs = [(b, a) for a, b in forward_pairs]
    piece = lax.ppermute(piece, both_axes, forward_pairs)
    shared_cols = jnp.concatenate(
        [
            lax.dynamic_slice_in_dim(shared_gate, q * gf, gf, 1),
            lax.dynamic_slice_in_dim(shared_up, q * gf, gf, 1),
        ],
        axis=1,
    )
    fold = rows_w * 2 * gf // dim
    bands = dim // (2 * gf)
    shared_rows = jnp.concatenate(
        [shared_cols[fold * band : fold * band + fold] for band in range(bands)], axis=1
    )
    own_rows = own_out + own_down
    weights = lax.all_gather(
        jnp.concatenate(
            [
                packed,
                fold_rows(piece[:own_out], total),
                fold_rows(jnp.concatenate([piece[own_out:], shared_rows], axis=0), total),
            ],
            axis=0,
        ),
        "shard",
        axis=0,
    )
    folded = rows_w + own_out * dim // total
    w_out = unfold_rows(weights[:, rows_w:folded], dim).reshape(gw, dim)
    second = unfold_rows(weights[:, folded:], dim)
    w_down = second[:, :own_down].reshape(gf, dim)
    w_shared = (
        second[:, own_down:]
        .reshape(sh, fold, bands, 2 * gf)
        .transpose(0, 2, 1, 3)
        .reshape(dim, 2 * gf)
    )

    route_ids = routes[0]
    expert_ids = jnp.arange(experts, dtype=jnp.int32)
    named = jnp.any(route_ids[:, :, None] == expert_ids[None, None, :], axis=1).astype(f32)
    earlier = (
        jnp.arange(toks)[:, None] > jnp.arange(toks)[None, :]
    ).astype(f32)
    rank = jnp.dot(earlier, named)
    dispatch = (
        (named.T[:, None, :] > 0.0)
        & (rank.T[:, None, :] == jnp.arange(CAP, dtype=f32)[None, :, None])
    ).astype(bf)
    slots = experts * CAP
    dispatch_flat = dispatch.reshape(slots, toks)
    live = (q * toks + jnp.arange(toks, dtype=jnp.int32) < lengths[0]).astype(f32)
    cot = out_cotangent[0].astype(f32) * live[:, None]
    cot_low = cot.astype(bf)

    local_slots = (sh, local_e, CAP)

    def in_slots(values):
        return times(dispatch_flat, values).astype(bf).reshape(sh, local_e * CAP, -1)

    def dispatched(sent):
        return to_shards(sent).reshape(*local_slots, -1)

    router_lane = at_router - (total - 128)
    lanes = jnp.arange(128, dtype=jnp.int32)
    named_lanes = jnp.pad(named, ((0, 0), (router_lane, 128 - router_lane - experts)))
    cot_sent = in_slots(jnp.concatenate([cot_low, named_lanes.astype(bf)], axis=1))
    cot_rows = dispatched(cot_sent)

    proj, x_r, w_all = project(x_all, weights, rows_w, cot_sent)

    small_all = weights[:, :rows_w, at_small:at_router].reshape(sh, -1)
    at = taps * conv_own
    conv_full = (
        small_all[:, :at].reshape(sh, taps, conv_own).transpose(1, 0, 2).reshape(taps, conv_all)
    )
    offset_full = small_all[:, at : at + conv_own].reshape(conv_all)
    at = at + conv_own
    bias_full = small_all[:, at : at + head_own].reshape(heads)
    decay_full = small_all[:, at + head_own : at + 2 * head_own].reshape(heads)
    skip_full = small_all[:, at + 2 * head_own : at + 3 * head_own].reshape(heads)
    router_full = weights[:, :rows_w, at_router:at_moe].reshape(dim, experts)
    moe_gain_full = weights[:, :rows_w, at_moe].reshape(dim).astype(f32)

    def group(values, width):
        return lax.dynamic_slice_in_dim(values, q * width, width, values.ndim - 1)

    conv_local = jnp.concatenate([group(conv_full, gw), conv_full[:, inner:]], axis=1).astype(f32)
    offset_local = jnp.concatenate([group(offset_full, gw), offset_full[inner:]]).astype(f32)
    bias_local = group(bias_full, gh).astype(f32)
    decay_local = group(decay_full, gh).astype(f32)
    skip_local = group(skip_full, gh).astype(f32)

    per_head = gw // gh
    taps_in = jnp.concatenate(
        [conv_local, offset_local[None], jnp.zeros((8 - taps - 1, gw + keys_w), f32)], axis=0
    )
    decay_rate = -jnp.exp(decay_local)
    head_in = jnp.pad(jnp.stack([bias_local, decay_rate]), ((0, 6), (0, 128 - gh)))
    skip_in = jnp.broadcast_to(jnp.repeat(skip_local, per_head)[None], (8, gw))
    mixed, q_low, square_part, starts = scan_forward(proj, taps_in, head_in, skip_in)

    cot_all = lax.all_gather(after(cot_low, w_all), "seq", axis=0, tiled=True)
    w_out, cot_all = lax.optimization_barrier((w_out, cot_all))
    out_part = times(q_low, w_out).astype(bf)
    out_sum = lax.psum_scatter(out_part, "seq", scatter_dimension=0, tiled=True)
    square = lax.psum(after(square_part.reshape(sq, toks), out_part), "seq")
    q_r = lax.rsqrt(square / inner + epsilon).reshape(seq_rows, 1)
    d_raw = expert_early(cot_rows, expert_down, square)
    tok_r = after(lax.dynamic_slice_in_dim(q_r, q * toks, toks, 0), d_raw)
    x_tok = x_low.astype(f32)
    added = out_sum.astype(f32) * tok_r
    resid = x_tok + added

    resid_r = row_scale(resid)
    resid_n = resid * resid_r
    moe_in = (resid_n * moe_gain_full[None, :]).astype(bf)
    moe_all = lax.all_gather(moe_in, "seq", axis=0, tiled=True)

    logits = times(moe_in, w_all[:, total - 128 :])
    top = jnp.max(jnp.where(named_lanes > 0.0, logits, -1e30), axis=1, keepdims=True)
    powers = jnp.where(
        named_lanes > 0.0, jnp.exp(jnp.where(named_lanes > 0.0, logits - top, 0.0)), 0.0
    )
    gates = (powers / jnp.sum(powers, axis=1, keepdims=True))[
        :, router_lane : router_lane + experts
    ]
    rows = dispatched(in_slots(moe_in))
    own_ids = lax.axis_index("shard") * local_e + jnp.arange(local_e, dtype=jnp.int32)
    marks = jnp.stack(
        [own_ids + router_lane, own_ids, own_ids + 64] + [jnp.full_like(own_ids, -1)] * 5, axis=1
    )
    marks = (marks[:, :, None] == lanes[None, None, :]).astype(f32)

    back_rows, e_act, e_scaled, d_g, d_v, both_part, s_act, d_both = expert_main(
        rows,
        cot_rows,
        d_raw,
        expert_gate,
        expert_up,
        w_all,
        marks,
        moe_all,
        cot_all,
        w_shared,
        w_down,
    )
    shared_both = lax.psum_scatter(both_part, "seq", scatter_dimension=0, tiled=True)
    d_moe_shared = shared_both[:, :dim]
    shared_sum = shared_both[:, dim:]
    d_returned = to_shards(back_rows.reshape(sh, local_e * CAP, dim + 128))
    e_out, e_grads = expert_late(rows, cot_rows, e_act, e_scaled, d_g, d_v, expert_down)
    d_returned, e_out = lax.optimization_barrier((d_returned, e_out))
    returned = to_shards(e_out.reshape(sh, local_e * CAP, dim))

    near = [(i, 2 * ((i // 2) ^ 1) + i % 2) for i in range(sq)]
    far = [(i, 2 * (sq // 2 - 1 - i // 2) + i % 2) for i in range(sq)]
    is_inner = ((z_at == 1) | (z_at == 2)).astype(jnp.int32)
    is_high = (z_at >= 2).astype(jnp.int32)
    e_mine = jnp.concatenate(
        [
            halve(e_grads[:, dim * part : dim * part + dim].reshape(local_e * dim, -1), core, mates)
            for part in range(3)
        ],
        axis=0,
    )
    cutoff = e_mine.shape[0] // 2

    grad_down_part = transposed_times(s_act, cot_all).astype(bf)
    grad_shared_part = transposed_times(moe_all, d_both).astype(bf)
    gates = after(after(gates, grad_down_part), grad_shared_part)
    d_flat = transposed_times(dispatch_flat, d_returned.reshape(slots, dim + 128))
    d_gates = d_flat[:, dim : dim + experts] + d_flat[:, dim + 64 : dim + 64 + experts]
    d_logits = gates * (d_gates - jnp.sum(gates * d_gates, axis=1, keepdims=True))
    d_moe = (
        d_flat[:, :dim]
        + d_moe_shared.astype(f32)
        + jnp.dot(d_logits, router_full.astype(f32).T, precision=highest)
    )
    grad_router = jnp.dot(moe_in.astype(f32).T, d_logits, precision=highest)
    grad_moe = jnp.sum(d_moe * resid_n, axis=0)
    d_scaled = d_moe * moe_gain_full[None, :]
    d_resid = (
        cot
        + d_scaled * resid_r
        - resid_n * (resid_r * jnp.mean(d_scaled * resid_n, axis=1, keepdims=True))
    )
    d_o = d_resid.astype(bf)
    kappa = jnp.sum(d_o.astype(f32) * added, axis=1) / inner
    for start in range(0, e_mine.shape[0], dim):
        kappa = after(kappa, e_mine[start:])
    kappa_high = kappa.astype(bf)
    kappa_low = (kappa - kappa_high.astype(f32)).astype(bf)
    d_o_ext = jnp.concatenate(
        [d_o, kappa_high[:, None], kappa_low[:, None], jnp.zeros((toks, 126), bf)], axis=1
    )
    d_o_all = lax.all_gather(d_o_ext, "seq", axis=0, tiled=True)
    kappa_all = jnp.sum(d_o_all[:, dim : dim + 2].astype(f32), axis=1, keepdims=True)

    d_gated = times_transposed(d_o_all, jnp.pad(w_out, ((0, 0), (0, 128))))
    grad_out_part = transposed_times(q_low, (q_r * d_o_all[:, :dim].astype(f32)).astype(bf))

    mid_part = jnp.concatenate(
        [
            grad_shared_part,
            grad_router.astype(bf),
            grad_moe[:, None].astype(bf),
            jnp.zeros((dim, 128 - experts - 1), bf),
        ],
        axis=1,
    )
    lane_w = mid_part.shape[1]
    bands = dim // lane_w

    def to_bands(values):
        return jnp.concatenate(
            [values[:, :, band * lane_w : band * lane_w + lane_w] for band in range(bands)], axis=1
        )

    early_part = jnp.concatenate(
        [
            to_bands(grad_out_part.astype(bf).reshape(sh, own_out, dim)),
            to_bands(grad_down_part.reshape(sh, own_down, dim)),
            mid_part.reshape(sh, rows_w, lane_w),
        ],
        axis=1,
    )
    moved_early = to_shards(early_part)

    e_one = halve(e_mine[:cutoff], is_inner, near, d_o_all)
    e_two = halve(e_mine[cutoff:], is_high, far, d_o_all)
    row_values = jnp.concatenate(
        [q_r, kappa_all, x_r, jnp.zeros((seq_rows, 5), f32)], axis=1
    )
    scan_inputs = (proj, mixed, d_gated, row_values, starts, taps_in, head_in, skip_in, w_all)
    chunks = seq_rows // CHUNK
    middle = chunks // 2
    *held, carry, sums = scan_backward(
        (middle, chunks),
        scan_inputs,
        (),
        jnp.zeros((136, gw + keys_w), f32),
        jnp.zeros((24, gw + keys_w), f32),
        (),
    )
    d_proj, back_part, carry, sums = scan_backward(
        (0, middle), scan_inputs, held, carry, sums, (returned, early_part, e_one, e_two)
    )
    d_taps, d_head, d_skip = sums[0:8], sums[8:16, :128], sums[16:24, :gw]
    grad_conv_local = d_taps[:taps]
    grad_offset_local = d_taps[taps]
    grad_bias_local = d_head[0, :gh]
    grad_decay_local = d_head[1, :gh] * decay_rate
    grad_skip_local = jnp.sum(d_skip[0].reshape(gh, per_head), axis=1)
    e_one, e_two = halve(e_one, is_high, far), halve(e_two, is_inner, near)
    back_sum = lax.psum_scatter(back_part, "seq", scatter_dimension=0, tiled=True).astype(f32)
    weighted = (gates.T[:, None, :] * dispatch.astype(f32)).reshape(slots, toks)
    combined = transposed_times(weighted.astype(bf), returned.reshape(slots, dim))
    block_output = ((resid + shared_sum.astype(f32) + combined) * live[:, None]).astype(bf)[None]
    tok_x_r = row_scale(x_tok)
    x_n = x_tok * tok_x_r
    input_grad = (
        d_resid + back_sum - x_n * (tok_x_r * jnp.mean(back_sum * x_tok, axis=1, keepdims=True))
    )[None]

    grad_in_part = transposed_times(x_all, d_proj).astype(bf)
    grad_in_part, moved_early = lax.optimization_barrier((grad_in_part, moved_early))

    def spread(local, count):
        wide = jnp.zeros(local.shape[:-1] + (count,), f32)
        return lax.dynamic_update_slice_in_dim(wide, local, q * local.shape[-1], local.ndim - 1)

    conv_rows = jnp.concatenate([grad_conv_local, grad_offset_local[None]], axis=0)
    conv_wide = jnp.concatenate([spread(conv_rows[:, :gw], inner), conv_rows[:, gw:]], axis=1)
    head_wide = spread(jnp.stack([grad_bias_local, grad_decay_local, grad_skip_local]), heads)
    small_part = jnp.concatenate(
        [
            conv_wide.reshape(taps + 1, sh, conv_own).transpose(1, 0, 2).reshape(sh, -1),
            head_wide.reshape(3, sh, head_own).transpose(1, 0, 2).reshape(sh, -1),
        ],
        axis=1,
    )
    small_count = small_part.shape[1]
    small_part = jnp.pad(
        small_part, ((0, 0), (0, rows_w * small_cols - small_count))
    ).reshape(sh, rows_w, small_cols)
    last_part = grad_in_part + jnp.pad(
        small_part.reshape(dim, small_cols), ((0, 0), (used, total - used - small_cols))
    )
    last_part = last_part.astype(bf)
    early_sum = jnp.sum(moved_early.astype(f32), axis=0).astype(bf)
    rows_sum = lax.ppermute(early_sum[: bands * own_rows], both_axes, backward_pairs)
    e_one, e_two = after(e_one, last_part), after(e_two, last_part)
    e_one, e_two = double(e_one, is_high, far), double(e_two, is_inner, near)
    e_one, e_two = double(e_one, is_inner, near), double(e_two, is_high, far)
    moved_last = to_shards(last_part.reshape(sh, rows_w, total))
    last_sum = jnp.sum(moved_last.astype(f32), axis=0)
    last_sum = after(after(after(last_sum, e_one), e_two), back_sum).astype(bf)
    e_mine = jnp.concatenate([e_one, e_two], axis=0)
    e_other = lax.ppermute(e_mine, "seq", mates)
    grad_e_gate, grad_e_up, grad_e_down = unpack_expert_grads(e_mine, e_other, core)
    side = lax.all_gather(
        jnp.concatenate(
            [rows_sum, early_sum[bands * own_rows :]]
            + [last_sum[:, lane_w * i : lane_w * i + lane_w] for i in range(total // lane_w)],
            axis=0,
        ),
        "seq",
        axis=0,
    )
    gain_out = norm_gain.astype(f32)[:, None]
    (
        grad_in,
        tail_sums,
        grad_out,
        norm_sums,
        grad_down,
        grad_shared_gate,
        grad_shared_up,
        mid_sums,
    ) = assemble(side, in_weight, gain_col, out_weight, gain_out, own_out, own_down)
    grad_norm = norm_sums[:, 0]
    grad_router_weight = mid_sums[:, :experts]
    grad_moe_gain = mid_sums[:, experts]
    grad_mixer_gain = tail_sums[:, 0]
    lane_at = used - (total - 128)
    small_sum = tail_sums[:, lane_at : lane_at + small_cols].reshape(-1)
    at = taps * conv_own
    grad_conv = small_sum[:at].reshape(taps, conv_own)
    grad_offset = small_sum[at : at + conv_own]
    at = at + conv_own
    grad_bias = small_sum[at : at + head_own]
    grad_decay = small_sum[at + head_own : at + 2 * head_own]
    grad_skip = small_sum[at + 2 * head_own : at + 3 * head_own]
    return (
        block_output,
        input_grad,
        grad_mixer_gain,
        grad_in,
        grad_conv,
        grad_offset,
        grad_bias,
        grad_decay,
        grad_skip,
        grad_norm,
        grad_out,
        grad_moe_gain,
        grad_router_weight,
        grad_shared_gate,
        grad_shared_up,
        grad_down,
        grad_e_gate,
        grad_e_up,
        grad_e_down,
    )


def solution(mesh):
    placed = (
        P("shard", "seq", None),
        P("shard"),
        P("shard", "seq", None),
        P("shard", "seq", None),
        P("shard"),
        P("shard", None),
        P(None, "shard"),
        P("shard"),
        P("shard"),
        P("shard"),
        P("shard"),
        P("shard"),
        P("shard", None),
        P("shard"),
        P("shard", None),
        P("shard", None),
        P("shard", None),
        P("shard", None),
        P("shard", None, None),
        P("shard", None, None),
        P("shard", None, None),
    )
    return jax.shard_map(
        on_device,
        mesh=mesh,
        in_specs=placed,
        out_specs=(
            P("shard", "seq", None),
            P("shard", "seq", None),
            P("shard"),
            P("shard", None),
            P(None, "shard"),
            P("shard"),
            P("shard"),
            P("shard"),
            P("shard"),
            P("shard"),
            P("shard", None),
            P("shard"),
            P("shard", None),
            P("shard", None),
            P("shard", None),
            P("shard", None),
            P("shard", None, None),
            P("shard", None, None),
            P("shard", None, None),
        ),
        check_vma=False,
    )
```

```python
import functools

import jax
import jax.numpy as jnp
from jax import lax
from jax.experimental import pallas as pl
from jax.experimental.pallas import tpu as pltpu
from jax.sharding import PartitionSpec as P

CAP = 32


epsilon = 1e-05
highest = lax.Precision.HIGHEST
both_axes = ("seq", "shard")


def times(left, right):
    return jnp.dot(left, right, preferred_element_type=jnp.float32)


def times_transposed(left, right):
    return lax.dot_general(
        left, right, (((1,), (1,)), ((), ())), preferred_element_type=jnp.float32
    )


def transposed_times(left, right):
    return lax.dot_general(
        left, right, (((0,), (0,)), ((), ())), preferred_element_type=jnp.float32
    )


def after(value, other):
    corner = other[(0,) * (other.ndim - 1)][:1].astype(jnp.float32)
    return (value.astype(jnp.float32) + 0.0 * corner).astype(value.dtype)


def silu_slope(values):
    sigma = jax.nn.sigmoid(values)
    return sigma * (1.0 + values * (1.0 - sigma))


def row_scale(values):
    return lax.rsqrt(jnp.mean(values * values, axis=-1, keepdims=True) + epsilon)


CHUNK = 128
WIDE = 384
CONVW = 640
PAIRS = 3
HEADS_HERE = 6


def split_two(values):
    high = values.astype(jnp.bfloat16)
    return high, (values - high.astype(jnp.float32)).astype(jnp.bfloat16)


def ones_times(ones, values):
    high, low = split_two(values)
    return times(ones, high) + times(ones, low)


def times_ones(values, ones):
    high, low = split_two(values)
    return times(high, ones) + times(low, ones)


def transposed_times_ones(values, ones):
    high, low = split_two(values)
    return transposed_times(high, ones) + transposed_times(low, ones)


def grid_of(shape):
    rows = lax.broadcasted_iota(jnp.int32, shape, 0)
    columns = lax.broadcasted_iota(jnp.int32, shape, 1)
    return rows, columns


def mark(condition):
    return jnp.where(condition, 1.0, 0.0).astype(jnp.bfloat16)


def chunk_parts(proj, before, taps_ref, head_ref, pad_ref):
    f32, bf = jnp.float32, jnp.bfloat16
    feed = proj[:, WIDE : WIDE + CONVW].astype(bf).astype(f32)
    pad_ref[0:8, :] = before
    pad_ref[8 : 8 + CHUNK, :] = feed
    conv = taps_ref[4:5, :]
    for tap in range(4):
        conv = conv + taps_ref[tap : tap + 1, :] * pad_ref[5 + tap : 5 + tap + CHUNK, :]
    sig = jax.nn.sigmoid(conv)
    act = conv * sig
    u = act[:, :WIDE]
    key = act[:, WIDE : WIDE + 128].astype(bf)
    query = act[:, WIDE + 128 :].astype(bf)
    step_low = proj[:, WIDE + CONVW :].astype(bf).astype(f32)
    pre = step_low + head_ref[0:1, :]
    rows, columns = grid_of((CHUNK, 128))
    here = columns < HEADS_HERE
    dt = jnp.where(here, jnp.maximum(pre, 0.0) + jnp.log1p(jnp.exp(-jnp.abs(pre))), 0.0)
    la = dt * head_ref[1:2, :]
    lower = mark(rows >= columns)
    cum = ones_times(lower, la)
    end = cum[CHUNK - 1 : CHUNK, :]
    wide_rows, wide_columns = grid_of((128, WIDE))
    widen = mark(wide_columns // 64 == wide_rows)
    dt_w = times_ones(dt, widen)
    e_w = times_ones(jnp.exp(cum), widen)
    w_w = times_ones(jnp.exp(end - cum), widen)
    full_rows, full_columns = grid_of((128, 2 * PAIRS * 128))
    la_full = times_ones(la, mark(full_columns // 128 == full_rows))
    scores = times_transposed(query, key)
    return dict(
        conv=conv, sig=sig, u=u, key=key, query=query, pre=pre, here=here, dt=dt, lower=lower,
        dt_w=dt_w, e_w=e_w, w_w=w_w, la_full=la_full, scores=scores, xs=u * dt_w,
    )


def pair_table(parts, pair):
    rows, columns = grid_of((CHUNK, 256))
    local = columns % 128
    steps = jnp.where(rows > local, parts["la_full"][:, 256 * pair : 256 * pair + 256], 0.0)
    gap = ones_times(parts["lower"], steps)
    causal = rows >= local
    decay = jnp.where(causal, jnp.exp(jnp.where(causal, gap, 0.0)), 0.0)
    scores = parts["scores"]
    return decay, decay * jnp.concatenate([scores, scores], axis=1)


def stack_heads(values, pair):
    both = values[:, 128 * pair : 128 * pair + 128]
    first = lax.broadcasted_iota(jnp.int32, both.shape, 1) < 64
    return jnp.concatenate(
        [jnp.where(first, both, 0.0), jnp.where(first, 0.0, both)], axis=0
    ).astype(jnp.bfloat16)


def front_kernel(
    x_ref, w_in_ref, rows_in_ref, place_ref, taps_ref, head_ref, skip_ref, earlier_0, earlier_1,
    proj_ref, scale_ref, w_ref, out_w_ref, mixed_ref, q_ref, out_ref, square_ref, start_ref,
    state_ref, pad_ref,
):
    f32, bf = jnp.float32, jnp.bfloat16
    width = w_ref.shape[1]

    @pl.when(pl.program_id(0) == 0)
    def _():
        state_ref[...] = jnp.zeros(state_ref.shape, f32)
        pad_ref[CHUNK : CHUNK + 8, :] = jnp.zeros((8, CONVW), f32)
        w_ref[...] = w_in_ref[...].reshape(-1, width)
        folded = rows_in_ref[...].reshape(-1, width)
        out_w_ref[:, :width] = times(place_ref[0], folded).astype(bf)
        rest = out_w_ref.shape[1] - width
        tail = jnp.zeros((out_w_ref.shape[0], rest), f32)
        for part in range(width // rest):
            tail = tail + times(place_ref[1 + part], folded[:, rest * part : rest * part + rest])
        out_w_ref[:, width:] = tail.astype(bf)

    x = x_ref[...]
    scale = row_scale(x.astype(f32))
    proj = times(x, w_ref[...]) * scale
    proj_ref[...] = proj
    scale_ref[...] = scale
    gated = []
    for at in range(0, x.shape[0], CHUNK):
        here = slice(at, at + CHUNK)
        before = pad_ref[CHUNK : CHUNK + 8, :]
        parts = chunk_parts(proj[here], before, taps_ref, head_ref, pad_ref)
        state = state_ref[...]
        start_ref[at // CHUNK] = state
        xs = parts["xs"]
        inside = []
        for pair in range(PAIRS):
            _, table = pair_table(parts, pair)
            inside.append(times(table.astype(bf), stack_heads(xs, pair)))
        across = times(parts["query"], state.astype(bf))
        y = (
            jnp.concatenate(inside, axis=1)
            + parts["e_w"] * across
            + skip_ref[0:1, :] * parts["u"]
        )
        mixed = y.astype(bf)
        mixed_ref[here, :] = mixed
        gate = proj[here, :WIDE]
        q_val = mixed.astype(f32) * (gate * jax.nn.sigmoid(gate))
        gated.append(q_val.astype(bf))
        square_ref[here, :] = jnp.sum(q_val * q_val, axis=1, keepdims=True)
        state_ref[...] = state * parts["e_w"][CHUNK - 1 : CHUNK, :] + transposed_times(
            parts["key"], (xs * parts["w_w"]).astype(bf)
        )
    gated = jnp.concatenate(gated, axis=0)
    q_ref[...] = gated
    out_ref[...] = times(gated, out_w_ref[...]).astype(bf)


def scan_backward_kernel(
    chunks, held_count, proj_ref, prev_ref, mixed_ref, d_o_ref, rows_ref, start_ref, taps_ref,
    head_ref, skip_ref, w_ref, out_w_ref, carry_in_ref, sums_in_ref, *refs,
):
    f32, bf = jnp.float32, jnp.bfloat16
    d_proj_ref, back_ref, carry_ref, sums_ref, state_ref, pad_ref, late_ref = refs[held_count:]
    step = pl.program_id(0)
    chunk = chunks[1] - 1 - step
    d_taps_ref = sums_ref.at[0:8, :]
    d_head_ref = sums_ref.at[8:16, 0:128]
    d_skip_ref = sums_ref.at[16:24, 0:WIDE]

    @pl.when(step == 0)
    def _():
        state_ref[...] = carry_in_ref[0:128, 0:WIDE]
        late_ref[CHUNK : CHUNK + 8, :] = carry_in_ref[128:136, :]
        sums_ref[...] = sums_in_ref[...]

    before = prev_ref[:, WIDE : WIDE + CONVW].astype(bf).astype(f32)
    before = jnp.where(chunk > 0, before, 0.0)
    parts = chunk_parts(proj_ref[...], before, taps_ref, head_ref, pad_ref)
    u, key, query, xs = parts["u"], parts["key"], parts["query"], parts["xs"]
    e_w, w_w, dt_w = parts["e_w"], parts["w_w"], parts["dt_w"]

    gate = proj_ref[:, :WIDE]
    gate_sig = jax.nn.sigmoid(gate)
    gate_act = gate * gate_sig
    mixed = mixed_ref[...].astype(f32)
    q_val = mixed * gate_act
    q_r = rows_ref[:, 0:1]
    dim = out_w_ref.shape[1]
    d_gated = times_transposed(d_o_ref[:, :dim], out_w_ref[...])
    kappa = d_o_ref[:, dim : dim + 1].astype(f32) + d_o_ref[:, dim + 1 : dim + 2].astype(f32)
    d_q = q_r * d_gated - q_val * (q_r * q_r * kappa)
    d_gate = d_q * mixed * (gate_sig * (1.0 + gate * (1.0 - gate_sig)))
    d_y = (d_q * gate_act).astype(bf).astype(f32)

    start = start_ref[0]
    start_low = start.astype(bf)
    d_end = state_ref[...]
    d_end_low = d_end.astype(bf)
    xw = xs * w_w
    ye = d_y * e_w
    ye_low = ye.astype(bf)
    across = times(query, start_low)
    pulled = times(key, d_end_low)
    d_query = times_transposed(ye_low, start_low)
    d_key = times_transposed(xw.astype(bf), d_end_low)
    state_ref[...] = d_end * e_w[CHUNK - 1 : CHUNK, :] + transposed_times(query, ye_low)
    d_scores = jnp.zeros((CHUNK, 128), f32)
    turns = jnp.zeros((CHUNK, 128), f32)
    d_xs = []
    for pair in range(PAIRS):
        decay, table = pair_table(parts, pair)
        xs_two = stack_heads(xs, pair)
        dy_two = stack_heads(d_y, pair)
        d_table = times_transposed(d_y[:, 128 * pair : 128 * pair + 128].astype(bf), xs_two)
        d_decay = d_table * decay
        d_scores = d_scores + d_decay[:, :128] + d_decay[:, 128:]
        d_gap = d_table * table
        table_low = table.astype(bf)
        d_xs.append(
            transposed_times(
                jnp.concatenate([table_low[:, :128], table_low[:, 128:]], axis=0), dy_two
            )
        )
        two_rows, two_columns = grid_of((256, 128))
        own = mark(two_columns == 2 * pair + two_rows // 128)
        turns = turns + times_ones(d_gap, own)
        turns = turns - transposed_times_ones(
            jnp.concatenate([d_gap[:, :128], d_gap[:, 128:]], axis=0), own
        )
    d_xs = jnp.concatenate(d_xs, axis=1) + w_w * pulled
    d_scores_low = d_scores.astype(bf)
    d_query = d_query + times(d_scores_low, key)
    d_key = d_key + transposed_times(d_scores_low, query)

    rows, columns = grid_of((CHUNK, 128))
    upper = mark(columns >= rows)
    strict = mark(columns < rows)
    sum_rows, sum_columns = grid_of((WIDE, 128))
    per_head = mark(sum_rows // 64 == sum_columns)
    end_row = jnp.sum(d_end * start, axis=0, keepdims=True) * e_w[CHUNK - 1 : CHUNK, :]
    wide = ones_times(upper, ye * across) + ones_times(strict, xw * pulled) + end_row
    d_la = ones_times(upper, turns) + times_ones(wide, per_head)
    d_dt = times_ones(d_xs * u, per_head) + d_la * head_ref[1:2, :]
    d_pre = jnp.where(parts["here"], d_dt * jax.nn.sigmoid(parts["pre"]), 0.0)
    d_head_ref[0:1, :] += jnp.sum(d_pre, axis=0, keepdims=True)
    d_head_ref[1:2, :] += jnp.sum(d_la * parts["dt"], axis=0, keepdims=True)
    d_skip_ref[0:1, :] += jnp.sum(d_y * u, axis=0, keepdims=True)

    d_u = d_xs * dt_w + skip_ref[0:1, :] * d_y
    conv, sig = parts["conv"], parts["sig"]
    d_conv = jnp.concatenate([d_u, d_key, d_query], axis=1) * (sig * (1.0 + conv * (1.0 - sig)))
    late_ref[0:CHUNK, :] = d_conv
    d_feed = jnp.zeros((CHUNK, CONVW), f32)
    for tap in range(4):
        d_feed = d_feed + taps_ref[tap : tap + 1, :] * late_ref[3 - tap : 3 - tap + CHUNK, :]
        d_taps_ref[tap : tap + 1, :] += jnp.sum(
            d_conv * pad_ref[5 + tap : 5 + tap + CHUNK, :], axis=0, keepdims=True
        )
    d_taps_ref[4:5, :] += jnp.sum(d_conv, axis=0, keepdims=True)
    late_ref[CHUNK : CHUNK + 8, :] = d_conv[0:8, :]
    carry_ref[0:128, 0:WIDE] = state_ref[...]
    carry_ref[128:136, :] = d_conv[0:8, :]
    scale = rows_ref[:, 1:2]
    d_proj = jnp.concatenate([d_gate, d_feed, d_pre], axis=1) * scale
    d_proj = d_proj.astype(bf)
    d_proj_ref[...] = d_proj
    back_ref[...] = times_transposed(d_proj, w_ref[...]).astype(bf)


def corner_of(array):
    return pl.BlockSpec(
        (1,) * (array.ndim - 2) + (min(16, array.shape[-2]), 128),
        lambda *step: (0,) * array.ndim,
    )


def whole(shape):
    return pl.BlockSpec(shape, lambda step: (0,) * len(shape))


def front(x_all, weights, rows_w, taps, head, skip, *earlier):
    f32, bf = jnp.float32, jnp.bfloat16
    rows, dim = x_all.shape
    sources, _, width = weights.shape
    own = WIDE // sources
    count = own * dim // width
    tile = 2 * CHUNK
    row = jnp.arange(WIDE)[:, None]
    slot = jnp.arange(sources * count)[None, :]
    same = row // own == slot // count
    deep = count - own
    place = [same & (row % own == slot % count)] + [
        same & (row % own // deep == part) & (row % deep + own == slot % count)
        for part in range(own // deep)
    ]
    place = jnp.stack(place).astype(bf)
    by_tile = lambda step: (step, 0)
    chunks = rows // CHUNK
    return pl.pallas_call(
        front_kernel,
        grid=(rows // tile,),
        in_specs=[
            pl.BlockSpec((tile, dim), by_tile),
            pl.BlockSpec((sources, rows_w, width), lambda step: (0, 0, 0)),
            pl.BlockSpec((sources, count, width), lambda step: (0, rows_w // count, 0)),
            whole(place.shape),
            whole(taps.shape),
            whole(head.shape),
            whole(skip.shape),
            *map(corner_of, earlier),
        ],
        out_specs=[
            pl.BlockSpec((tile, width), by_tile),
            pl.BlockSpec((tile, 1), by_tile),
            whole((dim, width)),
            whole((WIDE, dim)),
            pl.BlockSpec((tile, WIDE), by_tile),
            pl.BlockSpec((tile, WIDE), by_tile),
            pl.BlockSpec((tile, dim), by_tile),
            pl.BlockSpec((tile, 1), by_tile),
            pl.BlockSpec((tile // CHUNK, 128, WIDE), lambda step: (step, 0, 0)),
        ],
        out_shape=[
            jax.ShapeDtypeStruct((rows, width), f32),
            jax.ShapeDtypeStruct((rows, 1), f32),
            jax.ShapeDtypeStruct((dim, width), bf),
            jax.ShapeDtypeStruct((WIDE, dim), bf),
            jax.ShapeDtypeStruct((rows, WIDE), bf),
            jax.ShapeDtypeStruct((rows, WIDE), bf),
            jax.ShapeDtypeStruct((rows, dim), bf),
            jax.ShapeDtypeStruct((rows, 1), f32),
            jax.ShapeDtypeStruct((chunks, 128, WIDE), f32),
        ],
        scratch_shapes=[
            pltpu.VMEM((128, WIDE), f32),
            pltpu.VMEM((CHUNK + 8, CONVW), f32),
        ],
        compiler_params=pltpu.CompilerParams(vmem_limit_bytes=52 << 20),
        cost_estimate=pl.CostEstimate(
            flops=16 << 30, bytes_accessed=48 << 20, transcendentals=4 << 20
        ),
        name="front",
    )(x_all, weights, weights, place, taps, head, skip, *earlier)


def scan_backward(chunks, inputs, held, carry, sums, earlier):
    proj, mixed, d_o_all, row_values, starts, taps, head, skip, w_all, w_out = inputs
    rows, width = proj.shape
    dim = w_all.shape[0]
    at = lambda step: chunks[1] - 1 - step
    by_chunk = lambda step: (at(step), 0)
    given = (proj, proj, mixed, d_o_all, row_values, starts, taps, head, skip, w_all, w_out)
    given = given + (carry, sums)
    return pl.pallas_call(
        functools.partial(scan_backward_kernel, chunks, len(held) + len(earlier)),
        grid=(chunks[1] - chunks[0],),
        in_specs=[
            pl.BlockSpec((CHUNK, width), by_chunk),
            pl.BlockSpec(
                (8, width), lambda step: (jnp.maximum(at(step) * (CHUNK // 8) - 1, 0), 0)
            ),
            pl.BlockSpec((CHUNK, WIDE), by_chunk),
            pl.BlockSpec((CHUNK, d_o_all.shape[1]), by_chunk),
            pl.BlockSpec((CHUNK, row_values.shape[1]), by_chunk),
            pl.BlockSpec((1, 128, WIDE), lambda step: (at(step), 0, 0)),
            whole(taps.shape),
            whole(head.shape),
            whole(skip.shape),
            whole(w_all.shape),
            whole(w_out.shape),
            whole(carry.shape),
            whole(sums.shape),
            *[pl.BlockSpec(memory_space=pl.ANY) for _ in held],
            *map(corner_of, earlier),
        ],
        out_specs=[
            pl.BlockSpec((CHUNK, width), by_chunk),
            pl.BlockSpec((CHUNK, dim), by_chunk),
            whole(carry.shape),
            whole(sums.shape),
        ],
        out_shape=[
            jax.ShapeDtypeStruct((rows, width), jnp.bfloat16),
            jax.ShapeDtypeStruct((rows, dim), jnp.bfloat16),
            jax.ShapeDtypeStruct(carry.shape, jnp.float32),
            jax.ShapeDtypeStruct(sums.shape, jnp.float32),
        ],
        scratch_shapes=[
            pltpu.VMEM((128, WIDE), jnp.float32),
            pltpu.VMEM((CHUNK + 8, CONVW), jnp.float32),
            pltpu.VMEM((CHUNK + 8, CONVW), jnp.float32),
        ],
        input_output_aliases={len(given) + i: i for i in range(len(held))},
        compiler_params=pltpu.CompilerParams(vmem_limit_bytes=48 << 20),
        cost_estimate=pl.CostEstimate(
            flops=(1 << 20) if held else (10 << 30), bytes_accessed=1 << 20, transcendentals=0
        ),
        name="scan_backward",
    )(*given, *held, *earlier)


def token_front_kernel(x_ref, out_ref, scale_ref, gain_ref, slots_ref, resid_ref, moe_ref, sent_ref):
    f32, bf = jnp.float32, jnp.bfloat16
    resid = x_ref[...].astype(f32) + out_ref[...].astype(f32) * scale_ref[...]
    resid_ref[...] = resid
    moe_in = (resid * row_scale(resid) * gain_ref[0:1, :]).astype(bf)
    moe_ref[...] = moe_in
    sent_ref[...] = times(slots_ref[...], moe_in).astype(bf)


def token_front(x, out_sum, scale, gain, slots):
    rows, dim = x.shape
    return pl.pallas_call(
        token_front_kernel,
        out_shape=[
            jax.ShapeDtypeStruct((rows, dim), jnp.float32),
            jax.ShapeDtypeStruct((rows, dim), jnp.bfloat16),
            jax.ShapeDtypeStruct((slots.shape[0], dim), jnp.bfloat16),
        ],
        compiler_params=pltpu.CompilerParams(vmem_limit_bytes=24 << 20),
        cost_estimate=pl.CostEstimate(flops=1 << 28, bytes_accessed=5 << 20, transcendentals=0),
        name="token_front",
    )(x, out_sum, scale, gain, slots)


def token_back_kernel(
    back_ref, slots_ref, shared_ref, x_ref, resid_ref, gates_ref, router_ref, gain_ref, cot_ref,
    *refs,
):
    f32, bf = jnp.float32, jnp.bfloat16
    d_o_ref, d_resid_ref, d_logits_ref, d_gain_ref = refs[-4:]
    dim = x_ref.shape[1]
    sums = transposed_times(slots_ref[...], back_ref[...])
    scalars = sums[:, dim:]
    gates = gates_ref[...]
    d_gates = scalars + pltpu.roll(scalars, 64, 1)
    d_logits = gates * (d_gates - jnp.sum(gates * d_gates, axis=1, keepdims=True))
    d_logits_ref[...] = d_logits
    high, low = split_two(d_logits)
    router = router_ref[...]
    d_moe = (
        sums[:, :dim]
        + shared_ref[...].astype(f32)
        + times_transposed(high, router)
        + times_transposed(low, router)
    )
    resid = resid_ref[...]
    scale = row_scale(resid)
    normed = resid * scale
    d_gain_ref[0:1, :] = jnp.sum(d_moe * normed, axis=0, keepdims=True)
    d_gain_ref[1:8, :] = jnp.zeros((7, dim), f32)
    d_scaled = d_moe * gain_ref[0:1, :]
    mean = jnp.mean(d_scaled * normed, axis=1, keepdims=True)
    d_resid = cot_ref[...].astype(f32) + scale * (d_scaled - normed * mean)
    d_resid_ref[...] = d_resid
    d_o = d_resid.astype(bf)
    d_o_ref[:, :dim] = d_o
    added = resid - x_ref[...].astype(f32)
    kappa = jnp.sum(d_o.astype(f32) * added, axis=1, keepdims=True) * (1.0 / (2 * dim))
    kappa_high = kappa.astype(bf).astype(f32)
    lane = lax.broadcasted_iota(jnp.int32, scalars.shape, 1)
    both = jnp.where(lane == 0, kappa_high, jnp.where(lane == 1, kappa - kappa_high, 0.0))
    d_o_ref[:, dim:] = both.astype(bf)


def token_back(back, slots, shared_both, x, resid, gates, w_all, gain, cot, earlier):
    rows, dim = x.shape
    return pl.pallas_call(
        token_back_kernel,
        grid=(1,),
        in_specs=[
            whole(back.shape),
            whole(slots.shape),
            whole((rows, dim)),
            whole(x.shape),
            whole(resid.shape),
            whole(gates.shape),
            pl.BlockSpec((dim, 128), lambda step: (0, w_all.shape[1] // 128 - 1)),
            whole(gain.shape),
            whole(cot.shape),
            *map(corner_of, earlier),
        ],
        out_specs=[
            whole((rows, dim + 128)),
            whole((rows, dim)),
            whole((rows, 128)),
            whole((8, dim)),
        ],
        out_shape=[
            jax.ShapeDtypeStruct((rows, dim + 128), jnp.bfloat16),
            jax.ShapeDtypeStruct((rows, dim), jnp.float32),
            jax.ShapeDtypeStruct((rows, 128), jnp.float32),
            jax.ShapeDtypeStruct((8, dim), jnp.float32),
        ],
        compiler_params=pltpu.CompilerParams(vmem_limit_bytes=32 << 20),
        cost_estimate=pl.CostEstimate(flops=1 << 29, bytes_accessed=8 << 20, transcendentals=0),
        name="token_back",
    )(back, slots, shared_both, x, resid, gates, w_all, gain, cot, *earlier)


def expert_early_kernel(cot_ref, down_ref, earlier_ref, raw_ref):
    cot = cot_ref[...].reshape(-1, cot_ref.shape[-1])
    raw_ref[0] = times_transposed(cot, down_ref[0])


def expert_main_kernel(
    rows_ref, routed_ref, raw_ref, gate_ref, up_ref, router_ref, marks_ref,
    moe_ref, cot_ref, shared_ref, down_ref,
    back_ref, act_ref, scaled_ref, d_g_ref, d_v_ref, both_ref, s_act_ref, d_both_ref,
):
    f32, bf = jnp.float32, jnp.bfloat16
    dim = rows_ref.shape[-1]
    rows = rows_ref[...].reshape(-1, dim)
    routed = routed_ref[...].reshape(-1, 128).astype(f32) > 0.0
    logits = times(rows, router_ref[...])
    top = jnp.max(jnp.where(routed, logits, -1e30), axis=1, keepdims=True)
    powers = jnp.where(routed, jnp.exp(jnp.where(routed, logits - top, 0.0)), 0.0)
    own = jnp.sum(powers * marks_ref[0, 0:1, :], axis=1, keepdims=True)
    gate = own / jnp.maximum(jnp.sum(powers, axis=1, keepdims=True), 1e-30)
    g = times(rows, gate_ref[0])
    v = times(rows, up_ref[0])
    sig = jax.nn.sigmoid(g)
    silu = g * sig
    act = (silu * v).astype(bf)
    act_wide = act.astype(f32)
    raw = raw_ref[0]
    d_gate = jnp.sum(act_wide * raw, axis=1, keepdims=True)
    d_act = gate * raw
    d_g = (d_act * v * (sig * (1.0 + g * (1.0 - sig)))).astype(bf)
    d_v = (d_act * silu).astype(bf)
    d_row = times_transposed(d_g, gate_ref[0]) + times_transposed(d_v, up_ref[0])
    high = d_gate.astype(bf).astype(f32)
    scalars = high * marks_ref[0, 1:2, :] + (d_gate - high) * marks_ref[0, 2:3, :]
    lead = back_ref.shape[:-1]
    back_ref[:, :, :, :dim] = d_row.astype(bf).reshape(*lead, dim)
    back_ref[:, :, :, dim:] = scalars.astype(bf).reshape(*lead, 128)
    act_ref[0] = act
    scaled_ref[0] = (gate * act_wide).astype(bf)
    d_g_ref[0] = d_g
    d_v_ref[0] = d_v

    units = down_ref.shape[0]
    s_both = times(moe_ref[...], shared_ref[...])
    s_gate, s_up = s_both[:, :units], s_both[:, units:]
    s_sig = jax.nn.sigmoid(s_gate)
    s_silu = s_gate * s_sig
    s_act = (s_silu * s_up).astype(bf)
    d_sh = times_transposed(cot_ref[...], down_ref[...])
    d_gs = (d_sh * s_up * (s_sig * (1.0 + s_gate * (1.0 - s_sig)))).astype(bf)
    d_both = jnp.concatenate([d_gs, (d_sh * s_silu).astype(bf)], axis=1)
    both_ref[:, :dim] = times_transposed(d_both, shared_ref[...]).astype(bf)
    both_ref[:, dim:] = times(s_act, down_ref[...]).astype(bf)
    s_act_ref[...] = s_act
    d_both_ref[...] = d_both


def expert_late_kernel(
    rows_ref, cot_ref, act_ref, scaled_ref, d_g_ref, d_v_ref, down_ref,
    out_ref, grad_gate_ref, grad_up_ref, grad_down_ref,
):
    bf = jnp.bfloat16
    dim = rows_ref.shape[-1]
    rows = rows_ref[...].reshape(-1, dim)
    cot = cot_ref[...].reshape(-1, dim)
    out_ref[...] = times(act_ref[0], down_ref[0]).astype(bf).reshape(out_ref.shape)
    units = act_ref.shape[-1]
    grad_gate_ref[0] = transposed_times(rows, d_g_ref[0]).astype(bf)
    grad_up_ref[0] = transposed_times(rows, d_v_ref[0]).astype(bf)
    for block in range(dim // units):
        at = block * units
        grad_down_ref[0, at : at + units] = transposed_times(
            scaled_ref[0], cot[:, block * units : block * units + units]
        ).astype(bf)


def expert_slots(shape, start=0):
    return pl.BlockSpec(
        (shape[0], 1) + tuple(shape[2:]), lambda e: (0, e) + (0,) * (len(shape) - 3) + (start,)
    )


def per_expert(shape):
    return pl.BlockSpec((1,) + tuple(shape[1:]), lambda e: (e,) + (0,) * (len(shape) - 1))


def expert_params(flops, moved):
    return dict(
        compiler_params=pltpu.CompilerParams(vmem_limit_bytes=56 << 20),
        cost_estimate=pl.CostEstimate(flops=flops, bytes_accessed=moved, transcendentals=1 << 19),
    )


def expert_early(cot_rows, down, earlier):
    sources, local, cap, _ = cot_rows.shape
    units, dim = down.shape[1:]
    return pl.pallas_call(
        expert_early_kernel,
        grid=(local,),
        in_specs=[
            expert_slots((sources, local, cap, dim)),
            per_expert(down.shape),
            corner_of(earlier),
        ],
        out_specs=per_expert((local, sources * cap, units)),
        out_shape=jax.ShapeDtypeStruct((local, sources * cap, units), jnp.float32),
        name="expert_early",
        **expert_params(64 << 30, 256 << 20),
    )(cot_rows, down, earlier)


def expert_main(rows, cot_rows, raw, gate, up, w_all, marks, moe_all, cot_all, w_shared, w_down):
    sources, local, cap, dim = rows.shape
    units = gate.shape[2]
    count = sources * cap
    hidden = jax.ShapeDtypeStruct((local, count, units), jnp.bfloat16)
    back = (sources, local, cap, dim + 128)
    seq_rows = moe_all.shape[0]
    shared_units = w_down.shape[0]
    share = lambda width: pl.BlockSpec((seq_rows // local, width), lambda e: (e, 0))
    return pl.pallas_call(
        expert_main_kernel,
        grid=(local,),
        in_specs=[
            expert_slots(rows.shape),
            expert_slots((sources, local, cap, 128), dim // 128),
            per_expert(raw.shape),
            per_expert(gate.shape),
            per_expert(up.shape),
            pl.BlockSpec((dim, 128), lambda e: (0, w_all.shape[1] // 128 - 1)),
            per_expert(marks.shape),
            share(dim),
            share(dim),
            whole(w_shared.shape),
            whole(w_down.shape),
        ],
        out_specs=[expert_slots(back)]
        + [per_expert(hidden.shape)] * 4
        + [share(2 * dim), share(shared_units), share(2 * shared_units)],
        out_shape=[jax.ShapeDtypeStruct(back, jnp.bfloat16)]
        + [hidden] * 4
        + [
            jax.ShapeDtypeStruct((seq_rows, width), jnp.bfloat16)
            for width in (2 * dim, shared_units, 2 * shared_units)
        ],
        name="expert_main",
        **expert_params(8 << 30, 20 << 20),
    )(rows, cot_rows, raw, gate, up, w_all, marks, moe_all, cot_all, w_shared, w_down)


def expert_late(rows, cot_rows, act, scaled, d_g, d_v, down):
    sources, local, cap, dim = rows.shape
    units = down.shape[1]
    grads = (local, dim, units)
    return pl.pallas_call(
        expert_late_kernel,
        grid=(local,),
        in_specs=[expert_slots(rows.shape), expert_slots(rows.shape)]
        + [per_expert(act.shape)] * 4
        + [per_expert(down.shape)],
        out_specs=[
            expert_slots(rows.shape),
            per_expert(grads),
            per_expert(grads),
            per_expert(grads),
        ],
        out_shape=[
            jax.ShapeDtypeStruct(rows.shape, jnp.bfloat16),
            jax.ShapeDtypeStruct(grads, jnp.bfloat16),
            jax.ShapeDtypeStruct(grads, jnp.bfloat16),
            jax.ShapeDtypeStruct(grads, jnp.bfloat16),
        ],
        name="expert_late",
        **expert_params(7 << 30, 24 << 20),
    )(rows, cot_rows, act, scaled, d_g, d_v, down)


def assemble_kernel(
    own_out, own_down, side_ref, in_ref, in_gain_ref, out_ref, out_gain_ref,
    grad_in_ref, tail_ref, grad_out_ref, norm_ref, grad_down_ref, gate_ref, up_ref, mid_ref,
):
    f32 = jnp.float32
    groups = side_ref.shape[0]
    inner = groups * WIDE
    bands = out_ref.shape[1] // WIDE
    rows_w = in_ref.shape[0]
    gain = in_gain_ref[...]
    at_down = bands * own_out
    at_mid = at_down + bands * own_down
    at_in = at_mid + rows_w
    units = gate_ref.shape[1] // groups

    def block(group, start, rows):
        return side_ref[group, start : start + rows, :].astype(f32)

    grad_gain = jnp.zeros((rows_w, 1), f32)
    keys = jnp.zeros((rows_w, 256), f32)
    tail = jnp.zeros((rows_w, 128), f32)
    steps = jnp.zeros((rows_w, 128), f32)
    mid = jnp.zeros((rows_w, 128), f32)
    rows, columns = grid_of((128, 128))

    def put(start, values):
        stop = start + values.shape[1]
        grad_in_ref[:, start:stop] = values * gain
        weight = in_ref[:, start:stop].astype(f32)
        return jnp.sum(weight * values, axis=1, keepdims=True)

    for group in range(groups):
        grad_gain += put(group * WIDE, block(group, at_in, rows_w))
        grad_gain += put(inner + group * WIDE, block(group, at_in + rows_w, rows_w))
        last = block(group, at_in + 2 * rows_w, rows_w)
        keys = keys + last[:, :256]
        tail = tail + last[:, 256:]
        moved = mark((rows < HEADS_HERE) & (columns == rows + HEADS_HERE * group))
        steps = steps + times(last[:, 256:].astype(jnp.bfloat16), moved)
        shared = block(group, at_mid, rows_w)
        gate_ref[:, units * group : units * group + units] = shared[:, :units]
        up_ref[:, units * group : units * group + units] = shared[:, units : 2 * units]
        mid = mid + shared[:, 2 * units :]
    grad_gain += put(2 * inner, keys)
    grad_gain += put(2 * inner + 256, steps[:, : groups * HEADS_HERE])
    lane = lax.broadcasted_iota(jnp.int32, tail.shape, 1)
    tail_ref[...] = jnp.where(lane == 0, grad_gain, tail)
    mid_ref[...] = mid

    for group in range(groups):
        sums = jnp.zeros((own_out, 1), f32)
        mine = slice(own_out * group, own_out * group + own_out)
        for band in range(bands):
            wide = slice(WIDE * band, WIDE * band + WIDE)
            values = block(group, own_out * band, own_out)
            grad_out_ref[mine, wide] = values * out_gain_ref[mine, :]
            sums += jnp.sum(out_ref[mine, wide].astype(f32) * values, axis=1, keepdims=True)
            grad_down_ref[own_down * group : own_down * group + own_down, wide] = block(
                group, at_down + own_down * band, own_down
            )
        norm_ref[mine, :] = sums


def assemble(side, in_weight, in_gain, out_weight, out_gain, own_out, own_down):
    groups = side.shape[0]
    rows, width = in_weight.shape
    out_rows, dim = out_weight.shape
    shapes = [
        (rows, width),
        (rows, 128),
        (out_rows, dim),
        (out_rows, 1),
        (groups * own_down, dim),
        (rows, groups * 128),
        (rows, groups * 128),
        (rows, 128),
    ]
    return pl.pallas_call(
        functools.partial(assemble_kernel, own_out, own_down),
        in_specs=[pl.BlockSpec(memory_space=pltpu.VMEM)] * 5,
        out_specs=[pl.BlockSpec(memory_space=pltpu.VMEM)] * len(shapes),
        out_shape=[jax.ShapeDtypeStruct(shape, jnp.float32) for shape in shapes],
        compiler_params=pltpu.CompilerParams(vmem_limit_bytes=40 << 20),
        cost_estimate=pl.CostEstimate(flops=8 << 20, bytes_accessed=12 << 20, transcendentals=0),
        name="assemble",
    )(side, in_weight, in_gain, out_weight, out_gain)


def fold_rows(values, width):
    rest = values[:, width:]
    count = rest.shape[1] * values.shape[0] // width
    parts = [rest[at : at + count] for at in range(0, values.shape[0], count)]
    return jnp.concatenate([values[:, :width], jnp.concatenate(parts, axis=1)], axis=0)


def unfold_rows(values, dim):
    sources, rows, width = values.shape
    count = rows * width // dim
    rest = dim - width
    parts = [values[:, count:, at : at + rest] for at in range(0, width, rest)]
    return jnp.concatenate([values[:, :count], jnp.concatenate(parts, axis=1)], axis=2)


def gather_rows(values, core, z_at, mates):
    cores = 2
    chips = len(mates) // cores
    column = [values]
    for hop in range(1, chips):
        pairs = [
            (i, (i // cores + hop) % chips * cores + i % cores) for i in range(len(mates))
        ]
        column.append(lax.ppermute(values, "seq", pairs))
    column = jnp.stack(column)
    both = jnp.stack([column, lax.ppermute(column, "seq", mates)], axis=1)
    both = both.reshape((len(mates),) + values.shape)
    ordered = [
        lax.dynamic_index_in_dim(both, (z_at - z) % chips * cores + (c ^ core), 0, keepdims=False)
        for z in range(chips)
        for c in range(cores)
    ]
    return jnp.concatenate(ordered, axis=0)


def halve(values, bit, pairs, start=None):
    f32 = jnp.float32
    parts = values.reshape(2, values.shape[0] // 2, values.shape[1])
    sent = lax.dynamic_index_in_dim(parts, 1 - bit, 0, keepdims=False)
    kept = lax.dynamic_index_in_dim(parts, bit, 0, keepdims=False)
    if start is not None:
        sent = after(sent, start)
    other = lax.ppermute(sent, "seq", pairs)
    return (kept.astype(f32) + other.astype(f32)).astype(jnp.bfloat16)


def double(values, bit, pairs):
    other = lax.ppermute(values, "seq", pairs)
    first = jnp.where(bit == 0, values, other)
    second = jnp.where(bit == 0, other, values)
    return jnp.concatenate([first, second], axis=0)


def unpack_kernel(core_ref, own_ref, other_ref, gate_ref, up_ref, down_ref):
    part = pl.program_id(1)
    block = jnp.where(pl.program_id(0) == 0, own_ref[...], other_ref[...]).astype(jnp.float32)
    units = block.shape[1]

    @pl.when(part == 0)
    def _():
        gate_ref[0] = block

    @pl.when(part == 1)
    def _():
        up_ref[0] = block

    @pl.when(part == 2)
    def _():
        for at in range(0, block.shape[0], units):
            down_ref[0, :, at : at + units] = block[at : at + units]


def unpack_expert_grads(own, other, core):
    rows, units = own.shape
    dim = rows // 3
    to_expert = lambda who, part, core: (jnp.where(who == 0, core[0], 1 - core[0]), 0, 0)
    return pl.pallas_call(
        unpack_kernel,
        grid_spec=pltpu.PrefetchScalarGridSpec(
            num_scalar_prefetch=1,
            grid=(2, 3),
            in_specs=[
                pl.BlockSpec((dim, units), lambda who, part, core: (jnp.where(who == 0, part, 2), 0)),
                pl.BlockSpec((dim, units), lambda who, part, core: (jnp.where(who == 0, 0, part), 0)),
            ],
            out_specs=[
                pl.BlockSpec((1, dim, units), to_expert),
                pl.BlockSpec((1, dim, units), to_expert),
                pl.BlockSpec((1, units, dim), to_expert),
            ],
        ),
        out_shape=[
            jax.ShapeDtypeStruct((2, dim, units), jnp.float32),
            jax.ShapeDtypeStruct((2, dim, units), jnp.float32),
            jax.ShapeDtypeStruct((2, units, dim), jnp.float32),
        ],
        compiler_params=pltpu.CompilerParams(vmem_limit_bytes=40 << 20),
        cost_estimate=pl.CostEstimate(flops=1 << 20, bytes_accessed=28 << 20, transcendentals=0),
        name="unpack_expert_grads",
    )(core.reshape(1), own, other)


def on_device(
    block_input,
    lengths,
    routes,
    out_cotangent,
    mixer_gain,
    in_weight,
    conv_weight,
    conv_bias,
    step_bias,
    decay_log,
    skip_gain,
    norm_gain,
    out_weight,
    moe_gain,
    router_weight,
    shared_gate,
    shared_up,
    shared_down,
    expert_gate,
    expert_up,
    expert_down,
):
    sq = lax.axis_size("seq")
    sh = lax.axis_size("shard")
    q = lax.axis_index("seq")
    f32 = jnp.float32
    bf = jnp.bfloat16
    x_low = block_input[0]
    toks, dim = x_low.shape
    seq_rows = toks * sq
    heads = step_bias.shape[0] * sh
    inner = norm_gain.shape[0] * sh
    conv_all = conv_bias.shape[0] * sh
    keys_w = conv_all - inner
    gh = heads // sq
    gw = inner // sq
    rows_w = in_weight.shape[0]
    experts = router_weight.shape[1]
    local_e = expert_gate.shape[0]
    fs = shared_gate.shape[1]
    gf = fs // sq
    taps = conv_weight.shape[0]
    conv_own = conv_bias.shape[0]
    head_own = step_bias.shape[0]

    gain_col = mixer_gain.astype(f32)[:, None]

    def cols(start, width):
        return lax.dynamic_slice_in_dim(in_weight, start, width, 1)

    w_cols = jnp.concatenate(
        [
            cols(q * gw, gw),
            cols(inner + q * gw, gw),
            in_weight[:, 2 * inner : 2 * inner + keys_w],
            cols(2 * inner + keys_w + q * gh, gh),
        ],
        axis=1,
    )
    w_cols = (w_cols.astype(f32) * gain_col).astype(bf)
    used = 2 * gw + keys_w + gh
    small = jnp.concatenate(
        [conv_weight.reshape(-1), conv_bias, step_bias, decay_log, skip_gain, moe_gain]
    )
    small_cols = -(-(small.shape[0] - rows_w) // rows_w)
    at_router = used + small_cols
    total = -(-(at_router + experts) // 128) * 128
    packed = jnp.concatenate(
        [
            w_cols,
            jnp.zeros((rows_w, small_cols), bf),
            router_weight,
            jnp.zeros((rows_w, total - at_router - experts), bf),
        ],
        axis=1,
    )
    small_all = lax.all_gather(jnp.pad(small, (0, total - small.shape[0])), "shard", axis=0)

    def to_shards(values):
        return lax.all_to_all(values, "shard", split_axis=0, concat_axis=0, tiled=True)

    core, z_at = q % 2, q // 2
    mates = [(i, i ^ 1) for i in range(sq)]
    x_all = gather_rows(x_low, core, z_at, mates)

    out_scaled = (norm_gain.astype(f32)[:, None] * out_weight.astype(f32)).astype(bf)
    own_out = out_weight.shape[0] // sq
    own_down = shared_down.shape[0] // sq
    piece = jnp.concatenate(
        [
            lax.dynamic_slice_in_dim(out_scaled, q * own_out, own_out, 0),
            lax.dynamic_slice_in_dim(shared_down, q * own_down, own_down, 0),
        ],
        axis=0,
    )
    ratio = sh // sq
    forward_pairs = []
    for a in range(sh):
        for j in range(sq):
            s_to = sq * (a % ratio) + j
            q_to = a // ratio
            forward_pairs.append((j * sh + a, q_to * sh + s_to))
    backward_pairs = [(b, a) for a, b in forward_pairs]
    piece = lax.ppermute(piece, both_axes, forward_pairs)
    shared_cols = jnp.concatenate(
        [
            lax.dynamic_slice_in_dim(shared_gate, q * gf, gf, 1),
            lax.dynamic_slice_in_dim(shared_up, q * gf, gf, 1),
        ],
        axis=1,
    )
    fold = rows_w * 2 * gf // dim
    bands = dim // (2 * gf)
    shared_rows = jnp.concatenate(
        [shared_cols[fold * band : fold * band + fold] for band in range(bands)], axis=1
    )
    own_rows = own_out + own_down
    weights = lax.all_gather(
        jnp.concatenate(
            [
                packed,
                fold_rows(piece[:own_out], total),
                fold_rows(jnp.concatenate([piece[own_out:], shared_rows], axis=0), total),
            ],
            axis=0,
        ),
        "shard",
        axis=0,
    )
    folded = rows_w + own_out * dim // total
    second = unfold_rows(weights[:, folded:], dim)
    w_down = second[:, :own_down].reshape(gf, dim)
    w_shared = (
        second[:, own_down:]
        .reshape(sh, fold, bands, 2 * gf)
        .transpose(0, 2, 1, 3)
        .reshape(dim, 2 * gf)
    )

    route_ids = routes[0]
    expert_ids = jnp.arange(experts, dtype=jnp.int32)
    named = jnp.any(route_ids[:, :, None] == expert_ids[None, None, :], axis=1).astype(f32)
    earlier = (
        jnp.arange(toks)[:, None] > jnp.arange(toks)[None, :]
    ).astype(f32)
    rank = jnp.dot(earlier, named)
    dispatch = (
        (named.T[:, None, :] > 0.0)
        & (rank.T[:, None, :] == jnp.arange(CAP, dtype=f32)[None, :, None])
    ).astype(bf)
    slots = experts * CAP
    dispatch_flat = dispatch.reshape(slots, toks)
    live = (q * toks + jnp.arange(toks, dtype=jnp.int32) < lengths[0]).astype(f32)
    cot = out_cotangent[0].astype(f32) * live[:, None]
    cot_low = cot.astype(bf)

    local_slots = (sh, local_e, CAP)

    def in_slots(values):
        return times(dispatch_flat, values).astype(bf).reshape(sh, local_e * CAP, -1)

    def dispatched(sent):
        return to_shards(sent).reshape(*local_slots, -1)

    router_lane = at_router - (total - 128)
    lanes = jnp.arange(128, dtype=jnp.int32)
    named_lanes = jnp.pad(named, ((0, 0), (router_lane, 128 - router_lane - experts)))
    cot_all = gather_rows(after(cot_low, x_all), core, z_at, mates)
    cot_sent = in_slots(jnp.concatenate([cot_low, named_lanes.astype(bf)], axis=1))
    cot_rows = dispatched(cot_sent)

    at = taps * conv_own
    conv_full = (
        small_all[:, :at].reshape(sh, taps, conv_own).transpose(1, 0, 2).reshape(taps, conv_all)
    )
    offset_full = small_all[:, at : at + conv_own].reshape(conv_all)
    at = at + conv_own
    bias_full = small_all[:, at : at + head_own].reshape(heads)
    decay_full = small_all[:, at + head_own : at + 2 * head_own].reshape(heads)
    skip_full = small_all[:, at + 2 * head_own : at + 3 * head_own].reshape(heads)
    gain_at = at + 3 * head_own
    moe_gain_full = small_all[:, gain_at : gain_at + rows_w].reshape(1, dim).astype(f32)
    moe_gain_rows = jnp.broadcast_to(moe_gain_full, (8, dim))

    def group(values, width):
        return lax.dynamic_slice_in_dim(values, q * width, width, values.ndim - 1)

    conv_local = jnp.concatenate([group(conv_full, gw), conv_full[:, inner:]], axis=1).astype(f32)
    offset_local = jnp.concatenate([group(offset_full, gw), offset_full[inner:]]).astype(f32)
    bias_local = group(bias_full, gh).astype(f32)
    decay_local = group(decay_full, gh).astype(f32)
    skip_local = group(skip_full, gh).astype(f32)

    per_head = gw // gh
    taps_in = jnp.concatenate(
        [conv_local, offset_local[None], jnp.zeros((8 - taps - 1, gw + keys_w), f32)], axis=0
    )
    decay_rate = -jnp.exp(decay_local)
    head_in = jnp.pad(jnp.stack([bias_local, decay_rate]), ((0, 6), (0, 128 - gh)))
    skip_in = jnp.broadcast_to(jnp.repeat(skip_local, per_head)[None], (8, gw))
    proj, x_r, w_all, w_out, mixed, q_low, out_part, square_part, starts = front(
        x_all, weights, rows_w, taps_in, head_in, skip_in, cot_sent, cot_all
    )

    out_sum = lax.psum_scatter(out_part, "seq", scatter_dimension=0, tiled=True)
    square = lax.psum(square_part.reshape(sq, toks), "seq")
    q_r = lax.rsqrt(square / inner + epsilon).reshape(seq_rows, 1)
    d_raw = expert_early(cot_rows, expert_down, square)
    tok_r = after(lax.dynamic_slice_in_dim(q_r, q * toks, toks, 0), d_raw)
    x_tok = x_low.astype(f32)
    resid, moe_in, moe_sent = token_front(x_low, out_sum, tok_r, moe_gain_rows, dispatch_flat)

    moe_all = lax.all_gather(moe_in, "seq", axis=0, tiled=True)

    logits = times(moe_in, w_all[:, total - 128 :])
    top = jnp.max(jnp.where(named_lanes > 0.0, logits, -1e30), axis=1, keepdims=True)
    powers = jnp.where(
        named_lanes > 0.0, jnp.exp(jnp.where(named_lanes > 0.0, logits - top, 0.0)), 0.0
    )
    gates = powers / jnp.sum(powers, axis=1, keepdims=True)
    rows = dispatched(moe_sent.reshape(sh, local_e * CAP, dim))
    own_ids = lax.axis_index("shard") * local_e + jnp.arange(local_e, dtype=jnp.int32)
    marks = jnp.stack(
        [own_ids + router_lane, own_ids + router_lane, own_ids + router_lane + 64] + [jnp.full_like(own_ids, -1)] * 5, axis=1
    )
    marks = (marks[:, :, None] == lanes[None, None, :]).astype(f32)

    back_rows, e_act, e_scaled, d_g, d_v, both_part, s_act, d_both = expert_main(
        rows,
        cot_rows,
        d_raw,
        expert_gate,
        expert_up,
        w_all,
        marks,
        moe_all,
        cot_all,
        w_shared,
        w_down,
    )
    shared_both = lax.psum_scatter(both_part, "seq", scatter_dimension=0, tiled=True)
    shared_sum = shared_both[:, dim:]
    d_returned = to_shards(back_rows.reshape(sh, local_e * CAP, dim + 128))
    e_out, *e_grads = expert_late(rows, cot_rows, e_act, e_scaled, d_g, d_v, expert_down)
    d_returned, e_out = lax.optimization_barrier((d_returned, e_out))
    returned = to_shards(e_out.reshape(sh, local_e * CAP, dim))

    near = [(i, 2 * ((i // 2) ^ 1) + i % 2) for i in range(sq)]
    far = [(i, 2 * (sq // 2 - 1 - i // 2) + i % 2) for i in range(sq)]
    is_inner = ((z_at == 1) | (z_at == 2)).astype(jnp.int32)
    is_high = (z_at >= 2).astype(jnp.int32)
    e_parts = [halve(part.reshape(-1, part.shape[2]), core, mates) for part in e_grads]
    e_mine = jnp.concatenate(e_parts, axis=0)
    cutoff = e_mine.shape[0] // 2

    grad_down_part = transposed_times(s_act, cot_all).astype(bf)
    grad_shared_part = transposed_times(moe_all, d_both).astype(bf)
    d_o_ext, d_resid, d_logits, d_moe_gain = token_back(
        d_returned.reshape(slots, dim + 128),
        dispatch_flat,
        shared_both,
        x_low,
        resid,
        gates,
        w_all,
        moe_gain_rows,
        cot_low,
        (grad_down_part, grad_shared_part, *e_parts),
    )
    grad_router = jnp.dot(moe_in.astype(f32).T, d_logits, precision=highest)
    grad_router = grad_router + jnp.pad(d_moe_gain[0][:, None], ((0, 0), (0, 127)))
    d_o_all = lax.all_gather(d_o_ext, "seq", axis=0, tiled=True)

    grad_out_part = transposed_times(q_low, (q_r * d_o_all[:, :dim].astype(f32)).astype(bf))

    mid_part = jnp.concatenate(
        [
            grad_shared_part,
            grad_router.astype(bf),
        ],
        axis=1,
    )
    lane_w = mid_part.shape[1]
    bands = dim // lane_w

    def to_bands(values):
        return jnp.concatenate(
            [values[:, :, band * lane_w : band * lane_w + lane_w] for band in range(bands)], axis=1
        )

    early_part = jnp.concatenate(
        [
            to_bands(grad_out_part.astype(bf).reshape(sh, own_out, dim)),
            to_bands(grad_down_part.reshape(sh, own_down, dim)),
            mid_part.reshape(sh, rows_w, lane_w),
        ],
        axis=1,
    )
    moved_early = to_shards(early_part)

    e_one = halve(e_mine[:cutoff], is_inner, near, d_o_all)
    e_two = halve(e_mine[cutoff:], is_high, far, d_o_all)
    row_values = jnp.concatenate(
        [q_r, x_r, jnp.zeros((seq_rows, 6), f32)], axis=1
    )
    scan_inputs = (proj, mixed, d_o_all, row_values, starts, taps_in, head_in, skip_in, w_all, w_out)
    chunks = seq_rows // CHUNK
    middle = chunks // 2
    *held, carry, sums = scan_backward(
        (middle, chunks),
        scan_inputs,
        (),
        jnp.zeros((136, gw + keys_w), f32),
        jnp.zeros((24, gw + keys_w), f32),
        (),
    )
    d_proj, back_part, carry, sums = scan_backward(
        (0, middle), scan_inputs, held, carry, sums, (returned, early_part, e_one, e_two)
    )
    d_taps, d_head, d_skip = sums[0:8], sums[8:16, :128], sums[16:24, :gw]
    grad_conv_local = d_taps[:taps]
    grad_offset_local = d_taps[taps]
    grad_bias_local = d_head[0, :gh]
    grad_decay_local = d_head[1, :gh] * decay_rate
    grad_skip_local = jnp.sum(d_skip[0].reshape(gh, per_head), axis=1)
    e_one, e_two = halve(e_one, is_high, far), halve(e_two, is_inner, near)
    back_sum = lax.psum_scatter(back_part, "seq", scatter_dimension=0, tiled=True).astype(f32)
    route_gates = gates[:, router_lane : router_lane + experts]
    weighted = (route_gates.T[:, None, :] * dispatch.astype(f32)).reshape(slots, toks)
    combined = transposed_times(weighted.astype(bf), returned.reshape(slots, dim))
    block_output = ((resid + shared_sum.astype(f32) + combined) * live[:, None]).astype(bf)[None]
    tok_x_r = row_scale(x_tok)
    x_n = x_tok * tok_x_r
    input_grad = (
        d_resid + back_sum - x_n * (tok_x_r * jnp.mean(back_sum * x_tok, axis=1, keepdims=True))
    )[None]

    grad_in_part = transposed_times(x_all, d_proj).astype(bf)
    grad_in_part, moved_early = lax.optimization_barrier((grad_in_part, moved_early))

    def spread(local, count):
        wide = jnp.zeros(local.shape[:-1] + (count,), f32)
        return lax.dynamic_update_slice_in_dim(wide, local, q * local.shape[-1], local.ndim - 1)

    conv_rows = jnp.concatenate([grad_conv_local, grad_offset_local[None]], axis=0)
    conv_wide = jnp.concatenate([spread(conv_rows[:, :gw], inner), conv_rows[:, gw:]], axis=1)
    head_wide = spread(jnp.stack([grad_bias_local, grad_decay_local, grad_skip_local]), heads)
    small_part = jnp.concatenate(
        [
            conv_wide.reshape(taps + 1, sh, conv_own).transpose(1, 0, 2).reshape(sh, -1),
            head_wide.reshape(3, sh, head_own).transpose(1, 0, 2).reshape(sh, -1),
        ],
        axis=1,
    )
    small_count = small_part.shape[1]
    small_part = jnp.pad(
        small_part, ((0, 0), (0, rows_w * small_cols - small_count))
    ).reshape(sh, rows_w, small_cols)
    last_part = grad_in_part + jnp.pad(
        small_part.reshape(dim, small_cols), ((0, 0), (used, total - used - small_cols))
    )
    last_part = last_part.astype(bf)
    early_sum = jnp.sum(moved_early.astype(f32), axis=0).astype(bf)
    rows_sum = lax.ppermute(early_sum[: bands * own_rows], both_axes, backward_pairs)
    e_one, e_two = after(e_one, last_part), after(e_two, last_part)
    e_one, e_two = double(e_one, is_high, far), double(e_two, is_inner, near)
    e_one, e_two = double(e_one, is_inner, near), double(e_two, is_high, far)
    moved_last = to_shards(last_part.reshape(sh, rows_w, total))
    last_sum = jnp.sum(moved_last.astype(f32), axis=0)
    last_sum = after(after(after(last_sum, e_one), e_two), back_sum).astype(bf)
    e_mine = jnp.concatenate([e_one, e_two], axis=0)
    e_other = lax.ppermute(e_mine, "seq", mates)
    grad_e_gate, grad_e_up, grad_e_down = unpack_expert_grads(e_mine, e_other, core)
    side = lax.all_gather(
        jnp.concatenate(
            [rows_sum, early_sum[bands * own_rows :]]
            + [last_sum[:, lane_w * i : lane_w * i + lane_w] for i in range(total // lane_w)],
            axis=0,
        ),
        "seq",
        axis=0,
    )
    gain_out = norm_gain.astype(f32)[:, None]
    (
        grad_in,
        tail_sums,
        grad_out,
        norm_sums,
        grad_down,
        grad_shared_gate,
        grad_shared_up,
        mid_sums,
    ) = assemble(side, in_weight, gain_col, out_weight, gain_out, own_out, own_down)
    grad_norm = norm_sums[:, 0]
    grad_router_weight = mid_sums[:, router_lane : router_lane + experts]
    grad_moe_gain = mid_sums[:, 0]
    grad_mixer_gain = tail_sums[:, 0]
    lane_at = used - (total - 128)
    small_sum = tail_sums[:, lane_at : lane_at + small_cols].reshape(-1)
    at = taps * conv_own
    grad_conv = small_sum[:at].reshape(taps, conv_own)
    grad_offset = small_sum[at : at + conv_own]
    at = at + conv_own
    grad_bias = small_sum[at : at + head_own]
    grad_decay = small_sum[at + head_own : at + 2 * head_own]
    grad_skip = small_sum[at + 2 * head_own : at + 3 * head_own]
    return (
        block_output,
        input_grad,
        grad_mixer_gain,
        grad_in,
        grad_conv,
        grad_offset,
        grad_bias,
        grad_decay,
        grad_skip,
        grad_norm,
        grad_out,
        grad_moe_gain,
        grad_router_weight,
        grad_shared_gate,
        grad_shared_up,
        grad_down,
        grad_e_gate,
        grad_e_up,
        grad_e_down,
    )


def solution(mesh):
    placed = (
        P("shard", "seq", None),
        P("shard"),
        P("shard", "seq", None),
        P("shard", "seq", None),
        P("shard"),
        P("shard", None),
        P(None, "shard"),
        P("shard"),
        P("shard"),
        P("shard"),
        P("shard"),
        P("shard"),
        P("shard", None),
        P("shard"),
        P("shard", None),
        P("shard", None),
        P("shard", None),
        P("shard", None),
        P("shard", None, None),
        P("shard", None, None),
        P("shard", None, None),
    )
    return jax.shard_map(
        on_device,
        mesh=mesh,
        in_specs=placed,
        out_specs=(
            P("shard", "seq", None),
            P("shard", "seq", None),
            P("shard"),
            P("shard", None),
            P(None, "shard"),
            P("shard"),
            P("shard"),
            P("shard"),
            P("shard"),
            P("shard"),
            P("shard", None),
            P("shard"),
            P("shard", None),
            P("shard", None),
            P("shard", None),
            P("shard", None),
            P("shard", None, None),
            P("shard", None, None),
            P("shard", None, None),
        ),
        check_vma=False,
    )
```

```python
import functools

import jax
import jax.numpy as jnp
from jax import lax
from jax.experimental import pallas as pl
from jax.experimental.pallas import tpu as pltpu
from jax.sharding import PartitionSpec as P

CAP = 32
VMEM_LIMIT = 60 << 20


epsilon = 1e-05
highest = lax.Precision.HIGHEST
both_axes = ("seq", "shard")


def times(left, right):
    return jnp.dot(left, right, preferred_element_type=jnp.float32)


def times_transposed(left, right):
    return lax.dot_general(
        left, right, (((1,), (1,)), ((), ())), preferred_element_type=jnp.float32
    )


def transposed_times(left, right):
    return lax.dot_general(
        left, right, (((0,), (0,)), ((), ())), preferred_element_type=jnp.float32
    )


def after(value, *others):
    corners = [o[(0,) * (o.ndim - 1)][:1].astype(jnp.float32) for o in others]
    return (value.astype(jnp.float32) + 0.0 * sum(corners)).astype(value.dtype)


def silu_slope(values):
    sigma = jax.nn.sigmoid(values)
    return sigma * (1.0 + values * (1.0 - sigma))


def row_scale(values):
    return lax.rsqrt(jnp.mean(values * values, axis=-1, keepdims=True) + epsilon)


CHUNK = 128
WIDE = 384
CONVW = 640
PAIRS = 3
HEADS_HERE = 6


def split_two(values):
    high = values.astype(jnp.bfloat16)
    return high, (values - high.astype(jnp.float32)).astype(jnp.bfloat16)


def ones_times(ones, values):
    high, low = split_two(values)
    return times(ones, high) + times(ones, low)


def times_ones(values, ones):
    high, low = split_two(values)
    return times(high, ones) + times(low, ones)


def transposed_times_ones(values, ones):
    high, low = split_two(values)
    return transposed_times(high, ones) + transposed_times(low, ones)


def grid_of(shape):
    rows = lax.broadcasted_iota(jnp.int32, shape, 0)
    columns = lax.broadcasted_iota(jnp.int32, shape, 1)
    return rows, columns


def mark(condition):
    return jnp.where(condition, 1.0, 0.0).astype(jnp.bfloat16)


def chunk_parts(proj, before, taps_ref, head_ref, pad_ref):
    f32, bf = jnp.float32, jnp.bfloat16
    feed = proj[:, WIDE : WIDE + CONVW].astype(bf).astype(f32)
    pad_ref[0:8, :] = before
    pad_ref[8 : 8 + CHUNK, :] = feed
    conv = taps_ref[4:5, :]
    for tap in range(4):
        conv = conv + taps_ref[tap : tap + 1, :] * pad_ref[5 + tap : 5 + tap + CHUNK, :]
    sig = jax.nn.sigmoid(conv)
    act = conv * sig
    u = act[:, :WIDE]
    key = act[:, WIDE : WIDE + 128].astype(bf)
    query = act[:, WIDE + 128 :].astype(bf)
    step_low = proj[:, WIDE + CONVW :].astype(bf).astype(f32)
    pre = step_low + head_ref[0:1, :]
    rows, columns = grid_of((CHUNK, 128))
    here = columns < HEADS_HERE
    dt = jnp.where(here, jnp.maximum(pre, 0.0) + jnp.log1p(jnp.exp(-jnp.abs(pre))), 0.0)
    la = dt * head_ref[1:2, :]
    lower = mark(rows >= columns)
    cum = ones_times(lower, la)
    end = cum[CHUNK - 1 : CHUNK, :]
    wide_rows, wide_columns = grid_of((128, WIDE))
    widen = mark(wide_columns // 64 == wide_rows)
    dt_w = times_ones(dt, widen)
    e_w = times_ones(jnp.exp(cum), widen)
    w_w = times_ones(jnp.exp(end - cum), widen)
    full_rows, full_columns = grid_of((128, 2 * PAIRS * 128))
    la_full = times_ones(la, mark(full_columns // 128 == full_rows))
    scores = times_transposed(query, key)
    return dict(
        conv=conv, sig=sig, u=u, key=key, query=query, pre=pre, here=here, dt=dt, lower=lower,
        dt_w=dt_w, e_w=e_w, w_w=w_w, la_full=la_full, scores=scores, xs=u * dt_w,
    )


def pair_table(parts, pair):
    rows, columns = grid_of((CHUNK, 256))
    local = columns % 128
    steps = jnp.where(rows > local, parts["la_full"][:, 256 * pair : 256 * pair + 256], 0.0)
    gap = ones_times(parts["lower"], steps)
    causal = rows >= local
    decay = jnp.where(causal, jnp.exp(jnp.where(causal, gap, 0.0)), 0.0)
    scores = parts["scores"]
    return decay, decay * jnp.concatenate([scores, scores], axis=1)


def stack_heads(values, pair):
    both = values[:, 128 * pair : 128 * pair + 128]
    first = lax.broadcasted_iota(jnp.int32, both.shape, 1) < 64
    return jnp.concatenate(
        [jnp.where(first, both, 0.0), jnp.where(first, 0.0, both)], axis=0
    ).astype(jnp.bfloat16)


def front_kernel(
    x_ref, w_in_ref, rows_in_ref, place_ref, taps_ref, head_ref, skip_ref,
    proj_ref, scale_ref, w_ref, out_w_ref, mixed_ref, q_ref, out_ref, square_ref, start_ref,
    state_ref, pad_ref,
):
    f32, bf = jnp.float32, jnp.bfloat16
    width = w_ref.shape[1]

    @pl.when(pl.program_id(0) == 0)
    def _():
        state_ref[...] = jnp.zeros(state_ref.shape, f32)
        pad_ref[CHUNK : CHUNK + 8, :] = jnp.zeros((8, CONVW), f32)
        w_ref[...] = w_in_ref[...].reshape(-1, width)
        folded = rows_in_ref[...].reshape(-1, width)
        out_w_ref[:, :width] = times(place_ref[0], folded).astype(bf)
        rest = out_w_ref.shape[1] - width
        tail = jnp.zeros((out_w_ref.shape[0], rest), f32)
        for part in range(width // rest):
            tail = tail + times(place_ref[1 + part], folded[:, rest * part : rest * part + rest])
        out_w_ref[:, width:] = tail.astype(bf)

    x = x_ref[...]
    scale = row_scale(x.astype(f32))
    proj = times(x, w_ref[...]) * scale
    proj_ref[...] = proj
    scale_ref[...] = scale
    gated = []
    for at in range(0, x.shape[0], CHUNK):
        here = slice(at, at + CHUNK)
        before = pad_ref[CHUNK : CHUNK + 8, :]
        parts = chunk_parts(proj[here], before, taps_ref, head_ref, pad_ref)
        state = state_ref[...]
        start_ref[at // CHUNK] = state
        xs = parts["xs"]
        inside = []
        for pair in range(PAIRS):
            _, table = pair_table(parts, pair)
            inside.append(times(table.astype(bf), stack_heads(xs, pair)))
        across = times(parts["query"], state.astype(bf))
        y = (
            jnp.concatenate(inside, axis=1)
            + parts["e_w"] * across
            + skip_ref[0:1, :] * parts["u"]
        )
        mixed = y.astype(bf)
        mixed_ref[here, :] = mixed
        gate = proj[here, :WIDE]
        q_val = mixed.astype(f32) * (gate * jax.nn.sigmoid(gate))
        gated.append(q_val.astype(bf))
        square_ref[here, :] = jnp.sum(q_val * q_val, axis=1, keepdims=True)
        state_ref[...] = state * parts["e_w"][CHUNK - 1 : CHUNK, :] + transposed_times(
            parts["key"], (xs * parts["w_w"]).astype(bf)
        )
    gated = jnp.concatenate(gated, axis=0)
    q_ref[...] = gated
    out_ref[...] = times(gated, out_w_ref[...]).astype(bf)


def scan_backward_kernel(
    chunks, held_count, proj_ref, prev_ref, mixed_ref, d_o_ref, rows_ref, start_ref, taps_ref,
    head_ref, skip_ref, w_ref, out_w_ref, carry_in_ref, sums_in_ref, *refs,
):
    f32, bf = jnp.float32, jnp.bfloat16
    d_proj_ref, back_ref, carry_ref, sums_ref, state_ref, pad_ref, late_ref = refs[held_count:]
    step = pl.program_id(0)
    chunk = chunks[1] - 1 - step
    d_taps_ref = sums_ref.at[0:8, :]
    d_head_ref = sums_ref.at[8:16, 0:128]
    d_skip_ref = sums_ref.at[16:24, 0:WIDE]

    @pl.when(step == 0)
    def _():
        state_ref[...] = carry_in_ref[0:128, 0:WIDE]
        late_ref[CHUNK : CHUNK + 8, :] = carry_in_ref[128:136, :]
        sums_ref[...] = sums_in_ref[...]

    before = prev_ref[:, WIDE : WIDE + CONVW].astype(bf).astype(f32)
    before = jnp.where(chunk > 0, before, 0.0)
    parts = chunk_parts(proj_ref[...], before, taps_ref, head_ref, pad_ref)
    u, key, query, xs = parts["u"], parts["key"], parts["query"], parts["xs"]
    e_w, w_w, dt_w = parts["e_w"], parts["w_w"], parts["dt_w"]

    gate = proj_ref[:, :WIDE]
    gate_sig = jax.nn.sigmoid(gate)
    gate_act = gate * gate_sig
    mixed = mixed_ref[...].astype(f32)
    q_val = mixed * gate_act
    q_r = rows_ref[:, 0:1]
    dim = out_w_ref.shape[1]
    d_gated = times_transposed(d_o_ref[:, :dim], out_w_ref[...])
    kappa = d_o_ref[:, dim : dim + 1].astype(f32) + d_o_ref[:, dim + 1 : dim + 2].astype(f32)
    d_q = q_r * d_gated - q_val * (q_r * q_r * kappa)
    d_gate = d_q * mixed * (gate_sig * (1.0 + gate * (1.0 - gate_sig)))
    d_y = (d_q * gate_act).astype(bf).astype(f32)

    start = start_ref[0]
    start_low = start.astype(bf)
    d_end = state_ref[...]
    d_end_low = d_end.astype(bf)
    xw = xs * w_w
    ye = d_y * e_w
    ye_low = ye.astype(bf)
    across = times(query, start_low)
    pulled = times(key, d_end_low)
    d_query = times_transposed(ye_low, start_low)
    d_key = times_transposed(xw.astype(bf), d_end_low)
    state_ref[...] = d_end * e_w[CHUNK - 1 : CHUNK, :] + transposed_times(query, ye_low)
    d_scores = jnp.zeros((CHUNK, 128), f32)
    turns = jnp.zeros((CHUNK, 128), f32)
    d_xs = []
    for pair in range(PAIRS):
        decay, table = pair_table(parts, pair)
        xs_two = stack_heads(xs, pair)
        dy_two = stack_heads(d_y, pair)
        d_table = times_transposed(d_y[:, 128 * pair : 128 * pair + 128].astype(bf), xs_two)
        d_decay = d_table * decay
        d_scores = d_scores + d_decay[:, :128] + d_decay[:, 128:]
        d_gap = d_table * table
        table_low = table.astype(bf)
        d_xs.append(
            transposed_times(
                jnp.concatenate([table_low[:, :128], table_low[:, 128:]], axis=0), dy_two
            )
        )
        two_rows, two_columns = grid_of((256, 128))
        own = mark(two_columns == 2 * pair + two_rows // 128)
        turns = turns + times_ones(d_gap, own)
        turns = turns - transposed_times_ones(
            jnp.concatenate([d_gap[:, :128], d_gap[:, 128:]], axis=0), own
        )
    d_xs = jnp.concatenate(d_xs, axis=1) + w_w * pulled
    d_scores_low = d_scores.astype(bf)
    d_query = d_query + times(d_scores_low, key)
    d_key = d_key + transposed_times(d_scores_low, query)

    rows, columns = grid_of((CHUNK, 128))
    upper = mark(columns >= rows)
    strict = mark(columns < rows)
    sum_rows, sum_columns = grid_of((WIDE, 128))
    per_head = mark(sum_rows // 64 == sum_columns)
    end_row = jnp.sum(d_end * start, axis=0, keepdims=True) * e_w[CHUNK - 1 : CHUNK, :]
    wide = ones_times(upper, ye * across) + ones_times(strict, xw * pulled) + end_row
    d_la = ones_times(upper, turns) + times_ones(wide, per_head)
    d_dt = times_ones(d_xs * u, per_head) + d_la * head_ref[1:2, :]
    d_pre = jnp.where(parts["here"], d_dt * jax.nn.sigmoid(parts["pre"]), 0.0)
    d_head_ref[0:1, :] += jnp.sum(d_pre, axis=0, keepdims=True)
    d_head_ref[1:2, :] += jnp.sum(d_la * parts["dt"], axis=0, keepdims=True)
    d_skip_ref[0:1, :] += jnp.sum(d_y * u, axis=0, keepdims=True)

    d_u = d_xs * dt_w + skip_ref[0:1, :] * d_y
    conv, sig = parts["conv"], parts["sig"]
    d_conv = jnp.concatenate([d_u, d_key, d_query], axis=1) * (sig * (1.0 + conv * (1.0 - sig)))
    late_ref[0:CHUNK, :] = d_conv
    d_feed = jnp.zeros((CHUNK, CONVW), f32)
    for tap in range(4):
        d_feed = d_feed + taps_ref[tap : tap + 1, :] * late_ref[3 - tap : 3 - tap + CHUNK, :]
        d_taps_ref[tap : tap + 1, :] += jnp.sum(
            d_conv * pad_ref[5 + tap : 5 + tap + CHUNK, :], axis=0, keepdims=True
        )
    d_taps_ref[4:5, :] += jnp.sum(d_conv, axis=0, keepdims=True)
    late_ref[CHUNK : CHUNK + 8, :] = d_conv[0:8, :]
    carry_ref[0:128, 0:WIDE] = state_ref[...]
    carry_ref[128:136, :] = d_conv[0:8, :]
    scale = rows_ref[:, 1:2]
    d_proj = jnp.concatenate([d_gate, d_feed, d_pre], axis=1) * scale
    d_proj = d_proj.astype(bf)
    d_proj_ref[...] = d_proj
    back_ref[...] = times_transposed(d_proj, w_ref[...]).astype(bf)


def corner_of(array):
    return pl.BlockSpec(
        (1,) * (array.ndim - 2) + (min(16, array.shape[-2]), 128),
        lambda *step: (0,) * array.ndim,
    )


def whole(shape):
    return pl.BlockSpec(shape, lambda step: (0,) * len(shape))


def front(x_all, weights, rows_w, taps, head, skip):
    f32, bf = jnp.float32, jnp.bfloat16
    rows, dim = x_all.shape
    sources, _, width = weights.shape
    own = WIDE // sources
    count = own * dim // width
    tile = 2 * CHUNK
    row = jnp.arange(WIDE)[:, None]
    slot = jnp.arange(sources * count)[None, :]
    same = row // own == slot // count
    deep = count - own
    place = [same & (row % own == slot % count)] + [
        same & (row % own // deep == part) & (row % deep + own == slot % count)
        for part in range(own // deep)
    ]
    place = jnp.stack(place).astype(bf)
    by_tile = lambda step: (step, 0)
    chunks = rows // CHUNK
    return pl.pallas_call(
        front_kernel,
        grid=(rows // tile,),
        in_specs=[
            pl.BlockSpec((tile, dim), by_tile),
            pl.BlockSpec((sources, rows_w, width), lambda step: (0, 0, 0)),
            pl.BlockSpec((sources, count, width), lambda step: (0, rows_w // count, 0)),
            whole(place.shape),
            whole(taps.shape),
            whole(head.shape),
            whole(skip.shape),
        ],
        out_specs=[
            pl.BlockSpec((tile, width), by_tile),
            pl.BlockSpec((tile, 1), by_tile),
            whole((dim, width)),
            whole((WIDE, dim)),
            pl.BlockSpec((tile, WIDE), by_tile),
            pl.BlockSpec((tile, WIDE), by_tile),
            pl.BlockSpec((tile, dim), by_tile),
            pl.BlockSpec((tile, 1), by_tile),
            pl.BlockSpec((tile // CHUNK, 128, WIDE), lambda step: (step, 0, 0)),
        ],
        out_shape=[
            jax.ShapeDtypeStruct((rows, width), f32),
            jax.ShapeDtypeStruct((rows, 1), f32),
            jax.ShapeDtypeStruct((dim, width), bf),
            jax.ShapeDtypeStruct((WIDE, dim), bf),
            jax.ShapeDtypeStruct((rows, WIDE), bf),
            jax.ShapeDtypeStruct((rows, WIDE), bf),
            jax.ShapeDtypeStruct((rows, dim), bf),
            jax.ShapeDtypeStruct((rows, 1), f32),
            jax.ShapeDtypeStruct((chunks, 128, WIDE), f32),
        ],
        scratch_shapes=[
            pltpu.VMEM((128, WIDE), f32),
            pltpu.VMEM((CHUNK + 8, CONVW), f32),
        ],
        compiler_params=pltpu.CompilerParams(vmem_limit_bytes=VMEM_LIMIT),
        cost_estimate=pl.CostEstimate(
            flops=16 << 30, bytes_accessed=48 << 20, transcendentals=4 << 20
        ),
        name="front",
    )(x_all, weights, weights, place, taps, head, skip)


def scan_backward(chunks, inputs, held, carry, sums):
    proj, mixed, d_o_all, row_values, starts, taps, head, skip, w_all, w_out = inputs
    rows, width = proj.shape
    dim = w_all.shape[0]
    at = lambda step: chunks[1] - 1 - step
    by_chunk = lambda step: (at(step), 0)
    given = (proj, proj, mixed, d_o_all, row_values, starts, taps, head, skip, w_all, w_out)
    given = given + (carry, sums)
    return pl.pallas_call(
        functools.partial(scan_backward_kernel, chunks, len(held)),
        grid=(chunks[1] - chunks[0],),
        in_specs=[
            pl.BlockSpec((CHUNK, width), by_chunk),
            pl.BlockSpec(
                (8, width), lambda step: (jnp.maximum(at(step) * (CHUNK // 8) - 1, 0), 0)
            ),
            pl.BlockSpec((CHUNK, WIDE), by_chunk),
            pl.BlockSpec((CHUNK, d_o_all.shape[1]), by_chunk),
            pl.BlockSpec((CHUNK, row_values.shape[1]), by_chunk),
            pl.BlockSpec((1, 128, WIDE), lambda step: (at(step), 0, 0)),
            whole(taps.shape),
            whole(head.shape),
            whole(skip.shape),
            whole(w_all.shape),
            whole(w_out.shape),
            whole(carry.shape),
            whole(sums.shape),
            *[pl.BlockSpec(memory_space=pl.ANY) for _ in held],
        ],
        out_specs=[
            pl.BlockSpec((CHUNK, width), by_chunk),
            pl.BlockSpec((CHUNK, dim), by_chunk),
            whole(carry.shape),
            whole(sums.shape),
        ],
        out_shape=[
            jax.ShapeDtypeStruct((rows, width), jnp.bfloat16),
            jax.ShapeDtypeStruct((rows, dim), jnp.bfloat16),
            jax.ShapeDtypeStruct(carry.shape, jnp.float32),
            jax.ShapeDtypeStruct(sums.shape, jnp.float32),
        ],
        scratch_shapes=[
            pltpu.VMEM((128, WIDE), jnp.float32),
            pltpu.VMEM((CHUNK + 8, CONVW), jnp.float32),
            pltpu.VMEM((CHUNK + 8, CONVW), jnp.float32),
        ],
        input_output_aliases={len(given) + i: i for i in range(len(held))},
        compiler_params=pltpu.CompilerParams(vmem_limit_bytes=VMEM_LIMIT),
        cost_estimate=pl.CostEstimate(
            flops=(1 << 20) if held else (10 << 30), bytes_accessed=1 << 20, transcendentals=0
        ),
        name="scan_backward",
    )(*given, *held)


def token_front_kernel(
    x_ref, out_ref, scale_ref, gain_ref, slots_ref, router_ref, named_ref,
    resid_ref, moe_ref, sent_ref, gates_ref,
):
    f32, bf = jnp.float32, jnp.bfloat16
    resid = x_ref[...].astype(f32) + out_ref[...].astype(f32) * scale_ref[...]
    resid_ref[...] = resid
    moe_in = (resid * row_scale(resid) * gain_ref[0:1, :]).astype(bf)
    moe_ref[...] = moe_in
    sent_ref[...] = times(slots_ref[...], moe_in).astype(bf)
    named = named_ref[...] > 0.0
    logits = times(moe_in, router_ref[...])
    top = jnp.max(jnp.where(named, logits, -1e30), axis=1, keepdims=True)
    powers = jnp.where(named, jnp.exp(jnp.where(named, logits - top, 0.0)), 0.0)
    gates_ref[...] = powers / jnp.sum(powers, axis=1, keepdims=True)


def token_front(x, out_sum, scale, gain, slots, w_all, named):
    rows, dim = x.shape
    return pl.pallas_call(
        token_front_kernel,
        grid=(1,),
        in_specs=[
            whole(x.shape),
            whole(out_sum.shape),
            whole(scale.shape),
            whole(gain.shape),
            whole(slots.shape),
            pl.BlockSpec((dim, 128), lambda step: (0, w_all.shape[1] // 128 - 1)),
            whole(named.shape),
        ],
        out_specs=[
            whole((rows, dim)),
            whole((rows, dim)),
            whole((slots.shape[0], dim)),
            whole((rows, 128)),
        ],
        out_shape=[
            jax.ShapeDtypeStruct((rows, dim), jnp.float32),
            jax.ShapeDtypeStruct((rows, dim), jnp.bfloat16),
            jax.ShapeDtypeStruct((slots.shape[0], dim), jnp.bfloat16),
            jax.ShapeDtypeStruct((rows, 128), jnp.float32),
        ],
        compiler_params=pltpu.CompilerParams(vmem_limit_bytes=VMEM_LIMIT),
        cost_estimate=pl.CostEstimate(flops=1 << 28, bytes_accessed=5 << 20, transcendentals=0),
        name="token_front",
    )(x, out_sum, scale, gain, slots, w_all, named)


def token_back_kernel(
    back_ref, slots_ref, shared_ref, x_ref, resid_ref, gates_ref, router_ref, gain_ref, cot_ref,
    d_o_ref, d_resid_ref, d_logits_ref, d_gain_ref,
):
    f32, bf = jnp.float32, jnp.bfloat16
    dim = x_ref.shape[1]
    sums = transposed_times(slots_ref[...], back_ref[...])
    scalars = sums[:, dim:]
    gates = gates_ref[...]
    d_gates = scalars + pltpu.roll(scalars, 64, 1)
    d_logits = gates * (d_gates - jnp.sum(gates * d_gates, axis=1, keepdims=True))
    d_logits_ref[...] = d_logits
    high, low = split_two(d_logits)
    router = router_ref[...]
    d_moe = (
        sums[:, :dim]
        + shared_ref[...].astype(f32)
        + times_transposed(high, router)
        + times_transposed(low, router)
    )
    resid = resid_ref[...]
    scale = row_scale(resid)
    normed = resid * scale
    d_gain_ref[0:1, :] = jnp.sum(d_moe * normed, axis=0, keepdims=True)
    d_gain_ref[1:8, :] = jnp.zeros((7, dim), f32)
    d_scaled = d_moe * gain_ref[0:1, :]
    mean = jnp.mean(d_scaled * normed, axis=1, keepdims=True)
    d_resid = cot_ref[...].astype(f32) + scale * (d_scaled - normed * mean)
    d_resid_ref[...] = d_resid
    d_o = d_resid.astype(bf)
    d_o_ref[:, :dim] = d_o
    added = resid - x_ref[...].astype(f32)
    kappa = jnp.sum(d_o.astype(f32) * added, axis=1, keepdims=True) * (1.0 / (2 * dim))
    kappa_high = kappa.astype(bf).astype(f32)
    lane = lax.broadcasted_iota(jnp.int32, scalars.shape, 1)
    both = jnp.where(lane == 0, kappa_high, jnp.where(lane == 1, kappa - kappa_high, 0.0))
    d_o_ref[:, dim:] = both.astype(bf)


def token_back(back, slots, shared_both, x, resid, gates, w_all, gain, cot):
    rows, dim = x.shape
    return pl.pallas_call(
        token_back_kernel,
        grid=(1,),
        in_specs=[
            whole(back.shape),
            whole(slots.shape),
            whole((rows, dim)),
            whole(x.shape),
            whole(resid.shape),
            whole(gates.shape),
            pl.BlockSpec((dim, 128), lambda step: (0, w_all.shape[1] // 128 - 1)),
            whole(gain.shape),
            whole(cot.shape),
        ],
        out_specs=[
            whole((rows, dim + 128)),
            whole((rows, dim)),
            whole((rows, 128)),
            whole((8, dim)),
        ],
        out_shape=[
            jax.ShapeDtypeStruct((rows, dim + 128), jnp.bfloat16),
            jax.ShapeDtypeStruct((rows, dim), jnp.float32),
            jax.ShapeDtypeStruct((rows, 128), jnp.float32),
            jax.ShapeDtypeStruct((8, dim), jnp.float32),
        ],
        compiler_params=pltpu.CompilerParams(vmem_limit_bytes=VMEM_LIMIT),
        cost_estimate=pl.CostEstimate(flops=1 << 29, bytes_accessed=8 << 20, transcendentals=0),
        name="token_back",
    )(back, slots, shared_both, x, resid, gates, w_all, gain, cot)


def expert_early_kernel(cot_ref, down_ref, earlier_ref, raw_ref):
    cot = cot_ref[...].reshape(-1, cot_ref.shape[-1])
    raw_ref[0] = times_transposed(cot, down_ref[0])


def expert_main_kernel(
    rows_ref, routed_ref, raw_ref, gate_ref, up_ref, router_ref, marks_ref,
    moe_ref, cot_ref, shared_ref, down_ref,
    back_ref, act_ref, scaled_ref, d_g_ref, d_v_ref, both_ref, s_act_ref, d_both_ref,
):
    f32, bf = jnp.float32, jnp.bfloat16
    dim = rows_ref.shape[-1]
    rows = rows_ref[...].reshape(-1, dim)
    routed = routed_ref[...].reshape(-1, 128).astype(f32) > 0.0
    logits = times(rows, router_ref[...])
    top = jnp.max(jnp.where(routed, logits, -1e30), axis=1, keepdims=True)
    powers = jnp.where(routed, jnp.exp(jnp.where(routed, logits - top, 0.0)), 0.0)
    own = jnp.sum(powers * marks_ref[0, 0:1, :], axis=1, keepdims=True)
    gate = own / jnp.maximum(jnp.sum(powers, axis=1, keepdims=True), 1e-30)
    g = times(rows, gate_ref[0])
    v = times(rows, up_ref[0])
    sig = jax.nn.sigmoid(g)
    silu = g * sig
    act = (silu * v).astype(bf)
    act_wide = act.astype(f32)
    raw = raw_ref[0]
    d_gate = jnp.sum(act_wide * raw, axis=1, keepdims=True)
    d_act = gate * raw
    d_g = (d_act * v * (sig * (1.0 + g * (1.0 - sig)))).astype(bf)
    d_v = (d_act * silu).astype(bf)
    d_row = times_transposed(d_g, gate_ref[0]) + times_transposed(d_v, up_ref[0])
    high = d_gate.astype(bf).astype(f32)
    scalars = high * marks_ref[0, 1:2, :] + (d_gate - high) * marks_ref[0, 2:3, :]
    lead = back_ref.shape[:-1]
    back_ref[:, :, :, :dim] = d_row.astype(bf).reshape(*lead, dim)
    back_ref[:, :, :, dim:] = scalars.astype(bf).reshape(*lead, 128)
    act_ref[0] = act
    scaled_ref[0] = (gate * act_wide).astype(bf)
    d_g_ref[0] = d_g
    d_v_ref[0] = d_v

    units = down_ref.shape[0]
    s_both = times(moe_ref[...], shared_ref[...])
    s_gate, s_up = s_both[:, :units], s_both[:, units:]
    s_sig = jax.nn.sigmoid(s_gate)
    s_silu = s_gate * s_sig
    s_act = (s_silu * s_up).astype(bf)
    d_sh = times_transposed(cot_ref[...], down_ref[...])
    d_gs = (d_sh * s_up * (s_sig * (1.0 + s_gate * (1.0 - s_sig)))).astype(bf)
    d_both = jnp.concatenate([d_gs, (d_sh * s_silu).astype(bf)], axis=1)
    both_ref[:, :dim] = times_transposed(d_both, shared_ref[...]).astype(bf)
    both_ref[:, dim:] = times(s_act, down_ref[...]).astype(bf)
    s_act_ref[...] = s_act
    d_both_ref[...] = d_both


def expert_late_kernel(
    rows_ref, cot_ref, act_ref, scaled_ref, d_g_ref, d_v_ref, down_ref,
    out_ref, grad_gate_ref, grad_up_ref, grad_down_ref,
):
    bf = jnp.bfloat16
    dim = rows_ref.shape[-1]
    rows = rows_ref[...].reshape(-1, dim)
    cot = cot_ref[...].reshape(-1, dim)
    out_ref[...] = times(act_ref[0], down_ref[0]).astype(bf).reshape(out_ref.shape)
    units = act_ref.shape[-1]
    grad_gate_ref[0] = transposed_times(rows, d_g_ref[0]).astype(bf)
    grad_up_ref[0] = transposed_times(rows, d_v_ref[0]).astype(bf)
    for block in range(dim // units):
        at = block * units
        grad_down_ref[0, at : at + units] = transposed_times(
            scaled_ref[0], cot[:, block * units : block * units + units]
        ).astype(bf)


def expert_slots(shape, start=0):
    return pl.BlockSpec(
        (shape[0], 1) + tuple(shape[2:]), lambda e: (0, e) + (0,) * (len(shape) - 3) + (start,)
    )


def per_expert(shape):
    return pl.BlockSpec((1,) + tuple(shape[1:]), lambda e: (e,) + (0,) * (len(shape) - 1))


def expert_params(flops, moved):
    return dict(
        compiler_params=pltpu.CompilerParams(vmem_limit_bytes=VMEM_LIMIT),
        cost_estimate=pl.CostEstimate(flops=flops, bytes_accessed=moved, transcendentals=1 << 19),
    )


def expert_early(cot_rows, down, earlier):
    sources, local, cap, _ = cot_rows.shape
    units, dim = down.shape[1:]
    return pl.pallas_call(
        expert_early_kernel,
        grid=(local,),
        in_specs=[
            expert_slots((sources, local, cap, dim)),
            per_expert(down.shape),
            corner_of(earlier),
        ],
        out_specs=per_expert((local, sources * cap, units)),
        out_shape=jax.ShapeDtypeStruct((local, sources * cap, units), jnp.float32),
        name="expert_early",
        **expert_params(64 << 30, 256 << 20),
    )(cot_rows, down, earlier)


def expert_main(rows, cot_rows, raw, gate, up, w_all, marks, moe_all, cot_all, w_shared, w_down):
    sources, local, cap, dim = rows.shape
    units = gate.shape[2]
    count = sources * cap
    hidden = jax.ShapeDtypeStruct((local, count, units), jnp.bfloat16)
    back = (sources, local, cap, dim + 128)
    seq_rows = moe_all.shape[0]
    shared_units = w_down.shape[0]
    share = lambda width: pl.BlockSpec((seq_rows // local, width), lambda e: (e, 0))
    return pl.pallas_call(
        expert_main_kernel,
        grid=(local,),
        in_specs=[
            expert_slots(rows.shape),
            expert_slots((sources, local, cap, 128), dim // 128),
            per_expert(raw.shape),
            per_expert(gate.shape),
            per_expert(up.shape),
            pl.BlockSpec((dim, 128), lambda e: (0, w_all.shape[1] // 128 - 1)),
            per_expert(marks.shape),
            share(dim),
            share(dim),
            whole(w_shared.shape),
            whole(w_down.shape),
        ],
        out_specs=[expert_slots(back)]
        + [per_expert(hidden.shape)] * 4
        + [share(2 * dim), share(shared_units), share(2 * shared_units)],
        out_shape=[jax.ShapeDtypeStruct(back, jnp.bfloat16)]
        + [hidden] * 4
        + [
            jax.ShapeDtypeStruct((seq_rows, width), jnp.bfloat16)
            for width in (2 * dim, shared_units, 2 * shared_units)
        ],
        name="expert_main",
        **expert_params(8 << 30, 20 << 20),
    )(rows, cot_rows, raw, gate, up, w_all, marks, moe_all, cot_all, w_shared, w_down)


def expert_late(rows, cot_rows, act, scaled, d_g, d_v, down):
    sources, local, cap, dim = rows.shape
    units = down.shape[1]
    grads = (local, dim, units)
    return pl.pallas_call(
        expert_late_kernel,
        grid=(local,),
        in_specs=[expert_slots(rows.shape), expert_slots(rows.shape)]
        + [per_expert(act.shape)] * 4
        + [per_expert(down.shape)],
        out_specs=[
            expert_slots(rows.shape),
            per_expert(grads),
            per_expert(grads),
            per_expert(grads),
        ],
        out_shape=[
            jax.ShapeDtypeStruct(rows.shape, jnp.bfloat16),
            jax.ShapeDtypeStruct(grads, jnp.bfloat16),
            jax.ShapeDtypeStruct(grads, jnp.bfloat16),
            jax.ShapeDtypeStruct(grads, jnp.bfloat16),
        ],
        name="expert_late",
        **expert_params(7 << 30, 24 << 20),
    )(rows, cot_rows, act, scaled, d_g, d_v, down)


def assemble_kernel(
    own_out, own_down, side_ref, in_ref, in_gain_ref, out_ref, out_gain_ref,
    grad_in_ref, tail_ref, grad_out_ref, norm_ref, grad_down_ref, gate_ref, up_ref, mid_ref,
):
    f32 = jnp.float32
    groups = side_ref.shape[0]
    inner = groups * WIDE
    bands = out_ref.shape[1] // WIDE
    rows_w = in_ref.shape[0]
    gain = in_gain_ref[...]
    at_down = bands * own_out
    at_mid = at_down + bands * own_down
    at_in = at_mid + rows_w
    units = gate_ref.shape[1] // groups

    def block(group, start, rows):
        return side_ref[group, start : start + rows, :].astype(f32)

    grad_gain = jnp.zeros((rows_w, 1), f32)
    keys = jnp.zeros((rows_w, 256), f32)
    tail = jnp.zeros((rows_w, 128), f32)
    steps = jnp.zeros((rows_w, 128), f32)
    mid = jnp.zeros((rows_w, 128), f32)
    rows, columns = grid_of((128, 128))

    def put(start, values):
        stop = start + values.shape[1]
        grad_in_ref[:, start:stop] = values * gain
        weight = in_ref[:, start:stop].astype(f32)
        return jnp.sum(weight * values, axis=1, keepdims=True)

    for group in range(groups):
        grad_gain += put(group * WIDE, block(group, at_in, rows_w))
        grad_gain += put(inner + group * WIDE, block(group, at_in + rows_w, rows_w))
        last = block(group, at_in + 2 * rows_w, rows_w)
        keys = keys + last[:, :256]
        tail = tail + last[:, 256:]
        moved = mark((rows < HEADS_HERE) & (columns == rows + HEADS_HERE * group))
        steps = steps + times(last[:, 256:].astype(jnp.bfloat16), moved)
        shared = block(group, at_mid, rows_w)
        gate_ref[:, units * group : units * group + units] = shared[:, :units]
        up_ref[:, units * group : units * group + units] = shared[:, units : 2 * units]
        mid = mid + shared[:, 2 * units :]
    grad_gain += put(2 * inner, keys)
    grad_gain += put(2 * inner + 256, steps[:, : groups * HEADS_HERE])
    lane = lax.broadcasted_iota(jnp.int32, tail.shape, 1)
    tail_ref[...] = jnp.where(lane == 0, grad_gain, tail)
    mid_ref[...] = mid

    for group in range(groups):
        sums = jnp.zeros((own_out, 1), f32)
        mine = slice(own_out * group, own_out * group + own_out)
        for band in range(bands):
            wide = slice(WIDE * band, WIDE * band + WIDE)
            values = block(group, own_out * band, own_out)
            grad_out_ref[mine, wide] = values * out_gain_ref[mine, :]
            sums += jnp.sum(out_ref[mine, wide].astype(f32) * values, axis=1, keepdims=True)
            grad_down_ref[own_down * group : own_down * group + own_down, wide] = block(
                group, at_down + own_down * band, own_down
            )
        norm_ref[mine, :] = sums


def assemble(side, in_weight, in_gain, out_weight, out_gain, own_out, own_down):
    groups = side.shape[0]
    rows, width = in_weight.shape
    out_rows, dim = out_weight.shape
    shapes = [
        (rows, width),
        (rows, 128),
        (out_rows, dim),
        (out_rows, 1),
        (groups * own_down, dim),
        (rows, groups * 128),
        (rows, groups * 128),
        (rows, 128),
    ]
    return pl.pallas_call(
        functools.partial(assemble_kernel, own_out, own_down),
        in_specs=[pl.BlockSpec(memory_space=pltpu.VMEM)] * 5,
        out_specs=[pl.BlockSpec(memory_space=pltpu.VMEM)] * len(shapes),
        out_shape=[jax.ShapeDtypeStruct(shape, jnp.float32) for shape in shapes],
        compiler_params=pltpu.CompilerParams(vmem_limit_bytes=VMEM_LIMIT),
        cost_estimate=pl.CostEstimate(flops=8 << 20, bytes_accessed=12 << 20, transcendentals=0),
        name="assemble",
    )(side, in_weight, in_gain, out_weight, out_gain)


def fold_rows(values, width):
    rest = values[:, width:]
    count = rest.shape[1] * values.shape[0] // width
    parts = [rest[at : at + count] for at in range(0, values.shape[0], count)]
    return jnp.concatenate([values[:, :width], jnp.concatenate(parts, axis=1)], axis=0)


def unfold_rows(values, dim):
    sources, rows, width = values.shape
    count = rows * width // dim
    rest = dim - width
    parts = [values[:, count:, at : at + rest] for at in range(0, width, rest)]
    return jnp.concatenate([values[:, :count], jnp.concatenate(parts, axis=1)], axis=2)


def gather_rows(values, core, z_at, mates):
    cores = 2
    chips = len(mates) // cores
    column = [values]
    for hop in range(1, chips):
        pairs = [
            (i, (i // cores + hop) % chips * cores + i % cores) for i in range(len(mates))
        ]
        column.append(lax.ppermute(values, "seq", pairs))
    column = jnp.stack(column)
    both = jnp.stack([column, lax.ppermute(column, "seq", mates)], axis=1)
    both = both.reshape((len(mates),) + values.shape)
    ordered = [
        lax.dynamic_index_in_dim(both, (z_at - z) % chips * cores + (c ^ core), 0, keepdims=False)
        for z in range(chips)
        for c in range(cores)
    ]
    return jnp.concatenate(ordered, axis=0)


def halve(values, bit, pairs, start=None):
    f32 = jnp.float32
    parts = values.reshape(2, values.shape[0] // 2, values.shape[1])
    sent = lax.dynamic_index_in_dim(parts, 1 - bit, 0, keepdims=False)
    kept = lax.dynamic_index_in_dim(parts, bit, 0, keepdims=False)
    if start is not None:
        sent = after(sent, start)
    other = lax.ppermute(sent, "seq", pairs)
    return (kept.astype(f32) + other.astype(f32)).astype(jnp.bfloat16)


def double(values, bit, pairs):
    other = lax.ppermute(values, "seq", pairs)
    first = jnp.where(bit == 0, values, other)
    second = jnp.where(bit == 0, other, values)
    return jnp.concatenate([first, second], axis=0)


def unpack_kernel(core_ref, own_ref, other_ref, gate_ref, up_ref, down_ref):
    part = pl.program_id(1)
    block = jnp.where(pl.program_id(0) == 0, own_ref[...], other_ref[...]).astype(jnp.float32)
    units = block.shape[1]

    @pl.when(part == 0)
    def _():
        gate_ref[0] = block

    @pl.when(part == 1)
    def _():
        up_ref[0] = block

    @pl.when(part == 2)
    def _():
        for at in range(0, block.shape[0], units):
            down_ref[0, :, at : at + units] = block[at : at + units]


def unpack_expert_grads(own, other, core):
    rows, units = own.shape
    dim = rows // 3
    to_expert = lambda who, part, core: (jnp.where(who == 0, core[0], 1 - core[0]), 0, 0)
    return pl.pallas_call(
        unpack_kernel,
        grid_spec=pltpu.PrefetchScalarGridSpec(
            num_scalar_prefetch=1,
            grid=(2, 3),
            in_specs=[
                pl.BlockSpec((dim, units), lambda who, part, core: (jnp.where(who == 0, part, 2), 0)),
                pl.BlockSpec((dim, units), lambda who, part, core: (jnp.where(who == 0, 0, part), 0)),
            ],
            out_specs=[
                pl.BlockSpec((1, dim, units), to_expert),
                pl.BlockSpec((1, dim, units), to_expert),
                pl.BlockSpec((1, units, dim), to_expert),
            ],
        ),
        out_shape=[
            jax.ShapeDtypeStruct((2, dim, units), jnp.float32),
            jax.ShapeDtypeStruct((2, dim, units), jnp.float32),
            jax.ShapeDtypeStruct((2, units, dim), jnp.float32),
        ],
        compiler_params=pltpu.CompilerParams(vmem_limit_bytes=VMEM_LIMIT),
        cost_estimate=pl.CostEstimate(flops=1 << 20, bytes_accessed=28 << 20, transcendentals=0),
        name="unpack_expert_grads",
    )(core.reshape(1), own, other)


def on_device(
    block_input,
    lengths,
    routes,
    out_cotangent,
    mixer_gain,
    in_weight,
    conv_weight,
    conv_bias,
    step_bias,
    decay_log,
    skip_gain,
    norm_gain,
    out_weight,
    moe_gain,
    router_weight,
    shared_gate,
    shared_up,
    shared_down,
    expert_gate,
    expert_up,
    expert_down,
):
    sq = lax.axis_size("seq")
    sh = lax.axis_size("shard")
    q = lax.axis_index("seq")
    f32 = jnp.float32
    bf = jnp.bfloat16
    x_low = block_input[0]
    toks, dim = x_low.shape
    seq_rows = toks * sq
    heads = step_bias.shape[0] * sh
    inner = norm_gain.shape[0] * sh
    conv_all = conv_bias.shape[0] * sh
    keys_w = conv_all - inner
    gh = heads // sq
    gw = inner // sq
    rows_w = in_weight.shape[0]
    experts = router_weight.shape[1]
    local_e = expert_gate.shape[0]
    fs = shared_gate.shape[1]
    gf = fs // sq
    taps = conv_weight.shape[0]
    conv_own = conv_bias.shape[0]
    head_own = step_bias.shape[0]

    gain_col = mixer_gain.astype(f32)[:, None]

    def cols(start, width):
        return lax.dynamic_slice_in_dim(in_weight, start, width, 1)

    w_cols = jnp.concatenate(
        [
            cols(q * gw, gw),
            cols(inner + q * gw, gw),
            in_weight[:, 2 * inner : 2 * inner + keys_w],
            cols(2 * inner + keys_w + q * gh, gh),
        ],
        axis=1,
    )
    w_cols = (w_cols.astype(f32) * gain_col).astype(bf)
    used = 2 * gw + keys_w + gh
    small = jnp.concatenate(
        [conv_weight.reshape(-1), conv_bias, step_bias, decay_log, skip_gain, moe_gain]
    )
    small_cols = -(-(small.shape[0] - rows_w) // rows_w)
    at_router = used + small_cols
    total = -(-(at_router + experts) // 128) * 128
    packed = jnp.concatenate(
        [
            w_cols,
            jnp.zeros((rows_w, small_cols), bf),
            router_weight,
            jnp.zeros((rows_w, total - at_router - experts), bf),
        ],
        axis=1,
    )
    small_all = lax.all_gather(jnp.pad(small, (0, total - small.shape[0])), "shard", axis=0)

    def to_shards(values):
        return lax.all_to_all(values, "shard", split_axis=0, concat_axis=0, tiled=True)

    core, z_at = q % 2, q // 2
    mates = [(i, i ^ 1) for i in range(sq)]
    x_all = gather_rows(x_low, core, z_at, mates)

    out_scaled = (norm_gain.astype(f32)[:, None] * out_weight.astype(f32)).astype(bf)
    own_out = out_weight.shape[0] // sq
    own_down = shared_down.shape[0] // sq
    piece = jnp.concatenate(
        [
            lax.dynamic_slice_in_dim(out_scaled, q * own_out, own_out, 0),
            lax.dynamic_slice_in_dim(shared_down, q * own_down, own_down, 0),
        ],
        axis=0,
    )
    ratio = sh // sq
    forward_pairs = []
    for a in range(sh):
        for j in range(sq):
            s_to = sq * (a % ratio) + j
            q_to = a // ratio
            forward_pairs.append((j * sh + a, q_to * sh + s_to))
    backward_pairs = [(b, a) for a, b in forward_pairs]
    piece = lax.ppermute(piece, both_axes, forward_pairs)
    shared_cols = jnp.concatenate(
        [
            lax.dynamic_slice_in_dim(shared_gate, q * gf, gf, 1),
            lax.dynamic_slice_in_dim(shared_up, q * gf, gf, 1),
        ],
        axis=1,
    )
    fold = rows_w * 2 * gf // dim
    bands = dim // (2 * gf)
    shared_rows = jnp.concatenate(
        [shared_cols[fold * band : fold * band + fold] for band in range(bands)], axis=1
    )
    own_rows = own_out + own_down
    weights = lax.all_gather(
        jnp.concatenate(
            [
                packed,
                fold_rows(piece[:own_out], total),
                fold_rows(jnp.concatenate([piece[own_out:], shared_rows], axis=0), total),
            ],
            axis=0,
        ),
        "shard",
        axis=0,
    )
    folded = rows_w + own_out * dim // total
    second = unfold_rows(weights[:, folded:], dim)
    w_down = second[:, :own_down].reshape(gf, dim)
    w_shared = (
        second[:, own_down:]
        .reshape(sh, fold, bands, 2 * gf)
        .transpose(0, 2, 1, 3)
        .reshape(dim, 2 * gf)
    )

    route_ids = routes[0]
    expert_ids = jnp.arange(experts, dtype=jnp.int32)
    named = jnp.any(route_ids[:, :, None] == expert_ids[None, None, :], axis=1).astype(f32)
    earlier = (
        jnp.arange(toks)[:, None] > jnp.arange(toks)[None, :]
    ).astype(f32)
    rank = jnp.dot(earlier, named)
    dispatch = (
        (named.T[:, None, :] > 0.0)
        & (rank.T[:, None, :] == jnp.arange(CAP, dtype=f32)[None, :, None])
    ).astype(bf)
    slots = experts * CAP
    dispatch_flat = dispatch.reshape(slots, toks)
    live = (q * toks + jnp.arange(toks, dtype=jnp.int32) < lengths[0]).astype(f32)
    cot = out_cotangent[0].astype(f32) * live[:, None]
    cot_low = cot.astype(bf)

    local_slots = (sh, local_e, CAP)

    def in_slots(values):
        return times(dispatch_flat, values).astype(bf).reshape(sh, local_e * CAP, -1)

    def dispatched(sent):
        return to_shards(sent).reshape(*local_slots, -1)

    router_lane = at_router - (total - 128)
    lanes = jnp.arange(128, dtype=jnp.int32)
    named_lanes = jnp.pad(named, ((0, 0), (router_lane, 128 - router_lane - experts)))
    cot_sent = in_slots(jnp.concatenate([cot_low, named_lanes.astype(bf)], axis=1))
    cot_rows = dispatched(cot_sent)

    at = taps * conv_own
    conv_full = (
        small_all[:, :at].reshape(sh, taps, conv_own).transpose(1, 0, 2).reshape(taps, conv_all)
    )
    offset_full = small_all[:, at : at + conv_own].reshape(conv_all)
    at = at + conv_own
    bias_full = small_all[:, at : at + head_own].reshape(heads)
    decay_full = small_all[:, at + head_own : at + 2 * head_own].reshape(heads)
    skip_full = small_all[:, at + 2 * head_own : at + 3 * head_own].reshape(heads)
    gain_at = at + 3 * head_own
    moe_gain_full = small_all[:, gain_at : gain_at + rows_w].reshape(1, dim).astype(f32)
    moe_gain_rows = jnp.broadcast_to(moe_gain_full, (8, dim))

    def group(values, width):
        return lax.dynamic_slice_in_dim(values, q * width, width, values.ndim - 1)

    conv_local = jnp.concatenate([group(conv_full, gw), conv_full[:, inner:]], axis=1).astype(f32)
    offset_local = jnp.concatenate([group(offset_full, gw), offset_full[inner:]]).astype(f32)
    bias_local = group(bias_full, gh).astype(f32)
    decay_local = group(decay_full, gh).astype(f32)
    skip_local = group(skip_full, gh).astype(f32)

    per_head = gw // gh
    taps_in = jnp.concatenate(
        [conv_local, offset_local[None], jnp.zeros((8 - taps - 1, gw + keys_w), f32)], axis=0
    )
    decay_rate = -jnp.exp(decay_local)
    head_in = jnp.pad(jnp.stack([bias_local, decay_rate]), ((0, 6), (0, 128 - gh)))
    skip_in = jnp.broadcast_to(jnp.repeat(skip_local, per_head)[None], (8, gw))
    proj, x_r, w_all, w_out, mixed, q_low, out_part, square_part, starts = front(
        x_all, weights, rows_w, taps_in, after(head_in, cot_sent), skip_in
    )

    cot_all = lax.all_gather(after(cot_low, weights), "seq", axis=0, tiled=True)
    square_part = after(square_part.reshape(sq, toks), cot_all)
    out_sum = lax.psum_scatter(out_part, "seq", scatter_dimension=0, tiled=True)
    square = lax.psum(square_part, "seq")
    q_r = lax.rsqrt(square / inner + epsilon).reshape(seq_rows, 1)
    d_raw = expert_early(cot_rows, expert_down, square)
    tok_r = after(lax.dynamic_slice_in_dim(q_r, q * toks, toks, 0), d_raw)
    x_tok = x_low.astype(f32)
    resid, moe_in, moe_sent, gates = token_front(
        x_low, out_sum, tok_r, moe_gain_rows, dispatch_flat, w_all, named_lanes
    )

    moe_all = lax.all_gather(moe_in, "seq", axis=0, tiled=True)

    rows = dispatched(moe_sent.reshape(sh, local_e * CAP, dim))
    own_ids = lax.axis_index("shard") * local_e + jnp.arange(local_e, dtype=jnp.int32)
    marks = jnp.stack(
        [own_ids + router_lane, own_ids + router_lane, own_ids + router_lane + 64] + [jnp.full_like(own_ids, -1)] * 5, axis=1
    )
    marks = (marks[:, :, None] == lanes[None, None, :]).astype(f32)

    back_rows, e_act, e_scaled, d_g, d_v, both_part, s_act, d_both = expert_main(
        rows,
        cot_rows,
        d_raw,
        expert_gate,
        expert_up,
        w_all,
        marks,
        moe_all,
        cot_all,
        w_shared,
        w_down,
    )
    shared_both = lax.psum_scatter(both_part, "seq", scatter_dimension=0, tiled=True)
    shared_sum = shared_both[:, dim:]
    d_returned = to_shards(back_rows.reshape(sh, local_e * CAP, dim + 128))
    e_out, *e_grads = expert_late(rows, cot_rows, e_act, e_scaled, d_g, d_v, expert_down)
    d_returned, e_out = lax.optimization_barrier((d_returned, e_out))
    returned = to_shards(e_out.reshape(sh, local_e * CAP, dim))

    near = [(i, 2 * ((i // 2) ^ 1) + i % 2) for i in range(sq)]
    far = [(i, 2 * (sq // 2 - 1 - i // 2) + i % 2) for i in range(sq)]
    is_inner = ((z_at == 1) | (z_at == 2)).astype(jnp.int32)
    is_high = (z_at >= 2).astype(jnp.int32)
    e_parts = [
        halve(part[:, at : at + dim // 2].reshape(dim, -1), core, mates)
        for part in e_grads
        for at in (0, dim // 2)
    ]
    e_mine = jnp.concatenate(e_parts, axis=0)
    cutoff = e_mine.shape[0] // 2

    grad_down_part = transposed_times(s_act, cot_all).astype(bf)
    grad_shared_part = transposed_times(moe_all, d_both).astype(bf)
    d_o_ext, d_resid, d_logits, d_moe_gain = token_back(
        d_returned.reshape(slots, dim + 128),
        dispatch_flat,
        shared_both,
        x_low,
        resid,
        after(gates, grad_down_part, grad_shared_part, *e_parts),
        w_all,
        moe_gain_rows,
        cot_low,
    )
    grad_router = jnp.dot(moe_in.astype(f32).T, d_logits, precision=highest)
    grad_router = grad_router + jnp.pad(d_moe_gain[0][:, None], ((0, 0), (0, 127)))
    d_o_all = lax.all_gather(d_o_ext, "seq", axis=0, tiled=True)

    grad_out_part = transposed_times(q_low, (q_r * d_o_all[:, :dim].astype(f32)).astype(bf))

    mid_part = jnp.concatenate(
        [
            grad_shared_part,
            grad_router.astype(bf),
        ],
        axis=1,
    )
    lane_w = mid_part.shape[1]
    bands = dim // lane_w

    def to_bands(values):
        return jnp.concatenate(
            [values[:, :, band * lane_w : band * lane_w + lane_w] for band in range(bands)], axis=1
        )

    early_part = jnp.concatenate(
        [
            to_bands(grad_out_part.astype(bf).reshape(sh, own_out, dim)),
            to_bands(grad_down_part.reshape(sh, own_down, dim)),
            mid_part.reshape(sh, rows_w, lane_w),
        ],
        axis=1,
    )
    moved_early = to_shards(early_part)

    e_one = halve(e_mine[:cutoff], is_inner, near, d_o_all)
    e_two = halve(e_mine[cutoff:], is_high, far, d_o_all)
    row_values = jnp.concatenate(
        [q_r, x_r, jnp.zeros((seq_rows, 6), f32)], axis=1
    )
    scan_inputs = (proj, mixed, d_o_all, row_values, starts, taps_in)
    scan_inputs = scan_inputs + (head_in, skip_in, w_all, w_out)
    chunks = seq_rows // CHUNK
    middle = chunks // 2
    *held, carry, sums = scan_backward(
        (middle, chunks),
        scan_inputs,
        (),
        jnp.zeros((136, gw + keys_w), f32),
        jnp.zeros((24, gw + keys_w), f32),
    )
    route_gates = after(gates, carry)[:, router_lane : router_lane + experts]
    weighted = (route_gates.T[:, None, :] * dispatch.astype(f32)).reshape(slots, toks)
    combined = transposed_times(weighted.astype(bf), returned.reshape(slots, dim))
    carry = after(carry, combined, early_part, e_one, e_two)
    d_proj, back_part, carry, sums = scan_backward(
        (0, middle), scan_inputs, held, carry, sums
    )
    d_taps, d_head, d_skip = sums[0:8], sums[8:16, :128], sums[16:24, :gw]
    grad_conv_local = d_taps[:taps]
    grad_offset_local = d_taps[taps]
    grad_bias_local = d_head[0, :gh]
    grad_decay_local = d_head[1, :gh] * decay_rate
    grad_skip_local = jnp.sum(d_skip[0].reshape(gh, per_head), axis=1)
    e_one, e_two = halve(e_one, is_high, far), halve(e_two, is_inner, near)
    back_sum = lax.psum_scatter(back_part, "seq", scatter_dimension=0, tiled=True).astype(f32)
    block_output = ((resid + shared_sum.astype(f32) + combined) * live[:, None]).astype(bf)[None]
    tok_x_r = row_scale(x_tok)
    x_n = x_tok * tok_x_r
    input_grad = (
        d_resid + back_sum - x_n * (tok_x_r * jnp.mean(back_sum * x_tok, axis=1, keepdims=True))
    )[None]

    grad_in_part = transposed_times(x_all, d_proj).astype(bf)
    grad_in_part, moved_early = lax.optimization_barrier((grad_in_part, moved_early))

    def spread(local, count):
        wide = jnp.zeros(local.shape[:-1] + (count,), f32)
        return lax.dynamic_update_slice_in_dim(wide, local, q * local.shape[-1], local.ndim - 1)

    conv_rows = jnp.concatenate([grad_conv_local, grad_offset_local[None]], axis=0)
    conv_wide = jnp.concatenate([spread(conv_rows[:, :gw], inner), conv_rows[:, gw:]], axis=1)
    head_wide = spread(jnp.stack([grad_bias_local, grad_decay_local, grad_skip_local]), heads)
    small_part = jnp.concatenate(
        [
            conv_wide.reshape(taps + 1, sh, conv_own).transpose(1, 0, 2).reshape(sh, -1),
            head_wide.reshape(3, sh, head_own).transpose(1, 0, 2).reshape(sh, -1),
        ],
        axis=1,
    )
    small_count = small_part.shape[1]
    small_part = jnp.pad(
        small_part, ((0, 0), (0, rows_w * small_cols - small_count))
    ).reshape(sh, rows_w, small_cols)
    last_part = grad_in_part + jnp.pad(
        small_part.reshape(dim, small_cols), ((0, 0), (used, total - used - small_cols))
    )
    last_part = last_part.astype(bf)
    early_sum = jnp.sum(moved_early.astype(f32), axis=0).astype(bf)
    rows_sum = lax.ppermute(early_sum[: bands * own_rows], both_axes, backward_pairs)
    e_one, e_two = after(e_one, last_part), after(e_two, last_part)
    e_one, e_two = double(e_one, is_high, far), double(e_two, is_inner, near)
    e_one, e_two = double(e_one, is_inner, near), double(e_two, is_high, far)
    moved_last = to_shards(last_part.reshape(sh, rows_w, total))
    last_sum = jnp.sum(moved_last.astype(f32), axis=0)
    last_sum = after(after(after(last_sum, e_one), e_two), back_sum).astype(bf)
    e_mine = jnp.concatenate([e_one, e_two], axis=0)
    e_other = lax.ppermute(e_mine, "seq", mates)
    grad_e_gate, grad_e_up, grad_e_down = unpack_expert_grads(e_mine, e_other, core)
    side = lax.all_gather(
        jnp.concatenate(
            [rows_sum, early_sum[bands * own_rows :]]
            + [last_sum[:, lane_w * i : lane_w * i + lane_w] for i in range(total // lane_w)],
            axis=0,
        ),
        "seq",
        axis=0,
    )
    gain_out = norm_gain.astype(f32)[:, None]
    (
        grad_in,
        tail_sums,
        grad_out,
        norm_sums,
        grad_down,
        grad_shared_gate,
        grad_shared_up,
        mid_sums,
    ) = assemble(side, in_weight, gain_col, out_weight, gain_out, own_out, own_down)
    grad_norm = norm_sums[:, 0]
    grad_router_weight = mid_sums[:, router_lane : router_lane + experts]
    grad_moe_gain = mid_sums[:, 0]
    grad_mixer_gain = tail_sums[:, 0]
    lane_at = used - (total - 128)
    small_sum = tail_sums[:, lane_at : lane_at + small_cols].reshape(-1)
    at = taps * conv_own
    grad_conv = small_sum[:at].reshape(taps, conv_own)
    grad_offset = small_sum[at : at + conv_own]
    at = at + conv_own
    grad_bias = small_sum[at : at + head_own]
    grad_decay = small_sum[at + head_own : at + 2 * head_own]
    grad_skip = small_sum[at + 2 * head_own : at + 3 * head_own]
    return (
        block_output,
        input_grad,
        grad_mixer_gain,
        grad_in,
        grad_conv,
        grad_offset,
        grad_bias,
        grad_decay,
        grad_skip,
        grad_norm,
        grad_out,
        grad_moe_gain,
        grad_router_weight,
        grad_shared_gate,
        grad_shared_up,
        grad_down,
        grad_e_gate,
        grad_e_up,
        grad_e_down,
    )


def solution(mesh):
    placed = (
        P("shard", "seq", None),
        P("shard"),
        P("shard", "seq", None),
        P("shard", "seq", None),
        P("shard"),
        P("shard", None),
        P(None, "shard"),
        P("shard"),
        P("shard"),
        P("shard"),
        P("shard"),
        P("shard"),
        P("shard", None),
        P("shard"),
        P("shard", None),
        P("shard", None),
        P("shard", None),
        P("shard", None),
        P("shard", None, None),
        P("shard", None, None),
        P("shard", None, None),
    )
    return jax.shard_map(
        on_device,
        mesh=mesh,
        in_specs=placed,
        out_specs=(
            P("shard", "seq", None),
            P("shard", "seq", None),
            P("shard"),
            P("shard", None),
            P(None, "shard"),
            P("shard"),
            P("shard"),
            P("shard"),
            P("shard"),
            P("shard"),
            P("shard", None),
            P("shard"),
            P("shard", None),
            P("shard", None),
            P("shard", None),
            P("shard", None),
            P("shard", None, None),
            P("shard", None, None),
            P("shard", None, None),
        ),
        check_vma=False,
    )
```

```python
import functools

import jax
import jax.numpy as jnp
from jax import lax
from jax.experimental import pallas as pl
from jax.experimental.pallas import tpu as pltpu
from jax.sharding import PartitionSpec as P

CAP = 32


epsilon = 1e-05
highest = lax.Precision.HIGHEST
both_axes = ("seq", "shard")


def times(left, right):
    return jnp.dot(left, right, preferred_element_type=jnp.float32)


def times_transposed(left, right):
    return lax.dot_general(
        left, right, (((1,), (1,)), ((), ())), preferred_element_type=jnp.float32
    )


def transposed_times(left, right):
    return lax.dot_general(
        left, right, (((0,), (0,)), ((), ())), preferred_element_type=jnp.float32
    )


def after(value, *others):
    corners = [o[(0,) * (o.ndim - 1)][:1].astype(jnp.float32) for o in others]
    return (value.astype(jnp.float32) + 0.0 * sum(corners)).astype(value.dtype)


def corner_after(values, other):
    at = (0.0 * other[(0,) * other.ndim]).astype(jnp.int32)
    return lax.dynamic_slice(values, (at,) * values.ndim, (1,) * values.ndim)


def silu_slope(values):
    sigma = jax.nn.sigmoid(values)
    return sigma * (1.0 + values * (1.0 - sigma))


def row_scale(values):
    return lax.rsqrt(jnp.mean(values * values, axis=-1, keepdims=True) + epsilon)


CHUNK = 128
WIDE = 384
CONVW = 640
PAIRS = 3
HEADS_HERE = 6


def split_two(values):
    high = values.astype(jnp.bfloat16)
    return high, (values - high.astype(jnp.float32)).astype(jnp.bfloat16)


def ones_times(ones, values):
    high, low = split_two(values)
    return times(ones, high) + times(ones, low)


def times_ones(values, ones):
    high, low = split_two(values)
    return times(high, ones) + times(low, ones)


def transposed_times_ones(values, ones):
    high, low = split_two(values)
    return transposed_times(high, ones) + transposed_times(low, ones)


def grid_of(shape):
    rows = lax.broadcasted_iota(jnp.int32, shape, 0)
    columns = lax.broadcasted_iota(jnp.int32, shape, 1)
    return rows, columns


def mark(condition):
    return jnp.where(condition, 1.0, 0.0).astype(jnp.bfloat16)


def chunk_parts(proj, before, taps_ref, head_ref, pad_ref):
    f32, bf = jnp.float32, jnp.bfloat16
    feed = proj[:, WIDE : WIDE + CONVW].astype(bf).astype(f32)
    pad_ref[0:8, :] = before
    pad_ref[8 : 8 + CHUNK, :] = feed
    conv = taps_ref[4:5, :]
    for tap in range(4):
        conv = conv + taps_ref[tap : tap + 1, :] * pad_ref[5 + tap : 5 + tap + CHUNK, :]
    sig = jax.nn.sigmoid(conv)
    act = conv * sig
    u = act[:, :WIDE]
    key = act[:, WIDE : WIDE + 128].astype(bf)
    query = act[:, WIDE + 128 :].astype(bf)
    step_low = proj[:, WIDE + CONVW :].astype(bf).astype(f32)
    pre = step_low + head_ref[0:1, :]
    rows, columns = grid_of((CHUNK, 128))
    here = columns < HEADS_HERE
    dt = jnp.where(here, jnp.maximum(pre, 0.0) + jnp.log1p(jnp.exp(-jnp.abs(pre))), 0.0)
    la = dt * head_ref[1:2, :]
    lower = mark(rows >= columns)
    cum = ones_times(lower, la)
    end = cum[CHUNK - 1 : CHUNK, :]
    wide_rows, wide_columns = grid_of((128, WIDE))
    widen = mark(wide_columns // 64 == wide_rows)
    dt_w = times_ones(dt, widen)
    e_w = times_ones(jnp.exp(cum), widen)
    w_w = times_ones(jnp.exp(end - cum), widen)
    full_rows, full_columns = grid_of((128, 2 * PAIRS * 128))
    la_full = times_ones(la, mark(full_columns // 128 == full_rows))
    scores = times_transposed(query, key)
    return dict(
        conv=conv, sig=sig, u=u, key=key, query=query, pre=pre, here=here, dt=dt, lower=lower,
        dt_w=dt_w, e_w=e_w, w_w=w_w, la_full=la_full, scores=scores, xs=u * dt_w,
    )


def pair_table(parts, pair):
    rows, columns = grid_of((CHUNK, 256))
    local = columns % 128
    steps = jnp.where(rows > local, parts["la_full"][:, 256 * pair : 256 * pair + 256], 0.0)
    gap = ones_times(parts["lower"], steps)
    causal = rows >= local
    decay = jnp.where(causal, jnp.exp(jnp.where(causal, gap, 0.0)), 0.0)
    scores = parts["scores"]
    return decay, decay * jnp.concatenate([scores, scores], axis=1)


def stack_heads(values, pair):
    both = values[:, 128 * pair : 128 * pair + 128]
    first = lax.broadcasted_iota(jnp.int32, both.shape, 1) < 64
    return jnp.concatenate(
        [jnp.where(first, both, 0.0), jnp.where(first, 0.0, both)], axis=0
    ).astype(jnp.bfloat16)


def front_kernel(
    here_ref, column_ref, other_ref, w_in_ref, rows_in_ref, place_ref, taps_ref, head_ref, skip_ref,
    x_ref, proj_ref, scale_ref, w_ref, out_w_ref, mixed_ref, q_ref, out_ref, square_ref, start_ref,
    state_ref, pad_ref,
):
    f32, bf = jnp.float32, jnp.bfloat16
    width = w_ref.shape[1]

    @pl.when(pl.program_id(0) == 0)
    def _():
        state_ref[...] = jnp.zeros(state_ref.shape, f32)
        pad_ref[CHUNK : CHUNK + 8, :] = jnp.zeros((8, CONVW), f32)
        w_ref[...] = w_in_ref[...].reshape(-1, width)
        folded = rows_in_ref[...].reshape(-1, width)
        out_w_ref[:, :width] = times(place_ref[0], folded).astype(bf)
        rest = out_w_ref.shape[1] - width
        tail = jnp.zeros((out_w_ref.shape[0], rest), f32)
        for part in range(width // rest):
            tail = tail + times(place_ref[1 + part], folded[:, rest * part : rest * part + rest])
        out_w_ref[:, width:] = tail.astype(bf)

    column, other = column_ref[0].astype(f32), other_ref[0].astype(f32)
    first = here_ref[1] == 0
    x = jnp.concatenate(
        [jnp.where(first, column, other), jnp.where(first, other, column)], axis=0
    ).astype(bf)
    x_ref[...] = x
    scale = row_scale(x.astype(f32))
    proj = times(x, w_ref[...]) * scale
    proj_ref[...] = proj
    scale_ref[...] = scale
    gated = []
    for at in range(0, x.shape[0], CHUNK):
        here = slice(at, at + CHUNK)
        before = pad_ref[CHUNK : CHUNK + 8, :]
        parts = chunk_parts(proj[here], before, taps_ref, head_ref, pad_ref)
        state = state_ref[...]
        start_ref[at // CHUNK] = state
        xs = parts["xs"]
        inside = []
        for pair in range(PAIRS):
            _, table = pair_table(parts, pair)
            inside.append(times(table.astype(bf), stack_heads(xs, pair)))
        across = times(parts["query"], state.astype(bf))
        y = (
            jnp.concatenate(inside, axis=1)
            + parts["e_w"] * across
            + skip_ref[0:1, :] * parts["u"]
        )
        mixed = y.astype(bf)
        mixed_ref[here, :] = mixed
        gate = proj[here, :WIDE]
        q_val = mixed.astype(f32) * (gate * jax.nn.sigmoid(gate))
        gated.append(q_val.astype(bf))
        square_ref[here, :] = jnp.sum(q_val * q_val, axis=1, keepdims=True)
        state_ref[...] = state * parts["e_w"][CHUNK - 1 : CHUNK, :] + transposed_times(
            parts["key"], (xs * parts["w_w"]).astype(bf)
        )
    gated = jnp.concatenate(gated, axis=0)
    q_ref[...] = gated
    out_ref[...] = times(gated, out_w_ref[...]).astype(bf)


def scan_backward_kernel(
    chunks, held_count, proj_ref, prev_ref, mixed_ref, d_o_ref, rows_ref, start_ref, taps_ref,
    head_ref, skip_ref, w_ref, out_w_ref, carry_in_ref, sums_in_ref, *refs,
):
    f32, bf = jnp.float32, jnp.bfloat16
    d_proj_ref, back_ref, carry_ref, sums_ref, state_ref, pad_ref, late_ref = refs[held_count:]
    step = pl.program_id(0)
    chunk = chunks[1] - 1 - step
    d_taps_ref = sums_ref.at[0:8, :]
    d_head_ref = sums_ref.at[8:16, 0:128]
    d_skip_ref = sums_ref.at[16:24, 0:WIDE]

    @pl.when(step == 0)
    def _():
        state_ref[...] = carry_in_ref[0:128, 0:WIDE]
        late_ref[CHUNK : CHUNK + 8, :] = carry_in_ref[128:136, :]
        sums_ref[...] = sums_in_ref[...]

    before = prev_ref[:, WIDE : WIDE + CONVW].astype(bf).astype(f32)
    before = jnp.where(chunk > 0, before, 0.0)
    parts = chunk_parts(proj_ref[...], before, taps_ref, head_ref, pad_ref)
    u, key, query, xs = parts["u"], parts["key"], parts["query"], parts["xs"]
    e_w, w_w, dt_w = parts["e_w"], parts["w_w"], parts["dt_w"]

    gate = proj_ref[:, :WIDE]
    gate_sig = jax.nn.sigmoid(gate)
    gate_act = gate * gate_sig
    mixed = mixed_ref[...].astype(f32)
    q_val = mixed * gate_act
    q_r = rows_ref[:, 0:1]
    dim = out_w_ref.shape[1]
    d_gated = times_transposed(d_o_ref[:, :dim], out_w_ref[...])
    kappa = d_o_ref[:, dim : dim + 1].astype(f32) + d_o_ref[:, dim + 1 : dim + 2].astype(f32)
    d_q = q_r * d_gated - q_val * (q_r * q_r * kappa)
    d_gate = d_q * mixed * (gate_sig * (1.0 + gate * (1.0 - gate_sig)))
    d_y = (d_q * gate_act).astype(bf).astype(f32)

    start = start_ref[0]
    start_low = start.astype(bf)
    d_end = state_ref[...]
    d_end_low = d_end.astype(bf)
    xw = xs * w_w
    ye = d_y * e_w
    ye_low = ye.astype(bf)
    across = times(query, start_low)
    pulled = times(key, d_end_low)
    d_query = times_transposed(ye_low, start_low)
    d_key = times_transposed(xw.astype(bf), d_end_low)
    state_ref[...] = d_end * e_w[CHUNK - 1 : CHUNK, :] + transposed_times(query, ye_low)
    d_scores = jnp.zeros((CHUNK, 128), f32)
    turns = jnp.zeros((CHUNK, 128), f32)
    d_xs = []
    for pair in range(PAIRS):
        decay, table = pair_table(parts, pair)
        xs_two = stack_heads(xs, pair)
        dy_two = stack_heads(d_y, pair)
        d_table = times_transposed(d_y[:, 128 * pair : 128 * pair + 128].astype(bf), xs_two)
        d_decay = d_table * decay
        d_scores = d_scores + d_decay[:, :128] + d_decay[:, 128:]
        d_gap = d_table * table
        table_low = table.astype(bf)
        d_xs.append(
            transposed_times(
                jnp.concatenate([table_low[:, :128], table_low[:, 128:]], axis=0), dy_two
            )
        )
        two_rows, two_columns = grid_of((256, 128))
        own = mark(two_columns == 2 * pair + two_rows // 128)
        turns = turns + times_ones(d_gap, own)
        turns = turns - transposed_times_ones(
            jnp.concatenate([d_gap[:, :128], d_gap[:, 128:]], axis=0), own
        )
    d_xs = jnp.concatenate(d_xs, axis=1) + w_w * pulled
    d_scores_low = d_scores.astype(bf)
    d_query = d_query + times(d_scores_low, key)
    d_key = d_key + transposed_times(d_scores_low, query)

    rows, columns = grid_of((CHUNK, 128))
    upper = mark(columns >= rows)
    strict = mark(columns < rows)
    sum_rows, sum_columns = grid_of((WIDE, 128))
    per_head = mark(sum_rows // 64 == sum_columns)
    end_row = jnp.sum(d_end * start, axis=0, keepdims=True) * e_w[CHUNK - 1 : CHUNK, :]
    wide = ones_times(upper, ye * across) + ones_times(strict, xw * pulled) + end_row
    d_la = ones_times(upper, turns) + times_ones(wide, per_head)
    d_dt = times_ones(d_xs * u, per_head) + d_la * head_ref[1:2, :]
    d_pre = jnp.where(parts["here"], d_dt * jax.nn.sigmoid(parts["pre"]), 0.0)
    d_head_ref[0:1, :] += jnp.sum(d_pre, axis=0, keepdims=True)
    d_head_ref[1:2, :] += jnp.sum(d_la * parts["dt"], axis=0, keepdims=True)
    d_skip_ref[0:1, :] += jnp.sum(d_y * u, axis=0, keepdims=True)

    d_u = d_xs * dt_w + skip_ref[0:1, :] * d_y
    conv, sig = parts["conv"], parts["sig"]
    d_conv = jnp.concatenate([d_u, d_key, d_query], axis=1) * (sig * (1.0 + conv * (1.0 - sig)))
    late_ref[0:CHUNK, :] = d_conv
    d_feed = jnp.zeros((CHUNK, CONVW), f32)
    for tap in range(4):
        d_feed = d_feed + taps_ref[tap : tap + 1, :] * late_ref[3 - tap : 3 - tap + CHUNK, :]
        d_taps_ref[tap : tap + 1, :] += jnp.sum(
            d_conv * pad_ref[5 + tap : 5 + tap + CHUNK, :], axis=0, keepdims=True
        )
    d_taps_ref[4:5, :] += jnp.sum(d_conv, axis=0, keepdims=True)
    late_ref[CHUNK : CHUNK + 8, :] = d_conv[0:8, :]
    carry_ref[0:128, 0:WIDE] = state_ref[...]
    carry_ref[128:136, :] = d_conv[0:8, :]
    scale = rows_ref[:, 1:2]
    d_proj = jnp.concatenate([d_gate, d_feed, d_pre], axis=1) * scale
    d_proj = d_proj.astype(bf)
    d_proj_ref[...] = d_proj
    back_ref[...] = times_transposed(d_proj, w_ref[...]).astype(bf)


def corner_of(array):
    return pl.BlockSpec(
        (1,) * (array.ndim - 2) + (min(16, array.shape[-2]), 128),
        lambda *step: (0,) * array.ndim,
    )


def whole(shape):
    return pl.BlockSpec(shape, lambda *step: (0,) * len(shape))


def front(here, column, other, weights, rows_w, taps, head, skip):
    f32, bf = jnp.float32, jnp.bfloat16
    chips, block, dim = column.shape
    rows = 2 * chips * block
    sources, _, width = weights.shape
    own = WIDE // sources
    count = own * dim // width
    tile = 2 * block
    row = jnp.arange(WIDE)[:, None]
    slot = jnp.arange(sources * count)[None, :]
    same = row // own == slot // count
    deep = count - own
    place = [same & (row % own == slot % count)] + [
        same & (row % own // deep == part) & (row % deep + own == slot % count)
        for part in range(own // deep)
    ]
    place = jnp.stack(place).astype(bf)
    by_tile = lambda step, here: (step, 0)
    by_chip = lambda step, here: ((here[0] + chips - step) % chips, 0, 0)
    chunks = rows // CHUNK
    return pl.pallas_call(
        front_kernel,
        grid_spec=pltpu.PrefetchScalarGridSpec(
            num_scalar_prefetch=1,
        grid=(rows // tile,),
        in_specs=[
            pl.BlockSpec((1, block, dim), by_chip),
            pl.BlockSpec((1, block, dim), by_chip),
            pl.BlockSpec((sources, rows_w, width), lambda *step: (0, 0, 0)),
            pl.BlockSpec((sources, count, width), lambda *step: (0, rows_w // count, 0)),
            whole(place.shape),
            whole(taps.shape),
            whole(head.shape),
            whole(skip.shape),
        ],
        out_specs=[
            pl.BlockSpec((tile, dim), by_tile),
            pl.BlockSpec((tile, width), by_tile),
            pl.BlockSpec((tile, 1), by_tile),
            whole((dim, width)),
            whole((WIDE, dim)),
            pl.BlockSpec((tile, WIDE), by_tile),
            pl.BlockSpec((tile, WIDE), by_tile),
            pl.BlockSpec((tile, dim), by_tile),
            pl.BlockSpec((tile, 1), by_tile),
            pl.BlockSpec((tile // CHUNK, 128, WIDE), lambda step, here: (step, 0, 0)),
        ],
        scratch_shapes=[
            pltpu.VMEM((128, WIDE), f32),
            pltpu.VMEM((CHUNK + 8, CONVW), f32),
        ],
        ),
        out_shape=[
            jax.ShapeDtypeStruct((rows, dim), bf),
            jax.ShapeDtypeStruct((rows, width), f32),
            jax.ShapeDtypeStruct((rows, 1), f32),
            jax.ShapeDtypeStruct((dim, width), bf),
            jax.ShapeDtypeStruct((WIDE, dim), bf),
            jax.ShapeDtypeStruct((rows, WIDE), bf),
            jax.ShapeDtypeStruct((rows, WIDE), bf),
            jax.ShapeDtypeStruct((rows, dim), bf),
            jax.ShapeDtypeStruct((rows, 1), f32),
            jax.ShapeDtypeStruct((chunks, 128, WIDE), f32),
        ],
        compiler_params=pltpu.CompilerParams(vmem_limit_bytes=52 << 20),
        cost_estimate=pl.CostEstimate(
            flops=16 << 30, bytes_accessed=48 << 20, transcendentals=4 << 20
        ),
        name="front",
    )(here, column, other, weights, weights, place, taps, head, skip)


def scan_backward(chunks, inputs, held, carry, sums):
    proj, mixed, d_o_all, row_values, starts, taps, head, skip, w_all, w_out = inputs
    rows, width = proj.shape
    dim = w_all.shape[0]
    at = lambda step: chunks[1] - 1 - step
    by_chunk = lambda step: (at(step), 0)
    given = (proj, proj, mixed, d_o_all, row_values, starts, taps, head, skip, w_all, w_out)
    given = given + (carry, sums)
    return pl.pallas_call(
        functools.partial(scan_backward_kernel, chunks, len(held)),
        grid=(chunks[1] - chunks[0],),
        in_specs=[
            pl.BlockSpec((CHUNK, width), by_chunk),
            pl.BlockSpec(
                (8, width), lambda step: (jnp.maximum(at(step) * (CHUNK // 8) - 1, 0), 0)
            ),
            pl.BlockSpec((CHUNK, WIDE), by_chunk),
            pl.BlockSpec((CHUNK, d_o_all.shape[1]), by_chunk),
            pl.BlockSpec((CHUNK, row_values.shape[1]), by_chunk),
            pl.BlockSpec((1, 128, WIDE), lambda step: (at(step), 0, 0)),
            whole(taps.shape),
            whole(head.shape),
            whole(skip.shape),
            whole(w_all.shape),
            whole(w_out.shape),
            whole(carry.shape),
            whole(sums.shape),
            *[pl.BlockSpec(memory_space=pl.ANY) for _ in held],
        ],
        out_specs=[
            pl.BlockSpec((CHUNK, width), by_chunk),
            pl.BlockSpec((CHUNK, dim), by_chunk),
            whole(carry.shape),
            whole(sums.shape),
        ],
        out_shape=[
            jax.ShapeDtypeStruct((rows, width), jnp.bfloat16),
            jax.ShapeDtypeStruct((rows, dim), jnp.bfloat16),
            jax.ShapeDtypeStruct(carry.shape, jnp.float32),
            jax.ShapeDtypeStruct(sums.shape, jnp.float32),
        ],
        scratch_shapes=[
            pltpu.VMEM((128, WIDE), jnp.float32),
            pltpu.VMEM((CHUNK + 8, CONVW), jnp.float32),
            pltpu.VMEM((CHUNK + 8, CONVW), jnp.float32),
        ],
        input_output_aliases={len(given) + i: i for i in range(len(held))},
        compiler_params=pltpu.CompilerParams(vmem_limit_bytes=48 << 20),
        cost_estimate=pl.CostEstimate(
            flops=20 << 30, bytes_accessed=40 << 20, transcendentals=16 << 20
        ),
        name="scan_backward",
    )(*given, *held)


def token_front_kernel(
    x_ref, out_ref, scale_ref, gain_ref, slots_ref, router_ref, named_ref,
    resid_ref, moe_ref, sent_ref, gates_ref,
):
    f32, bf = jnp.float32, jnp.bfloat16
    resid = x_ref[...].astype(f32) + out_ref[...].astype(f32) * scale_ref[...]
    resid_ref[...] = resid
    moe_in = (resid * row_scale(resid) * gain_ref[0:1, :]).astype(bf)
    moe_ref[...] = moe_in
    sent_ref[...] = times(slots_ref[...], moe_in).astype(bf)
    named = named_ref[...] > 0.0
    logits = times(moe_in, router_ref[...])
    top = jnp.max(jnp.where(named, logits, -1e30), axis=1, keepdims=True)
    powers = jnp.where(named, jnp.exp(jnp.where(named, logits - top, 0.0)), 0.0)
    gates_ref[...] = powers / jnp.sum(powers, axis=1, keepdims=True)


def token_front(x, out_sum, scale, gain, slots, w_all, named):
    rows, dim = x.shape
    return pl.pallas_call(
        token_front_kernel,
        grid=(1,),
        in_specs=[
            whole(x.shape),
            whole(out_sum.shape),
            whole(scale.shape),
            whole(gain.shape),
            whole(slots.shape),
            pl.BlockSpec((dim, 128), lambda step: (0, w_all.shape[1] // 128 - 1)),
            whole(named.shape),
        ],
        out_specs=[
            whole((rows, dim)),
            whole((rows, dim)),
            whole((slots.shape[0], dim)),
            whole((rows, 128)),
        ],
        out_shape=[
            jax.ShapeDtypeStruct((rows, dim), jnp.float32),
            jax.ShapeDtypeStruct((rows, dim), jnp.bfloat16),
            jax.ShapeDtypeStruct((slots.shape[0], dim), jnp.bfloat16),
            jax.ShapeDtypeStruct((rows, 128), jnp.float32),
        ],
        compiler_params=pltpu.CompilerParams(vmem_limit_bytes=60 << 20),
        cost_estimate=pl.CostEstimate(flops=1 << 28, bytes_accessed=5 << 20, transcendentals=0),
        name="token_front",
    )(x, out_sum, scale, gain, slots, w_all, named)


def token_back_kernel(
    back_ref, slots_ref, shared_ref, x_ref, resid_ref, gates_ref, router_ref, gain_ref, cot_ref,
    d_o_ref, d_resid_ref, d_logits_ref, d_gain_ref,
):
    f32, bf = jnp.float32, jnp.bfloat16
    dim = x_ref.shape[1]
    sums = transposed_times(slots_ref[...], back_ref[...])
    scalars = sums[:, dim:]
    gates = gates_ref[...]
    d_gates = scalars + pltpu.roll(scalars, 64, 1)
    d_logits = gates * (d_gates - jnp.sum(gates * d_gates, axis=1, keepdims=True))
    d_logits_ref[...] = d_logits
    high, low = split_two(d_logits)
    router = router_ref[...]
    d_moe = (
        sums[:, :dim]
        + shared_ref[...].astype(f32)
        + times_transposed(high, router)
        + times_transposed(low, router)
    )
    resid = resid_ref[...]
    scale = row_scale(resid)
    normed = resid * scale
    d_gain_ref[0:1, :] = jnp.sum(d_moe * normed, axis=0, keepdims=True)
    d_gain_ref[1:8, :] = jnp.zeros((7, dim), f32)
    d_scaled = d_moe * gain_ref[0:1, :]
    mean = jnp.mean(d_scaled * normed, axis=1, keepdims=True)
    d_resid = cot_ref[...].astype(f32) + scale * (d_scaled - normed * mean)
    d_resid_ref[...] = d_resid
    d_o = d_resid.astype(bf)
    d_o_ref[:, :dim] = d_o
    added = resid - x_ref[...].astype(f32)
    kappa = jnp.sum(d_o.astype(f32) * added, axis=1, keepdims=True) * (1.0 / (2 * dim))
    kappa_high = kappa.astype(bf).astype(f32)
    lane = lax.broadcasted_iota(jnp.int32, scalars.shape, 1)
    both = jnp.where(lane == 0, kappa_high, jnp.where(lane == 1, kappa - kappa_high, 0.0))
    d_o_ref[:, dim:] = both.astype(bf)


def token_back(back, slots, shared_both, x, resid, gates, w_all, gain, cot):
    rows, dim = x.shape
    return pl.pallas_call(
        token_back_kernel,
        grid=(1,),
        in_specs=[
            whole(back.shape),
            whole(slots.shape),
            whole((rows, dim)),
            whole(x.shape),
            whole(resid.shape),
            whole(gates.shape),
            pl.BlockSpec((dim, 128), lambda step: (0, w_all.shape[1] // 128 - 1)),
            whole(gain.shape),
            whole(cot.shape),
        ],
        out_specs=[
            whole((rows, dim + 128)),
            whole((rows, dim)),
            whole((rows, 128)),
            whole((8, dim)),
        ],
        out_shape=[
            jax.ShapeDtypeStruct((rows, dim + 128), jnp.bfloat16),
            jax.ShapeDtypeStruct((rows, dim), jnp.float32),
            jax.ShapeDtypeStruct((rows, 128), jnp.float32),
            jax.ShapeDtypeStruct((8, dim), jnp.float32),
        ],
        compiler_params=pltpu.CompilerParams(vmem_limit_bytes=60 << 20),
        cost_estimate=pl.CostEstimate(flops=1 << 29, bytes_accessed=8 << 20, transcendentals=0),
        name="token_back",
    )(back, slots, shared_both, x, resid, gates, w_all, gain, cot)


def expert_early_kernel(cot_ref, down_ref, earlier_ref, raw_ref):
    cot = cot_ref[...].reshape(-1, cot_ref.shape[-1])
    raw_ref[0] = times_transposed(cot, down_ref[0])


def expert_main_kernel(
    rows_ref, routed_ref, raw_ref, gate_ref, up_ref, router_ref, marks_ref,
    moe_ref, cot_ref, shared_ref, down_ref,
    back_ref, act_ref, scaled_ref, d_g_ref, d_v_ref, both_ref, s_act_ref, d_both_ref,
):
    f32, bf = jnp.float32, jnp.bfloat16
    dim = rows_ref.shape[-1]
    rows = rows_ref[...].reshape(-1, dim)
    routed = routed_ref[...].reshape(-1, 128).astype(f32) > 0.0
    logits = times(rows, router_ref[...])
    top = jnp.max(jnp.where(routed, logits, -1e30), axis=1, keepdims=True)
    powers = jnp.where(routed, jnp.exp(jnp.where(routed, logits - top, 0.0)), 0.0)
    own = jnp.sum(powers * marks_ref[0, 0:1, :], axis=1, keepdims=True)
    gate = own / jnp.maximum(jnp.sum(powers, axis=1, keepdims=True), 1e-30)
    g = times(rows, gate_ref[0])
    v = times(rows, up_ref[0])
    sig = jax.nn.sigmoid(g)
    silu = g * sig
    act = (silu * v).astype(bf)
    act_wide = act.astype(f32)
    raw = raw_ref[0]
    d_gate = jnp.sum(act_wide * raw, axis=1, keepdims=True)
    d_act = gate * raw
    d_g = (d_act * v * (sig * (1.0 + g * (1.0 - sig)))).astype(bf)
    d_v = (d_act * silu).astype(bf)
    d_row = times_transposed(d_g, gate_ref[0]) + times_transposed(d_v, up_ref[0])
    high = d_gate.astype(bf).astype(f32)
    scalars = high * marks_ref[0, 1:2, :] + (d_gate - high) * marks_ref[0, 2:3, :]
    lead = back_ref.shape[:-1]
    back_ref[:, :, :, :dim] = d_row.astype(bf).reshape(*lead, dim)
    back_ref[:, :, :, dim:] = scalars.astype(bf).reshape(*lead, 128)
    act_ref[0] = act
    scaled_ref[0] = (gate * act_wide).astype(bf)
    d_g_ref[0] = d_g
    d_v_ref[0] = d_v

    units = down_ref.shape[0]
    s_both = times(moe_ref[...], shared_ref[...])
    s_gate, s_up = s_both[:, :units], s_both[:, units:]
    s_sig = jax.nn.sigmoid(s_gate)
    s_silu = s_gate * s_sig
    s_act = (s_silu * s_up).astype(bf)
    d_sh = times_transposed(cot_ref[...], down_ref[...])
    d_gs = (d_sh * s_up * (s_sig * (1.0 + s_gate * (1.0 - s_sig)))).astype(bf)
    d_both = jnp.concatenate([d_gs, (d_sh * s_silu).astype(bf)], axis=1)
    both_ref[:, :dim] = times_transposed(d_both, shared_ref[...]).astype(bf)
    both_ref[:, dim:] = times(s_act, down_ref[...]).astype(bf)
    s_act_ref[...] = s_act
    d_both_ref[...] = d_both


def expert_late_kernel(
    rows_ref, cot_ref, act_ref, scaled_ref, d_g_ref, d_v_ref, down_ref,
    out_ref, grad_gate_ref, grad_up_ref, grad_down_ref,
):
    bf = jnp.bfloat16
    dim = rows_ref.shape[-1]
    rows = rows_ref[...].reshape(-1, dim)
    cot = cot_ref[...].reshape(-1, dim)
    out_ref[...] = times(act_ref[0], down_ref[0]).astype(bf).reshape(out_ref.shape)
    units = act_ref.shape[-1]
    grad_gate_ref[0] = transposed_times(rows, d_g_ref[0]).astype(bf)
    grad_up_ref[0] = transposed_times(rows, d_v_ref[0]).astype(bf)
    for block in range(dim // units):
        at = block * units
        grad_down_ref[0, at : at + units] = transposed_times(
            scaled_ref[0], cot[:, block * units : block * units + units]
        ).astype(bf)


def expert_slots(shape, start=0):
    return pl.BlockSpec(
        (shape[0], 1) + tuple(shape[2:]), lambda e: (0, e) + (0,) * (len(shape) - 3) + (start,)
    )


def per_expert(shape):
    return pl.BlockSpec((1,) + tuple(shape[1:]), lambda e: (e,) + (0,) * (len(shape) - 1))


def expert_params(flops, moved):
    return dict(
        compiler_params=pltpu.CompilerParams(vmem_limit_bytes=56 << 20),
        cost_estimate=pl.CostEstimate(flops=flops, bytes_accessed=moved, transcendentals=1 << 19),
    )


def expert_early(cot_rows, down, earlier):
    sources, local, cap, _ = cot_rows.shape
    units, dim = down.shape[1:]
    return pl.pallas_call(
        expert_early_kernel,
        grid=(local,),
        in_specs=[
            expert_slots((sources, local, cap, dim)),
            per_expert(down.shape),
            corner_of(earlier),
        ],
        out_specs=per_expert((local, sources * cap, units)),
        out_shape=jax.ShapeDtypeStruct((local, sources * cap, units), jnp.float32),
        name="expert_early",
        **expert_params(64 << 30, 256 << 20),
    )(cot_rows, down, earlier)


def expert_main(rows, cot_rows, raw, gate, up, w_all, marks, moe_all, cot_all, w_shared, w_down):
    sources, local, cap, dim = rows.shape
    units = gate.shape[2]
    count = sources * cap
    hidden = jax.ShapeDtypeStruct((local, count, units), jnp.bfloat16)
    back = (sources, local, cap, dim + 128)
    seq_rows = moe_all.shape[0]
    shared_units = w_down.shape[0]
    share = lambda width: pl.BlockSpec((seq_rows // local, width), lambda e: (e, 0))
    return pl.pallas_call(
        expert_main_kernel,
        grid=(local,),
        in_specs=[
            expert_slots(rows.shape),
            expert_slots((sources, local, cap, 128), dim // 128),
            per_expert(raw.shape),
            per_expert(gate.shape),
            per_expert(up.shape),
            pl.BlockSpec((dim, 128), lambda e: (0, w_all.shape[1] // 128 - 1)),
            per_expert(marks.shape),
            share(dim),
            share(dim),
            whole(w_shared.shape),
            whole(w_down.shape),
        ],
        out_specs=[expert_slots(back)]
        + [per_expert(hidden.shape)] * 4
        + [share(2 * dim), share(shared_units), share(2 * shared_units)],
        out_shape=[jax.ShapeDtypeStruct(back, jnp.bfloat16)]
        + [hidden] * 4
        + [
            jax.ShapeDtypeStruct((seq_rows, width), jnp.bfloat16)
            for width in (2 * dim, shared_units, 2 * shared_units)
        ],
        name="expert_main",
        **expert_params(8 << 30, 20 << 20),
    )(rows, cot_rows, raw, gate, up, w_all, marks, moe_all, cot_all, w_shared, w_down)


def expert_late(rows, cot_rows, act, scaled, d_g, d_v, down):
    sources, local, cap, dim = rows.shape
    units = down.shape[1]
    grads = (local, dim, units)
    return pl.pallas_call(
        expert_late_kernel,
        grid=(local,),
        in_specs=[expert_slots(rows.shape), expert_slots(rows.shape)]
        + [per_expert(act.shape)] * 4
        + [per_expert(down.shape)],
        out_specs=[
            expert_slots(rows.shape),
            per_expert(grads),
            per_expert(grads),
            per_expert(grads),
        ],
        out_shape=[
            jax.ShapeDtypeStruct(rows.shape, jnp.bfloat16),
            jax.ShapeDtypeStruct(grads, jnp.bfloat16),
            jax.ShapeDtypeStruct(grads, jnp.bfloat16),
            jax.ShapeDtypeStruct(grads, jnp.bfloat16),
        ],
        name="expert_late",
        **expert_params(7 << 30, 24 << 20),
    )(rows, cot_rows, act, scaled, d_g, d_v, down)


def assemble_kernel(
    own_out, own_down, side_ref, in_ref, in_gain_ref, out_ref, out_gain_ref,
    grad_in_ref, tail_ref, grad_out_ref, norm_ref, grad_down_ref, gate_ref, up_ref, mid_ref,
):
    f32 = jnp.float32
    groups = side_ref.shape[0]
    inner = groups * WIDE
    bands = out_ref.shape[1] // WIDE
    rows_w = in_ref.shape[0]
    gain = in_gain_ref[...]
    at_down = bands * own_out
    at_mid = at_down + bands * own_down
    at_in = at_mid + rows_w
    units = gate_ref.shape[1] // groups

    def block(group, start, rows):
        return side_ref[group, start : start + rows, :].astype(f32)

    grad_gain = jnp.zeros((rows_w, 1), f32)
    keys = jnp.zeros((rows_w, 256), f32)
    tail = jnp.zeros((rows_w, 128), f32)
    steps = jnp.zeros((rows_w, 128), f32)
    mid = jnp.zeros((rows_w, 128), f32)
    rows, columns = grid_of((128, 128))

    def put(start, values):
        stop = start + values.shape[1]
        grad_in_ref[:, start:stop] = values * gain
        weight = in_ref[:, start:stop].astype(f32)
        return jnp.sum(weight * values, axis=1, keepdims=True)

    for group in range(groups):
        grad_gain += put(group * WIDE, block(group, at_in, rows_w))
        grad_gain += put(inner + group * WIDE, block(group, at_in + rows_w, rows_w))
        last = block(group, at_in + 2 * rows_w, rows_w)
        keys = keys + last[:, :256]
        tail = tail + last[:, 256:]
        moved = mark((rows < HEADS_HERE) & (columns == rows + HEADS_HERE * group))
        steps = steps + times(last[:, 256:].astype(jnp.bfloat16), moved)
        shared = block(group, at_mid, rows_w)
        gate_ref[:, units * group : units * group + units] = shared[:, :units]
        up_ref[:, units * group : units * group + units] = shared[:, units : 2 * units]
        mid = mid + shared[:, 2 * units :]
    grad_gain += put(2 * inner, keys)
    grad_gain += put(2 * inner + 256, steps[:, : groups * HEADS_HERE])
    lane = lax.broadcasted_iota(jnp.int32, tail.shape, 1)
    tail_ref[...] = jnp.where(lane == 0, grad_gain, tail)
    mid_ref[...] = mid

    for group in range(groups):
        sums = jnp.zeros((own_out, 1), f32)
        mine = slice(own_out * group, own_out * group + own_out)
        for band in range(bands):
            wide = slice(WIDE * band, WIDE * band + WIDE)
            values = block(group, own_out * band, own_out)
            grad_out_ref[mine, wide] = values * out_gain_ref[mine, :]
            sums += jnp.sum(out_ref[mine, wide].astype(f32) * values, axis=1, keepdims=True)
            grad_down_ref[own_down * group : own_down * group + own_down, wide] = block(
                group, at_down + own_down * band, own_down
            )
        norm_ref[mine, :] = sums


def assemble(side, in_weight, in_gain, out_weight, out_gain, own_out, own_down):
    groups = side.shape[0]
    rows, width = in_weight.shape
    out_rows, dim = out_weight.shape
    shapes = [
        (rows, width),
        (rows, 128),
        (out_rows, dim),
        (out_rows, 1),
        (groups * own_down, dim),
        (rows, groups * 128),
        (rows, groups * 128),
        (rows, 128),
    ]
    return pl.pallas_call(
        functools.partial(assemble_kernel, own_out, own_down),
        in_specs=[pl.BlockSpec(memory_space=pltpu.VMEM)] * 5,
        out_specs=[pl.BlockSpec(memory_space=pltpu.VMEM)] * len(shapes),
        out_shape=[jax.ShapeDtypeStruct(shape, jnp.float32) for shape in shapes],
        compiler_params=pltpu.CompilerParams(vmem_limit_bytes=40 << 20),
        cost_estimate=pl.CostEstimate(flops=8 << 20, bytes_accessed=12 << 20, transcendentals=0),
        name="assemble",
    )(side, in_weight, in_gain, out_weight, out_gain)


def fold_rows(values, width):
    rest = values[:, width:]
    count = rest.shape[1] * values.shape[0] // width
    parts = [rest[at : at + count] for at in range(0, values.shape[0], count)]
    return jnp.concatenate([values[:, :width], jnp.concatenate(parts, axis=1)], axis=0)


def unfold_rows(values, dim):
    sources, rows, width = values.shape
    count = rows * width // dim
    rest = dim - width
    parts = [values[:, count:, at : at + rest] for at in range(0, width, rest)]
    return jnp.concatenate([values[:, :count], jnp.concatenate(parts, axis=1)], axis=2)


def gather_blocks(values, mates):
    cores = 2
    chips = len(mates) // cores
    column = [values]
    for hop in range(1, chips):
        pairs = [
            (i, (i // cores + hop) % chips * cores + i % cores) for i in range(len(mates))
        ]
        column.append(lax.ppermute(values, "seq", pairs))
    column = jnp.stack(column)
    return column, lax.ppermute(column, "seq", mates)


def halves(values, bit):
    parts = values.reshape(2, values.shape[0] // 2, values.shape[1])
    sent = lax.dynamic_index_in_dim(parts, 1 - bit, 0, keepdims=False)
    return sent, lax.dynamic_index_in_dim(parts, bit, 0, keepdims=False)


def add_other(kept, sent, pairs):
    other = lax.ppermute(sent, "seq", pairs)
    return (kept.astype(jnp.float32) + other.astype(jnp.float32)).astype(jnp.bfloat16)


def halve(values, bit, pairs):
    sent, kept = halves(values, bit)
    return add_other(kept, sent, pairs)


def double(values, bit, pairs):
    other = lax.ppermute(values, "seq", pairs)
    first = jnp.where(bit == 0, values, other)
    second = jnp.where(bit == 0, other, values)
    return jnp.concatenate([first, second], axis=0)


def unpack_kernel(core_ref, own_ref, other_ref, gate_ref, up_ref, down_ref):
    part = pl.program_id(1)
    block = jnp.where(pl.program_id(0) == 0, own_ref[...], other_ref[...]).astype(jnp.float32)
    units = block.shape[1]

    @pl.when(part == 0)
    def _():
        gate_ref[0] = block

    @pl.when(part == 1)
    def _():
        up_ref[0] = block

    @pl.when(part == 2)
    def _():
        for at in range(0, block.shape[0], units):
            down_ref[0, :, at : at + units] = block[at : at + units]


def unpack_expert_grads(own, other, core):
    rows, units = own.shape
    dim = rows // 3
    to_expert = lambda who, part, core: (jnp.where(who == 0, core[0], 1 - core[0]), 0, 0)
    return pl.pallas_call(
        unpack_kernel,
        grid_spec=pltpu.PrefetchScalarGridSpec(
            num_scalar_prefetch=1,
            grid=(2, 3),
            in_specs=[
                pl.BlockSpec((dim, units), lambda who, part, core: (jnp.where(who == 0, part, 2), 0)),
                pl.BlockSpec((dim, units), lambda who, part, core: (jnp.where(who == 0, 0, part), 0)),
            ],
            out_specs=[
                pl.BlockSpec((1, dim, units), to_expert),
                pl.BlockSpec((1, dim, units), to_expert),
                pl.BlockSpec((1, units, dim), to_expert),
            ],
        ),
        out_shape=[
            jax.ShapeDtypeStruct((2, dim, units), jnp.float32),
            jax.ShapeDtypeStruct((2, dim, units), jnp.float32),
            jax.ShapeDtypeStruct((2, units, dim), jnp.float32),
        ],
        compiler_params=pltpu.CompilerParams(vmem_limit_bytes=40 << 20),
        cost_estimate=pl.CostEstimate(flops=1 << 20, bytes_accessed=28 << 20, transcendentals=0),
        name="unpack_expert_grads",
    )(core.reshape(1), own, other)


def on_device(
    block_input,
    lengths,
    routes,
    out_cotangent,
    mixer_gain,
    in_weight,
    conv_weight,
    conv_bias,
    step_bias,
    decay_log,
    skip_gain,
    norm_gain,
    out_weight,
    moe_gain,
    router_weight,
    shared_gate,
    shared_up,
    shared_down,
    expert_gate,
    expert_up,
    expert_down,
):
    sq = lax.axis_size("seq")
    sh = lax.axis_size("shard")
    q = lax.axis_index("seq")
    f32 = jnp.float32
    bf = jnp.bfloat16
    x_low = block_input[0]
    toks, dim = x_low.shape
    seq_rows = toks * sq
    heads = step_bias.shape[0] * sh
    inner = norm_gain.shape[0] * sh
    conv_all = conv_bias.shape[0] * sh
    keys_w = conv_all - inner
    gh = heads // sq
    gw = inner // sq
    rows_w = in_weight.shape[0]
    experts = router_weight.shape[1]
    local_e = expert_gate.shape[0]
    fs = shared_gate.shape[1]
    gf = fs // sq
    taps = conv_weight.shape[0]
    conv_own = conv_bias.shape[0]
    head_own = step_bias.shape[0]

    gain_col = mixer_gain.astype(f32)[:, None]

    def cols(start, width):
        return lax.dynamic_slice_in_dim(in_weight, start, width, 1)

    w_cols = jnp.concatenate(
        [
            cols(q * gw, gw),
            cols(inner + q * gw, gw),
            in_weight[:, 2 * inner : 2 * inner + keys_w],
            cols(2 * inner + keys_w + q * gh, gh),
        ],
        axis=1,
    )
    w_cols = (w_cols.astype(f32) * gain_col).astype(bf)
    used = 2 * gw + keys_w + gh
    small = jnp.concatenate(
        [conv_weight.reshape(-1), conv_bias, step_bias, decay_log, skip_gain, moe_gain]
    )
    small_cols = -(-(small.shape[0] - rows_w) // rows_w)
    at_router = used + small_cols
    total = -(-(at_router + experts) // 128) * 128
    packed = jnp.concatenate(
        [
            w_cols,
            jnp.zeros((rows_w, small_cols), bf),
            router_weight,
            jnp.zeros((rows_w, total - at_router - experts), bf),
        ],
        axis=1,
    )

    def to_shards(values):
        return lax.all_to_all(values, "shard", split_axis=0, concat_axis=0, tiled=True)

    core, z_at = q % 2, q // 2
    mates = [(i, i ^ 1) for i in range(sq)]
    x_column, x_other = gather_blocks(x_low, mates)

    out_scaled = (norm_gain.astype(f32)[:, None] * out_weight.astype(f32)).astype(bf)
    own_out = out_weight.shape[0] // sq
    own_down = shared_down.shape[0] // sq
    piece = jnp.concatenate(
        [
            lax.dynamic_slice_in_dim(out_scaled, q * own_out, own_out, 0),
            lax.dynamic_slice_in_dim(shared_down, q * own_down, own_down, 0),
        ],
        axis=0,
    )
    ratio = sh // sq
    forward_pairs = []
    for a in range(sh):
        for j in range(sq):
            s_to = sq * (a % ratio) + j
            q_to = a // ratio
            forward_pairs.append((j * sh + a, q_to * sh + s_to))
    backward_pairs = [(b, a) for a, b in forward_pairs]
    piece = lax.ppermute(piece, both_axes, forward_pairs)
    shared_cols = jnp.concatenate(
        [
            lax.dynamic_slice_in_dim(shared_gate, q * gf, gf, 1),
            lax.dynamic_slice_in_dim(shared_up, q * gf, gf, 1),
        ],
        axis=1,
    )
    fold = rows_w * 2 * gf // dim
    bands = dim // (2 * gf)
    shared_rows = jnp.concatenate(
        [shared_cols[fold * band : fold * band + fold] for band in range(bands)], axis=1
    )
    own_rows = own_out + own_down
    weights = lax.all_gather(
        jnp.concatenate(
            [
                packed,
                fold_rows(piece[:own_out], total),
                fold_rows(jnp.concatenate([piece[own_out:], shared_rows], axis=0), total),
            ],
            axis=0,
        ),
        "shard",
        axis=0,
    )
    folded = rows_w + own_out * dim // total
    second = unfold_rows(weights[:, folded:], dim)
    w_down = second[:, :own_down].reshape(gf, dim)
    w_shared = (
        second[:, own_down:]
        .reshape(sh, fold, bands, 2 * gf)
        .transpose(0, 2, 1, 3)
        .reshape(dim, 2 * gf)
    )

    route_ids = routes[0]
    expert_ids = jnp.arange(experts, dtype=jnp.int32)
    named = jnp.any(route_ids[:, :, None] == expert_ids[None, None, :], axis=1).astype(f32)
    earlier = (
        jnp.arange(toks)[:, None] > jnp.arange(toks)[None, :]
    ).astype(f32)
    rank = jnp.dot(earlier, named)
    dispatch = (
        (named.T[:, None, :] > 0.0)
        & (rank.T[:, None, :] == jnp.arange(CAP, dtype=f32)[None, :, None])
    ).astype(bf)
    slots = experts * CAP
    dispatch_flat = dispatch.reshape(slots, toks)
    live = (q * toks + jnp.arange(toks, dtype=jnp.int32) < lengths[0]).astype(f32)
    cot = out_cotangent[0].astype(f32) * live[:, None]
    cot_low = cot.astype(bf)

    local_slots = (sh, local_e, CAP)

    def in_slots(values):
        return times(dispatch_flat, values).astype(bf).reshape(sh, local_e * CAP, -1)

    def dispatched(sent):
        return to_shards(sent).reshape(*local_slots, -1)

    router_lane = at_router - (total - 128)
    lanes = jnp.arange(128, dtype=jnp.int32)
    named_lanes = jnp.pad(named, ((0, 0), (router_lane, 128 - router_lane - experts)))
    cot_sent = in_slots(jnp.concatenate([cot_low, named_lanes.astype(bf)], axis=1))
    weights, cot_late = lax.optimization_barrier((weights, cot_sent))
    cot_rows = dispatched(cot_late)
    small = after(jnp.pad(small, (0, total - small.shape[0])), cot_sent)
    small_all = to_shards(jnp.broadcast_to(small[None, None], (sh, 1, total)))[:, 0]

    at = taps * conv_own
    conv_full = (
        small_all[:, :at].reshape(sh, taps, conv_own).transpose(1, 0, 2).reshape(taps, conv_all)
    )
    offset_full = small_all[:, at : at + conv_own].reshape(conv_all)
    at = at + conv_own
    bias_full = small_all[:, at : at + head_own].reshape(heads)
    decay_full = small_all[:, at + head_own : at + 2 * head_own].reshape(heads)
    skip_full = small_all[:, at + 2 * head_own : at + 3 * head_own].reshape(heads)
    gain_at = at + 3 * head_own
    moe_gain_full = small_all[:, gain_at : gain_at + rows_w].reshape(1, dim).astype(f32)
    moe_gain_rows = jnp.broadcast_to(moe_gain_full, (8, dim))

    def group(values, width):
        return lax.dynamic_slice_in_dim(values, q * width, width, values.ndim - 1)

    conv_local = jnp.concatenate([group(conv_full, gw), conv_full[:, inner:]], axis=1).astype(f32)
    offset_local = jnp.concatenate([group(offset_full, gw), offset_full[inner:]]).astype(f32)
    bias_local = group(bias_full, gh).astype(f32)
    decay_local = group(decay_full, gh).astype(f32)
    skip_local = group(skip_full, gh).astype(f32)

    per_head = gw // gh
    taps_in = jnp.concatenate(
        [conv_local, offset_local[None], jnp.zeros((8 - taps - 1, gw + keys_w), f32)], axis=0
    )
    decay_rate = -jnp.exp(decay_local)
    head_in = jnp.pad(jnp.stack([bias_local, decay_rate]), ((0, 6), (0, 128 - gh)))
    skip_in = jnp.broadcast_to(jnp.repeat(skip_local, per_head)[None], (8, gw))
    place_here = jnp.stack([z_at, core]).astype(jnp.int32)
    x_all, proj, x_r, w_all, w_out, mixed, q_low, out_part, square_part, starts = front(
        place_here, x_column, x_other, weights, rows_w, taps_in, head_in, skip_in
    )

    cot_all = lax.all_gather(after(cot_low, x_column), "seq", axis=0, tiled=True)
    square_part = square_part.reshape(sq, toks)
    square_part = after(square_part, corner_after(cot_all, square_part))
    out_sum = lax.psum_scatter(out_part, "seq", scatter_dimension=0, tiled=True)
    square = lax.psum(square_part, "seq")
    q_r = lax.rsqrt(square / inner + epsilon).reshape(seq_rows, 1)
    d_raw = expert_early(cot_rows, expert_down, square)
    tok_r = lax.dynamic_slice_in_dim(q_r, q * toks, toks, 0)
    tok_r = after(tok_r, d_raw)
    x_tok = x_low.astype(f32)
    resid, moe_in, moe_sent, gates = token_front(
        x_low, out_sum, tok_r, moe_gain_rows, dispatch_flat, w_all, named_lanes
    )

    moe_all = lax.all_gather(moe_in, "seq", axis=0, tiled=True)

    rows = dispatched(moe_sent.reshape(sh, local_e * CAP, dim))
    own_ids = lax.axis_index("shard") * local_e + jnp.arange(local_e, dtype=jnp.int32)
    marks = jnp.stack(
        [own_ids + router_lane, own_ids + router_lane, own_ids + router_lane + 64] + [jnp.full_like(own_ids, -1)] * 5, axis=1
    )
    marks = (marks[:, :, None] == lanes[None, None, :]).astype(f32)

    back_rows, e_act, e_scaled, d_g, d_v, both_part, s_act, d_both = expert_main(
        rows,
        cot_rows,
        d_raw,
        expert_gate,
        expert_up,
        w_all,
        marks,
        moe_all,
        cot_all,
        w_shared,
        w_down,
    )
    shared_both = lax.psum_scatter(both_part, "seq", scatter_dimension=0, tiled=True)
    shared_sum = shared_both[:, dim:]
    d_returned = to_shards(back_rows.reshape(sh, local_e * CAP, dim + 128))
    e_out, *e_grads = expert_late(rows, cot_rows, e_act, e_scaled, d_g, d_v, expert_down)
    d_returned, e_out = lax.optimization_barrier((d_returned, e_out))
    returned = to_shards(e_out.reshape(sh, local_e * CAP, dim))

    near = [(i, 2 * ((i // 2) ^ 1) + i % 2) for i in range(sq)]
    far = [(i, 2 * (sq // 2 - 1 - i // 2) + i % 2) for i in range(sq)]
    is_inner = ((z_at == 1) | (z_at == 2)).astype(jnp.int32)
    is_high = (z_at >= 2).astype(jnp.int32)
    e_parts = [
        halve(part[:, at : at + dim // 2].reshape(dim, -1), core, mates)
        for part in e_grads
        for at in (0, dim // 2)
    ]
    e_mine = jnp.concatenate(e_parts, axis=0)
    cutoff = e_mine.shape[0] // 2

    grad_down_part = transposed_times(s_act, cot_all).astype(bf)
    grad_shared_part = transposed_times(moe_all, d_both).astype(bf)
    d_o_ext, d_resid, d_logits, d_moe_gain = token_back(
        d_returned.reshape(slots, dim + 128),
        dispatch_flat,
        shared_both,
        x_low,
        resid,
        after(gates, grad_down_part, grad_shared_part, *e_parts),
        w_all,
        moe_gain_rows,
        cot_low,
    )
    grad_router = jnp.dot(moe_in.astype(f32).T, d_logits, precision=highest)
    grad_router = grad_router + jnp.pad(d_moe_gain[0][:, None], ((0, 0), (0, 127)))
    d_o_all = lax.all_gather(d_o_ext, "seq", axis=0, tiled=True)

    sent_one, kept_one = halves(e_mine[:cutoff], is_inner)
    sent_two, kept_two = halves(e_mine[cutoff:], is_high)
    d_o_all, sent_one, sent_two = lax.optimization_barrier((d_o_all, sent_one, sent_two))
    grad_out_part = transposed_times(q_low, (q_r * d_o_all[:, :dim].astype(f32)).astype(bf))

    row_values = jnp.concatenate(
        [q_r, x_r, jnp.zeros((seq_rows, 6), f32)], axis=1
    )
    scan_inputs = (proj, mixed, d_o_all, row_values, starts, taps_in)
    scan_inputs = scan_inputs + (head_in, skip_in, w_all, w_out)
    chunks = seq_rows // CHUNK
    middle = chunks - 2
    *held, carry, sums = scan_backward(
        (middle, chunks),
        scan_inputs,
        (),
        jnp.zeros((136, gw + keys_w), f32),
        jnp.zeros((24, gw + keys_w), f32),
    )
    mid_part = jnp.concatenate(
        [
            grad_shared_part,
            after(grad_router, corner_after(returned, carry)).astype(bf),
        ],
        axis=1,
    )
    lane_w = mid_part.shape[1]
    bands = dim // lane_w

    def to_bands(values):
        return jnp.concatenate(
            [values[:, :, band * lane_w : band * lane_w + lane_w] for band in range(bands)], axis=1
        )

    early_part = jnp.concatenate(
        [
            to_bands(grad_out_part.astype(bf).reshape(sh, own_out, dim)),
            to_bands(grad_down_part.reshape(sh, own_down, dim)),
            mid_part.reshape(sh, rows_w, lane_w),
        ],
        axis=1,
    )
    moved_early = to_shards(early_part)
    d_proj, back_part, carry, sums = scan_backward((0, middle), scan_inputs, held, carry, sums)
    d_proj, moved_early = lax.optimization_barrier((d_proj, moved_early))
    e_one = add_other(after(kept_one, d_proj), sent_one, near)
    e_two = add_other(after(kept_two, d_proj), sent_two, far)
    d_taps, d_head, d_skip = sums[0:8], sums[8:16, :128], sums[16:24, :gw]
    grad_conv_local = d_taps[:taps]
    grad_offset_local = d_taps[taps]
    grad_bias_local = d_head[0, :gh]
    grad_decay_local = d_head[1, :gh] * decay_rate
    grad_skip_local = jnp.sum(d_skip[0].reshape(gh, per_head), axis=1)
    e_one, e_two = halve(e_one, is_high, far), halve(e_two, is_inner, near)
    back_sum = lax.psum_scatter(back_part, "seq", scatter_dimension=0, tiled=True).astype(f32)
    route_gates = gates[:, router_lane : router_lane + experts]
    weighted = (route_gates.T[:, None, :] * dispatch.astype(f32)).reshape(slots, toks)
    combined = transposed_times(weighted.astype(bf), returned.reshape(slots, dim))
    block_output = ((resid + shared_sum.astype(f32) + combined) * live[:, None]).astype(bf)[None]
    tok_x_r = row_scale(x_tok)
    x_n = x_tok * tok_x_r
    input_grad = (
        d_resid + back_sum - x_n * (tok_x_r * jnp.mean(back_sum * x_tok, axis=1, keepdims=True))
    )[None]

    grad_in_part = transposed_times(x_all, d_proj).astype(bf)

    def spread(local, count):
        wide = jnp.zeros(local.shape[:-1] + (count,), f32)
        return lax.dynamic_update_slice_in_dim(wide, local, q * local.shape[-1], local.ndim - 1)

    conv_rows = jnp.concatenate([grad_conv_local, grad_offset_local[None]], axis=0)
    conv_wide = jnp.concatenate([spread(conv_rows[:, :gw], inner), conv_rows[:, gw:]], axis=1)
    head_wide = spread(jnp.stack([grad_bias_local, grad_decay_local, grad_skip_local]), heads)
    small_part = jnp.concatenate(
        [
            conv_wide.reshape(taps + 1, sh, conv_own).transpose(1, 0, 2).reshape(sh, -1),
            head_wide.reshape(3, sh, head_own).transpose(1, 0, 2).reshape(sh, -1),
        ],
        axis=1,
    )
    small_count = small_part.shape[1]
    small_part = jnp.pad(
        small_part, ((0, 0), (0, rows_w * small_cols - small_count))
    ).reshape(sh, rows_w, small_cols)
    last_part = grad_in_part + jnp.pad(
        small_part.reshape(dim, small_cols), ((0, 0), (used, total - used - small_cols))
    )
    last_part = last_part.astype(bf)
    early_sum = jnp.sum(moved_early.astype(f32), axis=0).astype(bf)
    rows_sum = lax.ppermute(early_sum[: bands * own_rows], both_axes, backward_pairs)
    e_one, e_two = after(e_one, last_part), after(e_two, last_part)
    e_one, e_two = double(e_one, is_high, far), double(e_two, is_inner, near)
    e_one, e_two = double(e_one, is_inner, near), double(e_two, is_high, far)
    moved_last = to_shards(last_part.reshape(sh, rows_w, total))
    last_sum = jnp.sum(moved_last.astype(f32), axis=0)
    last_sum = after(after(after(last_sum, e_one), e_two), back_sum).astype(bf)
    e_mine = jnp.concatenate([e_one, e_two], axis=0)
    e_other = lax.ppermute(e_mine, "seq", mates)
    grad_e_gate, grad_e_up, grad_e_down = unpack_expert_grads(e_mine, e_other, core)
    side = lax.all_gather(
        jnp.concatenate(
            [rows_sum, early_sum[bands * own_rows :]]
            + [last_sum[:, lane_w * i : lane_w * i + lane_w] for i in range(total // lane_w)],
            axis=0,
        ),
        "seq",
        axis=0,
    )
    gain_out = norm_gain.astype(f32)[:, None]
    (
        grad_in,
        tail_sums,
        grad_out,
        norm_sums,
        grad_down,
        grad_shared_gate,
        grad_shared_up,
        mid_sums,
    ) = assemble(side, in_weight, gain_col, out_weight, gain_out, own_out, own_down)
    grad_norm = norm_sums[:, 0]
    grad_router_weight = mid_sums[:, router_lane : router_lane + experts]
    grad_moe_gain = mid_sums[:, 0]
    grad_mixer_gain = tail_sums[:, 0]
    lane_at = used - (total - 128)
    small_sum = tail_sums[:, lane_at : lane_at + small_cols].reshape(-1)
    at = taps * conv_own
    grad_conv = small_sum[:at].reshape(taps, conv_own)
    grad_offset = small_sum[at : at + conv_own]
    at = at + conv_own
    grad_bias = small_sum[at : at + head_own]
    grad_decay = small_sum[at + head_own : at + 2 * head_own]
    grad_skip = small_sum[at + 2 * head_own : at + 3 * head_own]
    return (
        block_output,
        input_grad,
        grad_mixer_gain,
        grad_in,
        grad_conv,
        grad_offset,
        grad_bias,
        grad_decay,
        grad_skip,
        grad_norm,
        grad_out,
        grad_moe_gain,
        grad_router_weight,
        grad_shared_gate,
        grad_shared_up,
        grad_down,
        grad_e_gate,
        grad_e_up,
        grad_e_down,
    )


def solution(mesh):
    placed = (
        P("shard", "seq", None),
        P("shard"),
        P("shard", "seq", None),
        P("shard", "seq", None),
        P("shard"),
        P("shard", None),
        P(None, "shard"),
        P("shard"),
        P("shard"),
        P("shard"),
        P("shard"),
        P("shard"),
        P("shard", None),
        P("shard"),
        P("shard", None),
        P("shard", None),
        P("shard", None),
        P("shard", None),
        P("shard", None, None),
        P("shard", None, None),
        P("shard", None, None),
    )
    return jax.shard_map(
        on_device,
        mesh=mesh,
        in_specs=placed,
        out_specs=(
            P("shard", "seq", None),
            P("shard", "seq", None),
            P("shard"),
            P("shard", None),
            P(None, "shard"),
            P("shard"),
            P("shard"),
            P("shard"),
            P("shard"),
            P("shard"),
            P("shard", None),
            P("shard"),
            P("shard", None),
            P("shard", None),
            P("shard", None),
            P("shard", None),
            P("shard", None, None),
            P("shard", None, None),
            P("shard", None, None),
        ),
        check_vma=False,
    )
```

```python
import functools

import jax
import jax.numpy as jnp
from jax import lax
from jax.experimental import pallas as pl
from jax.experimental.pallas import tpu as pltpu
from jax.sharding import PartitionSpec as P

CAP = 32


epsilon = 1e-05
highest = lax.Precision.HIGHEST
both_axes = ("seq", "shard")


def times(left, right):
    return jnp.dot(left, right, preferred_element_type=jnp.float32)


def times_transposed(left, right):
    return lax.dot_general(
        left, right, (((1,), (1,)), ((), ())), preferred_element_type=jnp.float32
    )


def transposed_times(left, right):
    return lax.dot_general(
        left, right, (((0,), (0,)), ((), ())), preferred_element_type=jnp.float32
    )


def after(value, *others):
    corners = [o[(0,) * (o.ndim - 1)][:1].astype(jnp.float32) for o in others]
    return (value.astype(jnp.float32) + 0.0 * sum(corners)).astype(value.dtype)


def corner_after(values, other):
    at = (0.0 * other[(0,) * other.ndim]).astype(jnp.int32)
    return lax.dynamic_slice(values, (at,) * values.ndim, (1,) * values.ndim)


def silu_slope(values):
    sigma = jax.nn.sigmoid(values)
    return sigma * (1.0 + values * (1.0 - sigma))


def row_scale(values):
    return lax.rsqrt(jnp.mean(values * values, axis=-1, keepdims=True) + epsilon)


CHUNK = 128
WIDE = 384
CONVW = 640
PAIRS = 3
HEADS_HERE = 6


def split_two(values):
    high = values.astype(jnp.bfloat16)
    return high, (values - high.astype(jnp.float32)).astype(jnp.bfloat16)


def ones_times(ones, values):
    high, low = split_two(values)
    return times(ones, high) + times(ones, low)


def times_ones(values, ones):
    high, low = split_two(values)
    return times(high, ones) + times(low, ones)


def transposed_times_ones(values, ones):
    high, low = split_two(values)
    return transposed_times(high, ones) + transposed_times(low, ones)


def grid_of(shape):
    rows = lax.broadcasted_iota(jnp.int32, shape, 0)
    columns = lax.broadcasted_iota(jnp.int32, shape, 1)
    return rows, columns


def mark(condition):
    return jnp.where(condition, 1.0, 0.0).astype(jnp.bfloat16)


def chunk_parts(proj, before, taps_ref, head_ref, pad_ref):
    f32, bf = jnp.float32, jnp.bfloat16
    feed = proj[:, WIDE : WIDE + CONVW].astype(bf).astype(f32)
    pad_ref[0:8, :] = before
    pad_ref[8 : 8 + CHUNK, :] = feed
    conv = taps_ref[4:5, :]
    for tap in range(4):
        conv = conv + taps_ref[tap : tap + 1, :] * pad_ref[5 + tap : 5 + tap + CHUNK, :]
    sig = jax.nn.sigmoid(conv)
    act = conv * sig
    u = act[:, :WIDE]
    key = act[:, WIDE : WIDE + 128].astype(bf)
    query = act[:, WIDE + 128 :].astype(bf)
    step_low = proj[:, WIDE + CONVW :].astype(bf).astype(f32)
    pre = step_low + head_ref[0:1, :]
    rows, columns = grid_of((CHUNK, 128))
    here = columns < HEADS_HERE
    dt = jnp.where(here, jnp.maximum(pre, 0.0) + jnp.log1p(jnp.exp(-jnp.abs(pre))), 0.0)
    la = dt * head_ref[1:2, :]
    lower = mark(rows >= columns)
    cum = ones_times(lower, la)
    end = cum[CHUNK - 1 : CHUNK, :]
    wide_rows, wide_columns = grid_of((128, WIDE))
    widen = mark(wide_columns // 64 == wide_rows)
    dt_w = times_ones(dt, widen)
    e_w = times_ones(jnp.exp(cum), widen)
    w_w = times_ones(jnp.exp(end - cum), widen)
    full_rows, full_columns = grid_of((128, 2 * PAIRS * 128))
    la_full = times_ones(la, mark(full_columns // 128 == full_rows))
    scores = times_transposed(query, key)
    return dict(
        conv=conv, sig=sig, u=u, key=key, query=query, pre=pre, here=here, dt=dt, lower=lower,
        dt_w=dt_w, e_w=e_w, w_w=w_w, la_full=la_full, scores=scores, xs=u * dt_w,
    )


def pair_table(parts, pair):
    rows, columns = grid_of((CHUNK, 256))
    local = columns % 128
    steps = jnp.where(rows > local, parts["la_full"][:, 256 * pair : 256 * pair + 256], 0.0)
    gap = ones_times(parts["lower"], steps)
    causal = rows >= local
    decay = jnp.where(causal, jnp.exp(jnp.where(causal, gap, 0.0)), 0.0)
    scores = parts["scores"]
    return decay, decay * jnp.concatenate([scores, scores], axis=1)


def stack_heads(values, pair):
    both = values[:, 128 * pair : 128 * pair + 128]
    first = lax.broadcasted_iota(jnp.int32, both.shape, 1) < 64
    return jnp.concatenate(
        [jnp.where(first, both, 0.0), jnp.where(first, 0.0, both)], axis=0
    ).astype(jnp.bfloat16)


def front_kernel(
    here_ref, column_ref, other_ref, w_in_ref, rows_in_ref, place_ref, taps_ref, head_ref, skip_ref,
    x_ref, proj_ref, scale_ref, w_ref, out_w_ref, mixed_ref, q_ref, out_ref, square_ref, start_ref,
    state_ref, pad_ref,
):
    f32, bf = jnp.float32, jnp.bfloat16
    width = w_ref.shape[1]

    @pl.when(pl.program_id(0) == 0)
    def _():
        state_ref[...] = jnp.zeros(state_ref.shape, f32)
        pad_ref[CHUNK : CHUNK + 8, :] = jnp.zeros((8, CONVW), f32)
        w_ref[...] = w_in_ref[...].reshape(-1, width)
        folded = rows_in_ref[...].reshape(-1, width)
        out_w_ref[:, :width] = times(place_ref[0], folded).astype(bf)
        rest = out_w_ref.shape[1] - width
        tail = jnp.zeros((out_w_ref.shape[0], rest), f32)
        for part in range(width // rest):
            tail = tail + times(place_ref[1 + part], folded[:, rest * part : rest * part + rest])
        out_w_ref[:, width:] = tail.astype(bf)

    column, other = column_ref[0].astype(f32), other_ref[0].astype(f32)
    first = here_ref[1] == 0
    x = jnp.concatenate(
        [jnp.where(first, column, other), jnp.where(first, other, column)], axis=0
    ).astype(bf)
    x_ref[...] = x
    scale = row_scale(x.astype(f32))
    proj = times(x, w_ref[...]) * scale
    proj_ref[...] = proj
    scale_ref[...] = scale
    gated = []
    for at in range(0, x.shape[0], CHUNK):
        here = slice(at, at + CHUNK)
        before = pad_ref[CHUNK : CHUNK + 8, :]
        parts = chunk_parts(proj[here], before, taps_ref, head_ref, pad_ref)
        state = state_ref[...]
        start_ref[at // CHUNK] = state
        xs = parts["xs"]
        inside = []
        for pair in range(PAIRS):
            _, table = pair_table(parts, pair)
            inside.append(times(table.astype(bf), stack_heads(xs, pair)))
        across = times(parts["query"], state.astype(bf))
        y = (
            jnp.concatenate(inside, axis=1)
            + parts["e_w"] * across
            + skip_ref[0:1, :] * parts["u"]
        )
        mixed = y.astype(bf)
        mixed_ref[here, :] = mixed
        gate = proj[here, :WIDE]
        q_val = mixed.astype(f32) * (gate * jax.nn.sigmoid(gate))
        gated.append(q_val.astype(bf))
        square_ref[here, :] = jnp.sum(q_val * q_val, axis=1, keepdims=True)
        state_ref[...] = state * parts["e_w"][CHUNK - 1 : CHUNK, :] + transposed_times(
            parts["key"], (xs * parts["w_w"]).astype(bf)
        )
    gated = jnp.concatenate(gated, axis=0)
    q_ref[...] = gated
    out_ref[...] = times(gated, out_w_ref[...]).astype(bf)


def scan_backward_kernel(
    chunks, held_count, proj_ref, prev_ref, mixed_ref, d_o_ref, rows_ref, start_ref, taps_ref,
    head_ref, skip_ref, w_ref, out_w_ref, carry_in_ref, sums_in_ref, *refs,
):
    f32, bf = jnp.float32, jnp.bfloat16
    d_proj_ref, back_ref, carry_ref, sums_ref, state_ref, pad_ref, late_ref = refs[held_count:]
    step = pl.program_id(0)
    chunk = chunks[1] - 1 - step
    d_taps_ref = sums_ref.at[0:8, :]
    d_head_ref = sums_ref.at[8:16, 0:128]
    d_skip_ref = sums_ref.at[16:24, 0:WIDE]

    @pl.when(step == 0)
    def _():
        state_ref[...] = carry_in_ref[0:128, 0:WIDE]
        late_ref[CHUNK : CHUNK + 8, :] = carry_in_ref[128:136, :]
        sums_ref[...] = sums_in_ref[...]

    before = prev_ref[:, WIDE : WIDE + CONVW].astype(bf).astype(f32)
    before = jnp.where(chunk > 0, before, 0.0)
    parts = chunk_parts(proj_ref[...], before, taps_ref, head_ref, pad_ref)
    u, key, query, xs = parts["u"], parts["key"], parts["query"], parts["xs"]
    e_w, w_w, dt_w = parts["e_w"], parts["w_w"], parts["dt_w"]

    gate = proj_ref[:, :WIDE]
    gate_sig = jax.nn.sigmoid(gate)
    gate_act = gate * gate_sig
    mixed = mixed_ref[...].astype(f32)
    q_val = mixed * gate_act
    q_r = rows_ref[:, 0:1]
    dim = out_w_ref.shape[1]
    d_gated = times_transposed(d_o_ref[:, :dim], out_w_ref[...])
    kappa = d_o_ref[:, dim : dim + 1].astype(f32) + d_o_ref[:, dim + 1 : dim + 2].astype(f32)
    d_q = q_r * d_gated - q_val * (q_r * q_r * kappa)
    d_gate = d_q * mixed * (gate_sig * (1.0 + gate * (1.0 - gate_sig)))
    d_y = (d_q * gate_act).astype(bf).astype(f32)

    start = start_ref[0]
    start_low = start.astype(bf)
    d_end = state_ref[...]
    d_end_low = d_end.astype(bf)
    xw = xs * w_w
    ye = d_y * e_w
    ye_low = ye.astype(bf)
    across = times(query, start_low)
    pulled = times(key, d_end_low)
    d_query = times_transposed(ye_low, start_low)
    d_key = times_transposed(xw.astype(bf), d_end_low)
    state_ref[...] = d_end * e_w[CHUNK - 1 : CHUNK, :] + transposed_times(query, ye_low)
    d_scores = jnp.zeros((CHUNK, 128), f32)
    turns = jnp.zeros((CHUNK, 128), f32)
    d_xs = []
    for pair in range(PAIRS):
        decay, table = pair_table(parts, pair)
        xs_two = stack_heads(xs, pair)
        dy_two = stack_heads(d_y, pair)
        d_table = times_transposed(d_y[:, 128 * pair : 128 * pair + 128].astype(bf), xs_two)
        d_decay = d_table * decay
        d_scores = d_scores + d_decay[:, :128] + d_decay[:, 128:]
        d_gap = d_table * table
        table_low = table.astype(bf)
        d_xs.append(
            transposed_times(
                jnp.concatenate([table_low[:, :128], table_low[:, 128:]], axis=0), dy_two
            )
        )
        two_rows, two_columns = grid_of((256, 128))
        own = mark(two_columns == 2 * pair + two_rows // 128)
        turns = turns + times_ones(d_gap, own)
        turns = turns - transposed_times_ones(
            jnp.concatenate([d_gap[:, :128], d_gap[:, 128:]], axis=0), own
        )
    d_xs = jnp.concatenate(d_xs, axis=1) + w_w * pulled
    d_scores_low = d_scores.astype(bf)
    d_query = d_query + times(d_scores_low, key)
    d_key = d_key + transposed_times(d_scores_low, query)

    rows, columns = grid_of((CHUNK, 128))
    upper = mark(columns >= rows)
    strict = mark(columns < rows)
    sum_rows, sum_columns = grid_of((WIDE, 128))
    per_head = mark(sum_rows // 64 == sum_columns)
    end_row = jnp.sum(d_end * start, axis=0, keepdims=True) * e_w[CHUNK - 1 : CHUNK, :]
    wide = ones_times(upper, ye * across) + ones_times(strict, xw * pulled) + end_row
    d_la = ones_times(upper, turns) + times_ones(wide, per_head)
    d_dt = times_ones(d_xs * u, per_head) + d_la * head_ref[1:2, :]
    d_pre = jnp.where(parts["here"], d_dt * jax.nn.sigmoid(parts["pre"]), 0.0)
    d_head_ref[0:1, :] += jnp.sum(d_pre, axis=0, keepdims=True)
    d_head_ref[1:2, :] += jnp.sum(d_la * parts["dt"], axis=0, keepdims=True)
    d_skip_ref[0:1, :] += jnp.sum(d_y * u, axis=0, keepdims=True)

    d_u = d_xs * dt_w + skip_ref[0:1, :] * d_y
    conv, sig = parts["conv"], parts["sig"]
    d_conv = jnp.concatenate([d_u, d_key, d_query], axis=1) * (sig * (1.0 + conv * (1.0 - sig)))
    late_ref[0:CHUNK, :] = d_conv
    d_feed = jnp.zeros((CHUNK, CONVW), f32)
    for tap in range(4):
        d_feed = d_feed + taps_ref[tap : tap + 1, :] * late_ref[3 - tap : 3 - tap + CHUNK, :]
        d_taps_ref[tap : tap + 1, :] += jnp.sum(
            d_conv * pad_ref[5 + tap : 5 + tap + CHUNK, :], axis=0, keepdims=True
        )
    d_taps_ref[4:5, :] += jnp.sum(d_conv, axis=0, keepdims=True)
    late_ref[CHUNK : CHUNK + 8, :] = d_conv[0:8, :]
    carry_ref[0:128, 0:WIDE] = state_ref[...]
    carry_ref[128:136, :] = d_conv[0:8, :]
    scale = rows_ref[:, 1:2]
    d_proj = jnp.concatenate([d_gate, d_feed, d_pre], axis=1) * scale
    d_proj = d_proj.astype(bf)
    d_proj_ref[...] = d_proj
    back_ref[...] = times_transposed(d_proj, w_ref[...]).astype(bf)


def corner_of(array):
    return pl.BlockSpec(
        (1,) * (array.ndim - 2) + (min(16, array.shape[-2]), 128),
        lambda *step: (0,) * array.ndim,
    )


def whole(shape):
    return pl.BlockSpec(shape, lambda *step: (0,) * len(shape))


def front(here, column, other, weights, rows_w, taps, head, skip):
    f32, bf = jnp.float32, jnp.bfloat16
    chips, block, dim = column.shape
    rows = 2 * chips * block
    sources, _, width = weights.shape
    own = WIDE // sources
    count = own * dim // width
    tile = 2 * block
    row = jnp.arange(WIDE)[:, None]
    slot = jnp.arange(sources * count)[None, :]
    same = row // own == slot // count
    deep = count - own
    place = [same & (row % own == slot % count)] + [
        same & (row % own // deep == part) & (row % deep + own == slot % count)
        for part in range(own // deep)
    ]
    place = jnp.stack(place).astype(bf)
    by_tile = lambda step, here: (step, 0)
    by_chip = lambda step, here: ((here[0] + chips - step) % chips, 0, 0)
    chunks = rows // CHUNK
    return pl.pallas_call(
        front_kernel,
        grid_spec=pltpu.PrefetchScalarGridSpec(
            num_scalar_prefetch=1,
        grid=(rows // tile,),
        in_specs=[
            pl.BlockSpec((1, block, dim), by_chip),
            pl.BlockSpec((1, block, dim), by_chip),
            pl.BlockSpec((sources, rows_w, width), lambda *step: (0, 0, 0)),
            pl.BlockSpec((sources, count, width), lambda *step: (0, rows_w // count, 0)),
            whole(place.shape),
            whole(taps.shape),
            whole(head.shape),
            whole(skip.shape),
        ],
        out_specs=[
            pl.BlockSpec((tile, dim), by_tile),
            pl.BlockSpec((tile, width), by_tile),
            pl.BlockSpec((tile, 1), by_tile),
            whole((dim, width)),
            whole((WIDE, dim)),
            pl.BlockSpec((tile, WIDE), by_tile),
            pl.BlockSpec((tile, WIDE), by_tile),
            pl.BlockSpec((tile, dim), by_tile),
            pl.BlockSpec((tile, 1), by_tile),
            pl.BlockSpec((tile // CHUNK, 128, WIDE), lambda step, here: (step, 0, 0)),
        ],
        scratch_shapes=[
            pltpu.VMEM((128, WIDE), f32),
            pltpu.VMEM((CHUNK + 8, CONVW), f32),
        ],
        ),
        out_shape=[
            jax.ShapeDtypeStruct((rows, dim), bf),
            jax.ShapeDtypeStruct((rows, width), f32),
            jax.ShapeDtypeStruct((rows, 1), f32),
            jax.ShapeDtypeStruct((dim, width), bf),
            jax.ShapeDtypeStruct((WIDE, dim), bf),
            jax.ShapeDtypeStruct((rows, WIDE), bf),
            jax.ShapeDtypeStruct((rows, WIDE), bf),
            jax.ShapeDtypeStruct((rows, dim), bf),
            jax.ShapeDtypeStruct((rows, 1), f32),
            jax.ShapeDtypeStruct((chunks, 128, WIDE), f32),
        ],
        compiler_params=pltpu.CompilerParams(vmem_limit_bytes=52 << 20),
        cost_estimate=pl.CostEstimate(
            flops=16 << 30, bytes_accessed=48 << 20, transcendentals=4 << 20
        ),
        name="front",
    )(here, column, other, weights, weights, place, taps, head, skip)


def scan_backward(chunks, inputs, held, carry, sums):
    proj, mixed, d_o_all, row_values, starts, taps, head, skip, w_all, w_out = inputs
    rows, width = proj.shape
    dim = w_all.shape[0]
    at = lambda step: chunks[1] - 1 - step
    by_chunk = lambda step: (at(step), 0)
    given = (proj, proj, mixed, d_o_all, row_values, starts, taps, head, skip, w_all, w_out)
    given = given + (carry, sums)
    return pl.pallas_call(
        functools.partial(scan_backward_kernel, chunks, len(held)),
        grid=(chunks[1] - chunks[0],),
        in_specs=[
            pl.BlockSpec((CHUNK, width), by_chunk),
            pl.BlockSpec(
                (8, width), lambda step: (jnp.maximum(at(step) * (CHUNK // 8) - 1, 0), 0)
            ),
            pl.BlockSpec((CHUNK, WIDE), by_chunk),
            pl.BlockSpec((CHUNK, d_o_all.shape[1]), by_chunk),
            pl.BlockSpec((CHUNK, row_values.shape[1]), by_chunk),
            pl.BlockSpec((1, 128, WIDE), lambda step: (at(step), 0, 0)),
            whole(taps.shape),
            whole(head.shape),
            whole(skip.shape),
            whole(w_all.shape),
            whole(w_out.shape),
            whole(carry.shape),
            whole(sums.shape),
            *[pl.BlockSpec(memory_space=pl.ANY) for _ in held],
        ],
        out_specs=[
            pl.BlockSpec((CHUNK, width), by_chunk),
            pl.BlockSpec((CHUNK, dim), by_chunk),
            whole(carry.shape),
            whole(sums.shape),
        ],
        out_shape=[
            jax.ShapeDtypeStruct((rows, width), jnp.bfloat16),
            jax.ShapeDtypeStruct((rows, dim), jnp.bfloat16),
            jax.ShapeDtypeStruct(carry.shape, jnp.float32),
            jax.ShapeDtypeStruct(sums.shape, jnp.float32),
        ],
        scratch_shapes=[
            pltpu.VMEM((128, WIDE), jnp.float32),
            pltpu.VMEM((CHUNK + 8, CONVW), jnp.float32),
            pltpu.VMEM((CHUNK + 8, CONVW), jnp.float32),
        ],
        input_output_aliases={len(given) + i: i for i in range(len(held))},
        compiler_params=pltpu.CompilerParams(vmem_limit_bytes=48 << 20),
        cost_estimate=pl.CostEstimate(
            flops=20 << 30, bytes_accessed=40 << 20, transcendentals=16 << 20
        ),
        name="scan_backward",
    )(*given, *held)


def token_front_kernel(
    x_ref, out_ref, scale_ref, gain_ref, slots_ref, router_ref, named_ref,
    resid_ref, moe_ref, sent_ref, gates_ref,
):
    f32, bf = jnp.float32, jnp.bfloat16
    resid = x_ref[...].astype(f32) + out_ref[...].astype(f32) * scale_ref[...]
    resid_ref[...] = resid
    moe_in = (resid * row_scale(resid) * gain_ref[0:1, :]).astype(bf)
    moe_ref[...] = moe_in
    sent_ref[...] = times(slots_ref[...], moe_in).astype(bf)
    named = named_ref[...] > 0.0
    logits = times(moe_in, router_ref[...])
    top = jnp.max(jnp.where(named, logits, -1e30), axis=1, keepdims=True)
    powers = jnp.where(named, jnp.exp(jnp.where(named, logits - top, 0.0)), 0.0)
    gates_ref[...] = powers / jnp.sum(powers, axis=1, keepdims=True)


def token_front(x, out_sum, scale, gain, slots, w_all, named):
    rows, dim = x.shape
    return pl.pallas_call(
        token_front_kernel,
        grid=(1,),
        in_specs=[
            whole(x.shape),
            whole(out_sum.shape),
            whole(scale.shape),
            whole(gain.shape),
            whole(slots.shape),
            pl.BlockSpec((dim, 128), lambda step: (0, w_all.shape[1] // 128 - 1)),
            whole(named.shape),
        ],
        out_specs=[
            whole((rows, dim)),
            whole((rows, dim)),
            whole((slots.shape[0], dim)),
            whole((rows, 128)),
        ],
        out_shape=[
            jax.ShapeDtypeStruct((rows, dim), jnp.float32),
            jax.ShapeDtypeStruct((rows, dim), jnp.bfloat16),
            jax.ShapeDtypeStruct((slots.shape[0], dim), jnp.bfloat16),
            jax.ShapeDtypeStruct((rows, 128), jnp.float32),
        ],
        compiler_params=pltpu.CompilerParams(vmem_limit_bytes=60 << 20),
        cost_estimate=pl.CostEstimate(flops=1 << 28, bytes_accessed=5 << 20, transcendentals=0),
        name="token_front",
    )(x, out_sum, scale, gain, slots, w_all, named)


def token_back_kernel(
    back_ref, slots_ref, shared_ref, x_ref, resid_ref, gates_ref, router_ref, gain_ref, cot_ref,
    d_o_ref, d_resid_ref, d_logits_ref, d_gain_ref,
):
    f32, bf = jnp.float32, jnp.bfloat16
    dim = x_ref.shape[1]
    sums = transposed_times(slots_ref[...], back_ref[...])
    scalars = sums[:, dim:]
    gates = gates_ref[...]
    d_gates = scalars + pltpu.roll(scalars, 64, 1)
    d_logits = gates * (d_gates - jnp.sum(gates * d_gates, axis=1, keepdims=True))
    d_logits_ref[...] = d_logits
    high, low = split_two(d_logits)
    router = router_ref[...]
    d_moe = (
        sums[:, :dim]
        + shared_ref[...].astype(f32)
        + times_transposed(high, router)
        + times_transposed(low, router)
    )
    resid = resid_ref[...]
    scale = row_scale(resid)
    normed = resid * scale
    d_gain_ref[0:1, :] = jnp.sum(d_moe * normed, axis=0, keepdims=True)
    d_gain_ref[1:8, :] = jnp.zeros((7, dim), f32)
    d_scaled = d_moe * gain_ref[0:1, :]
    mean = jnp.mean(d_scaled * normed, axis=1, keepdims=True)
    d_resid = cot_ref[...].astype(f32) + scale * (d_scaled - normed * mean)
    d_resid_ref[...] = d_resid
    d_o = d_resid.astype(bf)
    d_o_ref[:, :dim] = d_o
    added = resid - x_ref[...].astype(f32)
    kappa = jnp.sum(d_o.astype(f32) * added, axis=1, keepdims=True) * (1.0 / (2 * dim))
    kappa_high = kappa.astype(bf).astype(f32)
    lane = lax.broadcasted_iota(jnp.int32, scalars.shape, 1)
    both = jnp.where(lane == 0, kappa_high, jnp.where(lane == 1, kappa - kappa_high, 0.0))
    d_o_ref[:, dim:] = both.astype(bf)


def token_back(back, slots, shared_both, x, resid, gates, w_all, gain, cot):
    rows, dim = x.shape
    return pl.pallas_call(
        token_back_kernel,
        grid=(1,),
        in_specs=[
            whole(back.shape),
            whole(slots.shape),
            whole((rows, dim)),
            whole(x.shape),
            whole(resid.shape),
            whole(gates.shape),
            pl.BlockSpec((dim, 128), lambda step: (0, w_all.shape[1] // 128 - 1)),
            whole(gain.shape),
            whole(cot.shape),
        ],
        out_specs=[
            whole((rows, dim + 128)),
            whole((rows, dim)),
            whole((rows, 128)),
            whole((8, dim)),
        ],
        out_shape=[
            jax.ShapeDtypeStruct((rows, dim + 128), jnp.bfloat16),
            jax.ShapeDtypeStruct((rows, dim), jnp.float32),
            jax.ShapeDtypeStruct((rows, 128), jnp.float32),
            jax.ShapeDtypeStruct((8, dim), jnp.float32),
        ],
        compiler_params=pltpu.CompilerParams(vmem_limit_bytes=60 << 20),
        cost_estimate=pl.CostEstimate(flops=1 << 29, bytes_accessed=8 << 20, transcendentals=0),
        name="token_back",
    )(back, slots, shared_both, x, resid, gates, w_all, gain, cot)


def expert_early_kernel(cot_ref, down_ref, earlier_ref, raw_ref):
    cot = cot_ref[...].reshape(-1, cot_ref.shape[-1])
    raw_ref[0] = times_transposed(cot, down_ref[0])


def expert_main_kernel(
    rows_ref, routed_ref, raw_ref, gate_ref, up_ref, router_ref, marks_ref,
    moe_ref, cot_ref, shared_ref, down_ref,
    back_ref, act_ref, scaled_ref, d_g_ref, d_v_ref, both_ref, s_act_ref, d_both_ref,
):
    f32, bf = jnp.float32, jnp.bfloat16
    dim = rows_ref.shape[-1]
    rows = rows_ref[...].reshape(-1, dim)
    routed = routed_ref[...].reshape(-1, 128).astype(f32) > 0.0
    logits = times(rows, router_ref[...])
    top = jnp.max(jnp.where(routed, logits, -1e30), axis=1, keepdims=True)
    powers = jnp.where(routed, jnp.exp(jnp.where(routed, logits - top, 0.0)), 0.0)
    own = jnp.sum(powers * marks_ref[0, 0:1, :], axis=1, keepdims=True)
    gate = own / jnp.maximum(jnp.sum(powers, axis=1, keepdims=True), 1e-30)
    g = times(rows, gate_ref[0])
    v = times(rows, up_ref[0])
    sig = jax.nn.sigmoid(g)
    silu = g * sig
    act = (silu * v).astype(bf)
    act_wide = act.astype(f32)
    raw = raw_ref[0]
    d_gate = jnp.sum(act_wide * raw, axis=1, keepdims=True)
    d_act = gate * raw
    d_g = (d_act * v * (sig * (1.0 + g * (1.0 - sig)))).astype(bf)
    d_v = (d_act * silu).astype(bf)
    d_row = times_transposed(d_g, gate_ref[0]) + times_transposed(d_v, up_ref[0])
    high = d_gate.astype(bf).astype(f32)
    scalars = high * marks_ref[0, 1:2, :] + (d_gate - high) * marks_ref[0, 2:3, :]
    lead = back_ref.shape[:-1]
    back_ref[:, :, :, :dim] = d_row.astype(bf).reshape(*lead, dim)
    back_ref[:, :, :, dim:] = scalars.astype(bf).reshape(*lead, 128)
    act_ref[0] = act
    scaled_ref[0] = (gate * act_wide).astype(bf)
    d_g_ref[0] = d_g
    d_v_ref[0] = d_v

    units = down_ref.shape[0]
    s_both = times(moe_ref[...], shared_ref[...])
    s_gate, s_up = s_both[:, :units], s_both[:, units:]
    s_sig = jax.nn.sigmoid(s_gate)
    s_silu = s_gate * s_sig
    s_act = (s_silu * s_up).astype(bf)
    d_sh = times_transposed(cot_ref[...], down_ref[...])
    d_gs = (d_sh * s_up * (s_sig * (1.0 + s_gate * (1.0 - s_sig)))).astype(bf)
    d_both = jnp.concatenate([d_gs, (d_sh * s_silu).astype(bf)], axis=1)
    both_ref[:, :dim] = times_transposed(d_both, shared_ref[...]).astype(bf)
    both_ref[:, dim:] = times(s_act, down_ref[...]).astype(bf)
    s_act_ref[...] = s_act
    d_both_ref[...] = d_both


def expert_late_kernel(
    rows_ref, cot_ref, act_ref, scaled_ref, d_g_ref, d_v_ref, down_ref,
    out_ref, grad_gate_ref, grad_up_ref, grad_down_ref,
):
    bf = jnp.bfloat16
    dim = rows_ref.shape[-1]
    rows = rows_ref[...].reshape(-1, dim)
    cot = cot_ref[...].reshape(-1, dim)
    out_ref[...] = times(act_ref[0], down_ref[0]).astype(bf).reshape(out_ref.shape)
    units = act_ref.shape[-1]
    grad_gate_ref[0] = transposed_times(rows, d_g_ref[0]).astype(bf)
    grad_up_ref[0] = transposed_times(rows, d_v_ref[0]).astype(bf)
    for block in range(dim // units):
        at = block * units
        grad_down_ref[0, at : at + units] = transposed_times(
            scaled_ref[0], cot[:, block * units : block * units + units]
        ).astype(bf)


def expert_slots(shape, start=0):
    return pl.BlockSpec(
        (shape[0], 1) + tuple(shape[2:]), lambda e: (0, e) + (0,) * (len(shape) - 3) + (start,)
    )


def per_expert(shape):
    return pl.BlockSpec((1,) + tuple(shape[1:]), lambda e: (e,) + (0,) * (len(shape) - 1))


def expert_params(flops, moved):
    return dict(
        compiler_params=pltpu.CompilerParams(vmem_limit_bytes=56 << 20),
        cost_estimate=pl.CostEstimate(flops=flops, bytes_accessed=moved, transcendentals=1 << 19),
    )


def expert_early(cot_rows, down, earlier):
    sources, local, cap, _ = cot_rows.shape
    units, dim = down.shape[1:]
    return pl.pallas_call(
        expert_early_kernel,
        grid=(local,),
        in_specs=[
            expert_slots((sources, local, cap, dim)),
            per_expert(down.shape),
            corner_of(earlier),
        ],
        out_specs=per_expert((local, sources * cap, units)),
        out_shape=jax.ShapeDtypeStruct((local, sources * cap, units), jnp.float32),
        name="expert_early",
        **expert_params(64 << 30, 256 << 20),
    )(cot_rows, down, earlier)


def expert_main(rows, cot_rows, raw, gate, up, w_all, marks, moe_all, cot_all, w_shared, w_down):
    sources, local, cap, dim = rows.shape
    units = gate.shape[2]
    count = sources * cap
    hidden = jax.ShapeDtypeStruct((local, count, units), jnp.bfloat16)
    back = (sources, local, cap, dim + 128)
    seq_rows = moe_all.shape[0]
    shared_units = w_down.shape[0]
    share = lambda width: pl.BlockSpec((seq_rows // local, width), lambda e: (e, 0))
    return pl.pallas_call(
        expert_main_kernel,
        grid=(local,),
        in_specs=[
            expert_slots(rows.shape),
            expert_slots((sources, local, cap, 128), dim // 128),
            per_expert(raw.shape),
            per_expert(gate.shape),
            per_expert(up.shape),
            pl.BlockSpec((dim, 128), lambda e: (0, w_all.shape[1] // 128 - 1)),
            per_expert(marks.shape),
            share(dim),
            share(dim),
            whole(w_shared.shape),
            whole(w_down.shape),
        ],
        out_specs=[expert_slots(back)]
        + [per_expert(hidden.shape)] * 4
        + [share(2 * dim), share(shared_units), share(2 * shared_units)],
        out_shape=[jax.ShapeDtypeStruct(back, jnp.bfloat16)]
        + [hidden] * 4
        + [
            jax.ShapeDtypeStruct((seq_rows, width), jnp.bfloat16)
            for width in (2 * dim, shared_units, 2 * shared_units)
        ],
        name="expert_main",
        **expert_params(8 << 30, 20 << 20),
    )(rows, cot_rows, raw, gate, up, w_all, marks, moe_all, cot_all, w_shared, w_down)


def expert_late(rows, cot_rows, act, scaled, d_g, d_v, down):
    sources, local, cap, dim = rows.shape
    units = down.shape[1]
    grads = (local, dim, units)
    return pl.pallas_call(
        expert_late_kernel,
        grid=(local,),
        in_specs=[expert_slots(rows.shape), expert_slots(rows.shape)]
        + [per_expert(act.shape)] * 4
        + [per_expert(down.shape)],
        out_specs=[
            expert_slots(rows.shape),
            per_expert(grads),
            per_expert(grads),
            per_expert(grads),
        ],
        out_shape=[
            jax.ShapeDtypeStruct(rows.shape, jnp.bfloat16),
            jax.ShapeDtypeStruct(grads, jnp.bfloat16),
            jax.ShapeDtypeStruct(grads, jnp.bfloat16),
            jax.ShapeDtypeStruct(grads, jnp.bfloat16),
        ],
        name="expert_late",
        **expert_params(7 << 30, 24 << 20),
    )(rows, cot_rows, act, scaled, d_g, d_v, down)


def assemble_kernel(
    own_out, own_down, side_ref, in_ref, in_gain_ref, out_ref, out_gain_ref,
    grad_in_ref, tail_ref, grad_out_ref, norm_ref, grad_down_ref, gate_ref, up_ref, mid_ref,
):
    f32 = jnp.float32
    groups = side_ref.shape[0]
    inner = groups * WIDE
    bands = out_ref.shape[1] // WIDE
    rows_w = in_ref.shape[0]
    gain = in_gain_ref[...]
    at_down = bands * own_out
    at_mid = at_down + bands * own_down
    at_in = at_mid + rows_w
    units = gate_ref.shape[1] // groups

    def block(group, start, rows):
        return side_ref[group, start : start + rows, :].astype(f32)

    grad_gain = jnp.zeros((rows_w, 1), f32)
    keys = jnp.zeros((rows_w, 256), f32)
    tail = jnp.zeros((rows_w, 128), f32)
    steps = jnp.zeros((rows_w, 128), f32)
    mid = jnp.zeros((rows_w, 128), f32)
    rows, columns = grid_of((128, 128))

    def put(start, values):
        stop = start + values.shape[1]
        grad_in_ref[:, start:stop] = values * gain
        weight = in_ref[:, start:stop].astype(f32)
        return jnp.sum(weight * values, axis=1, keepdims=True)

    for group in range(groups):
        grad_gain += put(group * WIDE, block(group, at_in, rows_w))
        grad_gain += put(inner + group * WIDE, block(group, at_in + rows_w, rows_w))
        last = block(group, at_in + 2 * rows_w, rows_w)
        keys = keys + last[:, :256]
        tail = tail + last[:, 256:]
        moved = mark((rows < HEADS_HERE) & (columns == rows + HEADS_HERE * group))
        steps = steps + times(last[:, 256:].astype(jnp.bfloat16), moved)
        shared = block(group, at_mid, rows_w)
        gate_ref[:, units * group : units * group + units] = shared[:, :units]
        up_ref[:, units * group : units * group + units] = shared[:, units : 2 * units]
        mid = mid + shared[:, 2 * units :]
    grad_gain += put(2 * inner, keys)
    grad_gain += put(2 * inner + 256, steps[:, : groups * HEADS_HERE])
    lane = lax.broadcasted_iota(jnp.int32, tail.shape, 1)
    tail_ref[...] = jnp.where(lane == 0, grad_gain, tail)
    mid_ref[...] = mid

    for group in range(groups):
        sums = jnp.zeros((own_out, 1), f32)
        mine = slice(own_out * group, own_out * group + own_out)
        for band in range(bands):
            wide = slice(WIDE * band, WIDE * band + WIDE)
            values = block(group, own_out * band, own_out)
            grad_out_ref[mine, wide] = values * out_gain_ref[mine, :]
            sums += jnp.sum(out_ref[mine, wide].astype(f32) * values, axis=1, keepdims=True)
            grad_down_ref[own_down * group : own_down * group + own_down, wide] = block(
                group, at_down + own_down * band, own_down
            )
        norm_ref[mine, :] = sums


def assemble(side, in_weight, in_gain, out_weight, out_gain, own_out, own_down):
    groups = side.shape[0]
    rows, width = in_weight.shape
    out_rows, dim = out_weight.shape
    shapes = [
        (rows, width),
        (rows, 128),
        (out_rows, dim),
        (out_rows, 1),
        (groups * own_down, dim),
        (rows, groups * 128),
        (rows, groups * 128),
        (rows, 128),
    ]
    return pl.pallas_call(
        functools.partial(assemble_kernel, own_out, own_down),
        in_specs=[pl.BlockSpec(memory_space=pltpu.VMEM)] * 5,
        out_specs=[pl.BlockSpec(memory_space=pltpu.VMEM)] * len(shapes),
        out_shape=[jax.ShapeDtypeStruct(shape, jnp.float32) for shape in shapes],
        compiler_params=pltpu.CompilerParams(vmem_limit_bytes=40 << 20),
        cost_estimate=pl.CostEstimate(flops=8 << 20, bytes_accessed=12 << 20, transcendentals=0),
        name="assemble",
    )(side, in_weight, in_gain, out_weight, out_gain)


def fold_rows(values, width):
    rest = values[:, width:]
    count = rest.shape[1] * values.shape[0] // width
    parts = [rest[at : at + count] for at in range(0, values.shape[0], count)]
    return jnp.concatenate([values[:, :width], jnp.concatenate(parts, axis=1)], axis=0)


def unfold_rows(values, dim):
    sources, rows, width = values.shape
    count = rows * width // dim
    rest = dim - width
    parts = [values[:, count:, at : at + rest] for at in range(0, width, rest)]
    return jnp.concatenate([values[:, :count], jnp.concatenate(parts, axis=1)], axis=2)


def gather_blocks(values, mates):
    cores = 2
    chips = len(mates) // cores
    column = [values]
    for hop in range(1, chips):
        pairs = [
            (i, (i // cores + hop) % chips * cores + i % cores) for i in range(len(mates))
        ]
        column.append(lax.ppermute(values, "seq", pairs))
    column = jnp.stack(column)
    return column, lax.ppermute(column, "seq", mates)


def halves(values, bit):
    parts = values.reshape(2, values.shape[0] // 2, values.shape[1])
    sent = lax.dynamic_index_in_dim(parts, 1 - bit, 0, keepdims=False)
    return sent, lax.dynamic_index_in_dim(parts, bit, 0, keepdims=False)


def add_other(kept, sent, pairs):
    other = lax.ppermute(sent, "seq", pairs)
    return (kept.astype(jnp.float32) + other.astype(jnp.float32)).astype(jnp.bfloat16)


def halve(values, bit, pairs):
    sent, kept = halves(values, bit)
    return add_other(kept, sent, pairs)


def double(values, bit, pairs):
    other = lax.ppermute(values, "seq", pairs)
    first = jnp.where(bit == 0, values, other)
    second = jnp.where(bit == 0, other, values)
    return jnp.concatenate([first, second], axis=0)


def unpack_kernel(core_ref, own_ref, other_ref, gate_ref, up_ref, down_ref):
    part = pl.program_id(1)
    block = jnp.where(pl.program_id(0) == 0, own_ref[...], other_ref[...]).astype(jnp.float32)
    units = block.shape[1]

    @pl.when(part == 0)
    def _():
        gate_ref[0] = block

    @pl.when(part == 1)
    def _():
        up_ref[0] = block

    @pl.when(part == 2)
    def _():
        for at in range(0, block.shape[0], units):
            down_ref[0, :, at : at + units] = block[at : at + units]


def unpack_expert_grads(own, other, core):
    rows, units = own.shape
    dim = rows // 3
    to_expert = lambda who, part, core: (jnp.where(who == 0, core[0], 1 - core[0]), 0, 0)
    return pl.pallas_call(
        unpack_kernel,
        grid_spec=pltpu.PrefetchScalarGridSpec(
            num_scalar_prefetch=1,
            grid=(2, 3),
            in_specs=[
                pl.BlockSpec((dim, units), lambda who, part, core: (jnp.where(who == 0, part, 2), 0)),
                pl.BlockSpec((dim, units), lambda who, part, core: (jnp.where(who == 0, 0, part), 0)),
            ],
            out_specs=[
                pl.BlockSpec((1, dim, units), to_expert),
                pl.BlockSpec((1, dim, units), to_expert),
                pl.BlockSpec((1, units, dim), to_expert),
            ],
        ),
        out_shape=[
            jax.ShapeDtypeStruct((2, dim, units), jnp.float32),
            jax.ShapeDtypeStruct((2, dim, units), jnp.float32),
            jax.ShapeDtypeStruct((2, units, dim), jnp.float32),
        ],
        compiler_params=pltpu.CompilerParams(vmem_limit_bytes=40 << 20),
        cost_estimate=pl.CostEstimate(flops=1 << 20, bytes_accessed=28 << 20, transcendentals=0),
        name="unpack_expert_grads",
    )(core.reshape(1), own, other)


def on_device(
    block_input,
    lengths,
    routes,
    out_cotangent,
    mixer_gain,
    in_weight,
    conv_weight,
    conv_bias,
    step_bias,
    decay_log,
    skip_gain,
    norm_gain,
    out_weight,
    moe_gain,
    router_weight,
    shared_gate,
    shared_up,
    shared_down,
    expert_gate,
    expert_up,
    expert_down,
):
    sq = lax.axis_size("seq")
    sh = lax.axis_size("shard")
    q = lax.axis_index("seq")
    f32 = jnp.float32
    bf = jnp.bfloat16
    x_low = block_input[0]
    toks, dim = x_low.shape
    seq_rows = toks * sq
    heads = step_bias.shape[0] * sh
    inner = norm_gain.shape[0] * sh
    conv_all = conv_bias.shape[0] * sh
    keys_w = conv_all - inner
    gh = heads // sq
    gw = inner // sq
    rows_w = in_weight.shape[0]
    experts = router_weight.shape[1]
    local_e = expert_gate.shape[0]
    fs = shared_gate.shape[1]
    gf = fs // sq
    taps = conv_weight.shape[0]
    conv_own = conv_bias.shape[0]
    head_own = step_bias.shape[0]

    gain_col = mixer_gain.astype(f32)[:, None]

    def cols(start, width):
        return lax.dynamic_slice_in_dim(in_weight, start, width, 1)

    w_cols = jnp.concatenate(
        [
            cols(q * gw, gw),
            cols(inner + q * gw, gw),
            in_weight[:, 2 * inner : 2 * inner + keys_w],
            cols(2 * inner + keys_w + q * gh, gh),
        ],
        axis=1,
    )
    w_cols = (w_cols.astype(f32) * gain_col).astype(bf)
    used = 2 * gw + keys_w + gh
    small = jnp.concatenate(
        [conv_weight.reshape(-1), conv_bias, step_bias, decay_log, skip_gain, moe_gain]
    )
    small_cols = -(-(small.shape[0] - rows_w) // rows_w)
    at_router = used + small_cols
    total = -(-(at_router + experts) // 128) * 128
    packed = jnp.concatenate(
        [
            w_cols,
            jnp.zeros((rows_w, small_cols), bf),
            router_weight,
            jnp.zeros((rows_w, total - at_router - experts), bf),
        ],
        axis=1,
    )

    def to_shards(values):
        return lax.all_to_all(values, "shard", split_axis=0, concat_axis=0, tiled=True)

    core, z_at = q % 2, q // 2
    mates = [(i, i ^ 1) for i in range(sq)]
    x_column, x_other = gather_blocks(x_low, mates)

    out_scaled = (norm_gain.astype(f32)[:, None] * out_weight.astype(f32)).astype(bf)
    own_out = out_weight.shape[0] // sq
    own_down = shared_down.shape[0] // sq
    piece = jnp.concatenate(
        [
            lax.dynamic_slice_in_dim(out_scaled, q * own_out, own_out, 0),
            lax.dynamic_slice_in_dim(shared_down, q * own_down, own_down, 0),
        ],
        axis=0,
    )
    ratio = sh // sq
    forward_pairs = []
    for a in range(sh):
        for j in range(sq):
            s_to = sq * (a % ratio) + j
            q_to = a // ratio
            forward_pairs.append((j * sh + a, q_to * sh + s_to))
    backward_pairs = [(b, a) for a, b in forward_pairs]
    piece = lax.ppermute(piece, both_axes, forward_pairs)
    shared_cols = jnp.concatenate(
        [
            lax.dynamic_slice_in_dim(shared_gate, q * gf, gf, 1),
            lax.dynamic_slice_in_dim(shared_up, q * gf, gf, 1),
        ],
        axis=1,
    )
    fold = rows_w * 2 * gf // dim
    bands = dim // (2 * gf)
    shared_rows = jnp.concatenate(
        [shared_cols[fold * band : fold * band + fold] for band in range(bands)], axis=1
    )
    own_rows = own_out + own_down
    weights = lax.all_gather(
        jnp.concatenate(
            [
                packed,
                fold_rows(piece[:own_out], total),
                fold_rows(jnp.concatenate([piece[own_out:], shared_rows], axis=0), total),
            ],
            axis=0,
        ),
        "shard",
        axis=0,
    )
    folded = rows_w + own_out * dim // total
    second = unfold_rows(weights[:, folded:], dim)
    w_down = second[:, :own_down].reshape(gf, dim)
    w_shared = (
        second[:, own_down:]
        .reshape(sh, fold, bands, 2 * gf)
        .transpose(0, 2, 1, 3)
        .reshape(dim, 2 * gf)
    )

    route_ids = routes[0]
    expert_ids = jnp.arange(experts, dtype=jnp.int32)
    named = jnp.any(route_ids[:, :, None] == expert_ids[None, None, :], axis=1).astype(f32)
    earlier = (
        jnp.arange(toks)[:, None] > jnp.arange(toks)[None, :]
    ).astype(f32)
    rank = jnp.dot(earlier, named)
    dispatch = (
        (named.T[:, None, :] > 0.0)
        & (rank.T[:, None, :] == jnp.arange(CAP, dtype=f32)[None, :, None])
    ).astype(bf)
    slots = experts * CAP
    dispatch_flat = dispatch.reshape(slots, toks)
    live = (q * toks + jnp.arange(toks, dtype=jnp.int32) < lengths[0]).astype(f32)
    cot = out_cotangent[0].astype(f32) * live[:, None]
    cot_low = cot.astype(bf)

    local_slots = (sh, local_e, CAP)

    def in_slots(values):
        return times(dispatch_flat, values).astype(bf).reshape(sh, local_e * CAP, -1)

    def dispatched(sent):
        return to_shards(sent).reshape(*local_slots, -1)

    router_lane = at_router - (total - 128)
    lanes = jnp.arange(128, dtype=jnp.int32)
    named_lanes = jnp.pad(named, ((0, 0), (router_lane, 128 - router_lane - experts)))
    cot_sent = in_slots(jnp.concatenate([cot_low, named_lanes.astype(bf)], axis=1))
    weights, cot_late = lax.optimization_barrier((weights, cot_sent))
    cot_rows = dispatched(cot_late)
    small = after(jnp.pad(small, (0, total - small.shape[0])), cot_sent)
    small_all = to_shards(jnp.broadcast_to(small[None, None], (sh, 1, total)))[:, 0]

    at = taps * conv_own
    conv_full = (
        small_all[:, :at].reshape(sh, taps, conv_own).transpose(1, 0, 2).reshape(taps, conv_all)
    )
    offset_full = small_all[:, at : at + conv_own].reshape(conv_all)
    at = at + conv_own
    bias_full = small_all[:, at : at + head_own].reshape(heads)
    decay_full = small_all[:, at + head_own : at + 2 * head_own].reshape(heads)
    skip_full = small_all[:, at + 2 * head_own : at + 3 * head_own].reshape(heads)
    gain_at = at + 3 * head_own
    moe_gain_full = small_all[:, gain_at : gain_at + rows_w].reshape(1, dim).astype(f32)
    moe_gain_rows = jnp.broadcast_to(moe_gain_full, (8, dim))

    def group(values, width):
        return lax.dynamic_slice_in_dim(values, q * width, width, values.ndim - 1)

    conv_local = jnp.concatenate([group(conv_full, gw), conv_full[:, inner:]], axis=1).astype(f32)
    offset_local = jnp.concatenate([group(offset_full, gw), offset_full[inner:]]).astype(f32)
    bias_local = group(bias_full, gh).astype(f32)
    decay_local = group(decay_full, gh).astype(f32)
    skip_local = group(skip_full, gh).astype(f32)

    per_head = gw // gh
    taps_in = jnp.concatenate(
        [conv_local, offset_local[None], jnp.zeros((8 - taps - 1, gw + keys_w), f32)], axis=0
    )
    decay_rate = -jnp.exp(decay_local)
    head_in = jnp.pad(jnp.stack([bias_local, decay_rate]), ((0, 6), (0, 128 - gh)))
    skip_in = jnp.broadcast_to(jnp.repeat(skip_local, per_head)[None], (8, gw))
    place_here = jnp.stack([z_at, core]).astype(jnp.int32)
    x_all, proj, x_r, w_all, w_out, mixed, q_low, out_part, square_part, starts = front(
        place_here, x_column, x_other, weights, rows_w, taps_in, head_in, skip_in
    )

    cot_all = lax.all_gather(after(cot_low, x_column), "seq", axis=0, tiled=True)
    square_part = square_part.reshape(sq, toks)
    square_part = after(square_part, corner_after(cot_all, square_part))
    out_sum = lax.psum_scatter(out_part, "seq", scatter_dimension=0, tiled=True)
    square = lax.psum(square_part, "seq")
    q_r = lax.rsqrt(square / inner + epsilon).reshape(seq_rows, 1)
    d_raw = expert_early(cot_rows, expert_down, square)
    tok_r = lax.dynamic_slice_in_dim(q_r, q * toks, toks, 0)
    tok_r = after(tok_r, d_raw)
    x_tok = x_low.astype(f32)
    resid, moe_in, moe_sent, gates = token_front(
        x_low, out_sum, tok_r, moe_gain_rows, dispatch_flat, w_all, named_lanes
    )

    moe_all = lax.all_gather(moe_in, "seq", axis=0, tiled=True)

    rows = dispatched(moe_sent.reshape(sh, local_e * CAP, dim))
    own_ids = lax.axis_index("shard") * local_e + jnp.arange(local_e, dtype=jnp.int32)
    marks = jnp.stack(
        [own_ids + router_lane, own_ids + router_lane, own_ids + router_lane + 64] + [jnp.full_like(own_ids, -1)] * 5, axis=1
    )
    marks = (marks[:, :, None] == lanes[None, None, :]).astype(f32)

    back_rows, e_act, e_scaled, d_g, d_v, both_part, s_act, d_both = expert_main(
        rows,
        cot_rows,
        d_raw,
        expert_gate,
        expert_up,
        w_all,
        marks,
        moe_all,
        cot_all,
        w_shared,
        w_down,
    )
    shared_both = lax.psum_scatter(both_part, "seq", scatter_dimension=0, tiled=True)
    shared_sum = shared_both[:, dim:]
    d_returned = to_shards(back_rows.reshape(sh, local_e * CAP, dim + 128))
    e_out, *e_grads = expert_late(rows, cot_rows, e_act, e_scaled, d_g, d_v, expert_down)
    d_returned, e_out = lax.optimization_barrier((d_returned, e_out))
    returned = to_shards(e_out.reshape(sh, local_e * CAP, dim))

    near = [(i, 2 * ((i // 2) ^ 1) + i % 2) for i in range(sq)]
    far = [(i, 2 * (sq // 2 - 1 - i // 2) + i % 2) for i in range(sq)]
    is_inner = ((z_at == 1) | (z_at == 2)).astype(jnp.int32)
    is_high = (z_at >= 2).astype(jnp.int32)
    e_parts = [
        halve(part[:, at : at + dim // 2].reshape(dim, -1), core, mates)
        for part in e_grads
        for at in (0, dim // 2)
    ]
    e_mine = jnp.concatenate(e_parts, axis=0)
    cutoff = e_mine.shape[0] // 2

    grad_down_part = transposed_times(s_act, cot_all).astype(bf)
    grad_shared_part = transposed_times(moe_all, d_both).astype(bf)
    d_o_ext, d_resid, d_logits, d_moe_gain = token_back(
        d_returned.reshape(slots, dim + 128),
        dispatch_flat,
        shared_both,
        x_low,
        resid,
        after(gates, grad_down_part, grad_shared_part, *e_parts),
        w_all,
        moe_gain_rows,
        cot_low,
    )
    grad_router = jnp.dot(moe_in.astype(f32).T, d_logits, precision=highest)
    grad_router = lax.optimization_barrier(grad_router)
    d_o_all = lax.all_gather(d_o_ext, "seq", axis=0, tiled=True)

    sent_one, kept_one = halves(e_mine[:cutoff], is_inner)
    sent_two, kept_two = halves(e_mine[cutoff:], is_high)
    d_o_all, sent_one, sent_two = lax.optimization_barrier((d_o_all, sent_one, sent_two))
    grad_out_part = transposed_times(q_low, (q_r * d_o_all[:, :dim].astype(f32)).astype(bf))

    row_values = jnp.concatenate(
        [q_r, x_r, jnp.zeros((seq_rows, 6), f32)], axis=1
    )
    scan_inputs = (proj, mixed, d_o_all, row_values, starts, taps_in)
    scan_inputs = scan_inputs + (head_in, skip_in, w_all, w_out)
    chunks = seq_rows // CHUNK
    middle = chunks - 2
    *held, carry, sums = scan_backward(
        (middle, chunks),
        scan_inputs,
        (),
        jnp.zeros((136, gw + keys_w), f32),
        jnp.zeros((24, gw + keys_w), f32),
    )
    moe_column = jnp.pad(d_moe_gain[0][:, None], ((0, 0), (0, 127)))
    grad_router = grad_router + after(moe_column, corner_after(returned, carry))
    mid_part = jnp.concatenate(
        [
            grad_shared_part,
            grad_router.astype(bf),
        ],
        axis=1,
    )
    lane_w = mid_part.shape[1]
    bands = dim // lane_w

    def to_bands(values):
        return jnp.concatenate(
            [values[:, :, band * lane_w : band * lane_w + lane_w] for band in range(bands)], axis=1
        )

    early_part = jnp.concatenate(
        [
            to_bands(grad_out_part.astype(bf).reshape(sh, own_out, dim)),
            to_bands(grad_down_part.reshape(sh, own_down, dim)),
            mid_part.reshape(sh, rows_w, lane_w),
        ],
        axis=1,
    )
    moved_early = to_shards(early_part)
    e_one = add_other(kept_one, sent_one, near)
    e_two = add_other(kept_two, sent_two, far)
    carry = after(carry, e_one, e_two)
    d_proj, back_part, carry, sums = scan_backward((0, middle), scan_inputs, held, carry, sums)
    d_taps, d_head, d_skip = sums[0:8], sums[8:16, :128], sums[16:24, :gw]
    grad_conv_local = d_taps[:taps]
    grad_offset_local = d_taps[taps]
    grad_bias_local = d_head[0, :gh]
    grad_decay_local = d_head[1, :gh] * decay_rate
    grad_skip_local = jnp.sum(d_skip[0].reshape(gh, per_head), axis=1)
    sent_one, kept_one = halves(e_one, is_high)
    sent_two, kept_two = halves(e_two, is_inner)
    e_one = add_other(kept_one, sent_one, far)
    e_two = add_other(kept_two, sent_two, near)
    back_sum = lax.psum_scatter(back_part, "seq", scatter_dimension=0, tiled=True).astype(f32)
    route_gates = gates[:, router_lane : router_lane + experts]
    weighted = (route_gates.T[:, None, :] * dispatch.astype(f32)).reshape(slots, toks)
    combined = transposed_times(weighted.astype(bf), returned.reshape(slots, dim))
    block_output = ((resid + shared_sum.astype(f32) + combined) * live[:, None]).astype(bf)[None]
    tok_x_r = row_scale(x_tok)
    x_n = x_tok * tok_x_r
    input_grad = (
        d_resid + back_sum - x_n * (tok_x_r * jnp.mean(back_sum * x_tok, axis=1, keepdims=True))
    )[None]

    grad_in_part = transposed_times(x_all, d_proj).astype(bf)

    def spread(local, count):
        wide = jnp.zeros(local.shape[:-1] + (count,), f32)
        return lax.dynamic_update_slice_in_dim(wide, local, q * local.shape[-1], local.ndim - 1)

    conv_rows = jnp.concatenate([grad_conv_local, grad_offset_local[None]], axis=0)
    conv_wide = jnp.concatenate([spread(conv_rows[:, :gw], inner), conv_rows[:, gw:]], axis=1)
    head_wide = spread(jnp.stack([grad_bias_local, grad_decay_local, grad_skip_local]), heads)
    small_part = jnp.concatenate(
        [
            conv_wide.reshape(taps + 1, sh, conv_own).transpose(1, 0, 2).reshape(sh, -1),
            head_wide.reshape(3, sh, head_own).transpose(1, 0, 2).reshape(sh, -1),
        ],
        axis=1,
    )
    small_part = after(small_part, e_one, e_two)
    small_count = small_part.shape[1]
    small_part = jnp.pad(
        small_part, ((0, 0), (0, rows_w * small_cols - small_count))
    ).reshape(sh, rows_w, small_cols)
    last_part = grad_in_part + jnp.pad(
        small_part.reshape(dim, small_cols), ((0, 0), (used, total - used - small_cols))
    )
    last_part = last_part.astype(bf)
    last_part, moved_early = lax.optimization_barrier((last_part, moved_early))
    early_sum = jnp.sum(moved_early.astype(f32), axis=0).astype(bf)
    rows_sum = lax.ppermute(early_sum[: bands * own_rows], both_axes, backward_pairs)
    e_one, e_two, last_part = lax.optimization_barrier((e_one, e_two, last_part))
    e_one, e_two = double(e_one, is_high, far), double(e_two, is_inner, near)
    e_one, e_two = double(e_one, is_inner, near), double(e_two, is_high, far)
    moved_last = to_shards(last_part.reshape(sh, rows_w, total))
    last_sum = jnp.sum(moved_last.astype(f32), axis=0)
    last_sum = after(last_sum, e_one, e_two).astype(bf)
    rows_sum = after(rows_sum, e_one)
    e_mine = jnp.concatenate([e_one, e_two], axis=0)
    e_other = lax.ppermute(e_mine, "seq", mates)
    grad_e_gate, grad_e_up, grad_e_down = unpack_expert_grads(e_mine, e_other, core)
    side = lax.all_gather(
        jnp.concatenate(
            [rows_sum, early_sum[bands * own_rows :]]
            + [last_sum[:, lane_w * i : lane_w * i + lane_w] for i in range(total // lane_w)],
            axis=0,
        ),
        "seq",
        axis=0,
    )
    gain_out = norm_gain.astype(f32)[:, None]
    (
        grad_in,
        tail_sums,
        grad_out,
        norm_sums,
        grad_down,
        grad_shared_gate,
        grad_shared_up,
        mid_sums,
    ) = assemble(side, in_weight, gain_col, out_weight, gain_out, own_out, own_down)
    grad_norm = norm_sums[:, 0]
    grad_router_weight = mid_sums[:, router_lane : router_lane + experts]
    grad_moe_gain = mid_sums[:, 0]
    grad_mixer_gain = tail_sums[:, 0]
    lane_at = used - (total - 128)
    small_sum = tail_sums[:, lane_at : lane_at + small_cols].reshape(-1)
    at = taps * conv_own
    grad_conv = small_sum[:at].reshape(taps, conv_own)
    grad_offset = small_sum[at : at + conv_own]
    at = at + conv_own
    grad_bias = small_sum[at : at + head_own]
    grad_decay = small_sum[at + head_own : at + 2 * head_own]
    grad_skip = small_sum[at + 2 * head_own : at + 3 * head_own]
    return (
        block_output,
        input_grad,
        grad_mixer_gain,
        grad_in,
        grad_conv,
        grad_offset,
        grad_bias,
        grad_decay,
        grad_skip,
        grad_norm,
        grad_out,
        grad_moe_gain,
        grad_router_weight,
        grad_shared_gate,
        grad_shared_up,
        grad_down,
        grad_e_gate,
        grad_e_up,
        grad_e_down,
    )


def solution(mesh):
    placed = (
        P("shard", "seq", None),
        P("shard"),
        P("shard", "seq", None),
        P("shard", "seq", None),
        P("shard"),
        P("shard", None),
        P(None, "shard"),
        P("shard"),
        P("shard"),
        P("shard"),
        P("shard"),
        P("shard"),
        P("shard", None),
        P("shard"),
        P("shard", None),
        P("shard", None),
        P("shard", None),
        P("shard", None),
        P("shard", None, None),
        P("shard", None, None),
        P("shard", None, None),
    )
    return jax.shard_map(
        on_device,
        mesh=mesh,
        in_specs=placed,
        out_specs=(
            P("shard", "seq", None),
            P("shard", "seq", None),
            P("shard"),
            P("shard", None),
            P(None, "shard"),
            P("shard"),
            P("shard"),
            P("shard"),
            P("shard"),
            P("shard"),
            P("shard", None),
            P("shard"),
            P("shard", None),
            P("shard", None),
            P("shard", None),
            P("shard", None),
            P("shard", None, None),
            P("shard", None, None),
            P("shard", None, None),
        ),
        check_vma=False,
    )
```
